256 devices in a mesh: img: 8 (over z_lo, core), txt: 32 (over z_hi, y, x).
Axes of the slice: x: 4, y: 4, z: 8 (z_hi: 2, z_lo: 4; z = z_hi * 4 + z_lo), core: 2. Of those that a mesh axis runs over, the one named last changes fastest.
Arguments:
- image_emb: bfloat16 [16384, 1280], P(('img', 'txt')), may hold values from -1 to 1
- text_emb: bfloat16 [16384, 1280], P(('txt', 'img')), may hold values from -1 to 1
- logit_scale: float32 [1], replicated, may hold values from 15 to 30
Outputs:
- mean_loss: float32 [1], replicated
- image_grad: bfloat16 [16384, 1280], P(('img', 'txt'))
- text_grad: bfloat16 [16384, 1280], P(('txt', 'img'))
The draws below stay inside these ranges and needn't reach their ends.
All inputs are finite; a program needn't handle non-finite values.
Results may differ from the reference program's by a relative error of at most 0.023.
Values may be sent and summed in bfloat16 or wider, within the bound.
No kernel may reach another device: no remote copies, remote signals or barrier semaphores. Data moves between devices by JAX's collectives and lax.ppermute only.
A program may use at most 64 MiB of HBM per device.

```python
import math
import jax
import jax.numpy as jnp
from jax import lax

EMBED = 1280
ROWS_DEV = 64
BATCH = 16384
N_IMG = 8
N_TXT = 32


def shared_parts(key):
    key_image = jax.random.fold_in(key, 11)
    key_text = jax.random.fold_in(key, 12)
    key_iscale = jax.random.fold_in(key, 13)
    key_tscale = jax.random.fold_in(key, 14)
    root = jnp.sqrt(jnp.float32(EMBED))
    image_noise = jnp.clip(jax.random.normal(key_image, (BATCH, EMBED), jnp.float32), -4.0, 4.0) / root
    text_noise = jnp.clip(jax.random.normal(key_text, (BATCH, EMBED), jnp.float32), -4.0, 4.0) / root
    image_scale = jnp.exp(jax.random.uniform(key_iscale, (BATCH, 1), jnp.float32, jnp.log(0.35), jnp.log(3.5)))
    text_scale = jnp.exp(jax.random.uniform(key_tscale, (BATCH, 1), jnp.float32, jnp.log(0.35), jnp.log(3.5)))
    image_rows = image_scale * image_noise
    text_rows = text_scale * (text_noise + 0.3 * image_noise)
    return (jnp.clip(image_rows, -1.0, 1.0), jnp.clip(text_rows, -1.0, 1.0))


def draw_image_emb(key, part):
    image_rows, text_rows = shared_parts(key)
    return image_rows.astype(jnp.bfloat16)


def draw_text_emb(key, part):
    image_rows, text_rows = shared_parts(key)
    return text_rows.astype(jnp.bfloat16)


def setup_inputs(seed: int = 0) -> dict:
    streams_of = jax.random.split(jax.random.key(seed), 4)
    return {
        "image_emb": draw_image_emb(jax.random.fold_in(streams_of[3], 71), 0),
        "text_emb": draw_text_emb(jax.random.fold_in(streams_of[3], 71), 0),
        "logit_scale": jnp.clip(jnp.exp(jax.random.uniform(streams_of[2], (1,), jnp.float32, math.log(15.0), math.log(30.0))), 15.0, 30.0),
    }


def reference(image_emb, text_emb, logit_scale):
    multiplier = logit_scale[0]
    row_count = ROWS_DEV * N_TXT
    col_count = ROWS_DEV * N_IMG
    image_slabs = image_emb.reshape(N_IMG, row_count, EMBED)
    text_slabs = text_emb.reshape(BATCH // col_count, col_count, EMBED)

    def logits(image_slab):
        return multiplier * jnp.dot(image_slab, text_emb.T, preferred_element_type=jnp.float32)

    def first_pass(state_pair, image_slab):
        col_top, col_total = state_pair
        tile_vals = logits(image_slab)
        row_top = jnp.max(tile_vals, axis=1)
        row_lse = row_top + jnp.log(jnp.sum(jnp.exp(tile_vals - row_top[:, None]), axis=1))
        new_top = jnp.maximum(col_top, jnp.max(tile_vals, axis=0))
        col_total = col_total * jnp.exp(col_top - new_top) + jnp.sum(jnp.exp(tile_vals - new_top[None, :]), axis=0)
        return (new_top, col_total), row_lse

    start_pair = (jnp.full((BATCH,), -jnp.inf, jnp.float32), jnp.zeros((BATCH,), jnp.float32))
    (col_top, col_total), row_lse = lax.scan(first_pass, start_pair, image_slabs)
    col_lse = col_top + jnp.log(col_total)
    matched = multiplier * jnp.sum(image_emb.astype(jnp.float32) * text_emb.astype(jnp.float32), axis=1)
    mean_loss = jnp.sum(row_lse.reshape(BATCH) + col_lse - 2.0 * matched) / (2.0 * BATCH)
    columns = jnp.arange(BATCH, dtype=jnp.int32)

    def second_pass(running, inputs):
        image_slab, slab_lse, position = inputs
        tile_vals = logits(image_slab)
        row_ids = position * row_count + jnp.arange(row_count, dtype=jnp.int32)
        labels = (row_ids[:, None] == columns[None, :]).astype(jnp.float32)
        weights = (0.5 * jnp.exp(tile_vals - slab_lse[:, None]) + 0.5 * jnp.exp(tile_vals - col_lse[None, :]) - labels).astype(jnp.bfloat16)
        parted = jnp.transpose(weights.reshape(row_count, BATCH // col_count, col_count), (1, 0, 2))

        def column_term(image_sum, pair):
            weight_part, text_slab = pair
            term = (multiplier * jnp.dot(weight_part, text_slab, preferred_element_type=jnp.float32)).astype(jnp.bfloat16)
            term = lax.optimization_barrier(term)
            return image_sum + term.astype(jnp.float32), None

        image_sum, _ = lax.scan(column_term, jnp.zeros((row_count, EMBED), jnp.float32), (parted, text_slabs))
        text_term = (multiplier * jnp.dot(weights.T, image_slab, preferred_element_type=jnp.float32)).astype(jnp.bfloat16)
        text_term = lax.optimization_barrier(text_term)
        return running + text_term.astype(jnp.float32), image_sum.astype(jnp.bfloat16)

    text_sum, image_parts = lax.scan(second_pass, jnp.zeros((BATCH, EMBED), jnp.float32),
                                     (image_slabs, row_lse, jnp.arange(N_IMG, dtype=jnp.int32)))
    image_grad = image_parts.reshape(BATCH, EMBED)
    return mean_loss.reshape(1), image_grad, text_sum.astype(jnp.bfloat16)
```

```python
import jax
import jax.numpy as jnp
from jax import lax
from jax.sharding import Mesh, PartitionSpec as P

AXES = ("zl", "core", "zh", "y", "x")
NX, NY, NZ = 4, 4, 8
Z_SHIFTS = (0, 1, -1, 2)
Z_OFFSETS = tuple((-k + 4 * h) % NZ for k in Z_SHIFTS for h in range(2))


def plane_shift(v, k, primary):
    pairs = []
    for c in range(2):
        for h in range(2):
            for y in range(NY):
                for x in range(NX):
                    if (c == 0) == primary:
                        to = (y, (x + k) % NX)
                    else:
                        to = ((y + k) % NY, x)
                    base = (c * 2 + h) * NY
                    pairs.append(((base + y) * NX + x, (base + to[0]) * NX + to[1]))
    return lax.ppermute(v, ("core", "zh", "y", "x"), pairs)


def z_index(z):
    return (z % 4) * 2 + z // 4


def z_shift(v, k):
    return lax.ppermute(v, ("zl", "zh"), [(z_index(z), z_index((z + k) % NZ)) for z in range(NZ)])


def core_swap(v):
    return lax.ppermute(v, "core", [(0, 1), (1, 0)])


def lse(parts):
    top = parts[0]
    for p in parts[1:]:
        top = jnp.maximum(top, p)
    total = sum(jnp.exp(p - top) for p in parts)
    return top + jnp.log(total)


def add(parts):
    return sum(p.astype(jnp.float32) for p in parts)


def local(image_emb, text_emb, logit_scale):
    bf16, f32 = jnp.bfloat16, jnp.float32
    multiplier = logit_scale[0]
    rows = image_emb.shape[0]
    zl, core, zh = lax.axis_index("zl"), lax.axis_index("core"), lax.axis_index("zh")
    y, x = lax.axis_index("y"), lax.axis_index("x")
    z = zh * 4 + zl

    pair = jnp.concatenate([text_emb, z_shift(text_emb, 4)])
    own = jnp.concatenate([image_emb] + [plane_shift(image_emb, k, True) for k in (1, 2, 3)])
    text_own = jnp.concatenate([pair] + [z_shift(pair, k) for k in Z_SHIFTS[1:]])
    image_block = jnp.concatenate([own] + [plane_shift(own, k, False) for k in (1, 2, 3)])
    text_block = jnp.concatenate([text_own, core_swap(text_own)])

    steps = jnp.arange(4, dtype=jnp.int32)
    prim, second = steps[None, :], steps[:, None]
    row_x = jnp.where(core == 0, x - prim, x - second) % NX
    row_y = jnp.where(core == 0, y - second, y - prim) % NY
    row_blocks = ((zl * 2 + core) * 2 + zh) * 16 + row_y * 4 + row_x
    col_z = (z + jnp.array(Z_OFFSETS, jnp.int32)) % NZ
    cores = jnp.stack([core, 1 - core])[:, None]
    col_blocks = ((col_z // 4) * 16 + y * 4 + x) * 8 + (col_z % 4) * 2 + cores
    span = jnp.arange(rows, dtype=jnp.int32)
    row_ids = (row_blocks.reshape(16, 1) * rows + span).reshape(-1)
    col_ids = (col_blocks.reshape(16, 1) * rows + span).reshape(-1)
    matches = row_ids[:, None] == col_ids[None, :]

    logits = multiplier * lax.dot_general(
        image_block, text_block, (((1,), (1,)), ((), ())), preferred_element_type=f32
    )
    row_top = jnp.max(logits, axis=1)
    col_top = jnp.max(logits, axis=0)
    row_part = row_top + jnp.log(jnp.sum(jnp.exp(logits - row_top[:, None]), axis=1))
    col_part = col_top + jnp.log(jnp.sum(jnp.exp(logits - col_top[None, :]), axis=0))
    matched = jnp.sum(jnp.where(matches, logits, 0.0))

    r = row_part.reshape(4, 4, rows)
    r = lse([r] + [jnp.roll(plane_shift(r, k, True), k, axis=1) for k in (1, 2, 3)])
    r = lse([r] + [jnp.roll(plane_shift(r, k, False), k, axis=0) for k in (1, 2, 3)])
    row_lse = r.reshape(-1)
    order = {o: i for i, o in enumerate(Z_OFFSETS)}

    def align(v, k):
        return jnp.stack([v[:, order[(o + k) % NZ]] for o in Z_OFFSETS], axis=1)

    q = col_part.reshape(2, 8, rows)
    q = lse([q, align(z_shift(q, 4), 4)])
    q = lse([q] + [align(z_shift(q, k), k % NZ) for k in Z_SHIFTS[1:]])
    other = core_swap(q)
    q = lse([q, jnp.stack([other[1], other[0]])])
    col_lse = q.reshape(-1)

    weights = (
        0.5 * jnp.exp(logits - row_lse[:, None])
        + 0.5 * jnp.exp(logits - col_lse[None, :])
        - matches.astype(f32)
    ).astype(bf16)

    text_part = (
        multiplier
        * lax.dot_general(weights, image_block, (((0,), (0,)), ((), ())), preferred_element_type=f32)
    ).astype(bf16)
    half = 8 * rows
    t = add([text_part[:half], core_swap(text_part[half:])]).astype(bf16)
    image_part = (multiplier * jnp.dot(weights, text_block, preferred_element_type=f32)).astype(bf16)
    chunk = 4 * rows
    g = add(
        [image_part[:chunk]]
        + [plane_shift(image_part[k * chunk : (k + 1) * chunk], -k, False) for k in (1, 2, 3)]
    ).astype(bf16)
    t = add(
        [t[: 2 * rows]]
        + [
            z_shift(t[2 * i * rows : 2 * (i + 1) * rows], -k)
            for i, k in enumerate(Z_SHIFTS)
            if i
        ]
    ).astype(bf16)
    image_grad = add(
        [g[:rows]] + [plane_shift(g[k * rows : (k + 1) * rows], -k, True) for k in (1, 2, 3)]
    ).astype(bf16)
    text_grad = add([t[:rows], z_shift(t[rows:], 4)]).astype(bf16)

    share = jnp.sum(row_lse) / 16.0 + jnp.sum(col_lse) / 16.0 - 2.0 * matched
    s = jnp.broadcast_to(share, (8, 128))
    for bit in (1, 2):
        s = s + lax.ppermute(s, "x", [(i, i ^ bit) for i in range(NX)])
        s = s + lax.ppermute(s, "y", [(i, i ^ bit) for i in range(NY)])
    for bit in (1, 2, 4):
        s = s + lax.ppermute(s, ("zl", "zh"), [(z_index(i), z_index(i ^ bit)) for i in range(NZ)])
    s = s + core_swap(s)
    mean_loss = (s[0, :1] / (2.0 * rows * 256)).reshape(1)
    return mean_loss, image_grad, text_grad


def solution(mesh):
    fine = Mesh(mesh.devices.reshape(4, 2, 2, 4, 4), AXES)
    return jax.shard_map(
        local,
        mesh=fine,
        in_specs=(P(AXES, None), P(("zh", "y", "x", "zl", "core"), None), P()),
        out_specs=(P(), P(AXES, None), P(("zh", "y", "x", "zl", "core"), None)),
        check_vma=False,
    )
```

```python
import jax
import jax.numpy as jnp
from jax import lax
from jax.experimental import pallas as pl
from jax.experimental.pallas import tpu as pltpu
from jax.sharding import Mesh, PartitionSpec as P

AXES = ("zl", "core", "zh", "y", "x")
NX, NY, NZ = 4, 4, 8
ROWS, EMBED = 64, 1280
CHUNK = 4 * ROWS
BLOCK = 16 * ROWS
BF16, F32 = jnp.bfloat16, jnp.float32
VMEM = pl.BlockSpec(memory_space=pltpu.VMEM)
SMEM = pl.BlockSpec(memory_space=pltpu.SMEM)
PARAMS = pltpu.CompilerParams(vmem_limit_bytes=36 * 1024 * 1024)


def plane_shift(v, k, primary):
    pairs = []
    for c in range(2):
        for h in range(2):
            for y in range(NY):
                for x in range(NX):
                    if (c == 0) == primary:
                        to = (y, (x + k) % NX)
                    else:
                        to = ((y + k) % NY, x)
                    base = (c * 2 + h) * NY
                    pairs.append(((base + y) * NX + x, (base + to[0]) * NX + to[1]))
    return lax.ppermute(v, ("core", "zh", "y", "x"), pairs)


def z_index(z):
    return (z % 4) * 2 + z // 4


def z_shift(v, k):
    pairs = []
    for c in range(2):
        for z in range(NZ):
            to = (z + (k if c == 0 else -k)) % NZ
            pairs.append((((z % 4) * 2 + c) * 2 + z // 4, ((to % 4) * 2 + c) * 2 + to // 4))
    return lax.ppermute(v, ("zl", "core", "zh"), pairs)


def core_swap(v):
    return lax.ppermute(v, "core", [(0, 1), (1, 0)])


def flip(v, axis, bit):
    if axis == "z":
        return lax.ppermute(v, ("zl", "zh"), [(z_index(i), z_index(i ^ bit)) for i in range(NZ)])
    return lax.ppermute(v, axis, [(i, i ^ bit) for i in range(lax.axis_size(axis))])


def lse2(a, b):
    top = jnp.maximum(a, b)
    return top + jnp.log(jnp.exp(a - top) + jnp.exp(b - top))


def row_place(where, a, b):
    zl, c, zh, y, x = where
    p, s = jnp.where(c == 0, b, a), jnp.where(c == 0, a, b)
    n = ((y - s) & 3) * 4 + ((x - p) & 3)
    return n, ((zl * 2 + c) * 2 + zh) * 16 + n


def col_place(where, j, i):
    zl, c, zh, y, x = where
    core = c if j < 2 else 1 - c
    sign = 1 - 2 * core
    off = sign * ((0, 0, 2, 2)[i] + j % 2) + (0, 4, 0, 4)[i]
    z = (zh * 4 + zl + off) & 7
    return z * 2 + core, ((z >> 2) * 16 + y * 4 + x) * 8 + (z & 3) * 2 + core


def row_ids(where, a):
    span = lax.broadcasted_iota(jnp.int32, (ROWS, 128), 0)
    return [row_place(where, a, b)[1] * ROWS + span for b in range(4)]


def col_ids(where):
    lane = lax.broadcasted_iota(jnp.int32, (8, 128), 1)
    out = []
    for t in range(8):
        lo = col_place(where, t // 2, (t % 2) * 2)[1] * ROWS
        hi = col_place(where, t // 2, (t % 2) * 2 + 1)[1] * ROWS - ROWS
        out.append(lane + jnp.where(lane < ROWS, lo, hi))
    return out


def pack_body(n, *refs):
    at = 0
    for r in refs[:n]:
        refs[n][at : at + r.shape[0], :] = r[...]
        at += r.shape[0]


def pack(*parts):
    rows = sum(p.shape[0] for p in parts)
    return pl.pallas_call(
        lambda *refs: pack_body(len(parts), *refs),
        out_shape=jax.ShapeDtypeStruct((rows, EMBED), BF16),
        in_specs=[VMEM] * len(parts),
        out_specs=VMEM,
        compiler_params=PARAMS,
    )(*parts)


def logits_body(place, scale, *refs):
    images, texts = refs[:4], refs[4:8]
    logits, row_out, col_out, match_out = refs[8:12]
    row_wide = refs[12]
    where = [place[i] for i in range(5)]
    multiplier = scale[0]
    for a in range(4):
        for j in range(4):
            logits[a * CHUNK : (a + 1) * CHUNK, j * CHUNK : (j + 1) * CHUNK] = (
                multiplier
                * lax.dot_general(
                    images[a][...],
                    texts[j][...],
                    (((1,), (1,)), ((), ())),
                    preferred_element_type=F32,
                )
            )
    cols = col_ids(where)
    step = 32
    matched = jnp.zeros((8, 128), F32)
    col_top = [jnp.full((8, 128), -jnp.inf, F32) for _ in range(8)]
    for a in range(4):
        ids = row_ids(where, a)
        for b in range(4):
            for half in range(ROWS // step):
                at = a * CHUNK + b * ROWS + half * step
                tiles = [logits[at : at + step, t * 128 : (t + 1) * 128] for t in range(8)]
                top = tiles[0]
                for t in range(1, 8):
                    top = jnp.maximum(top, tiles[t])
                top = jnp.max(top, axis=1, keepdims=True)
                mine = ids[b][half * step : (half + 1) * step]
                total = jnp.zeros((step, 128), F32)
                for t in range(8):
                    total += jnp.exp(tiles[t] - top)
                    folded = tiles[t].reshape(step // 8, 8, 128)
                    col_top[t] = jnp.maximum(col_top[t], jnp.max(folded, axis=0))
                    hit = jnp.where(mine == cols[t][0:1], tiles[t], 0.0)
                    matched += jnp.sum(hit.reshape(step // 8, 8, 128), axis=0)
                part = top + jnp.log(jnp.sum(total, axis=1, keepdims=True))
                row_wide[at : at + step, :] = jnp.broadcast_to(part, (step, 128))
    match_out[...] = jnp.broadcast_to(jnp.sum(matched, keepdims=True), (8, 128))
    col_out[...] = jnp.zeros((16, 128), F32)
    row_out[...] = jnp.zeros((16, 128), F32)
    for t in range(8):
        top = jnp.max(col_top[t], axis=0, keepdims=True)

        def cols_pass(i, total, t=t, top=top):
            tile = logits[pl.ds(pl.multiple_of(i * 128, 128), 128), t * 128 : (t + 1) * 128]
            return total + jnp.sum(jnp.exp(tile - top).reshape(16, 8, 128), axis=0)

        total = lax.fori_loop(0, 8, cols_pass, jnp.zeros((8, 128), F32), unroll=True)
        part = top + jnp.log(jnp.sum(total, axis=0, keepdims=True))
        j, i = t // 2, (t % 2) * 2
        col_out[pl.ds(col_place(where, j, i)[0], 1), :] = part
        col_out[pl.ds(col_place(where, j, i + 1)[0], 1), :] = pltpu.roll(part, 64, 1)
        line = jnp.transpose(row_wide[t * 128 : (t + 1) * 128, :])[0:1]
        row_out[pl.ds(row_place(where, j, i)[0], 1), :] = line
        row_out[pl.ds(row_place(where, j, i + 1)[0], 1), :] = pltpu.roll(line, 64, 1)


def logits_call(place, scale, images, texts):
    return pl.pallas_call(
        logits_body,
        out_shape=(
            jax.ShapeDtypeStruct((BLOCK, BLOCK), F32),
            jax.ShapeDtypeStruct((16, 128), F32),
            jax.ShapeDtypeStruct((16, 128), F32),
            jax.ShapeDtypeStruct((8, 128), F32),
        ),
        in_specs=[SMEM, SMEM] + [VMEM] * 8,
        out_specs=(VMEM,) * 4,
        scratch_shapes=[pltpu.VMEM((BLOCK, 128), F32)],
        compiler_params=PARAMS,
    )(place, scale, *images, *texts)


def text_body(place, scale, logits, row_lse, col_lse, *refs):
    images = refs[:4]
    weights = refs[4]
    outs = refs[5:9]
    row_wide = refs[9]
    where = [place[i] for i in range(5)]
    multiplier = scale[0]
    lane = lax.broadcasted_iota(jnp.int32, (1, 128), 1)
    cols = col_ids(where)
    col_line = []
    for t in range(8):
        j, i = t // 2, (t % 2) * 2
        lo = col_lse[pl.ds(col_place(where, j, i)[0], 1), :]
        hi = col_lse[pl.ds(col_place(where, j, i + 1)[0], 1), :]
        col_line.append(jnp.where(lane < ROWS, lo, pltpu.roll(hi, 64, 1)))
        lo = row_lse[pl.ds(row_place(where, j, i)[0], 1), :]
        hi = row_lse[pl.ds(row_place(where, j, i + 1)[0], 1), :]
        line = jnp.where(lane < ROWS, lo, pltpu.roll(hi, 64, 1))
        row_wide[t * 128 : (t + 1) * 128, :] = jnp.transpose(jnp.broadcast_to(line, (128, 128)))
    for a in range(4):
        ids = row_ids(where, a)
        for b in range(4):
            at = a * CHUNK + b * ROWS
            wide = row_wide[at : at + ROWS, :]
            for t in range(8):
                tile = logits[at : at + ROWS, t * 128 : (t + 1) * 128]
                both = 0.5 * jnp.exp(tile - wide) + 0.5 * jnp.exp(tile - col_line[t])
                both = both - jnp.where(ids[b] == cols[t][0:1], 1.0, 0.0)
                weights[at : at + ROWS, t * 128 : (t + 1) * 128] = both.astype(BF16)
    for j in (3, 2, 1, 0):
        for e in range(5):
            acc = None
            for a in range(4):
                term = lax.dot_general(
                    weights[a * CHUNK : (a + 1) * CHUNK, j * CHUNK : (j + 1) * CHUNK],
                    images[a][:, e * 256 : (e + 1) * 256],
                    (((0,), (0,)), ((), ())),
                    preferred_element_type=F32,
                )
                acc = term if acc is None else acc + term
            outs[j][:, e * 256 : (e + 1) * 256] = (multiplier * acc).astype(BF16)


def text_call(place, scale, logits, row_lse, col_lse, images):
    part = jax.ShapeDtypeStruct((CHUNK, EMBED), BF16)
    return pl.pallas_call(
        text_body,
        out_shape=(jax.ShapeDtypeStruct((BLOCK, BLOCK), BF16), part, part, part, part),
        in_specs=[SMEM, SMEM] + [VMEM] * 7,
        out_specs=(VMEM,) * 5,
        scratch_shapes=[pltpu.VMEM((BLOCK, 128), F32)],
        compiler_params=PARAMS,
    )(place, scale, logits, row_lse, col_lse, *images)


def image_body(scale, weights, *refs):
    texts, outs = refs[:4], refs[4:]
    multiplier = scale[0]
    for a in (2, 1, 3, 0):
        for e in range(5):
            acc = None
            for j in range(4):
                term = jnp.dot(
                    weights[a * CHUNK : (a + 1) * CHUNK, j * CHUNK : (j + 1) * CHUNK],
                    texts[j][:, e * 256 : (e + 1) * 256],
                    preferred_element_type=F32,
                )
                acc = term if acc is None else acc + term
            outs[a][:, e * 256 : (e + 1) * 256] = (multiplier * acc).astype(BF16)


def image_call(scale, weights, texts):
    part = jax.ShapeDtypeStruct((CHUNK, EMBED), BF16)
    return pl.pallas_call(
        image_body,
        out_shape=(part,) * 4,
        in_specs=[SMEM] + [VMEM] * 5,
        out_specs=(VMEM,) * 4,
        compiler_params=PARAMS,
    )(scale, weights, *texts)


def add_body(n, *refs):
    outs = refs[n:]
    rows = outs[0].shape[0]
    for o, out in enumerate(outs):
        for at in range(0, rows, 16):
            total = refs[0][o * rows + at : o * rows + at + 16, :].astype(F32)
            for r in refs[1:n]:
                total += r[o * rows + at : o * rows + at + 16, :].astype(F32)
            out[at : at + 16, :] = total.astype(out.dtype)


def add(parts, pieces=1):
    rows = parts[0].shape[0] // pieces
    out = pl.pallas_call(
        lambda *refs: add_body(len(parts), *refs),
        out_shape=(jax.ShapeDtypeStruct((rows, EMBED), BF16),) * pieces,
        in_specs=[VMEM] * len(parts),
        out_specs=(VMEM,) * pieces,
        compiler_params=PARAMS,
    )(*parts)
    return out if pieces > 1 else out[0]


def local(image_emb, text_emb, logit_scale):
    place = jnp.stack([lax.axis_index(n) for n in AXES]).astype(jnp.int32)

    far = z_shift(text_emb, 4)
    near = [plane_shift(image_emb, k, True) for k in (1, 2, 3)]
    pair = pack(text_emb, far)
    own = pack(image_emb, *near)
    text_0 = pack(pair, z_shift(pair, -2))
    images = [own] + [plane_shift(own, k, False) for k in (1, 2, 3)]
    text_1 = z_shift(text_0, -1)
    texts = [text_0, text_1, core_swap(text_0), core_swap(text_1)]

    logits, row_part, col_part, matched = logits_call(place, logit_scale, images, texts)

    row_lse, col_lse = row_part, col_part
    for axis, bit, col_axis, col_bit in (
        ("x", 2, "z", 4),
        ("x", 1, "z", 2),
        ("y", 2, "z", 1),
        ("y", 1, "core", 1),
    ):
        row_lse = lse2(row_lse, flip(row_lse, axis, bit))
        col_lse = lse2(col_lse, flip(col_lse, col_axis, col_bit))

    weights, *text_parts = text_call(place, logit_scale, logits, row_lse, col_lse, images)
    back_1, back_0 = core_swap(text_parts[3]), core_swap(text_parts[2])
    image_parts = image_call(logit_scale, weights, texts)

    back = [plane_shift(image_parts[k], -k, False) for k in (2, 1, 3)]
    t = z_shift(add([text_parts[1], back_1]), 1)
    t_near, t_far = add([text_parts[0], back_0, t], pieces=2)
    pieces = add([image_parts[0]] + back, pieces=4)
    t_near, t_far = add([t_near, z_shift(t_far, 2)], pieces=2)
    image_grad = add([pieces[0]] + [plane_shift(pieces[k], -k, True) for k in (2, 1, 3)])
    text_grad = add([t_near, z_shift(t_far, 4)])

    real = lax.broadcasted_iota(jnp.int32, (16, 128), 1) < ROWS
    lses = jnp.sum(jnp.where(real, row_lse + col_lse, 0.0)) / 16.0
    s = jnp.broadcast_to(lses - 2.0 * matched[0, 0], (8, 128))
    for axis, bit in (("x", 2), ("x", 1), ("y", 2), ("y", 1), ("z", 4), ("z", 2), ("z", 1), ("core", 1)):
        s = s + flip(s, axis, bit)
    mean_loss = s[0, :1] / (2.0 * ROWS * 256)
    return mean_loss, image_grad, text_grad


def solution(mesh):
    fine = Mesh(mesh.devices.reshape(4, 2, 2, 4, 4), AXES)
    return jax.shard_map(
        local,
        mesh=fine,
        in_specs=(P(AXES, None), P(("zh", "y", "x", "zl", "core"), None), P()),
        out_specs=(P(), P(AXES, None), P(("zh", "y", "x", "zl", "core"), None)),
        check_vma=False,
    )
```

```python
import jax
import jax.numpy as jnp
from jax import lax
from jax.experimental import pallas as pl
from jax.experimental.pallas import tpu as pltpu
from jax.sharding import Mesh, PartitionSpec as P

AXES = ("zl", "core", "zh", "y", "x")
NX, NY, NZ = 4, 4, 8
ROWS, EMBED = 64, 1280
CHUNK = 4 * ROWS
BLOCK = 16 * ROWS
BF16, F32 = jnp.bfloat16, jnp.float32
VMEM = pl.BlockSpec(memory_space=pltpu.VMEM)
SMEM = pl.BlockSpec(memory_space=pltpu.SMEM)
PARAMS = pltpu.CompilerParams(vmem_limit_bytes=36 * 1024 * 1024)


def plane_shift(v, k, primary):
    pairs = []
    for c in range(2):
        for h in range(2):
            for y in range(NY):
                for x in range(NX):
                    if (c == 0) == primary:
                        to = (y, (x + k) % NX)
                    else:
                        to = ((y + k) % NY, x)
                    base = (c * 2 + h) * NY
                    pairs.append(((base + y) * NX + x, (base + to[0]) * NX + to[1]))
    return lax.ppermute(v, ("core", "zh", "y", "x"), pairs)


def z_shift(v, k):
    pairs = []
    for c in range(2):
        for z in range(NZ):
            to = (z + (k if c == 0 else -k)) % NZ
            pairs.append((((z % 4) * 2 + c) * 2 + z // 4, ((to % 4) * 2 + c) * 2 + to // 4))
    return lax.ppermute(v, ("zl", "core", "zh"), pairs)


def core_swap(v):
    return lax.ppermute(v, "core", [(0, 1), (1, 0)])


def split_move(v, to_0, to_1):
    pairs = []
    for c, to in ((0, to_0), (1, to_1)):
        if to is None:
            continue
        for z in range(NZ):
            for y in range(NY):
                for x in range(NX):
                    ty, tx, tz = to(y, x, z)
                    pairs.append((device(c, y, x, z), device(c, ty % NY, tx % NX, tz % NZ)))
    return lax.ppermute(v, AXES, pairs)


def device(c, y, x, z):
    return ((((z % 4) * 2 + c) * 2 + z // 4) * NY + y) * NX + x


def lse(parts):
    top = parts[0]
    for p in parts[1:]:
        top = jnp.maximum(top, p)
    return top + jnp.log(sum(jnp.exp(p - top) for p in parts))


def in_order(parts, at):
    out = []
    for i in range(4):
        k = (at - i) & 3
        v = parts[3]
        for n in (2, 1, 0):
            v = jnp.where(k == n, parts[n], v)
        out.append(v)
    return out


def row_place(where, a, b):
    zl, c, zh, y, x = where
    p, s = jnp.where(c == 0, b, a), jnp.where(c == 0, a, b)
    n = ((y - s) & 3) * 4 + ((x - p) & 3)
    return n, ((zl * 2 + c) * 2 + zh) * 16 + n


def col_place(where, j, i):
    zl, c, zh, y, x = where
    core = c if j < 2 else 1 - c
    sign = 1 - 2 * core
    off = sign * ((0, 0, 2, 2)[i] + j % 2) + (0, 4, 0, 4)[i]
    z = (zh * 4 + zl + off) & 7
    return z * 2 + core, ((z >> 2) * 16 + y * 4 + x) * 8 + (z & 3) * 2 + core


def row_ids(where, a):
    span = lax.broadcasted_iota(jnp.int32, (ROWS, 128), 0)
    return [row_place(where, a, b)[1] * ROWS + span for b in range(4)]


def col_ids(where):
    lane = lax.broadcasted_iota(jnp.int32, (8, 128), 1)
    out = []
    for t in range(8):
        lo = col_place(where, t // 2, (t % 2) * 2)[1] * ROWS
        hi = col_place(where, t // 2, (t % 2) * 2 + 1)[1] * ROWS - ROWS
        out.append(lane + jnp.where(lane < ROWS, lo, hi))
    return out


def pack_body(counts, *refs):
    at = 0
    for n, out in zip(counts, refs[sum(counts) :]):
        row = 0
        for r in refs[at : at + n]:
            out[row : row + r.shape[0], :] = r[...]
            row += r.shape[0]
        at += n


def pack(*groups):
    parts = [p for g in groups for p in g]
    shapes = [jax.ShapeDtypeStruct((sum(p.shape[0] for p in g), EMBED), BF16) for g in groups]
    return pl.pallas_call(
        lambda *refs: pack_body([len(g) for g in groups], *refs),
        out_shape=tuple(shapes),
        in_specs=[VMEM] * len(parts),
        out_specs=(VMEM,) * len(groups),
        compiler_params=PARAMS,
    )(*parts)


def logits_body(place, scale, *refs):
    images, texts = refs[:4], refs[4:8]
    logits, row_out, col_out, match_out = refs[8:12]
    row_wide = refs[12]
    where = [place[i] for i in range(5)]
    multiplier = scale[0]
    for a in range(4):
        for j in range(4):
            logits[a * CHUNK : (a + 1) * CHUNK, j * CHUNK : (j + 1) * CHUNK] = (
                multiplier
                * lax.dot_general(
                    images[a][...],
                    texts[j][...],
                    (((1,), (1,)), ((), ())),
                    preferred_element_type=F32,
                )
            )
    cols = col_ids(where)
    step = 32
    matched = jnp.zeros((8, 128), F32)
    col_top = [jnp.full((8, 128), -jnp.inf, F32) for _ in range(8)]
    for a in range(4):
        ids = row_ids(where, a)
        for b in range(4):
            for half in range(ROWS // step):
                at = a * CHUNK + b * ROWS + half * step
                tiles = [logits[at : at + step, t * 128 : (t + 1) * 128] for t in range(8)]
                top = tiles[0]
                for t in range(1, 8):
                    top = jnp.maximum(top, tiles[t])
                top = jnp.max(top, axis=1, keepdims=True)
                mine = ids[b][half * step : (half + 1) * step]
                total = jnp.zeros((step, 128), F32)
                for t in range(8):
                    total += jnp.exp(tiles[t] - top)
                    folded = tiles[t].reshape(step // 8, 8, 128)
                    col_top[t] = jnp.maximum(col_top[t], jnp.max(folded, axis=0))
                    hit = jnp.where(mine == cols[t][0:1], tiles[t], 0.0)
                    matched += jnp.sum(hit.reshape(step // 8, 8, 128), axis=0)
                part = top + jnp.log(jnp.sum(total, axis=1, keepdims=True))
                row_wide[at : at + step, :] = jnp.broadcast_to(part, (step, 128))
    match_out[...] = jnp.broadcast_to(jnp.sum(matched, keepdims=True), (8, 128))
    col_out[...] = jnp.zeros((16, 128), F32)
    row_out[...] = jnp.zeros((16, 128), F32)
    for t in range(8):
        top = jnp.max(col_top[t], axis=0, keepdims=True)

        def cols_pass(i, total, t=t, top=top):
            tile = logits[pl.ds(pl.multiple_of(i * 128, 128), 128), t * 128 : (t + 1) * 128]
            return total + jnp.sum(jnp.exp(tile - top).reshape(16, 8, 128), axis=0)

        total = lax.fori_loop(0, 8, cols_pass, jnp.zeros((8, 128), F32), unroll=True)
        part = top + jnp.log(jnp.sum(total, axis=0, keepdims=True))
        j, i = t // 2, (t % 2) * 2
        col_out[pl.ds(col_place(where, j, i)[0], 1), :] = part
        col_out[pl.ds(col_place(where, j, i + 1)[0], 1), :] = pltpu.roll(part, 64, 1)
        line = jnp.transpose(row_wide[t * 128 : (t + 1) * 128, :])[0:1]
        row_out[pl.ds(row_place(where, j, i)[0], 1), :] = line
        row_out[pl.ds(row_place(where, j, i + 1)[0], 1), :] = pltpu.roll(line, 64, 1)


def logits_call(place, scale, images, texts):
    return pl.pallas_call(
        logits_body,
        out_shape=(
            jax.ShapeDtypeStruct((BLOCK, BLOCK), F32),
            jax.ShapeDtypeStruct((16, 128), F32),
            jax.ShapeDtypeStruct((16, 128), F32),
            jax.ShapeDtypeStruct((8, 128), F32),
        ),
        in_specs=[SMEM, SMEM] + [VMEM] * 8,
        out_specs=(VMEM,) * 4,
        scratch_shapes=[pltpu.VMEM((BLOCK, 128), F32)],
        compiler_params=PARAMS,
    )(place, scale, *images, *texts)


def weights_body(place, scale, logits, row_lse, col_lse, *refs):
    images = refs[:4]
    weights = refs[4]
    outs = refs[5:7]
    row_wide = refs[7]
    where = [place[i] for i in range(5)]
    multiplier = scale[0]
    lane = lax.broadcasted_iota(jnp.int32, (1, 128), 1)
    cols = col_ids(where)
    col_line = []
    for t in range(8):
        j, i = t // 2, (t % 2) * 2
        lo = col_lse[pl.ds(col_place(where, j, i)[0], 1), :]
        hi = col_lse[pl.ds(col_place(where, j, i + 1)[0], 1), :]
        col_line.append(jnp.where(lane < ROWS, lo, pltpu.roll(hi, 64, 1)))
        lo = row_lse[pl.ds(row_place(where, j, i)[0], 1), :]
        hi = row_lse[pl.ds(row_place(where, j, i + 1)[0], 1), :]
        line = jnp.where(lane < ROWS, lo, pltpu.roll(hi, 64, 1))
        row_wide[t * 128 : (t + 1) * 128, :] = jnp.transpose(jnp.broadcast_to(line, (128, 128)))
    for a in range(4):
        ids = row_ids(where, a)
        for b in range(4):
            at = a * CHUNK + b * ROWS
            wide = row_wide[at : at + ROWS, :]
            for t in range(8):
                tile = logits[at : at + ROWS, t * 128 : (t + 1) * 128]
                both = 0.5 * jnp.exp(tile - wide) + 0.5 * jnp.exp(tile - col_line[t])
                both = both - jnp.where(ids[b] == cols[t][0:1], 1.0, 0.0)
                weights[at : at + ROWS, t * 128 : (t + 1) * 128] = both.astype(BF16)
    text_terms(multiplier, weights, images, {1: outs[0], 3: outs[1]})


def text_terms(multiplier, weights, images, outs):
    for j, out in outs.items():
        for e in range(5):
            acc = None
            for a in range(4):
                term = lax.dot_general(
                    weights[a * CHUNK : (a + 1) * CHUNK, j * CHUNK : (j + 1) * CHUNK],
                    images[a][:, e * 256 : (e + 1) * 256],
                    (((0,), (0,)), ((), ())),
                    preferred_element_type=F32,
                )
                acc = term if acc is None else acc + term
            out[:, e * 256 : (e + 1) * 256] = (multiplier * acc).astype(BF16)


def image_terms(multiplier, weights, texts, outs):
    for a, out in outs.items():
        for e in range(5):
            acc = None
            for j in range(4):
                term = jnp.dot(
                    weights[a * CHUNK : (a + 1) * CHUNK, j * CHUNK : (j + 1) * CHUNK],
                    texts[j][:, e * 256 : (e + 1) * 256],
                    preferred_element_type=F32,
                )
                acc = term if acc is None else acc + term
            out[:, e * 256 : (e + 1) * 256] = (multiplier * acc).astype(BF16)


PART = jax.ShapeDtypeStruct((CHUNK, EMBED), BF16)


def weights_call(place, scale, logits, row_lse, col_lse, images):
    return pl.pallas_call(
        weights_body,
        out_shape=(jax.ShapeDtypeStruct((BLOCK, BLOCK), BF16), PART, PART),
        in_specs=[SMEM, SMEM] + [VMEM] * 7,
        out_specs=(VMEM,) * 3,
        scratch_shapes=[pltpu.VMEM((BLOCK, 128), F32)],
        compiler_params=PARAMS,
    )(place, scale, logits, row_lse, col_lse, *images)


def image_body(scale, weights, *refs):
    image_terms(scale[0], weights, refs[:4], dict(zip((2, 1, 3), refs[4:])))


def image_call(scale, weights, texts):
    return pl.pallas_call(
        image_body,
        out_shape=(PART,) * 3,
        in_specs=[SMEM] + [VMEM] * 5,
        out_specs=(VMEM,) * 3,
        compiler_params=PARAMS,
    )(scale, weights, *texts)


def rest_body(scale, weights, *refs):
    images, texts, outs = refs[:4], refs[4:8], refs[8:]
    text_terms(scale[0], weights, images, {2: outs[1], 0: outs[0]})
    image_terms(scale[0], weights, texts, {0: outs[2]})


def rest_call(scale, weights, images, texts):
    return pl.pallas_call(
        rest_body,
        out_shape=(PART,) * 3,
        in_specs=[SMEM] + [VMEM] * 9,
        out_specs=(VMEM,) * 3,
        compiler_params=PARAMS,
    )(scale, weights, *images, *texts)


def add_body(n, *refs):
    outs = refs[n:]
    rows = outs[0].shape[0]
    for o, out in enumerate(outs):
        for at in range(0, rows, 16):
            total = refs[0][o * rows + at : o * rows + at + 16, :].astype(F32)
            for r in refs[1:n]:
                total += r[o * rows + at : o * rows + at + 16, :].astype(F32)
            out[at : at + 16, :] = total.astype(out.dtype)


def add(parts, pieces=1):
    rows = parts[0].shape[0] // pieces
    out = pl.pallas_call(
        lambda *refs: add_body(len(parts), *refs),
        out_shape=(jax.ShapeDtypeStruct((rows, EMBED), BF16),) * pieces,
        in_specs=[VMEM] * len(parts),
        out_specs=(VMEM,) * pieces,
        compiler_params=PARAMS,
    )(*parts)
    return out if pieces > 1 else out[0]


def local(image_emb, text_emb, logit_scale):
    place = jnp.stack([lax.axis_index(n) for n in AXES]).astype(jnp.int32)

    far = z_shift(text_emb, 4)
    near = [plane_shift(image_emb, k, True) for k in (1, 2, 3)]
    pair, own = pack([text_emb, far], [image_emb] + near)
    (text_0,) = pack([pair, z_shift(pair, -2)])
    images = [own] + [plane_shift(own, k, False) for k in (1, 2, 3)]
    text_1 = z_shift(text_0, -1)
    texts = [text_0, text_1, core_swap(text_0), core_swap(text_1)]

    logits, row_part, col_part, matched = logits_call(place, logit_scale, images, texts)

    first = place[1] == 0
    got = core_swap(jnp.concatenate([jnp.where(first, col_part, row_part), matched]))
    rows_first = jnp.concatenate([row_part, got[:16]])
    cols_first = jnp.concatenate([lse([col_part, got[:16]])] * 2)
    state = jnp.where(first, rows_first, cols_first)
    hits = matched + got[16:]

    def join(parts, at):
        parts = in_order(parts, at)
        kept = lse([p[:32] for p in parts])
        return jnp.concatenate([kept, parts[0][32:] + parts[1][32:] + (parts[2][32:] + parts[3][32:])])

    state = jnp.concatenate([state, hits])
    z = place[2] * 4 + place[0]
    state = join(
        [state]
        + [
            split_move(state, lambda y, x, z: (y, x + k, z), lambda y, x, z: (y, x, z + 2 * k))
            for k in (1, 2, 3)
        ],
        jnp.where(first, place[4], z >> 1),
    )
    moved = [
        split_move(
            state, lambda y, x, z: (y + k, x, z), (lambda y, x, z: (y, x, z ^ 1)) if k == 1 else None
        )
        for k in (1, 2, 3)
    ]
    state = jnp.where(first, join([state] + moved, place[3]), jnp.concatenate([lse([state[:32], moved[0][:32]]), hits]))
    got = core_swap(jnp.where(first, state[16:32], state[:16]))
    row_lse = jnp.where(first, state[:16], got)
    col_lse = jnp.where(first, got, state[:16])

    weights, text_1_term, text_3_term = weights_call(place, logit_scale, logits, row_lse, col_lse, images)
    back_1 = core_swap(text_3_term)
    image_terms_far = image_call(logit_scale, weights, texts)
    text_0_term, text_2_term, image_0_term = rest_call(logit_scale, weights, images, texts)
    back_0 = core_swap(text_2_term)

    back = [plane_shift(v, -k, False) for v, k in zip(image_terms_far, (2, 1, 3))]
    t = z_shift(add([text_1_term, back_1]), 1)
    t_near, t_far = add([text_0_term, back_0, t], pieces=2)
    pieces = add([image_0_term] + back, pieces=4)
    t_near, t_far = add([t_near, z_shift(t_far, 2)], pieces=2)
    image_grad = add([pieces[0]] + [plane_shift(pieces[k], -k, True) for k in (2, 1, 3)])
    text_grad = add([t_near, z_shift(t_far, 4)])

    real = lax.broadcasted_iota(jnp.int32, (16, 128), 1) < ROWS
    half = [jnp.sum(jnp.where(real, v, 0.0)) for v in (state[:16], state[16:32])]
    share = jnp.where(first, half[0] + half[1] - 2.0 * state[32, 0], half[0])
    s = jnp.broadcast_to(share, (8, 128))
    s = s + split_move(s, lambda y, x, z: (y, x, z ^ 4), lambda y, x, z: (y, x ^ 2, z))
    s = s + split_move(s, lambda y, x, z: (y, x, z ^ 2), lambda y, x, z: (y, x ^ 1, z))
    s = s + split_move(s, lambda y, x, z: (y, x, z ^ 1), lambda y, x, z: (y ^ 2, x, z))
    s = s + split_move(s, None, lambda y, x, z: (y ^ 1, x, z))
    s = s + core_swap(s)
    mean_loss = s[0, :1] / (2.0 * ROWS * 256)
    return mean_loss, image_grad, text_grad


def solution(mesh):
    fine = Mesh(mesh.devices.reshape(4, 2, 2, 4, 4), AXES)
    return jax.shard_map(
        local,
        mesh=fine,
        in_specs=(P(AXES, None), P(("zh", "y", "x", "zl", "core"), None), P()),
        out_specs=(P(), P(AXES, None), P(("zh", "y", "x", "zl", "core"), None)),
        check_vma=False,
    )
```

```python
import jax
import jax.numpy as jnp
from jax import lax
from jax.experimental import pallas as pl
from jax.experimental.pallas import tpu as pltpu
from jax.sharding import Mesh, PartitionSpec as P

AXES = ("zl", "core", "zh", "y", "x")
NX, NY, NZ = 4, 4, 8
ROWS, EMBED = 64, 1280
CHUNK = 4 * ROWS
BLOCK = 16 * ROWS
BF16, F32 = jnp.bfloat16, jnp.float32
VMEM = pl.BlockSpec(memory_space=pltpu.VMEM)
SMEM = pl.BlockSpec(memory_space=pltpu.SMEM)
ANY = pl.BlockSpec(memory_space=pl.ANY)
PARAMS = pltpu.CompilerParams(vmem_limit_bytes=12 * 1024 * 1024)


def plane_shift(v, k, primary):
    pairs = []
    for c in range(2):
        for h in range(2):
            for y in range(NY):
                for x in range(NX):
                    if (c == 0) == primary:
                        to = (y, (x + k) % NX)
                    else:
                        to = ((y + k) % NY, x)
                    base = (c * 2 + h) * NY
                    pairs.append(((base + y) * NX + x, (base + to[0]) * NX + to[1]))
    return lax.ppermute(v, ("core", "zh", "y", "x"), pairs)


def z_shift(v, k):
    pairs = []
    for c in range(2):
        for z in range(NZ):
            to = (z + (k if c == 0 else -k)) % NZ
            pairs.append((((z % 4) * 2 + c) * 2 + z // 4, ((to % 4) * 2 + c) * 2 + to // 4))
    return lax.ppermute(v, ("zl", "core", "zh"), pairs)


def core_swap(v):
    return lax.ppermute(v, "core", [(0, 1), (1, 0)])


def split_move(v, to_0, to_1):
    pairs = []
    for c, to in ((0, to_0), (1, to_1)):
        if to is None:
            continue
        for z in range(NZ):
            for y in range(NY):
                for x in range(NX):
                    ty, tx, tz = to(y, x, z)
                    pairs.append((device(c, y, x, z), device(c, ty % NY, tx % NX, tz % NZ)))
    return lax.ppermute(v, AXES, pairs)


def device(c, y, x, z):
    return ((((z % 4) * 2 + c) * 2 + z // 4) * NY + y) * NX + x


def lse2(a, b):
    top = jnp.maximum(a, b)
    return top + jnp.log(jnp.exp(a - top) + jnp.exp(b - top))


def row_place(where, a, b):
    zl, c, zh, y, x = where
    p, s = jnp.where(c == 0, b, a), jnp.where(c == 0, a, b)
    n = ((y - s) & 3) * 4 + ((x - p) & 3)
    return n, ((zl * 2 + c) * 2 + zh) * 16 + n


def col_place(where, j, i):
    zl, c, zh, y, x = where
    core = c if (i < 2) == (j != 2) else 1 - c
    sign = 1 - 2 * c
    off = sign * ((0, 1, -1, 2 if i < 2 else -2)[j]) + 4 * (i % 2)
    z = (zh * 4 + zl + off) & 7
    return z * 2 + core, ((z >> 2) * 16 + y * 4 + x) * 8 + (z & 3) * 2 + core


def row_ids(where, a):
    span = lax.broadcasted_iota(jnp.int32, (ROWS, 128), 0)
    return [row_place(where, a, b)[1] * ROWS + span for b in range(4)]


def col_ids(where):
    lane = lax.broadcasted_iota(jnp.int32, (8, 128), 1)
    out = []
    for t in range(8):
        lo = col_place(where, t // 2, (t % 2) * 2)[1] * ROWS
        hi = col_place(where, t // 2, (t % 2) * 2 + 1)[1] * ROWS - ROWS
        out.append(lane + jnp.where(lane < ROWS, lo, hi))
    return out


def pack_body(counts, *refs):
    n = sum(counts)
    outs, sem = refs[n:-1], refs[-1]
    at = 0
    local_copy = None
    for count, out in zip(counts, outs):
        row = 0
        for r in refs[at : at + count]:
            rows = out.at[row : row + r.shape[0], :]
            if at == 0 and row == 0:
                local_copy = pltpu.make_async_copy(r, rows, sem)
                local_copy.start()
            else:
                rows[...] = r[...]
            row += r.shape[0]
        at += count
    local_copy.wait()


def pack(*groups):
    parts = [p for g in groups for p in g]
    shapes = [jax.ShapeDtypeStruct((sum(p.shape[0] for p in g), EMBED), BF16) for g in groups]
    return pl.pallas_call(
        lambda *refs: pack_body([len(g) for g in groups], *refs),
        out_shape=tuple(shapes),
        in_specs=[ANY] + [VMEM] * (len(parts) - 1),
        out_specs=(VMEM,) * len(groups),
        scratch_shapes=[pltpu.SemaphoreType.DMA],
        compiler_params=PARAMS,
    )(*parts)


def logits_body(place, scale, *refs):
    images, texts = refs[:4], refs[4:8]
    logits, row_out, col_out, match_out = refs[8:12]
    row_wide = refs[12]
    where = [place[i] for i in range(5)]
    multiplier = scale[0]
    for a in range(4):
        for j in range(4):
            logits[a * CHUNK : (a + 1) * CHUNK, j * CHUNK : (j + 1) * CHUNK] = (
                multiplier
                * lax.dot_general(
                    images[a][...],
                    texts[j][...],
                    (((1,), (1,)), ((), ())),
                    preferred_element_type=F32,
                )
            )
    cols = col_ids(where)
    step = 32
    matched = jnp.zeros((8, 128), F32)
    col_top = [jnp.full((8, 128), -jnp.inf, F32) for _ in range(8)]
    for a in range(4):
        ids = row_ids(where, a)
        for b in range(4):
            for half in range(ROWS // step):
                at = a * CHUNK + b * ROWS + half * step
                tiles = [logits[at : at + step, t * 128 : (t + 1) * 128] for t in range(8)]
                top = tiles[0]
                for t in range(1, 8):
                    top = jnp.maximum(top, tiles[t])
                top = jnp.max(top, axis=1, keepdims=True)
                mine = ids[b][half * step : (half + 1) * step]
                total = jnp.zeros((step, 128), F32)
                for t in range(8):
                    total += jnp.exp(tiles[t] - top)
                    folded = tiles[t].reshape(step // 8, 8, 128)
                    col_top[t] = jnp.maximum(col_top[t], jnp.max(folded, axis=0))
                    hit = jnp.where(mine == cols[t][0:1], tiles[t], 0.0)
                    matched += jnp.sum(hit.reshape(step // 8, 8, 128), axis=0)
                part = top + jnp.log(jnp.sum(total, axis=1, keepdims=True))
                row_wide[at : at + step, :] = jnp.broadcast_to(part, (step, 128))
    match_out[...] = jnp.broadcast_to(jnp.sum(matched, keepdims=True), (8, 128))
    col_out[...] = jnp.zeros((16, 128), F32)
    row_out[...] = jnp.zeros((16, 128), F32)
    for t in range(8):
        top = jnp.max(col_top[t], axis=0, keepdims=True)

        def cols_pass(i, total, t=t, top=top):
            tile = logits[pl.ds(pl.multiple_of(i * 128, 128), 128), t * 128 : (t + 1) * 128]
            return total + jnp.sum(jnp.exp(tile - top).reshape(16, 8, 128), axis=0)

        total = lax.fori_loop(0, 8, cols_pass, jnp.zeros((8, 128), F32), unroll=True)
        part = top + jnp.log(jnp.sum(total, axis=0, keepdims=True))
        j, i = t // 2, (t % 2) * 2
        col_out[pl.ds(col_place(where, j, i)[0], 1), :] = part
        col_out[pl.ds(col_place(where, j, i + 1)[0], 1), :] = pltpu.roll(part, 64, 1)
        line = jnp.transpose(row_wide[t * 128 : (t + 1) * 128, :])[0:1]
        row_out[pl.ds(row_place(where, j, i)[0], 1), :] = line
        row_out[pl.ds(row_place(where, j, i + 1)[0], 1), :] = pltpu.roll(line, 64, 1)


def logits_call(place, scale, images, texts):
    return pl.pallas_call(
        logits_body,
        out_shape=(
            jax.ShapeDtypeStruct((BLOCK, BLOCK), F32),
            jax.ShapeDtypeStruct((16, 128), F32),
            jax.ShapeDtypeStruct((16, 128), F32),
            jax.ShapeDtypeStruct((8, 128), F32),
        ),
        in_specs=[SMEM, SMEM] + [VMEM] * 8,
        out_specs=(VMEM,) * 4,
        scratch_shapes=[pltpu.VMEM((BLOCK, 128), F32)],
        compiler_params=PARAMS,
    )(place, scale, *images, *texts)


def weights_body(place, scale, logits, row_lse, col_lse, *refs):
    images = refs[:4]
    weights = refs[4]
    outs = refs[5:9]
    row_wide = refs[9]
    where = [place[i] for i in range(5)]
    multiplier = scale[0]
    lane = lax.broadcasted_iota(jnp.int32, (1, 128), 1)
    cols = col_ids(where)
    col_line = []
    for t in range(8):
        j, i = t // 2, (t % 2) * 2
        lo = col_lse[pl.ds(col_place(where, j, i)[0], 1), :]
        hi = col_lse[pl.ds(col_place(where, j, i + 1)[0], 1), :]
        col_line.append(jnp.where(lane < ROWS, lo, pltpu.roll(hi, 64, 1)))
        lo = row_lse[pl.ds(row_place(where, j, i)[0], 1), :]
        hi = row_lse[pl.ds(row_place(where, j, i + 1)[0], 1), :]
        line = jnp.where(lane < ROWS, lo, pltpu.roll(hi, 64, 1))
        row_wide[t * 128 : (t + 1) * 128, :] = jnp.transpose(jnp.broadcast_to(line, (128, 128)))
    for a in range(4):
        ids = row_ids(where, a)
        for b in range(4):
            at = a * CHUNK + b * ROWS
            wide = row_wide[at : at + ROWS, :]
            for t in range(8):
                tile = logits[at : at + ROWS, t * 128 : (t + 1) * 128]
                both = 0.5 * jnp.exp(tile - wide) + 0.5 * jnp.exp(tile - col_line[t])
                both = both - jnp.where(ids[b] == cols[t][0:1], 1.0, 0.0)
                weights[at : at + ROWS, t * 128 : (t + 1) * 128] = both.astype(BF16)
    text_terms(multiplier, weights, images, ((2, 0, outs[0]), (3, 128, outs[1]), (3, 0, outs[2]), (1, 0, outs[3])))


def text_terms(multiplier, weights, images, outs):
    for j, skip, out in outs:
        at = j * CHUNK + skip
        for e in range(5):
            acc = None
            for a in range(4):
                term = lax.dot_general(
                    weights[a * CHUNK : (a + 1) * CHUNK, at : at + out.shape[0]],
                    images[a][:, e * 256 : (e + 1) * 256],
                    (((0,), (0,)), ((), ())),
                    preferred_element_type=F32,
                )
                acc = term if acc is None else acc + term
            out[:, e * 256 : (e + 1) * 256] = (multiplier * acc).astype(BF16)


def image_terms(multiplier, weights, texts, outs):
    for a, out in outs.items():
        for e in range(5):
            acc = None
            for j in range(4):
                term = jnp.dot(
                    weights[a * CHUNK : (a + 1) * CHUNK, j * CHUNK : (j + 1) * CHUNK],
                    texts[j][:, e * 256 : (e + 1) * 256],
                    preferred_element_type=F32,
                )
                acc = term if acc is None else acc + term
            out[:, e * 256 : (e + 1) * 256] = (multiplier * acc).astype(BF16)


PART = jax.ShapeDtypeStruct((CHUNK, EMBED), BF16)


HALF = jax.ShapeDtypeStruct((CHUNK // 2, EMBED), BF16)


def weights_call(place, scale, logits, row_lse, col_lse, images):
    return pl.pallas_call(
        weights_body,
        out_shape=(jax.ShapeDtypeStruct((BLOCK, BLOCK), BF16), PART, HALF, HALF, PART),
        in_specs=[SMEM, SMEM] + [VMEM] * 7,
        out_specs=(VMEM,) * 5,
        scratch_shapes=[pltpu.VMEM((BLOCK, 128), F32)],
        compiler_params=PARAMS,
    )(place, scale, logits, row_lse, col_lse, *images)


def image_body(scale, after, weights, *refs):
    image_terms(scale[0], weights, refs[:4], dict(zip((2, 1, 3), refs[4:])))


def image_call(scale, after, weights, texts):
    return pl.pallas_call(
        image_body,
        out_shape=(PART,) * 3,
        in_specs=[SMEM] + [VMEM] * 6,
        out_specs=(VMEM,) * 3,
        compiler_params=PARAMS,
    )(scale, after, weights, *texts)


def rest_body(scale, weights, *refs):
    images, texts, outs = refs[:4], refs[4:8], refs[8:]
    text_terms(scale[0], weights, images, ((0, 0, outs[0]),))
    image_terms(scale[0], weights, texts, {0: outs[1]})


def rest_call(scale, weights, images, texts):
    return pl.pallas_call(
        rest_body,
        out_shape=(PART,) * 2,
        in_specs=[SMEM] + [VMEM] * 9,
        out_specs=(VMEM,) * 2,
        compiler_params=PARAMS,
    )(scale, weights, *images, *texts)


def sums_body(n, plan, *refs):
    for (rows, terms), out in zip(plan, refs[n:]):
        for at in range(0, rows, 16):
            total = None
            for i, skip in terms:
                v = refs[i][skip + at : skip + at + 16, :].astype(F32)
                total = v if total is None else total + v
            out[at : at + 16, :] = total.astype(out.dtype)


def sums(arrays, *plan):
    out = pl.pallas_call(
        lambda *refs: sums_body(len(arrays), plan, *refs),
        out_shape=tuple(jax.ShapeDtypeStruct((rows, EMBED), BF16) for rows, _ in plan),
        in_specs=[VMEM] * len(arrays),
        out_specs=(VMEM,) * len(plan),
        compiler_params=PARAMS,
    )(*arrays)
    return out if len(plan) > 1 else out[0]


def share_body(place, state, out):
    real = lax.broadcasted_iota(jnp.int32, (16, 128), 1) < ROWS
    both = jnp.where(real, state[:16, :], 0.0)
    more = jnp.where(real, state[16:32, :], 0.0)
    first = place[1] == 0
    both = both + jnp.where(first, more, 0.0)
    total = jnp.sum(both, keepdims=True) - jnp.where(first, 2.0, 0.0) * state[32:33, 0:1]
    out[...] = jnp.broadcast_to(total, (8, 128))


def share_call(place, state):
    return pl.pallas_call(
        share_body,
        out_shape=jax.ShapeDtypeStruct((8, 128), F32),
        in_specs=[SMEM, VMEM],
        out_specs=VMEM,
        compiler_params=PARAMS,
    )(place, state)


def mean_body(a, b, out):
    out[...] = (a[0:1, 0:1] + b[0:1, 0:1]) * (1.0 / (2.0 * ROWS * 256))


def mean_call(a, b):
    return pl.pallas_call(
        mean_body,
        out_shape=jax.ShapeDtypeStruct((1, 1), F32),
        in_specs=[VMEM] * 2,
        out_specs=VMEM,
        compiler_params=PARAMS,
    )(a, b)


def local(image_emb, text_emb, logit_scale):
    place = jnp.stack([lax.axis_index(n) for n in AXES]).astype(jnp.int32)

    far = z_shift(text_emb, 4)
    near = [plane_shift(image_emb, k, True) for k in (1, 2, 3)]
    (pair,) = pack([text_emb, far])
    own, text_0 = pack([image_emb] + near, [pair, core_swap(pair)])
    text_1 = z_shift(text_0, -1)
    text_3 = z_shift(pair, -2)
    images = [own] + [plane_shift(own, k, False) for k in (1, 2, 3)]
    (text_3,) = pack([text_3, core_swap(text_3)])
    texts = [text_0, text_1, core_swap(text_1), text_3]

    logits, row_part, col_part, matched = logits_call(place, logit_scale, images, texts)

    first = place[1] == 0
    got = core_swap(jnp.concatenate([jnp.where(first, col_part, row_part), matched]))
    rows_first = jnp.concatenate([row_part, got[:16]])
    cols_first = jnp.concatenate([lse2(col_part, got[:16])] * 2)
    state = jnp.concatenate([jnp.where(first, rows_first, cols_first), matched + got[16:]])
    for to_0, to_1 in (
        (lambda y, x, z: (y, x ^ 2, z), lambda y, x, z: (y, x, z ^ 4)),
        (lambda y, x, z: (y, x ^ 1, z), lambda y, x, z: (y, x, z ^ 2)),
        (lambda y, x, z: (y ^ 2, x, z), lambda y, x, z: (y, x, z ^ 1)),
        (lambda y, x, z: (y ^ 1, x, z), None),
    ):
        other = split_move(state, to_0, to_1)
        joined = jnp.concatenate([lse2(state[:32], other[:32]), state[32:] + other[32:]])
        state = joined if to_1 is not None else jnp.where(first, joined, state)
    got = core_swap(jnp.where(first, state[16:32], state[:16]))
    row_lse = jnp.where(first, state[:16], got)
    col_lse = jnp.where(first, got, state[:16])

    s = share_call(place, state)
    s_1 = s + split_move(s, lambda y, x, z: (y, x, z ^ 4), lambda y, x, z: (y, x ^ 2, z))
    s_2 = s_1 + split_move(s_1, lambda y, x, z: (y, x, z ^ 2), lambda y, x, z: (y, x ^ 1, z))
    s = s_2 + split_move(s_2, lambda y, x, z: (y, x, z ^ 1), lambda y, x, z: (y ^ 2, x, z))
    s = s + split_move(s, None, lambda y, x, z: (y ^ 1, x, z))
    mean_loss = mean_call(s, core_swap(s)).reshape(1)

    weights, text_2, text_3b, text_3a, text_1 = weights_call(
        place, logit_scale, logits, row_lse, col_lse, images
    )
    near, far = core_swap(text_2), core_swap(text_3b)
    image_parts = image_call(logit_scale, s_1, weights, texts)
    near, far = sums([text_1, near, text_3a, far, s_2], (256, ((0, 0), (1, 0))), (128, ((2, 0), (3, 0))))
    near, far = z_shift(near, 1), z_shift(far, 2)
    back = [plane_shift(v, -k, False) for v, k in zip(image_parts, (2, 1, 3))]
    text_0, image_0 = rest_call(logit_scale, weights, images, texts)
    mine, other = sums(
        [text_0, near, far], (128, ((0, 0), (1, 0), (2, 0))), (128, ((0, 128), (1, 128)))
    )
    mine, far = sums([mine, core_swap(other)], (64, ((0, 0), (1, 0))), (64, ((0, 64), (1, 64))))
    pieces = sums([image_0] + back, *[(64, [(i, 64 * k) for i in range(4)]) for k in range(4)])
    shards = [pieces[0]] + [plane_shift(pieces[k], -k, True) for k in (2, 1, 3)]
    image_grad = sums(shards, (64, [(i, 0) for i in range(4)]))
    text_grad = sums([mine, z_shift(far, 4)], (64, ((0, 0), (1, 0))))
    return mean_loss, image_grad, text_grad


def solution(mesh):
    fine = Mesh(mesh.devices.reshape(4, 2, 2, 4, 4), AXES)
    return jax.shard_map(
        local,
        mesh=fine,
        in_specs=(P(AXES, None), P(("zh", "y", "x", "zl", "core"), None), P()),
        out_specs=(P(), P(AXES, None), P(("zh", "y", "x", "zl", "core"), None)),
        check_vma=False,
    )
```

```python
import jax
import jax.numpy as jnp
from jax import lax
from jax.experimental import pallas as pl
from jax.experimental.pallas import tpu as pltpu
from jax.sharding import Mesh, PartitionSpec as P

AXES = ("zl", "core", "zh", "y", "x")
NX, NY, NZ = 4, 4, 8
ROWS, EMBED = 64, 1280
CHUNK = 4 * ROWS
BLOCK = 16 * ROWS
BF16, F32 = jnp.bfloat16, jnp.float32
VMEM = pl.BlockSpec(memory_space=pltpu.VMEM)
SMEM = pl.BlockSpec(memory_space=pltpu.SMEM)
HBM = pl.BlockSpec(memory_space=pltpu.HBM)
PARAMS = pltpu.CompilerParams(vmem_limit_bytes=12 * 1024 * 1024)


def plane_shift(v, k, primary):
    pairs = []
    for c in range(2):
        for h in range(2):
            for y in range(NY):
                for x in range(NX):
                    if (c == 0) == primary:
                        to = (y, (x + k) % NX)
                    else:
                        to = ((y + k) % NY, x)
                    base = (c * 2 + h) * NY
                    pairs.append(((base + y) * NX + x, (base + to[0]) * NX + to[1]))
    return lax.ppermute(v, ("core", "zh", "y", "x"), pairs)


def z_shift(v, k):
    pairs = []
    for c in range(2):
        for z in range(NZ):
            to = (z + (k if c == 0 else -k)) % NZ
            pairs.append((((z % 4) * 2 + c) * 2 + z // 4, ((to % 4) * 2 + c) * 2 + to // 4))
    return lax.ppermute(v, ("zl", "core", "zh"), pairs)


def core_swap(v):
    return lax.ppermute(v, "core", [(0, 1), (1, 0)])


def device(c, y, x, z):
    return ((((z % 4) * 2 + c) * 2 + z // 4) * NY + y) * NX + x


def groups(plane_core):
    out = []
    for c in range(2):
        if c == plane_core:
            out += [[device(c, y, x, z) for y in range(NY) for x in range(NX)] for z in range(NZ)]
        else:
            out += [
                [device(c, y + d, x, z) for z in range(NZ) for d in (0, 2)]
                for y in range(2)
                for x in range(NX)
            ]
    return out


def exchange(v, plane_core):
    return lax.all_to_all(v, AXES, 0, 0, axis_index_groups=groups(plane_core))


def row_place(where, a, b):
    zl, c, zh, y, x = where
    p, s = jnp.where(c == 0, b, a), jnp.where(c == 0, a, b)
    n = ((y - s) & 3) * 4 + ((x - p) & 3)
    return n, ((zl * 2 + c) * 2 + zh) * 16 + n


def col_place(where, j, i):
    zl, c, zh, y, x = where
    core = c if (i % 2 == 0) == (j < 2) else 1 - c
    sign = 1 - 2 * c
    off = ((0, 0, 1, 1), (2, 2, 3, 3), (-2, -2, -3, -3), (-1, -1, 4, 4))[j][i]
    off = 4 if off == 4 else sign * off
    z = (zh * 4 + zl + off) & 7
    return z * 2 + core, ((z >> 2) * 16 + y * 4 + x) * 8 + (z & 3) * 2 + core


def row_ids(where, a):
    span = lax.broadcasted_iota(jnp.int32, (ROWS, 128), 0)
    return [row_place(where, a, b)[1] * ROWS + span for b in range(4)]


def col_ids(where):
    lane = lax.broadcasted_iota(jnp.int32, (8, 128), 1)
    out = []
    for t in range(8):
        lo = col_place(where, t // 2, (t % 2) * 2)[1] * ROWS
        hi = col_place(where, t // 2, (t % 2) * 2 + 1)[1] * ROWS - ROWS
        out.append(lane + jnp.where(lane < ROWS, lo, hi))
    return out


def pack_body(plan, n, *refs):
    outs, sem = refs[n:-1], refs[-1]
    local_copy = None
    for parts, out in zip(plan, outs):
        row = 0
        for i, skip, rows in parts:
            into = out.at[row : row + rows, :]
            if i == 0:
                local_copy = pltpu.make_async_copy(refs[i], into, sem)
                local_copy.start()
            else:
                into[...] = refs[i][skip : skip + rows, :]
            row += rows
    local_copy.wait()


def pack(arrays, *plan):
    shapes = [jax.ShapeDtypeStruct((sum(p[2] for p in parts), EMBED), BF16) for parts in plan]
    return pl.pallas_call(
        lambda *refs: pack_body(plan, len(arrays), *refs),
        out_shape=tuple(shapes),
        in_specs=[HBM] + [VMEM] * (len(arrays) - 1),
        out_specs=(VMEM,) * len(plan),
        scratch_shapes=[pltpu.SemaphoreType.DMA],
        compiler_params=PARAMS,
    )(*arrays)


def logits_body(place, scale, *refs):
    images = refs[:4]
    texts = (*refs[4:7], refs[14])
    logits, row_out, col_out, message, match_out, text_3 = refs[9:15]
    row_wide = refs[15]
    text_3[: 3 * ROWS, :] = refs[7][...]
    text_3[3 * ROWS :, :] = refs[8][...]
    where = [place[i] for i in range(5)]
    multiplier = scale[0]
    for a in range(4):
        for j in range(4):
            logits[a * CHUNK : (a + 1) * CHUNK, j * CHUNK : (j + 1) * CHUNK] = (
                multiplier
                * lax.dot_general(
                    images[a][...],
                    texts[j][...],
                    (((1,), (1,)), ((), ())),
                    preferred_element_type=F32,
                )
            )
    cols = col_ids(where)
    step = 32
    matched = jnp.zeros((8, 128), F32)
    col_top = [jnp.full((8, 128), -jnp.inf, F32) for _ in range(8)]
    for a in range(4):
        ids = row_ids(where, a)
        for b in range(4):
            for half in range(ROWS // step):
                at = a * CHUNK + b * ROWS + half * step
                tiles = [logits[at : at + step, t * 128 : (t + 1) * 128] for t in range(8)]
                top = tiles[0]
                for t in range(1, 8):
                    top = jnp.maximum(top, tiles[t])
                top = jnp.max(top, axis=1, keepdims=True)
                mine = ids[b][half * step : (half + 1) * step]
                total = jnp.zeros((step, 128), F32)
                for t in range(8):
                    total += jnp.exp(tiles[t] - top)
                    folded = tiles[t].reshape(step // 8, 8, 128)
                    col_top[t] = jnp.maximum(col_top[t], jnp.max(folded, axis=0))
                    hit = jnp.where(mine == cols[t][0:1], tiles[t], 0.0)
                    matched += jnp.sum(hit.reshape(step // 8, 8, 128), axis=0)
                part = top + jnp.log(jnp.sum(total, axis=1, keepdims=True))
                row_wide[at : at + step, :] = jnp.broadcast_to(part, (step, 128))
    matched = jnp.broadcast_to(jnp.sum(matched, keepdims=True), (8, 128))
    match_out[...] = matched
    message[16:24, :] = matched
    for t in range(8):
        top = jnp.max(col_top[t], axis=0, keepdims=True)

        def cols_pass(i, total, t=t, top=top):
            tile = logits[pl.ds(pl.multiple_of(i * 128, 128), 128), t * 128 : (t + 1) * 128]
            return total + jnp.sum(jnp.exp(tile - top).reshape(16, 8, 128), axis=0)

        total = lax.fori_loop(0, 8, cols_pass, jnp.zeros((8, 128), F32), unroll=True)
        part = top + jnp.log(jnp.sum(total, axis=0, keepdims=True))
        j, i = t // 2, (t % 2) * 2
        col_out[pl.ds(col_place(where, j, i)[0], 1), :] = part
        col_out[pl.ds(col_place(where, j, i + 1)[0], 1), :] = pltpu.roll(part, 64, 1)
        line = jnp.transpose(row_wide[t * 128 : (t + 1) * 128, :])[0:1]
        row_out[pl.ds(row_place(where, j, i)[0], 1), :] = line
        row_out[pl.ds(row_place(where, j, i + 1)[0], 1), :] = pltpu.roll(line, 64, 1)
    message[:16, :] = jnp.where(where[1] == 0, col_out[...], row_out[...])


def logits_call(place, scale, images, texts):
    return pl.pallas_call(
        logits_body,
        out_shape=(
            jax.ShapeDtypeStruct((BLOCK, BLOCK), F32),
            jax.ShapeDtypeStruct((16, 128), F32),
            jax.ShapeDtypeStruct((16, 128), F32),
            jax.ShapeDtypeStruct((24, 128), F32),
            jax.ShapeDtypeStruct((8, 128), F32),
            PART,
        ),
        in_specs=[SMEM, SMEM] + [VMEM] * 9,
        out_specs=(VMEM,) * 6,
        scratch_shapes=[pltpu.VMEM((BLOCK, 128), F32)],
        compiler_params=PARAMS,
    )(place, scale, *images, *texts)


def spread_body(place, row, col, matched, got, out):
    first = place[1] == 0
    mine, other = row[...], got[:16, :]
    top = jnp.maximum(col[...], other)
    both = top + jnp.log(jnp.exp(col[...] - top) + jnp.exp(other - top))
    hits = matched[...] + got[16:24, :]
    for i in range(16):
        out[i, :16, :] = jnp.where(first, mine, both)
        out[i, 16:32, :] = jnp.where(first, other, both)
        out[i, 32:40, :] = hits


def spread_call(place, *parts):
    return pl.pallas_call(
        spread_body,
        out_shape=jax.ShapeDtypeStruct((16, 40, 128), F32),
        in_specs=[SMEM] + [VMEM] * 4,
        out_specs=VMEM,
        compiler_params=PARAMS,
    )(place, *parts)


def in_ring(place, i, plane_core):
    return jnp.logical_or(place[1] == plane_core, (place[3] >> 1) == i % 2)


def join_body(place, got, mine, message, share):
    first = place[1] == 0
    parts = [jnp.where(in_ring(place, i, 0), got[i, :32, :], -jnp.inf) for i in range(16)]
    top = parts[0]
    for p in parts[1:]:
        top = jnp.maximum(top, p)
    total = jnp.exp(parts[0] - top)
    for p in parts[1:]:
        total += jnp.exp(p - top)
    state = top + jnp.log(total)
    hits = got[0, 32:40, :]
    for i in range(1, 16):
        hits += got[i, 32:40, :]
    mine[...] = state[:16]
    message[...] = jnp.where(first, state[16:], state[:16])
    real = lax.broadcasted_iota(jnp.int32, (16, 128), 1) < ROWS
    both = jnp.where(real, state[:16] + jnp.where(first, state[16:], 0.0), 0.0)
    share[...] = jnp.sum(both, keepdims=True) - jnp.where(first, 2.0 * hits, 0.0)


def join_call(place, got):
    return pl.pallas_call(
        join_body,
        out_shape=(
            jax.ShapeDtypeStruct((16, 128), F32),
            jax.ShapeDtypeStruct((16, 128), F32),
            jax.ShapeDtypeStruct((8, 128), F32),
        ),
        in_specs=[SMEM, VMEM],
        out_specs=(VMEM,) * 3,
        compiler_params=PARAMS,
    )(place, got)


def loss_body(place, got, out):
    total = None
    for i in range(16):
        v = jnp.where(in_ring(place, i, 1), got[i], 0.0)
        total = v if total is None else total + v
    out[...] = total


def loss_call(place, got):
    return pl.pallas_call(
        loss_body,
        out_shape=jax.ShapeDtypeStruct((8, 128), F32),
        in_specs=[SMEM, VMEM],
        out_specs=VMEM,
        compiler_params=PARAMS,
    )(place, got)


def weights_body(place, scale, logits, mine, other, *refs):
    images = refs[:4]
    weights = refs[4]
    outs = refs[5:9]
    row_wide, row_lse, col_lse = refs[9:12]
    first = place[1] == 0
    row_lse[...] = jnp.where(first, mine[...], other[...])
    col_lse[...] = jnp.where(first, other[...], mine[...])
    where = [place[i] for i in range(5)]
    multiplier = scale[0]
    lane = lax.broadcasted_iota(jnp.int32, (1, 128), 1)
    cols = col_ids(where)
    col_line = []
    for t in range(8):
        j, i = t // 2, (t % 2) * 2
        lo = col_lse[pl.ds(col_place(where, j, i)[0], 1), :]
        hi = col_lse[pl.ds(col_place(where, j, i + 1)[0], 1), :]
        col_line.append(jnp.where(lane < ROWS, lo, pltpu.roll(hi, 64, 1)))
        lo = row_lse[pl.ds(row_place(where, j, i)[0], 1), :]
        hi = row_lse[pl.ds(row_place(where, j, i + 1)[0], 1), :]
        line = jnp.where(lane < ROWS, lo, pltpu.roll(hi, 64, 1))
        row_wide[t * 128 : (t + 1) * 128, :] = jnp.transpose(jnp.broadcast_to(line, (128, 128)))
    for a in range(4):
        ids = row_ids(where, a)
        for b in range(4):
            at = a * CHUNK + b * ROWS
            wide = row_wide[at : at + ROWS, :]
            for t in range(8):
                tile = logits[at : at + ROWS, t * 128 : (t + 1) * 128]
                both = 0.5 * jnp.exp(tile - wide) + 0.5 * jnp.exp(tile - col_line[t])
                both = both - jnp.where(ids[b] == cols[t][0:1], 1.0, 0.0)
                weights[at : at + ROWS, t * 128 : (t + 1) * 128] = both.astype(BF16)
    text_terms(multiplier, weights, images, ((2, 0, outs[0]), (3, 0, outs[1]), (1, 0, outs[2]), (3, 3 * ROWS, outs[3])))


def text_terms(multiplier, weights, images, outs):
    for j, skip, out in outs:
        at = j * CHUNK + skip
        for e in range(5):
            acc = None
            for a in range(4):
                term = lax.dot_general(
                    weights[a * CHUNK : (a + 1) * CHUNK, at : at + out.shape[0]],
                    images[a][:, e * 256 : (e + 1) * 256],
                    (((0,), (0,)), ((), ())),
                    preferred_element_type=F32,
                )
                acc = term if acc is None else acc + term
            out[:, e * 256 : (e + 1) * 256] = (multiplier * acc).astype(BF16)


def image_terms(multiplier, weights, texts, outs):
    for a, out in outs.items():
        for e in range(5):
            acc = None
            for j in range(4):
                term = jnp.dot(
                    weights[a * CHUNK : (a + 1) * CHUNK, j * CHUNK : (j + 1) * CHUNK],
                    texts[j][:, e * 256 : (e + 1) * 256],
                    preferred_element_type=F32,
                )
                acc = term if acc is None else acc + term
            out[:, e * 256 : (e + 1) * 256] = (multiplier * acc).astype(BF16)


PART = jax.ShapeDtypeStruct((CHUNK, EMBED), BF16)


def weights_call(place, scale, logits, mine, other, images):
    return pl.pallas_call(
        weights_body,
        out_shape=(
            jax.ShapeDtypeStruct((BLOCK, BLOCK), BF16),
            PART,
            jax.ShapeDtypeStruct((3 * ROWS, EMBED), BF16),
            PART,
            jax.ShapeDtypeStruct((ROWS, EMBED), BF16),
        ),
        in_specs=[SMEM, SMEM] + [VMEM] * 7,
        out_specs=(VMEM,) * 5,
        scratch_shapes=[
            pltpu.VMEM((BLOCK, 128), F32),
            pltpu.VMEM((16, 128), F32),
            pltpu.VMEM((16, 128), F32),
        ],
        compiler_params=PARAMS,
    )(place, scale, logits, mine, other, *images)


def image_body(scale, weights, *refs):
    image_terms(scale[0], weights, refs[:4], dict(zip((2, 1, 3), refs[4:])))


def image_call(scale, weights, texts):
    return pl.pallas_call(
        image_body,
        out_shape=(PART,) * 3,
        in_specs=[SMEM] + [VMEM] * 5,
        out_specs=(VMEM,) * 3,
        compiler_params=PARAMS,
    )(scale, weights, *texts)


def rest_body(scale, share, weights, *refs):
    images, texts, outs = refs[:4], refs[4:8], refs[8:]
    text_terms(scale[0], weights, images, ((0, 0, outs[0]),))
    image_terms(scale[0], weights, texts, {0: outs[1]})
    for i in range(16):
        outs[2][i] = share[...]


def rest_call(scale, share, weights, images, texts):
    return pl.pallas_call(
        rest_body,
        out_shape=(PART, PART, jax.ShapeDtypeStruct((16, 8, 128), F32)),
        in_specs=[SMEM] + [VMEM] * 10,
        out_specs=(VMEM,) * 3,
        compiler_params=PARAMS,
    )(scale, share, weights, *images, *texts)


def sums_body(n, plan, *refs):
    for (rows, terms), out in zip(plan, refs[n:]):
        for at in range(0, rows, 16):
            total = None
            for i, skip in terms:
                v = refs[i][skip + at : skip + at + 16, :].astype(F32)
                total = v if total is None else total + v
            out[at : at + 16, :] = total.astype(out.dtype)


def sums(arrays, *plan):
    out = pl.pallas_call(
        lambda *refs: sums_body(len(arrays), plan, *refs),
        out_shape=tuple(jax.ShapeDtypeStruct((rows, EMBED), BF16) for rows, _ in plan),
        in_specs=[VMEM] * len(arrays),
        out_specs=(VMEM,) * len(plan),
        compiler_params=PARAMS,
    )(*arrays)
    return out if len(plan) > 1 else out[0]


def mean_body(a, b, out):
    out[...] = (a[0:1, 0:1] + b[0:1, 0:1]) * (1.0 / (2.0 * ROWS * 256))


def mean_call(a, b):
    return pl.pallas_call(
        mean_body,
        out_shape=jax.ShapeDtypeStruct((1, 1), F32),
        in_specs=[VMEM] * 2,
        out_specs=VMEM,
        compiler_params=PARAMS,
    )(a, b)


def local(image_emb, text_emb, logit_scale):
    place = jnp.stack([lax.axis_index(n) for n in AXES]).astype(jnp.int32)

    (chip,) = pack([text_emb, core_swap(text_emb)], ((0, 0, 64), (1, 0, 64)))
    next_1, next_4 = z_shift(chip, -1), z_shift(text_emb, 4)
    near = [plane_shift(image_emb, k, True) for k in (1, 2, 3)]
    own, text_0, side = pack(
        [image_emb] + near + [chip, next_1, next_4],
        ((0, 0, 64), (1, 0, 64), (2, 0, 64), (3, 0, 64)),
        ((4, 0, 128), (5, 0, 128)),
        ((5, 0, 128), (6, 0, 64)),
    )
    text_1, text_3 = z_shift(text_0, -2), core_swap(side)
    images = [own] + [plane_shift(own, k, False) for k in (1, 2, 3)]
    texts = [text_0, text_1, core_swap(text_1)]

    logits, row_part, col_part, message, matched, text_3 = logits_call(
        place, logit_scale, images, texts + [text_3, next_4]
    )
    texts.append(text_3)

    spread = spread_call(place, row_part, col_part, matched, core_swap(message))
    mine, message, share = join_call(place, exchange(spread, 0))
    weights, text_2, text_3, text_1, far = weights_call(
        place, logit_scale, logits, mine, core_swap(message), images
    )

    other_1, other_3 = core_swap(text_2), core_swap(text_3)
    pairs, far = sums(
        [text_1, other_1, far, other_3], (256, ((0, 0), (1, 0))), (64, ((2, 0), (3, 128)))
    )
    pairs = z_shift(pairs, 2)
    image_parts = image_call(logit_scale, weights, texts)
    back = [plane_shift(v, -k, False) for v, k in zip(image_parts, (2, 1, 3))]
    text_0, image_0, shares = rest_call(logit_scale, share, weights, images, texts)

    s = loss_call(place, exchange(shares, 1))
    mean_loss = mean_call(s, core_swap(s)).reshape(1)

    next_1, mine, *pieces = sums(
        [text_0, other_3, pairs, image_0] + back + [s],
        (128, ((0, 128), (1, 0), (2, 128))),
        (128, ((0, 0), (2, 0))),
        *[(64, [(i, 64 * k) for i in range(3, 7)]) for k in range(4)],
    )
    next_1, next_4 = z_shift(next_1, 1), z_shift(far, 4)
    shards = [pieces[0]] + [plane_shift(pieces[k], -k, True) for k in (2, 1, 3)]
    mine, other = sums([mine, next_1], (64, ((0, 0), (1, 0))), (64, ((0, 64), (1, 64))))
    image_grad = sums(shards, (64, [(i, 0) for i in range(4)]))
    text_grad = sums([mine, core_swap(other), next_4], (64, ((0, 0), (1, 0), (2, 0))))
    return mean_loss, image_grad, text_grad


def solution(mesh):
    fine = Mesh(mesh.devices.reshape(4, 2, 2, 4, 4), AXES)
    return jax.shard_map(
        local,
        mesh=fine,
        in_specs=(P(AXES, None), P(("zh", "y", "x", "zl", "core"), None), P()),
        out_specs=(P(), P(AXES, None), P(("zh", "y", "x", "zl", "core"), None)),
        check_vma=False,
    )
```

```python
import math

import jax
import jax.numpy as jnp
from jax import lax
from jax.experimental import pallas as pl
from jax.experimental.pallas import tpu as pltpu
from jax.sharding import Mesh, PartitionSpec as P

AXES = ("zl", "core", "zh", "y", "x")
NX, NY, NZ = 4, 4, 8
ROWS, EMBED = 64, 1280
CHUNK = 4 * ROWS
BLOCK = 16 * ROWS
BF16, F32 = jnp.bfloat16, jnp.float32
LOG2E, LN2 = math.log2(math.e), math.log(2.0)
VMEM = pl.BlockSpec(memory_space=pltpu.VMEM)
SMEM = pl.BlockSpec(memory_space=pltpu.SMEM)
PARAMS = pltpu.CompilerParams(vmem_limit_bytes=12 * 1024 * 1024)


def plane_shift(v, k, primary):
    pairs = []
    for c in range(2):
        for h in range(2):
            for y in range(NY):
                for x in range(NX):
                    if (c == 0) == primary:
                        to = (y, (x + k) % NX)
                    else:
                        to = ((y + k) % NY, x)
                    base = (c * 2 + h) * NY
                    pairs.append(((base + y) * NX + x, (base + to[0]) * NX + to[1]))
    return lax.ppermute(v, ("core", "zh", "y", "x"), pairs)


def z_shift(v, k):
    pairs = []
    for c in range(2):
        for z in range(NZ):
            to = (z + (k if c == 0 else -k)) % NZ
            pairs.append((((z % 4) * 2 + c) * 2 + z // 4, ((to % 4) * 2 + c) * 2 + to // 4))
    return lax.ppermute(v, ("zl", "core", "zh"), pairs)


def core_swap(v):
    return lax.ppermute(v, "core", [(0, 1), (1, 0)])


def device(c, y, x, z):
    return ((((z % 4) * 2 + c) * 2 + z // 4) * NY + y) * NX + x


def plane_or_ring():
    out = [[device(0, y, x, z) for y in range(NY) for x in range(NX)] for z in range(NZ)]
    return out + [
        [device(1, y + d, x, z) for z in range(NZ) for d in (0, 2)] for y in range(2) for x in range(NX)
    ]


def slanted():
    return [
        [device(c, p // 4, p % 4, (g + p // 2) % NZ) for p in range(16)] for c in range(2) for g in range(NZ)
    ]


def exchange(v, groups):
    return lax.all_to_all(v, AXES, 0, 0, axis_index_groups=groups)


def row_place(where, a, b):
    zl, c, zh, y, x = where
    p, s = jnp.where(c == 0, b, a), jnp.where(c == 0, a, b)
    n = ((y - s) & 3) * 4 + ((x - p) & 3)
    return n, ((zl * 2 + c) * 2 + zh) * 16 + n


def col_place(where, j, i):
    zl, c, zh, y, x = where
    core = c if (i % 2 == 0) == (j < 2) else 1 - c
    sign = 1 - 2 * c
    off = ((0, 0, 1, 1), (2, 2, 3, 3), (-2, -2, -3, -3), (-1, -1, 4, 4))[j][i]
    off = 4 if off == 4 else sign * off
    z = (zh * 4 + zl + off) & 7
    return z * 2 + core, ((z >> 2) * 16 + y * 4 + x) * 8 + (z & 3) * 2 + core


def row_ids(where, a):
    span = lax.broadcasted_iota(jnp.int32, (ROWS, 128), 0)
    return [row_place(where, a, b)[1] * ROWS + span for b in range(4)]


def col_ids(where):
    lane = lax.broadcasted_iota(jnp.int32, (8, 128), 1)
    out = []
    for t in range(8):
        lo = col_place(where, t // 2, (t % 2) * 2)[1] * ROWS
        hi = col_place(where, t // 2, (t % 2) * 2 + 1)[1] * ROWS - ROWS
        out.append(lane + jnp.where(lane < ROWS, lo, hi))
    return out


def pack_body(plan, n, *refs):
    for parts, out in zip(plan, refs[n:]):
        row = 0
        for i, rows in parts:
            out[row : row + rows, :] = refs[i][...]
            row += rows


def pack(arrays, *plan):
    shapes = [jax.ShapeDtypeStruct((sum(p[1] for p in parts), EMBED), BF16) for parts in plan]
    return pl.pallas_call(
        lambda *refs: pack_body(plan, len(arrays), *refs),
        out_shape=tuple(shapes),
        in_specs=[VMEM] * len(arrays),
        out_specs=(VMEM,) * len(plan),
        compiler_params=PARAMS,
    )(*arrays)


def logits_body(place, scale, *refs):
    images = refs[:4]
    texts = (*refs[4:7], refs[15])
    logits, row_out, col_out, message, match_out, text_3 = refs[10:16]
    row_wide = refs[16]
    text_3[: 2 * ROWS, :] = refs[7][...]
    text_3[2 * ROWS : 3 * ROWS, :] = refs[8][...]
    text_3[3 * ROWS :, :] = refs[9][...]
    where = [place[i] for i in range(5)]
    multiplier = scale[0] * LOG2E
    for a in range(4):
        for j in range(4):
            logits[a * CHUNK : (a + 1) * CHUNK, j * CHUNK : (j + 1) * CHUNK] = (
                multiplier
                * lax.dot_general(
                    images[a][...],
                    texts[j][...],
                    (((1,), (1,)), ((), ())),
                    preferred_element_type=F32,
                )
            )
    cols = col_ids(where)
    step = 32
    matched = jnp.zeros((8, 128), F32)
    col_top = [jnp.full((8, 128), -jnp.inf, F32) for _ in range(8)]
    for a in range(4):
        ids = row_ids(where, a)
        for b in range(4):
            for half in range(ROWS // step):
                at = a * CHUNK + b * ROWS + half * step
                tiles = [logits[at : at + step, t * 128 : (t + 1) * 128] for t in range(8)]
                top = tiles[0]
                for t in range(1, 8):
                    top = jnp.maximum(top, tiles[t])
                top = jnp.max(top, axis=1, keepdims=True)
                mine = ids[b][half * step : (half + 1) * step]
                total = jnp.zeros((step, 128), F32)
                for t in range(8):
                    total += jnp.exp2(tiles[t] - top)
                    folded = tiles[t].reshape(step // 8, 8, 128)
                    col_top[t] = jnp.maximum(col_top[t], jnp.max(folded, axis=0))
                    hit = jnp.where(mine == cols[t][0:1], tiles[t], 0.0)
                    matched += jnp.sum(hit.reshape(step // 8, 8, 128), axis=0)
                part = top + LOG2E * jnp.log(jnp.sum(total, axis=1, keepdims=True))
                row_wide[at : at + step, :] = jnp.broadcast_to(part, (step, 128))
    matched = jnp.broadcast_to(jnp.sum(matched, keepdims=True), (8, 128))
    match_out[...] = matched
    message[16:24, :] = matched
    for t in range(8):
        top = jnp.max(col_top[t], axis=0, keepdims=True)

        def cols_pass(i, total, t=t, top=top):
            tile = logits[pl.ds(pl.multiple_of(i * 128, 128), 128), t * 128 : (t + 1) * 128]
            return total + jnp.sum(jnp.exp2(tile - top).reshape(16, 8, 128), axis=0)

        total = lax.fori_loop(0, 8, cols_pass, jnp.zeros((8, 128), F32), unroll=True)
        part = top + LOG2E * jnp.log(jnp.sum(total, axis=0, keepdims=True))
        j, i = t // 2, (t % 2) * 2
        col_out[pl.ds(col_place(where, j, i)[0], 1), :] = part
        col_out[pl.ds(col_place(where, j, i + 1)[0], 1), :] = pltpu.roll(part, 64, 1)
        line = jnp.transpose(row_wide[t * 128 : (t + 1) * 128, :])[0:1]
        row_out[pl.ds(row_place(where, j, i)[0], 1), :] = line
        row_out[pl.ds(row_place(where, j, i + 1)[0], 1), :] = pltpu.roll(line, 64, 1)
    message[:16, :] = jnp.where(where[1] == 0, col_out[...], row_out[...])


def logits_call(place, scale, images, texts):
    return pl.pallas_call(
        logits_body,
        out_shape=(
            jax.ShapeDtypeStruct((BLOCK, BLOCK), F32),
            jax.ShapeDtypeStruct((16, 128), F32),
            jax.ShapeDtypeStruct((16, 128), F32),
            jax.ShapeDtypeStruct((24, 128), F32),
            jax.ShapeDtypeStruct((8, 128), F32),
            PART,
        ),
        in_specs=[SMEM, SMEM] + [VMEM] * 10,
        out_specs=(VMEM,) * 6,
        scratch_shapes=[pltpu.VMEM((BLOCK, 128), F32)],
        compiler_params=PARAMS,
    )(place, scale, *images, *texts)


def spread_body(place, row, col, matched, got, out):
    first = place[1] == 0
    mine, other = row[...], got[:16, :]
    top = jnp.maximum(col[...], other)
    both = top + LOG2E * jnp.log(jnp.exp2(col[...] - top) + jnp.exp2(other - top))
    hits = matched[...] + got[16:24, :]
    for i in range(16):
        out[i, :16, :] = jnp.where(first, mine, both)
        out[i, 16:32, :] = jnp.where(first, other, both)
        out[i, 32:40, :] = hits


def spread_call(place, *parts):
    return pl.pallas_call(
        spread_body,
        out_shape=jax.ShapeDtypeStruct((16, 40, 128), F32),
        in_specs=[SMEM] + [VMEM] * 4,
        out_specs=VMEM,
        compiler_params=PARAMS,
    )(place, *parts)


def join_body(place, got, mine, message):
    first = place[1] == 0
    counts = [jnp.logical_or(first, (place[3] >> 1) == i % 2) for i in range(16)]
    parts = [jnp.where(counts[i], got[i, :32, :], -jnp.inf) for i in range(16)]
    top = parts[0]
    for p in parts[1:]:
        top = jnp.maximum(top, p)
    total = jnp.exp2(parts[0] - top)
    for p in parts[1:]:
        total += jnp.exp2(p - top)
    state = top + LOG2E * jnp.log(total)
    hits = got[0, 32:40, :]
    for i in range(1, 16):
        hits += got[i, 32:40, :]
    real = lax.broadcasted_iota(jnp.int32, (16, 128), 1) < ROWS
    both = jnp.where(real, state[:16] + jnp.where(first, state[16:], 0.0), 0.0)
    share = jnp.sum(both, keepdims=True) - jnp.where(first, 2.0 * hits, 0.0)
    mine[:16, :] = state[:16]
    mine[16:24, :] = share
    message[:16, :] = jnp.where(first, state[16:], state[:16])
    message[16:24, :] = share


def join_call(place, got):
    return pl.pallas_call(
        join_body,
        out_shape=(jax.ShapeDtypeStruct((24, 128), F32),) * 2,
        in_specs=[SMEM, VMEM],
        out_specs=(VMEM,) * 2,
        compiler_params=PARAMS,
    )(place, got)


def loss_body(place, got, out):
    group = place[2] * 4 + place[0] - ((place[3] * 4 + place[4]) >> 1)
    total = got[0, 4:5, 0:1]
    for p in range(1, 16):
        total = total + got[p, 4:5, 0:1]
    for z in range(NZ):
        total = total + got[2 * ((z - group) & 7), 0:1, 0:1]
    out[...] = total * (LN2 / (2.0 * ROWS * 256))


def loss_call(place, got):
    return pl.pallas_call(
        loss_body,
        out_shape=jax.ShapeDtypeStruct((1, 1), F32),
        in_specs=[SMEM, VMEM],
        out_specs=VMEM,
        compiler_params=PARAMS,
    )(place, got)


def weights_body(place, scale, logits, mine, other, *refs):
    images = refs[:4]
    weights = refs[4]
    outs = refs[5:9]
    row_wide, row_lse, col_lse = refs[9:12]
    first = place[1] == 0
    row_lse[...] = jnp.where(first, mine[:16, :], other[:16, :]) + 1.0
    col_lse[...] = jnp.where(first, other[:16, :], mine[:16, :]) + 1.0
    where = [place[i] for i in range(5)]
    multiplier = scale[0]
    lane = lax.broadcasted_iota(jnp.int32, (1, 128), 1)
    cols = col_ids(where)
    col_line = []
    for t in range(8):
        j, i = t // 2, (t % 2) * 2
        lo = col_lse[pl.ds(col_place(where, j, i)[0], 1), :]
        hi = col_lse[pl.ds(col_place(where, j, i + 1)[0], 1), :]
        col_line.append(jnp.where(lane < ROWS, lo, pltpu.roll(hi, 64, 1)))
        lo = row_lse[pl.ds(row_place(where, j, i)[0], 1), :]
        hi = row_lse[pl.ds(row_place(where, j, i + 1)[0], 1), :]
        line = jnp.where(lane < ROWS, lo, pltpu.roll(hi, 64, 1))
        row_wide[t * 128 : (t + 1) * 128, :] = jnp.transpose(jnp.broadcast_to(line, (128, 128)))
    for a in range(4):
        ids = row_ids(where, a)
        for b in range(4):
            at = a * CHUNK + b * ROWS
            wide = row_wide[at : at + ROWS, :]
            for t in range(8):
                tile = logits[at : at + ROWS, t * 128 : (t + 1) * 128]
                both = jnp.exp2(tile - wide) + jnp.exp2(tile - col_line[t])
                both = both - jnp.where(ids[b] == cols[t][0:1], 1.0, 0.0)
                weights[at : at + ROWS, t * 128 : (t + 1) * 128] = both.astype(BF16)
    text_terms(multiplier, weights, images, ((2, 0, outs[0]), (3, 0, outs[1]), (1, 0, outs[2]), (3, 3 * ROWS, outs[3])))


def text_terms(multiplier, weights, images, outs):
    for j, skip, out in outs:
        at = j * CHUNK + skip
        for e in range(5):
            acc = None
            for a in range(4):
                term = lax.dot_general(
                    weights[a * CHUNK : (a + 1) * CHUNK, at : at + out.shape[0]],
                    images[a][:, e * 256 : (e + 1) * 256],
                    (((0,), (0,)), ((), ())),
                    preferred_element_type=F32,
                )
                acc = term if acc is None else acc + term
            out[:, e * 256 : (e + 1) * 256] = (multiplier * acc).astype(BF16)


def image_terms(multiplier, weights, texts, outs):
    for a, out in outs.items():
        for e in range(5):
            acc = None
            for j in range(4):
                term = jnp.dot(
                    weights[a * CHUNK : (a + 1) * CHUNK, j * CHUNK : (j + 1) * CHUNK],
                    texts[j][:, e * 256 : (e + 1) * 256],
                    preferred_element_type=F32,
                )
                acc = term if acc is None else acc + term
            out[:, e * 256 : (e + 1) * 256] = (multiplier * acc).astype(BF16)


PART = jax.ShapeDtypeStruct((CHUNK, EMBED), BF16)


def weights_call(place, scale, logits, mine, other, images):
    return pl.pallas_call(
        weights_body,
        out_shape=(
            jax.ShapeDtypeStruct((BLOCK, BLOCK), BF16),
            PART,
            jax.ShapeDtypeStruct((3 * ROWS, EMBED), BF16),
            PART,
            jax.ShapeDtypeStruct((ROWS, EMBED), BF16),
        ),
        in_specs=[SMEM, SMEM] + [VMEM] * 7,
        out_specs=(VMEM,) * 5,
        scratch_shapes=[
            pltpu.VMEM((BLOCK, 128), F32),
            pltpu.VMEM((16, 128), F32),
            pltpu.VMEM((16, 128), F32),
        ],
        compiler_params=PARAMS,
    )(place, scale, logits, mine, other, *images)


def image_body(scale, weights, *refs):
    image_terms(scale[0], weights, refs[:4], dict(zip((2, 1, 3), refs[4:])))


def image_call(scale, weights, texts):
    return pl.pallas_call(
        image_body,
        out_shape=(PART,) * 3,
        in_specs=[SMEM] + [VMEM] * 5,
        out_specs=(VMEM,) * 3,
        compiler_params=PARAMS,
    )(scale, weights, *texts)


def rest_body(place, scale, mine, other, weights, *refs):
    images, texts, outs = refs[:4], refs[4:8], refs[8:]
    text_terms(scale[0], weights, images, ((0, 0, outs[0]),))
    image_terms(scale[0], weights, texts, {0: outs[1]})
    core_0 = jnp.where(place[1] == 0, mine[16:24, :], other[16:24, :])
    core_1 = jnp.where(place[1] == 0, other[16:24, :], mine[16:24, :])
    both = jnp.where(lax.broadcasted_iota(jnp.int32, (8, 128), 0) < 4, core_0, core_1)
    for i in range(16):
        outs[2][i] = both


def rest_call(place, scale, mine, other, weights, images, texts):
    return pl.pallas_call(
        rest_body,
        out_shape=(PART, PART, jax.ShapeDtypeStruct((16, 8, 128), F32)),
        in_specs=[SMEM, SMEM] + [VMEM] * 11,
        out_specs=(VMEM,) * 3,
        compiler_params=PARAMS,
    )(place, scale, mine, other, weights, *images, *texts)


def sums_body(n, plan, *refs):
    for (rows, terms), out in zip(plan, refs[n:]):
        for at in range(0, rows, 16):
            total = None
            for i, skip in terms:
                v = refs[i][skip + at : skip + at + 16, :].astype(F32)
                total = v if total is None else total + v
            out[at : at + 16, :] = total.astype(out.dtype)


def sums(arrays, *plan):
    out = pl.pallas_call(
        lambda *refs: sums_body(len(arrays), plan, *refs),
        out_shape=tuple(jax.ShapeDtypeStruct((rows, EMBED), BF16) for rows, _ in plan),
        in_specs=[VMEM] * len(arrays),
        out_specs=(VMEM,) * len(plan),
        compiler_params=PARAMS,
    )(*arrays)
    return out if len(plan) > 1 else out[0]


def local(image_emb, text_emb, logit_scale):
    place = jnp.stack([lax.axis_index(n) for n in AXES]).astype(jnp.int32)

    chip, image = pack([text_emb, core_swap(text_emb), image_emb], ((0, 64), (1, 64)), ((2, 64),))
    next_1, next_4 = z_shift(chip, -1), z_shift(text_emb, 4)
    near = [plane_shift(image, k, True) for k in (1, 2, 3)]
    own, text_0, next_4 = pack(
        [image] + near + [chip, next_1, next_4],
        ((0, 64), (1, 64), (2, 64), (3, 64)),
        ((4, 128), (5, 128)),
        ((6, 64),),
    )
    text_1 = z_shift(text_0, -2)
    images = [own] + [plane_shift(own, k, False) for k in (1, 2, 3)]
    texts = [text_0, text_1, core_swap(text_1)]

    logits, row_part, col_part, message, matched, text_3 = logits_call(
        place, logit_scale, images, texts + [core_swap(next_1), core_swap(next_4), next_4]
    )
    texts.append(text_3)

    spread = spread_call(place, row_part, col_part, matched, core_swap(message))
    mine, message = join_call(place, exchange(spread, plane_or_ring()))
    other = core_swap(message)
    weights, text_2, text_3, text_1, far = weights_call(place, logit_scale, logits, mine, other, images)

    other_1, other_3 = core_swap(text_2), core_swap(text_3)
    pairs, far = sums(
        [text_1, other_1, far, other_3], (256, ((0, 0), (1, 0))), (64, ((2, 0), (3, 128)))
    )
    pairs, next_4 = z_shift(pairs, 2), z_shift(far, 4)
    image_parts = image_call(logit_scale, weights, texts)
    back = [plane_shift(v, -k, False) for v, k in zip(image_parts, (2, 1, 3))]
    text_0, image_0, shares = rest_call(place, logit_scale, mine, other, weights, images, texts)
    mean_loss = loss_call(place, exchange(shares, slanted()))

    next_1, mine, *pieces = sums(
        [text_0, other_3, pairs, image_0] + back + [next_4, mean_loss],
        (128, ((0, 128), (1, 0), (2, 128))),
        (128, ((0, 0), (2, 0))),
        *[(64, [(i, 64 * k) for i in range(3, 7)]) for k in range(4)],
    )
    next_1 = z_shift(next_1, 1)
    shards = [pieces[0]] + [plane_shift(pieces[k], -k, True) for k in (2, 1, 3)]
    mine, other = sums([mine, next_1], (64, ((0, 0), (1, 0))), (64, ((0, 64), (1, 64))))
    image_grad = sums(shards, (64, [(i, 0) for i in range(4)]))
    text_grad = sums([mine, core_swap(other), next_4], (64, ((0, 0), (1, 0), (2, 0))))
    return mean_loss.reshape(1), image_grad, text_grad


def solution(mesh):
    fine = Mesh(mesh.devices.reshape(4, 2, 2, 4, 4), AXES)
    return jax.shard_map(
        local,
        mesh=fine,
        in_specs=(P(AXES, None), P(("zh", "y", "x", "zl", "core"), None), P()),
        out_specs=(P(), P(AXES, None), P(("zh", "y", "x", "zl", "core"), None)),
        check_vma=False,
    )
```

```python
import math

import jax
import jax.numpy as jnp
from jax import lax
from jax.experimental import pallas as pl
from jax.experimental.pallas import tpu as pltpu
from jax.sharding import Mesh, PartitionSpec as P

AXES = ("zl", "core", "zh", "y", "x")
NX, NY, NZ = 4, 4, 8
ROWS, EMBED = 64, 1280
CHUNK = 4 * ROWS
TAIL, DIGITS = 16, 13
BLOCK = 16 * ROWS
BF16, F32 = jnp.bfloat16, jnp.float32
LOG2E, LN2 = math.log2(math.e), math.log(2.0)
VMEM = pl.BlockSpec(memory_space=pltpu.VMEM)
SMEM = pl.BlockSpec(memory_space=pltpu.SMEM)
PARAMS = pltpu.CompilerParams(vmem_limit_bytes=12 * 1024 * 1024)


def plane_shift(v, k, primary):
    pairs = []
    for c in range(2):
        for h in range(2):
            for y in range(NY):
                for x in range(NX):
                    if (c == 0) == primary:
                        to = (y, (x + k) % NX)
                    else:
                        to = ((y + k) % NY, x)
                    base = (c * 2 + h) * NY
                    pairs.append(((base + y) * NX + x, (base + to[0]) * NX + to[1]))
    return lax.ppermute(v, ("core", "zh", "y", "x"), pairs)


def z_shift(v, k):
    pairs = []
    for c in range(2):
        for z in range(NZ):
            to = (z + (k if c == 0 else -k)) % NZ
            pairs.append((((z % 4) * 2 + c) * 2 + z // 4, ((to % 4) * 2 + c) * 2 + to // 4))
    return lax.ppermute(v, ("zl", "core", "zh"), pairs)


def core_swap(v):
    return lax.ppermute(v, "core", [(0, 1), (1, 0)])


def device(c, y, x, z):
    return ((((z % 4) * 2 + c) * 2 + z // 4) * NY + y) * NX + x


def plane_or_ring():
    out = [[device(0, y, x, z) for y in range(NY) for x in range(NX)] for z in range(NZ)]
    return out + [
        [device(1, y + d, x, z) for z in range(NZ) for d in (0, 2)] for y in range(2) for x in range(NX)
    ]


def exchange(v, groups):
    return lax.all_to_all(v, AXES, 0, 0, axis_index_groups=groups)


def row_place(where, a, b):
    zl, c, zh, y, x = where
    p, s = jnp.where(c == 0, b, a), jnp.where(c == 0, a, b)
    n = ((y - s) & 3) * 4 + ((x - p) & 3)
    return n, ((zl * 2 + c) * 2 + zh) * 16 + n


def col_place(where, j, i):
    zl, c, zh, y, x = where
    core = c if (i % 2 == 0) == (j < 2) else 1 - c
    sign = 1 - 2 * c
    off = ((0, 0, 1, 1), (2, 2, 3, 3), (-2, -2, -3, -3), (-1, -1, 4, 4))[j][i]
    off = 4 if off == 4 else sign * off
    z = (zh * 4 + zl + off) & 7
    return z * 2 + core, ((z >> 2) * 16 + y * 4 + x) * 8 + (z & 3) * 2 + core


def row_ids(where, a):
    span = lax.broadcasted_iota(jnp.int32, (ROWS, 128), 0)
    return [row_place(where, a, b)[1] * ROWS + span for b in range(4)]


def col_ids(where):
    lane = lax.broadcasted_iota(jnp.int32, (8, 128), 1)
    out = []
    for t in range(8):
        lo = col_place(where, t // 2, (t % 2) * 2)[1] * ROWS
        hi = col_place(where, t // 2, (t % 2) * 2 + 1)[1] * ROWS - ROWS
        out.append(lane + jnp.where(lane < ROWS, lo, hi))
    return out


def pack_body(plan, n, *refs):
    for parts, out in zip(plan, refs[n:]):
        row = 0
        for i, rows in parts:
            out[row : row + rows, :] = refs[i][...]
            row += rows


def pack(arrays, *plan):
    shapes = [jax.ShapeDtypeStruct((sum(p[1] for p in parts), EMBED), BF16) for parts in plan]
    return pl.pallas_call(
        lambda *refs: pack_body(plan, len(arrays), *refs),
        out_shape=tuple(shapes),
        in_specs=[VMEM] * len(arrays),
        out_specs=(VMEM,) * len(plan),
        compiler_params=PARAMS,
    )(*arrays)


def block_logits(multiplier, images, texts, logits):
    for a in range(4):
        for j, text in enumerate(texts):
            logits[a * CHUNK : (a + 1) * CHUNK, j * CHUNK : (j + 1) * CHUNK] = (
                multiplier
                * lax.dot_general(
                    images[a][...], text[...], (((1,), (1,)), ((), ())), preferred_element_type=F32
                )
            )


def fold(v):
    return v.reshape(v.shape[0] // 8, 8, 128)


def column_part(logits, t, top):
    top = jnp.max(top, axis=0, keepdims=True)

    def step(i, total):
        tile = logits[pl.ds(pl.multiple_of(i * 128, 128), 128), t * 128 : (t + 1) * 128]
        return total + jnp.sum(fold(jnp.exp2(tile - top)), axis=0)

    total = lax.fori_loop(0, 8, step, jnp.zeros((8, 128), F32), unroll=True)
    return top + LOG2E * jnp.log(jnp.sum(total, axis=0, keepdims=True))


def first_body(scale, *refs):
    images, texts = refs[:4], refs[4:6]
    logits, col_out = refs[6:]
    block_logits(scale[0] * LOG2E, images, texts, logits)
    for t in range(4):
        top = jnp.max(fold(logits[:128, t * 128 : (t + 1) * 128]), axis=0)
        for i in range(1, 8):
            tile = logits[i * 128 : (i + 1) * 128, t * 128 : (t + 1) * 128]
            top = jnp.maximum(top, jnp.max(fold(tile), axis=0))
        col_out[t : t + 1, :] = column_part(logits, t, top)


def first_call(scale, images, texts):
    return pl.pallas_call(
        first_body,
        out_shape=(
            jax.ShapeDtypeStruct((BLOCK, BLOCK // 2), F32),
            jax.ShapeDtypeStruct((8, 128), F32),
        ),
        in_specs=[SMEM] + [VMEM] * 6,
        out_specs=(VMEM,) * 2,
        compiler_params=PARAMS,
    )(scale, *images, *texts)


def second_body(place, scale, logits_0, col_parts, *refs):
    images = refs[:4]
    logits_1, row_out, col_out, message, match_out, text_3 = refs[7:13]
    row_wide = refs[13]
    text_3[: 3 * ROWS, :] = refs[5][...]
    text_3[3 * ROWS :, :] = refs[6][...]
    where = [place[i] for i in range(5)]
    block_logits(scale[0] * LOG2E, images, (refs[4], text_3), logits_1)
    halves = (logits_0, logits_1)
    cols = col_ids(where)
    step = 32
    matched = jnp.zeros((8, 128), F32)
    col_top = [jnp.full((8, 128), -jnp.inf, F32) for _ in range(4)]
    for a in range(4):
        ids = row_ids(where, a)
        for b in range(4):
            for half in range(ROWS // step):
                at = a * CHUNK + b * ROWS + half * step
                tiles = [
                    halves[t // 4][at : at + step, (t % 4) * 128 : (t % 4 + 1) * 128] for t in range(8)
                ]
                top = tiles[0]
                for t in range(1, 8):
                    top = jnp.maximum(top, tiles[t])
                top = jnp.max(top, axis=1, keepdims=True)
                mine = ids[b][half * step : (half + 1) * step]
                total = jnp.zeros((step, 128), F32)
                for t in range(8):
                    total += jnp.exp2(tiles[t] - top)
                    if t > 3:
                        col_top[t - 4] = jnp.maximum(col_top[t - 4], jnp.max(fold(tiles[t]), axis=0))
                    hit = jnp.where(mine == cols[t][0:1], tiles[t], 0.0)
                    matched += jnp.sum(fold(hit), axis=0)
                part = top + LOG2E * jnp.log(jnp.sum(total, axis=1, keepdims=True))
                row_wide[at : at + step, :] = jnp.broadcast_to(part, (step, 128))
    matched = jnp.broadcast_to(jnp.sum(matched, keepdims=True), (8, 128))
    match_out[...] = matched
    message[16:24, :] = matched
    for t in range(8):
        part = col_parts[t : t + 1, :] if t < 4 else column_part(logits_1, t - 4, col_top[t - 4])
        j, i = t // 2, (t % 2) * 2
        col_out[pl.ds(col_place(where, j, i)[0], 1), :] = part
        col_out[pl.ds(col_place(where, j, i + 1)[0], 1), :] = pltpu.roll(part, 64, 1)
        line = jnp.transpose(row_wide[t * 128 : (t + 1) * 128, :])[0:1]
        row_out[pl.ds(row_place(where, j, i)[0], 1), :] = line
        row_out[pl.ds(row_place(where, j, i + 1)[0], 1), :] = pltpu.roll(line, 64, 1)
    message[:16, :] = jnp.where(where[1] == 0, col_out[...], row_out[...])


def second_call(place, scale, logits_0, col_parts, images, texts):
    return pl.pallas_call(
        second_body,
        out_shape=(
            jax.ShapeDtypeStruct((BLOCK, BLOCK // 2), F32),
            jax.ShapeDtypeStruct((16, 128), F32),
            jax.ShapeDtypeStruct((16, 128), F32),
            jax.ShapeDtypeStruct((24, 128), F32),
            jax.ShapeDtypeStruct((8, 128), F32),
            PART,
        ),
        in_specs=[SMEM, SMEM] + [VMEM] * 9,
        out_specs=(VMEM,) * 6,
        scratch_shapes=[pltpu.VMEM((BLOCK, 128), F32)],
        compiler_params=PARAMS,
    )(place, scale, logits_0, col_parts, *images, *texts)


def spread_body(place, row, col, matched, got, out):
    first = place[1] == 0
    mine, other = row[...], got[:16, :]
    top = jnp.maximum(col[...], other)
    both = top + LOG2E * jnp.log(jnp.exp2(col[...] - top) + jnp.exp2(other - top))
    hits = matched[...] + got[16:24, :]
    for i in range(16):
        out[i, :16, :] = jnp.where(first, mine, both)
        out[i, 16:32, :] = jnp.where(first, other, both)
        out[i, 32:40, :] = hits


def spread_call(place, *parts):
    return pl.pallas_call(
        spread_body,
        out_shape=jax.ShapeDtypeStruct((16, 40, 128), F32),
        in_specs=[SMEM] + [VMEM] * 4,
        out_specs=VMEM,
        compiler_params=PARAMS,
    )(place, *parts)


def join_body(place, got, mine, message):
    first = place[1] == 0
    counts = [jnp.logical_or(first, (place[3] >> 1) == i % 2) for i in range(16)]
    parts = [jnp.where(counts[i], got[i, :32, :], -jnp.inf) for i in range(16)]
    top = parts[0]
    for p in parts[1:]:
        top = jnp.maximum(top, p)
    total = jnp.exp2(parts[0] - top)
    for p in parts[1:]:
        total += jnp.exp2(p - top)
    state = top + LOG2E * jnp.log(total)
    hits = got[0, 32:40, :]
    for i in range(1, 16):
        hits += got[i, 32:40, :]
    real = lax.broadcasted_iota(jnp.int32, (16, 128), 1) < ROWS
    both = jnp.where(real, state[:16] + jnp.where(first, state[16:], 0.0), 0.0)
    share = jnp.sum(both, keepdims=True) - jnp.where(first, 2.0 * hits, 0.0)
    mine[:16, :] = state[:16]
    mine[16:24, :] = share
    message[:16, :] = jnp.where(first, state[16:], state[:16])
    message[16:24, :] = share


def join_call(place, got):
    return pl.pallas_call(
        join_body,
        out_shape=(jax.ShapeDtypeStruct((24, 128), F32),) * 2,
        in_specs=[SMEM, VMEM],
        out_specs=(VMEM,) * 2,
        compiler_params=PARAMS,
    )(place, got)


def digits_of(v):
    place = lax.broadcasted_iota(jnp.int32, (16, 128), 0)
    out = jnp.zeros((16, 128), F32)
    for i in range(DIGITS):
        unit = 16.0 ** (7 - i)
        d = jnp.floor(v * (1.0 / unit) + 0.5)
        v = v - d * unit
        out = jnp.where(place == i, d, out)
    return out


def value_of(digits):
    place = lax.broadcasted_iota(jnp.int32, (16, 128), 0)
    units = jnp.zeros((16, 128), F32)
    for i in range(DIGITS):
        units = jnp.where(place == i, 16.0 ** (7 - i), units)
    return jnp.sum(digits * units, axis=0, keepdims=True)


def weights_body(place, scale, logits_0, logits_1, mine, other, *refs):
    images = refs[:4]
    weights = refs[4]
    outs = refs[5:8]
    row_wide, row_lse, col_lse = refs[8:11]
    first = place[1] == 0
    shares = jnp.where(first, mine[16:17, :], other[16:17, :]), jnp.where(first, other[16:17, :], mine[16:17, :])
    for i, share in enumerate(shares):
        tail = digits_of(share).astype(BF16)
        for e in range(EMBED // 128):
            outs[2][i * TAIL : (i + 1) * TAIL, e * 128 : (e + 1) * 128] = tail
    row_lse[...] = jnp.where(first, mine[:16, :], other[:16, :]) + 1.0
    col_lse[...] = jnp.where(first, other[:16, :], mine[:16, :]) + 1.0
    where = [place[i] for i in range(5)]
    multiplier = scale[0]
    lane = lax.broadcasted_iota(jnp.int32, (1, 128), 1)
    cols = col_ids(where)
    col_line = []
    for t in range(8):
        j, i = t // 2, (t % 2) * 2
        lo = col_lse[pl.ds(col_place(where, j, i)[0], 1), :]
        hi = col_lse[pl.ds(col_place(where, j, i + 1)[0], 1), :]
        col_line.append(jnp.where(lane < ROWS, lo, pltpu.roll(hi, 64, 1)))
        lo = row_lse[pl.ds(row_place(where, j, i)[0], 1), :]
        hi = row_lse[pl.ds(row_place(where, j, i + 1)[0], 1), :]
        line = jnp.where(lane < ROWS, lo, pltpu.roll(hi, 64, 1))
        row_wide[t * 128 : (t + 1) * 128, :] = jnp.transpose(jnp.broadcast_to(line, (128, 128)))
    for a in range(4):
        ids = row_ids(where, a)
        for b in range(4):
            at = a * CHUNK + b * ROWS
            wide = row_wide[at : at + ROWS, :]
            for t in range(8):
                tile = (logits_0, logits_1)[t // 4][at : at + ROWS, (t % 4) * 128 : (t % 4 + 1) * 128]
                both = jnp.exp2(tile - wide) + jnp.exp2(tile - col_line[t])
                both = both - jnp.where(ids[b] == cols[t][0:1], 1.0, 0.0)
                weights[at : at + ROWS, t * 128 : (t + 1) * 128] = both.astype(BF16)
    text_terms(multiplier, weights, images, ((2, 0, outs[0]), (3, 0, outs[1])))


def text_terms(multiplier, weights, images, outs):
    for j, skip, out in outs:
        at = j * CHUNK + skip
        for e in range(5):
            acc = None
            for a in range(4):
                term = lax.dot_general(
                    weights[a * CHUNK : (a + 1) * CHUNK, at : at + out.shape[0]],
                    images[a][:, e * 256 : (e + 1) * 256],
                    (((0,), (0,)), ((), ())),
                    preferred_element_type=F32,
                )
                acc = term if acc is None else acc + term
            out[:, e * 256 : (e + 1) * 256] = (multiplier * acc).astype(BF16)


def image_terms(multiplier, weights, texts, outs):
    for a, out in outs.items():
        for e in range(5):
            acc = None
            for j in range(4):
                term = jnp.dot(
                    weights[a * CHUNK : (a + 1) * CHUNK, j * CHUNK : (j + 1) * CHUNK],
                    texts[j][:, e * 256 : (e + 1) * 256],
                    preferred_element_type=F32,
                )
                acc = term if acc is None else acc + term
            out[:CHUNK, e * 256 : (e + 1) * 256] = (multiplier * acc).astype(BF16)


PART = jax.ShapeDtypeStruct((CHUNK, EMBED), BF16)


def weights_call(place, scale, logits, mine, other, images):
    return pl.pallas_call(
        weights_body,
        out_shape=(
            jax.ShapeDtypeStruct((BLOCK, BLOCK), BF16),
            PART,
            jax.ShapeDtypeStruct((3 * ROWS, EMBED), BF16),
            jax.ShapeDtypeStruct((2 * TAIL, EMBED), BF16),
        ),
        in_specs=[SMEM, SMEM] + [VMEM] * 8,
        out_specs=(VMEM,) * 4,
        scratch_shapes=[
            pltpu.VMEM((BLOCK, 128), F32),
            pltpu.VMEM((16, 128), F32),
            pltpu.VMEM((16, 128), F32),
        ],
        compiler_params=PARAMS,
    )(place, scale, *logits, mine, other, *images)


def text_body(scale, weights, *refs):
    text_terms(scale[0], weights, refs[:4], ((1, 0, refs[4]), (3, 3 * ROWS, refs[5])))


def text_call(scale, weights, images):
    return pl.pallas_call(
        text_body,
        out_shape=(PART, jax.ShapeDtypeStruct((ROWS, EMBED), BF16)),
        in_specs=[SMEM] + [VMEM] * 5,
        out_specs=(VMEM,) * 2,
        compiler_params=PARAMS,
    )(scale, weights, *images)


def image_body(scale, after, digits, weights, *refs):
    image_terms(scale[0], weights, refs[:4], dict(zip((2, 1, 3), refs[4:])))
    for out in refs[4:]:
        out[CHUNK:, :] = digits[TAIL:, :]


def image_call(scale, after, digits, weights, texts):
    return pl.pallas_call(
        image_body,
        out_shape=(jax.ShapeDtypeStruct((CHUNK + TAIL, EMBED), BF16),) * 3,
        in_specs=[SMEM] + [VMEM] * 7,
        out_specs=(VMEM,) * 3,
        compiler_params=PARAMS,
    )(scale, after, digits, weights, *texts)


def rest_body(scale, weights, *refs):
    images, texts, outs = refs[:4], refs[4:8], refs[8:]
    text_terms(scale[0], weights, images, ((0, 0, outs[0]),))
    image_terms(scale[0], weights, texts, {0: outs[1]})


def rest_call(scale, weights, images, texts):
    return pl.pallas_call(
        rest_body,
        out_shape=(PART, PART),
        in_specs=[SMEM] + [VMEM] * 9,
        out_specs=(VMEM,) * 2,
        compiler_params=PARAMS,
    )(scale, weights, *images, *texts)


def add_rows(refs, rows, terms, out, to):
    for at in range(0, rows, 16):
        total = None
        for i, skip in terms:
            v = refs[i][skip + at : skip + at + 16, :].astype(F32)
            total = v if total is None else total + v
        out[to + at : to + at + 16, :] = total.astype(out.dtype)


def sums_body(n, plan, *refs):
    for parts, out in zip(plan, refs[n:]):
        to = 0
        for rows, terms in parts:
            add_rows(refs, rows, terms, out, to)
            to += rows


def sums(arrays, *plan):
    return pl.pallas_call(
        lambda *refs: sums_body(len(arrays), plan, *refs),
        out_shape=tuple(
            jax.ShapeDtypeStruct((sum(rows for rows, _ in parts), EMBED), BF16) for parts in plan
        ),
        in_specs=[VMEM] * len(arrays),
        out_specs=(VMEM,) * len(plan),
        compiler_params=PARAMS,
    )(*arrays)


def last_body(*refs):
    digits, image_out, text_out, loss_out = refs[7:]
    add_rows(refs, ROWS, [(i, 0) for i in range(4)], image_out, 0)
    add_rows(refs, ROWS, [(i, 0) for i in range(4, 7)], text_out, 0)
    total = -digits[:TAIL, :128].astype(F32)
    for r in refs[:7]:
        total += r[ROWS:, :128].astype(F32)
    loss_out[...] = value_of(total)[:, 0:1] * (LN2 / (2.0 * ROWS * 256))


def last_call(shards, texts, digits):
    grad = jax.ShapeDtypeStruct((ROWS, EMBED), BF16)
    return pl.pallas_call(
        last_body,
        out_shape=(grad, grad, jax.ShapeDtypeStruct((1, 1), F32)),
        in_specs=[VMEM] * 8,
        out_specs=(VMEM,) * 3,
        compiler_params=PARAMS,
    )(*shards, *texts, digits)


def local(image_emb, text_emb, logit_scale):
    place = jnp.stack([lax.axis_index(n) for n in AXES]).astype(jnp.int32)

    chip, image = pack([text_emb, core_swap(text_emb), image_emb], ((0, 64), (1, 64)), ((2, 64),))
    next_1, next_4 = z_shift(chip, -1), z_shift(text_emb, 4)
    near = [plane_shift(image, k, True) for k in (1, 2, 3)]
    own, text_0, side = pack(
        [image] + near + [chip, next_1, next_4],
        ((0, 64), (1, 64), (2, 64), (3, 64)),
        ((4, 128), (5, 128)),
        ((5, 128), (6, 64)),
    )
    text_1 = z_shift(text_0, -2)
    images = [own] + [plane_shift(own, k, False) for k in (1, 2, 3)]
    text_2 = core_swap(text_1)
    logits_0, col_parts = first_call(logit_scale, images, [text_0, text_1])
    logits_1, row_part, col_part, message, matched, text_3 = second_call(
        place, logit_scale, logits_0, col_parts, images, [text_2, core_swap(side), next_4]
    )
    texts = [text_0, text_1, text_2, text_3]

    spread = spread_call(place, row_part, col_part, matched, core_swap(message))
    mine, message = join_call(place, exchange(spread, plane_or_ring()))
    weights, text_2, text_3, digits = weights_call(
        place, logit_scale, (logits_0, logits_1), mine, core_swap(message), images
    )

    other_1, other_3 = core_swap(text_2), core_swap(text_3)
    text_1, far = text_call(logit_scale, weights, images)
    rows_tail = (TAIL, ((4, 0),))
    pairs, far = sums(
        [text_1, other_1, far, other_3, digits],
        ((256, ((0, 0), (1, 0))), rows_tail),
        ((64, ((2, 0), (3, 128))), rows_tail),
    )
    image_parts = image_call(logit_scale, pairs, digits, weights, texts)
    pairs, next_4 = z_shift(pairs, 2), z_shift(far, 4)
    back = [plane_shift(v, -k, False) for v, k in zip(image_parts, (2, 1, 3))]
    text_0, image_0 = rest_call(logit_scale, weights, images, texts)

    rows_tail = (TAIL, ((2, 256), (7, 0)))
    cols_tail = (TAIL, ((4, 256), (5, 256), (6, 256), (7, 16)))
    next_1, mine, *pieces = sums(
        [text_0, other_3, pairs, image_0] + back + [digits, next_4],
        ((128, ((0, 128), (1, 0), (2, 128))), rows_tail),
        ((128, ((0, 0), (2, 0))), rows_tail),
        *[((64, [(i, 64 * k) for i in range(3, 7)]), cols_tail) for k in range(4)],
    )
    next_1 = z_shift(next_1, 1)
    shards = [pieces[0]] + [plane_shift(pieces[k], -k, True) for k in (2, 1, 3)]
    rows_tail = (TAIL, ((0, 128), (1, 128)))
    mine, other = sums(
        [mine, next_1],
        ((64, ((0, 0), (1, 0))), rows_tail),
        ((64, ((0, 64), (1, 64))), rows_tail),
    )
    image_grad, text_grad, mean_loss = last_call(shards, [mine, core_swap(other), next_4], digits)
    return mean_loss.reshape(1), image_grad, text_grad


def solution(mesh):
    fine = Mesh(mesh.devices.reshape(4, 2, 2, 4, 4), AXES)
    return jax.shard_map(
        local,
        mesh=fine,
        in_specs=(P(AXES, None), P(("zh", "y", "x", "zl", "core"), None), P()),
        out_specs=(P(), P(AXES, None), P(("zh", "y", "x", "zl", "core"), None)),
        check_vma=False,
    )
```

```python
import math

import jax
import jax.numpy as jnp
from jax import lax
from jax.experimental import pallas as pl
from jax.experimental.pallas import tpu as pltpu
from jax.sharding import Mesh, PartitionSpec as P

AXES = ("zl", "core", "zh", "y", "x")
NX, NY, NZ = 4, 4, 8
ROWS, EMBED = 64, 1280
CHUNK = 4 * ROWS
TAIL, DIGITS = 16, 13
BLOCK = 16 * ROWS
BF16, F32 = jnp.bfloat16, jnp.float32
LOG2E, LN2 = math.log2(math.e), math.log(2.0)
VMEM = pl.BlockSpec(memory_space=pltpu.VMEM)
SMEM = pl.BlockSpec(memory_space=pltpu.SMEM)
PARAMS = pltpu.CompilerParams(vmem_limit_bytes=12 * 1024 * 1024)


def plane_shift(v, k, primary):
    pairs = []
    for c in range(2):
        for h in range(2):
            for y in range(NY):
                for x in range(NX):
                    if (c == 0) == primary:
                        to = (y, (x + k) % NX)
                    else:
                        to = ((y + k) % NY, x)
                    base = (c * 2 + h) * NY
                    pairs.append(((base + y) * NX + x, (base + to[0]) * NX + to[1]))
    return lax.ppermute(v, ("core", "zh", "y", "x"), pairs)


def z_shift(v, k):
    pairs = []
    for c in range(2):
        for z in range(NZ):
            to = (z + (k if c == 0 else -k)) % NZ
            pairs.append((((z % 4) * 2 + c) * 2 + z // 4, ((to % 4) * 2 + c) * 2 + to // 4))
    return lax.ppermute(v, ("zl", "core", "zh"), pairs)


def core_swap(v):
    return lax.ppermute(v, "core", [(0, 1), (1, 0)])


def device(c, y, x, z):
    return ((((z % 4) * 2 + c) * 2 + z // 4) * NY + y) * NX + x


def plane_or_ring():
    out = [[device(0, y, x, z) for y in range(NY) for x in range(NX)] for z in range(NZ)]
    return out + [
        [device(1, y + d, x, z) for z in range(NZ) for d in (0, 2)] for y in range(2) for x in range(NX)
    ]


def exchange(v, groups):
    return lax.all_to_all(v, AXES, 0, 0, axis_index_groups=groups)


def row_place(where, a, b):
    zl, c, zh, y, x = where
    p, s = jnp.where(c == 0, b, a), jnp.where(c == 0, a, b)
    n = ((y - s) & 3) * 4 + ((x - p) & 3)
    return n, ((zl * 2 + c) * 2 + zh) * 16 + n


def col_place(where, j, i):
    zl, c, zh, y, x = where
    core = c if (i % 2 == 0) == (j < 2) else 1 - c
    sign = 1 - 2 * c
    off = ((0, 0, 1, 1), (2, 2, 3, 3), (-2, -2, -3, -3), (-1, -1, 4, 4))[j][i]
    off = 4 if off == 4 else sign * off
    z = (zh * 4 + zl + off) & 7
    return z * 2 + core, ((z >> 2) * 16 + y * 4 + x) * 8 + (z & 3) * 2 + core


def row_ids(where, a):
    span = lax.broadcasted_iota(jnp.int32, (ROWS, 128), 0)
    return [row_place(where, a, b)[1] * ROWS + span for b in range(4)]


def col_ids(where):
    lane = lax.broadcasted_iota(jnp.int32, (8, 128), 1)
    out = []
    for t in range(8):
        lo = col_place(where, t // 2, (t % 2) * 2)[1] * ROWS
        hi = col_place(where, t // 2, (t % 2) * 2 + 1)[1] * ROWS - ROWS
        out.append(lane + jnp.where(lane < ROWS, lo, hi))
    return out


PART = jax.ShapeDtypeStruct((CHUNK, EMBED), BF16)
ALL = jax.ShapeDtypeStruct((BLOCK, EMBED), BF16)


def pack_body(plan, n, *refs):
    for parts, out in zip(plan, refs[n:]):
        row = 0
        for i, rows in parts:
            out[row : row + rows, :] = refs[i][...]
            row += rows


def pack(arrays, *plan):
    shapes = [jax.ShapeDtypeStruct((sum(p[1] for p in parts), EMBED), BF16) for parts in plan]
    return pl.pallas_call(
        lambda *refs: pack_body(plan, len(arrays), *refs),
        out_shape=tuple(shapes),
        in_specs=[VMEM] * len(arrays),
        out_specs=(VMEM,) * len(plan),
        compiler_params=PARAMS,
    )(*arrays)


def fold(v):
    return v.reshape(v.shape[0] // 8, 8, 128)


def column_part(logits, t, top):
    top = jnp.max(top, axis=0, keepdims=True)

    def step(i, total):
        tile = logits[pl.ds(pl.multiple_of(i * 128, 128), 128), t * 128 : (t + 1) * 128]
        return total + jnp.sum(fold(jnp.exp2(tile - top)), axis=0)

    total = lax.fori_loop(0, 8, step, jnp.zeros((8, 128), F32), unroll=True)
    return top + LOG2E * jnp.log(jnp.sum(total, axis=0, keepdims=True))


def logits_body(place, scale, *refs):
    images, texts = refs[:4], refs[4:7]
    logits, row_out, col_out, message, match_out, all_images, all_texts = refs[9:16]
    row_wide, sems = refs[16:]
    copies = []
    for i, (out, at) in enumerate(
        [(all_texts, 3 * CHUNK), (all_texts, BLOCK - ROWS)]
        + [(all_images, a * CHUNK) for a in range(4)]
        + [(all_texts, j * CHUNK) for j in range(3)]
    ):
        source = (refs[7], refs[8], *images, *texts)[i]
        into = out.at[at : at + source.shape[0], :]
        copies.append(pltpu.make_async_copy(source, into, sems.at[i]))
        copies[-1].start()
    where = [place[i] for i in range(5)]
    multiplier = scale[0] * LOG2E
    for j in range(4):
        if j == 3:
            copies[0].wait()
            copies[1].wait()
        for a in range(4):
            text = texts[j][...] if j < 3 else all_texts[3 * CHUNK :, :]
            logits[a * CHUNK : (a + 1) * CHUNK, j * CHUNK : (j + 1) * CHUNK] = multiplier * lax.dot_general(
                images[a][...], text, (((1,), (1,)), ((), ())), preferred_element_type=F32
            )
    cols = col_ids(where)
    step = 32
    matched = jnp.zeros((8, 128), F32)
    col_top = [jnp.full((8, 128), -jnp.inf, F32) for _ in range(8)]
    for a in range(4):
        ids = row_ids(where, a)
        for b in range(4):
            for half in range(ROWS // step):
                at = a * CHUNK + b * ROWS + half * step
                tiles = [logits[at : at + step, t * 128 : (t + 1) * 128] for t in range(8)]
                top = tiles[0]
                for t in range(1, 8):
                    top = jnp.maximum(top, tiles[t])
                top = jnp.max(top, axis=1, keepdims=True)
                mine = ids[b][half * step : (half + 1) * step]
                total = jnp.zeros((step, 128), F32)
                for t in range(8):
                    total += jnp.exp2(tiles[t] - top)
                    col_top[t] = jnp.maximum(col_top[t], jnp.max(fold(tiles[t]), axis=0))
                    hit = jnp.where(mine == cols[t][0:1], tiles[t], 0.0)
                    matched += jnp.sum(fold(hit), axis=0)
                part = top + LOG2E * jnp.log(jnp.sum(total, axis=1, keepdims=True))
                row_wide[at : at + step, :] = jnp.broadcast_to(part, (step, 128))
    matched = jnp.broadcast_to(jnp.sum(matched, keepdims=True), (8, 128))
    match_out[...] = matched
    message[16:24, :] = matched
    for t in range(8):
        part = column_part(logits, t, col_top[t])
        j, i = t // 2, (t % 2) * 2
        col_out[pl.ds(col_place(where, j, i)[0], 1), :] = part
        col_out[pl.ds(col_place(where, j, i + 1)[0], 1), :] = pltpu.roll(part, 64, 1)
        line = jnp.transpose(row_wide[t * 128 : (t + 1) * 128, :])[0:1]
        row_out[pl.ds(row_place(where, j, i)[0], 1), :] = line
        row_out[pl.ds(row_place(where, j, i + 1)[0], 1), :] = pltpu.roll(line, 64, 1)
    message[:16, :] = jnp.where(where[1] == 0, col_out[...], row_out[...])
    for copy in copies[2:]:
        copy.wait()


def logits_call(place, scale, images, texts):
    return pl.pallas_call(
        logits_body,
        out_shape=(
            jax.ShapeDtypeStruct((BLOCK, BLOCK), F32),
            jax.ShapeDtypeStruct((16, 128), F32),
            jax.ShapeDtypeStruct((16, 128), F32),
            jax.ShapeDtypeStruct((24, 128), F32),
            jax.ShapeDtypeStruct((8, 128), F32),
            ALL,
            ALL,
        ),
        in_specs=[SMEM, SMEM] + [VMEM] * 9,
        out_specs=(VMEM,) * 7,
        scratch_shapes=[pltpu.VMEM((BLOCK, 128), F32), pltpu.SemaphoreType.DMA((9,))],
        compiler_params=PARAMS,
    )(place, scale, *images, *texts)


def spread_body(place, row, col, matched, got, out):
    first = place[1] == 0
    mine, other = row[...], got[:16, :]
    top = jnp.maximum(col[...], other)
    both = top + LOG2E * jnp.log(jnp.exp2(col[...] - top) + jnp.exp2(other - top))
    hits = matched[...] + got[16:24, :]
    for i in range(16):
        out[i, :16, :] = jnp.where(first, mine, both)
        out[i, 16:32, :] = jnp.where(first, other, both)
        out[i, 32:40, :] = hits


def spread_call(place, *parts):
    return pl.pallas_call(
        spread_body,
        out_shape=jax.ShapeDtypeStruct((16, 40, 128), F32),
        in_specs=[SMEM] + [VMEM] * 4,
        out_specs=VMEM,
        compiler_params=PARAMS,
    )(place, *parts)


def join_body(place, got, mine, message):
    first = place[1] == 0
    counts = [jnp.logical_or(first, (place[3] >> 1) == i % 2) for i in range(16)]
    parts = [jnp.where(counts[i], got[i, :32, :], -jnp.inf) for i in range(16)]
    top = parts[0]
    for p in parts[1:]:
        top = jnp.maximum(top, p)
    total = jnp.exp2(parts[0] - top)
    for p in parts[1:]:
        total += jnp.exp2(p - top)
    state = top + LOG2E * jnp.log(total)
    hits = got[0, 32:40, :]
    for i in range(1, 16):
        hits += got[i, 32:40, :]
    real = lax.broadcasted_iota(jnp.int32, (16, 128), 1) < ROWS
    both = jnp.where(real, state[:16] + jnp.where(first, state[16:], 0.0), 0.0)
    share = jnp.sum(both, keepdims=True) - jnp.where(first, 2.0 * hits, 0.0)
    mine[:16, :] = state[:16]
    mine[16:24, :] = share
    message[:16, :] = jnp.where(first, state[16:], state[:16])
    message[16:24, :] = share


def join_call(place, got):
    return pl.pallas_call(
        join_body,
        out_shape=(jax.ShapeDtypeStruct((24, 128), F32),) * 2,
        in_specs=[SMEM, VMEM],
        out_specs=(VMEM,) * 2,
        compiler_params=PARAMS,
    )(place, got)


def digits_of(v):
    place = lax.broadcasted_iota(jnp.int32, (16, 128), 0)
    out = jnp.zeros((16, 128), F32)
    for i in range(DIGITS):
        unit = 16.0 ** (7 - i)
        d = jnp.floor(v * (1.0 / unit) + 0.5)
        v = v - d * unit
        out = jnp.where(place == i, d, out)
    return out


def value_of(digits):
    place = lax.broadcasted_iota(jnp.int32, (16, 128), 0)
    units = jnp.zeros((16, 128), F32)
    for i in range(DIGITS):
        units = jnp.where(place == i, 16.0 ** (7 - i), units)
    return jnp.sum(digits * units, axis=0, keepdims=True)


def weights_body(place, scale, logits, mine, other, images, *refs):
    weights, outs = refs[0], refs[1:4]
    row_wide, row_lse, col_lse = refs[4:]
    first = place[1] == 0
    shares = jnp.where(first, mine[16:17, :], other[16:17, :]), jnp.where(first, other[16:17, :], mine[16:17, :])
    for i, share in enumerate(shares):
        tail = digits_of(share).astype(BF16)
        for e in range(EMBED // 128):
            outs[2][i * TAIL : (i + 1) * TAIL, e * 128 : (e + 1) * 128] = tail
    row_lse[...] = jnp.where(first, mine[:16, :], other[:16, :]) + 1.0
    col_lse[...] = jnp.where(first, other[:16, :], mine[:16, :]) + 1.0
    where = [place[i] for i in range(5)]
    multiplier = scale[0]
    lane = lax.broadcasted_iota(jnp.int32, (1, 128), 1)
    cols = col_ids(where)
    col_line = []
    for t in range(8):
        j, i = t // 2, (t % 2) * 2
        lo = col_lse[pl.ds(col_place(where, j, i)[0], 1), :]
        hi = col_lse[pl.ds(col_place(where, j, i + 1)[0], 1), :]
        col_line.append(jnp.where(lane < ROWS, lo, pltpu.roll(hi, 64, 1)))
        lo = row_lse[pl.ds(row_place(where, j, i)[0], 1), :]
        hi = row_lse[pl.ds(row_place(where, j, i + 1)[0], 1), :]
        line = jnp.where(lane < ROWS, lo, pltpu.roll(hi, 64, 1))
        row_wide[t * 128 : (t + 1) * 128, :] = jnp.transpose(jnp.broadcast_to(line, (128, 128)))
    for a in range(4):
        ids = row_ids(where, a)
        for b in range(4):
            at = a * CHUNK + b * ROWS
            wide = row_wide[at : at + ROWS, :]
            for t in range(8):
                tile = logits[at : at + ROWS, t * 128 : (t + 1) * 128]
                both = jnp.exp2(tile - wide) + jnp.exp2(tile - col_line[t])
                both = both - jnp.where(ids[b] == cols[t][0:1], 1.0, 0.0)
                weights[at : at + ROWS, t * 128 : (t + 1) * 128] = both.astype(BF16)
    text_terms(multiplier, weights, images, ((2 * CHUNK, outs[0]), (3 * CHUNK, outs[1])))


def text_terms(multiplier, weights, images, outs):
    for skip, out in outs:
        for e in range(5):
            term = lax.dot_general(
                weights[:, skip : skip + out.shape[0]],
                images[:, e * 256 : (e + 1) * 256],
                (((0,), (0,)), ((), ())),
                preferred_element_type=F32,
            )
            out[:, e * 256 : (e + 1) * 256] = (multiplier * term).astype(BF16)


def image_terms(multiplier, weights, texts, outs):
    for a, out in outs.items():
        for e in range(5):
            term = jnp.dot(
                weights[a * CHUNK : (a + 1) * CHUNK, :],
                texts[:, e * 256 : (e + 1) * 256],
                preferred_element_type=F32,
            )
            out[:CHUNK, e * 256 : (e + 1) * 256] = (multiplier * term).astype(BF16)


def weights_call(place, scale, logits, mine, other, images):
    return pl.pallas_call(
        weights_body,
        out_shape=(
            jax.ShapeDtypeStruct((BLOCK, BLOCK), BF16),
            PART,
            jax.ShapeDtypeStruct((3 * ROWS, EMBED), BF16),
            jax.ShapeDtypeStruct((2 * TAIL, EMBED), BF16),
        ),
        in_specs=[SMEM, SMEM] + [VMEM] * 4,
        out_specs=(VMEM,) * 4,
        scratch_shapes=[
            pltpu.VMEM((BLOCK, 128), F32),
            pltpu.VMEM((16, 128), F32),
            pltpu.VMEM((16, 128), F32),
        ],
        compiler_params=PARAMS,
    )(place, scale, logits, mine, other, images)


def text_body(scale, weights, images, near, far):
    text_terms(scale[0], weights, images, ((CHUNK, near), (BLOCK - ROWS, far)))


def text_call(scale, weights, images):
    return pl.pallas_call(
        text_body,
        out_shape=(PART, jax.ShapeDtypeStruct((ROWS, EMBED), BF16)),
        in_specs=[SMEM] + [VMEM] * 2,
        out_specs=(VMEM,) * 2,
        compiler_params=PARAMS,
    )(scale, weights, images)


def image_body(scale, after, digits, weights, texts, *outs):
    image_terms(scale[0], weights, texts, dict(zip((2, 1, 3), outs)))
    for out in outs:
        out[CHUNK:, :] = digits[TAIL:, :]


def image_call(scale, after, digits, weights, texts):
    return pl.pallas_call(
        image_body,
        out_shape=(jax.ShapeDtypeStruct((CHUNK + TAIL, EMBED), BF16),) * 3,
        in_specs=[SMEM] + [VMEM] * 4,
        out_specs=(VMEM,) * 3,
        compiler_params=PARAMS,
    )(scale, after, digits, weights, texts)


def rest_body(scale, weights, images, texts, text_out, image_out):
    text_terms(scale[0], weights, images, ((0, text_out),))
    image_terms(scale[0], weights, texts, {0: image_out})


def rest_call(scale, weights, images, texts):
    return pl.pallas_call(
        rest_body,
        out_shape=(PART, PART),
        in_specs=[SMEM] + [VMEM] * 3,
        out_specs=(VMEM,) * 2,
        compiler_params=PARAMS,
    )(scale, weights, images, texts)


def add_rows(refs, rows, terms, out, to):
    for at in range(0, rows, 16):
        total = None
        for i, skip in terms:
            v = refs[i][skip + at : skip + at + 16, :].astype(F32)
            total = v if total is None else total + v
        out[to + at : to + at + 16, :] = total.astype(out.dtype)


def sums_body(n, plan, *refs):
    for parts, out in zip(plan, refs[n:]):
        to = 0
        for rows, terms in parts:
            add_rows(refs, rows, terms, out, to)
            to += rows


def sums(arrays, *plan):
    return pl.pallas_call(
        lambda *refs: sums_body(len(arrays), plan, *refs),
        out_shape=tuple(
            jax.ShapeDtypeStruct((sum(rows for rows, _ in parts), EMBED), BF16) for parts in plan
        ),
        in_specs=[VMEM] * len(arrays),
        out_specs=(VMEM,) * len(plan),
        compiler_params=PARAMS,
    )(*arrays)


def last_body(*refs):
    digits, image_out, text_out, loss_out = refs[6:]
    add_rows(refs, ROWS, [(i, 0) for i in range(4)], image_out, 0)
    add_rows(refs, ROWS, [(4, 0), (5, 0)], text_out, 0)
    total = -digits[:TAIL, :128].astype(F32)
    for r in refs[:6]:
        total += r[ROWS : ROWS + TAIL, :128].astype(F32)
    loss_out[...] = value_of(total)[:, 0:1] * (LN2 / (2.0 * ROWS * 256))


def last_call(shards, texts, digits):
    grad = jax.ShapeDtypeStruct((ROWS, EMBED), BF16)
    return pl.pallas_call(
        last_body,
        out_shape=(grad, grad, jax.ShapeDtypeStruct((1, 1), F32)),
        in_specs=[VMEM] * 7,
        out_specs=(VMEM,) * 3,
        compiler_params=PARAMS,
    )(*shards, *texts, digits)


def local(image_emb, text_emb, logit_scale):
    place = jnp.stack([lax.axis_index(n) for n in AXES]).astype(jnp.int32)

    chip, image = pack([text_emb, core_swap(text_emb), image_emb], ((0, 64), (1, 64)), ((2, 64),))
    next_1, next_4 = z_shift(chip, -1), z_shift(text_emb, 4)
    near = [plane_shift(image, k, True) for k in (1, 2, 3)]
    own, text_0, side = pack(
        [image] + near + [chip, next_1, next_4],
        ((0, 64), (1, 64), (2, 64), (3, 64)),
        ((4, 128), (5, 128)),
        ((5, 128), (6, 64)),
    )
    text_1 = z_shift(text_0, -2)
    near = [own] + [plane_shift(own, k, False) for k in (1, 2, 3)]
    logits, row_part, col_part, message, matched, images, texts = logits_call(
        place, logit_scale, near, [text_0, text_1, core_swap(text_1), core_swap(side), next_4]
    )

    spread = spread_call(place, row_part, col_part, matched, core_swap(message))
    mine, message = join_call(place, exchange(spread, plane_or_ring()))
    weights, text_2, text_3, digits = weights_call(
        place, logit_scale, logits, mine, core_swap(message), images
    )

    other_1, other_3 = core_swap(text_2), core_swap(text_3)
    text_1, far = text_call(logit_scale, weights, images)
    rows_tail = (TAIL, ((4, 0),))
    pairs, far = sums(
        [text_1, other_1, far, other_3, digits],
        ((256, ((0, 0), (1, 0))), rows_tail),
        ((64, ((2, 0), (3, 128))), rows_tail),
    )
    image_parts = image_call(logit_scale, pairs, digits, weights, texts)
    pairs, next_4 = z_shift(pairs, 2), z_shift(far, 4)
    back = [plane_shift(v, -k, False) for v, k in zip(image_parts, (2, 1, 3))]
    text_0, image_0 = rest_call(logit_scale, weights, images, texts)

    next_1, mine = sums(
        [text_0, other_3, pairs, next_4, digits],
        ((128, ((0, 128), (1, 0), (2, 128))), (TAIL, ((2, 256), (4, 0)))),
        (
            (64, ((0, 0), (2, 0), (3, 0))),
            (64, ((0, 64), (2, 64))),
            (TAIL, ((2, 256), (3, 64), (4, 0))),
            (TAIL, ((2, 256), (4, 0))),
        ),
    )
    next_1 = z_shift(next_1, 1)
    mine, other = sums(
        [mine, next_1],
        ((64, ((0, 0), (1, 0))), (TAIL, ((0, 128), (1, 128)))),
        ((64, ((0, 64), (1, 64))), (TAIL, ((0, 144), (1, 128)))),
    )

    cols_tail = (TAIL, ((1, 256), (2, 256), (3, 256), (4, 16)))
    pieces = sums(
        [image_0] + back + [digits],
        *[((64, [(i, 64 * k) for i in range(4)]), cols_tail) for k in range(4)],
    )
    shards = [pieces[0]] + [plane_shift(pieces[k], -k, True) for k in (2, 1, 3)]
    image_grad, text_grad, mean_loss = last_call(shards, [mine, core_swap(other)], digits)
    return mean_loss.reshape(1), image_grad, text_grad


def solution(mesh):
    fine = Mesh(mesh.devices.reshape(4, 2, 2, 4, 4), AXES)
    return jax.shard_map(
        local,
        mesh=fine,
        in_specs=(P(AXES, None), P(("zh", "y", "x", "zl", "core"), None), P()),
        out_specs=(P(), P(AXES, None), P(("zh", "y", "x", "zl", "core"), None)),
        check_vma=False,
    )
```

```python
import math

import jax
import jax.numpy as jnp
from jax import lax
from jax.experimental import pallas as pl
from jax.experimental.pallas import tpu as pltpu
from jax.sharding import Mesh, PartitionSpec as P

AXES = ("zl", "core", "zh", "y", "x")
NX, NY, NZ = 4, 4, 8
ROWS, EMBED = 64, 1280
CHUNK = 4 * ROWS
TAIL, DIGITS = 16, 13
BLOCK = 16 * ROWS
BF16, F32 = jnp.bfloat16, jnp.float32
LOG2E, LN2 = math.log2(math.e), math.log(2.0)
VMEM = pl.BlockSpec(memory_space=pltpu.VMEM)
SMEM = pl.BlockSpec(memory_space=pltpu.SMEM)
PARAMS = pltpu.CompilerParams(vmem_limit_bytes=12 * 1024 * 1024)


def plane_shift(v, k, primary):
    pairs = []
    for c in range(2):
        for h in range(2):
            for y in range(NY):
                for x in range(NX):
                    if (c == 0) == primary:
                        to = (y, (x + k) % NX)
                    else:
                        to = ((y + k) % NY, x)
                    base = (c * 2 + h) * NY
                    pairs.append(((base + y) * NX + x, (base + to[0]) * NX + to[1]))
    return lax.ppermute(v, ("core", "zh", "y", "x"), pairs)


def z_shift(v, k):
    pairs = []
    for c in range(2):
        for z in range(NZ):
            to = (z + (k if c == 0 else -k)) % NZ
            pairs.append((((z % 4) * 2 + c) * 2 + z // 4, ((to % 4) * 2 + c) * 2 + to // 4))
    return lax.ppermute(v, ("zl", "core", "zh"), pairs)


def core_swap(v):
    return lax.ppermute(v, "core", [(0, 1), (1, 0)])


def device(c, y, x, z):
    return ((((z % 4) * 2 + c) * 2 + z // 4) * NY + y) * NX + x


def plane_or_ring():
    out = [[device(0, y, x, z) for y in range(NY) for x in range(NX)] for z in range(NZ)]
    return out + [
        [device(1, y + d, x, z) for z in range(NZ) for d in (0, 2)] for y in range(2) for x in range(NX)
    ]


def exchange(v, groups):
    return lax.all_to_all(v, AXES, 0, 0, axis_index_groups=groups)


def row_place(where, a, b):
    zl, c, zh, y, x = where
    p, s = jnp.where(c == 0, b, a), jnp.where(c == 0, a, b)
    n = ((y - s) & 3) * 4 + ((x - p) & 3)
    return n, ((zl * 2 + c) * 2 + zh) * 16 + n


def col_place(where, j, i):
    zl, c, zh, y, x = where
    core = c if (i % 2 == 0) == (j < 2) else 1 - c
    sign = 1 - 2 * c
    off = ((0, 0, 1, 1), (2, 2, 3, 3), (-2, -2, -3, -3), (-1, -1, 4, 4))[j][i]
    off = 4 if off == 4 else sign * off
    z = (zh * 4 + zl + off) & 7
    return z * 2 + core, ((z >> 2) * 16 + y * 4 + x) * 8 + (z & 3) * 2 + core


def row_ids(where, a):
    span = lax.broadcasted_iota(jnp.int32, (ROWS, 128), 0)
    return [row_place(where, a, b)[1] * ROWS + span for b in range(4)]


def col_ids(where):
    lane = lax.broadcasted_iota(jnp.int32, (8, 128), 1)
    out = []
    for t in range(8):
        lo = col_place(where, t // 2, (t % 2) * 2)[1] * ROWS
        hi = col_place(where, t // 2, (t % 2) * 2 + 1)[1] * ROWS - ROWS
        out.append(lane + jnp.where(lane < ROWS, lo, hi))
    return out


PART = jax.ShapeDtypeStruct((CHUNK, EMBED), BF16)
ALL = jax.ShapeDtypeStruct((BLOCK, EMBED), BF16)


def pack_body(plan, n, *refs):
    for parts, out in zip(plan, refs[n:]):
        row = 0
        for i, rows in parts:
            out[row : row + rows, :] = refs[i][...]
            row += rows


def pack(arrays, *plan):
    shapes = [jax.ShapeDtypeStruct((sum(p[1] for p in parts), EMBED), BF16) for parts in plan]
    return pl.pallas_call(
        lambda *refs: pack_body(plan, len(arrays), *refs),
        out_shape=tuple(shapes),
        in_specs=[VMEM] * len(arrays),
        out_specs=(VMEM,) * len(plan),
        compiler_params=PARAMS,
    )(*arrays)


def fold(v):
    return v.reshape(v.shape[0] // 8, 8, 128)


def column_part(logits, t, top):
    top = jnp.max(top, axis=0, keepdims=True)

    def step(i, total):
        tile = logits[pl.ds(pl.multiple_of(i * 128, 128), 128), t * 128 : (t + 1) * 128]
        return total + jnp.sum(fold(jnp.exp2(tile - top)), axis=0)

    total = lax.fori_loop(0, 8, step, jnp.zeros((8, 128), F32), unroll=True)
    return top + LOG2E * jnp.log(jnp.sum(total, axis=0, keepdims=True))


def logits_body(place, scale, *refs):
    images, texts = refs[:4], refs[4:7]
    logits, row_out, col_out, message, match_out, all_images, all_texts = refs[9:16]
    row_wide = refs[16]
    all_texts[3 * CHUNK : BLOCK - ROWS, :] = refs[7][...]
    all_texts[BLOCK - ROWS :, :] = refs[8][...]
    where = [place[i] for i in range(5)]
    multiplier = scale[0] * LOG2E
    for j in range(4):
        if j < 3:
            all_texts[j * CHUNK : (j + 1) * CHUNK, :] = texts[j][...]
        all_images[j * CHUNK : (j + 1) * CHUNK, :] = images[j][...]
        for a in range(4):
            text = texts[j][...] if j < 3 else all_texts[3 * CHUNK :, :]
            logits[a * CHUNK : (a + 1) * CHUNK, j * CHUNK : (j + 1) * CHUNK] = multiplier * lax.dot_general(
                images[a][...], text, (((1,), (1,)), ((), ())), preferred_element_type=F32
            )
    cols = col_ids(where)
    step = 32
    matched = jnp.zeros((8, 128), F32)
    col_top = [jnp.full((8, 128), -jnp.inf, F32) for _ in range(8)]
    for a in range(4):
        ids = row_ids(where, a)
        for b in range(4):
            for half in range(ROWS // step):
                at = a * CHUNK + b * ROWS + half * step
                tiles = [logits[at : at + step, t * 128 : (t + 1) * 128] for t in range(8)]
                top = tiles[0]
                for t in range(1, 8):
                    top = jnp.maximum(top, tiles[t])
                top = jnp.max(top, axis=1, keepdims=True)
                mine = ids[b][half * step : (half + 1) * step]
                total = jnp.zeros((step, 128), F32)
                for t in range(8):
                    total += jnp.exp2(tiles[t] - top)
                    col_top[t] = jnp.maximum(col_top[t], jnp.max(fold(tiles[t]), axis=0))
                    hit = jnp.where(mine == cols[t][0:1], tiles[t], 0.0)
                    matched += jnp.sum(fold(hit), axis=0)
                part = top + LOG2E * jnp.log(jnp.sum(total, axis=1, keepdims=True))
                row_wide[at : at + step, :] = jnp.broadcast_to(part, (step, 128))
    matched = jnp.broadcast_to(jnp.sum(matched, keepdims=True), (8, 128))
    match_out[...] = matched
    message[16:24, :] = matched
    for t in range(8):
        part = column_part(logits, t, col_top[t])
        j, i = t // 2, (t % 2) * 2
        col_out[pl.ds(col_place(where, j, i)[0], 1), :] = part
        col_out[pl.ds(col_place(where, j, i + 1)[0], 1), :] = pltpu.roll(part, 64, 1)
        line = jnp.transpose(row_wide[t * 128 : (t + 1) * 128, :])[0:1]
        row_out[pl.ds(row_place(where, j, i)[0], 1), :] = line
        row_out[pl.ds(row_place(where, j, i + 1)[0], 1), :] = pltpu.roll(line, 64, 1)
    message[:16, :] = jnp.where(where[1] == 0, col_out[...], row_out[...])


def logits_call(place, scale, images, texts):
    return pl.pallas_call(
        logits_body,
        out_shape=(
            jax.ShapeDtypeStruct((BLOCK, BLOCK), F32),
            jax.ShapeDtypeStruct((16, 128), F32),
            jax.ShapeDtypeStruct((16, 128), F32),
            jax.ShapeDtypeStruct((24, 128), F32),
            jax.ShapeDtypeStruct((8, 128), F32),
            ALL,
            ALL,
        ),
        in_specs=[SMEM, SMEM] + [VMEM] * 9,
        out_specs=(VMEM,) * 7,
        scratch_shapes=[pltpu.VMEM((BLOCK, 128), F32)],
        compiler_params=PARAMS,
    )(place, scale, *images, *texts)


def pair_up(rows):
    low = lax.broadcasted_iota(jnp.int32, (1, 128), 1) < ROWS
    pairs = [
        jnp.where(low, rows[i : i + 1], pltpu.roll(rows[i + 1 : i + 2], 64, 1))
        for i in range(0, rows.shape[0], 2)
    ]
    return jnp.concatenate(pairs)


def spread_body(place, row, col, matched, got, out):
    first = place[1] == 0
    mine, other = row[...], got[:16, :]
    top = jnp.maximum(col[...], other)
    both = top + LOG2E * jnp.log(jnp.exp2(col[...] - top) + jnp.exp2(other - top))
    low = pair_up(jnp.where(first, mine, both))
    high = pair_up(other)
    hits = matched[...] + got[16:24, :]
    for i in range(16):
        out[i, :8, :] = low
        out[i, 8:16, :] = high
        out[i, 16:24, :] = hits


def spread_call(place, *parts):
    return pl.pallas_call(
        spread_body,
        out_shape=jax.ShapeDtypeStruct((16, 24, 128), F32),
        in_specs=[SMEM] + [VMEM] * 4,
        out_specs=VMEM,
        compiler_params=PARAMS,
    )(place, *parts)


def join_body(place, got, mine, message):
    first = place[1] == 0
    counts = [jnp.logical_or(first, (place[3] >> 1) == i % 2) for i in range(16)]
    parts = [jnp.where(counts[i], got[i, :16, :], -jnp.inf) for i in range(16)]
    top = parts[0]
    for p in parts[1:]:
        top = jnp.maximum(top, p)
    total = jnp.exp2(parts[0] - top)
    for p in parts[1:]:
        total += jnp.exp2(p - top)
    state = top + LOG2E * jnp.log(total)
    low, high = state[:8], state[8:]
    hits = got[0, 16:24, :]
    for i in range(1, 16):
        hits += got[i, 16:24, :]
    both = low + jnp.where(first, high, 0.0)
    share = jnp.sum(both, keepdims=True) - jnp.where(first, 2.0 * hits, 0.0)
    for out, pairs in ((mine, low), (message, jnp.where(first, high, low))):
        for i in range(8):
            out[2 * i : 2 * i + 1, :] = pairs[i : i + 1]
            out[2 * i + 1 : 2 * i + 2, :] = pltpu.roll(pairs[i : i + 1], 64, 1)
        out[16:24, :] = share


def join_call(place, got):
    return pl.pallas_call(
        join_body,
        out_shape=(jax.ShapeDtypeStruct((24, 128), F32),) * 2,
        in_specs=[SMEM, VMEM],
        out_specs=(VMEM,) * 2,
        compiler_params=PARAMS,
    )(place, got)


def digits_of(v):
    place = lax.broadcasted_iota(jnp.int32, (16, 128), 0)
    out = jnp.zeros((16, 128), F32)
    for i in range(DIGITS):
        unit = 16.0 ** (7 - i)
        d = jnp.floor(v * (1.0 / unit) + 0.5)
        v = v - d * unit
        out = jnp.where(place == i, d, out)
    return out


def value_of(digits):
    place = lax.broadcasted_iota(jnp.int32, (16, 128), 0)
    units = jnp.zeros((16, 128), F32)
    for i in range(DIGITS):
        units = jnp.where(place == i, 16.0 ** (7 - i), units)
    return jnp.sum(digits * units, axis=0, keepdims=True)


def weights_body(place, scale, logits, mine, other, images, *refs):
    weights, outs = refs[0], refs[1:4]
    row_wide, row_lse, col_lse = refs[4:]
    first = place[1] == 0
    shares = jnp.where(first, mine[16:17, :], other[16:17, :]), jnp.where(first, other[16:17, :], mine[16:17, :])
    for i, share in enumerate(shares):
        tail = digits_of(share).astype(BF16)
        for e in range(EMBED // 128):
            outs[2][i * TAIL : (i + 1) * TAIL, e * 128 : (e + 1) * 128] = tail
    row_lse[...] = jnp.where(first, mine[:16, :], other[:16, :]) + 1.0
    col_lse[...] = jnp.where(first, other[:16, :], mine[:16, :]) + 1.0
    where = [place[i] for i in range(5)]
    multiplier = scale[0]
    lane = lax.broadcasted_iota(jnp.int32, (1, 128), 1)
    cols = col_ids(where)
    col_line = []
    for t in range(8):
        j, i = t // 2, (t % 2) * 2
        lo = col_lse[pl.ds(col_place(where, j, i)[0], 1), :]
        hi = col_lse[pl.ds(col_place(where, j, i + 1)[0], 1), :]
        col_line.append(jnp.where(lane < ROWS, lo, pltpu.roll(hi, 64, 1)))
        lo = row_lse[pl.ds(row_place(where, j, i)[0], 1), :]
        hi = row_lse[pl.ds(row_place(where, j, i + 1)[0], 1), :]
        line = jnp.where(lane < ROWS, lo, pltpu.roll(hi, 64, 1))
        row_wide[t * 128 : (t + 1) * 128, :] = jnp.transpose(jnp.broadcast_to(line, (128, 128)))
    for a in range(4):
        ids = row_ids(where, a)
        for b in range(4):
            at = a * CHUNK + b * ROWS
            wide = row_wide[at : at + ROWS, :]
            for t in range(8):
                tile = logits[at : at + ROWS, t * 128 : (t + 1) * 128]
                both = jnp.exp2(tile - wide) + jnp.exp2(tile - col_line[t])
                both = both - jnp.where(ids[b] == cols[t][0:1], 1.0, 0.0)
                weights[at : at + ROWS, t * 128 : (t + 1) * 128] = both.astype(BF16)
    text_terms(multiplier, weights, images, ((2 * CHUNK, outs[0]), (3 * CHUNK, outs[1])))


def text_terms(multiplier, weights, images, outs):
    for skip, out in outs:
        for e in range(5):
            term = lax.dot_general(
                weights[:, skip : skip + out.shape[0]],
                images[:, e * 256 : (e + 1) * 256],
                (((0,), (0,)), ((), ())),
                preferred_element_type=F32,
            )
            out[:, e * 256 : (e + 1) * 256] = (multiplier * term).astype(BF16)


def image_terms(multiplier, weights, texts, outs):
    for a, out in outs.items():
        for e in range(5):
            term = jnp.dot(
                weights[a * CHUNK : (a + 1) * CHUNK, :],
                texts[:, e * 256 : (e + 1) * 256],
                preferred_element_type=F32,
            )
            out[:CHUNK, e * 256 : (e + 1) * 256] = (multiplier * term).astype(BF16)


def weights_call(place, scale, logits, mine, other, images):
    return pl.pallas_call(
        weights_body,
        out_shape=(
            jax.ShapeDtypeStruct((BLOCK, BLOCK), BF16),
            PART,
            jax.ShapeDtypeStruct((3 * ROWS, EMBED), BF16),
            jax.ShapeDtypeStruct((2 * TAIL, EMBED), BF16),
        ),
        in_specs=[SMEM, SMEM] + [VMEM] * 4,
        out_specs=(VMEM,) * 4,
        scratch_shapes=[
            pltpu.VMEM((BLOCK, 128), F32),
            pltpu.VMEM((16, 128), F32),
            pltpu.VMEM((16, 128), F32),
        ],
        compiler_params=PARAMS,
    )(place, scale, logits, mine, other, images)


def text_body(scale, weights, images, near, far):
    text_terms(scale[0], weights, images, ((CHUNK, near), (BLOCK - ROWS, far)))


def text_call(scale, weights, images):
    return pl.pallas_call(
        text_body,
        out_shape=(PART, jax.ShapeDtypeStruct((ROWS, EMBED), BF16)),
        in_specs=[SMEM] + [VMEM] * 2,
        out_specs=(VMEM,) * 2,
        compiler_params=PARAMS,
    )(scale, weights, images)


def image_body(scale, after, digits, weights, texts, *outs):
    image_terms(scale[0], weights, texts, dict(zip((2, 1, 3), outs)))
    for out in outs:
        out[CHUNK:, :] = digits[TAIL:, :]


def image_call(scale, after, digits, weights, texts):
    return pl.pallas_call(
        image_body,
        out_shape=(jax.ShapeDtypeStruct((CHUNK + TAIL, EMBED), BF16),) * 3,
        in_specs=[SMEM] + [VMEM] * 4,
        out_specs=(VMEM,) * 3,
        compiler_params=PARAMS,
    )(scale, after, digits, weights, texts)


def rest_body(scale, weights, images, texts, text_out, image_out):
    text_terms(scale[0], weights, images, ((0, text_out),))
    image_terms(scale[0], weights, texts, {0: image_out})


def rest_call(scale, weights, images, texts):
    return pl.pallas_call(
        rest_body,
        out_shape=(PART, PART),
        in_specs=[SMEM] + [VMEM] * 3,
        out_specs=(VMEM,) * 2,
        compiler_params=PARAMS,
    )(scale, weights, images, texts)


def add_rows(refs, rows, terms, out, to):
    for at in range(0, rows, 16):
        total = None
        for i, skip in terms:
            v = refs[i][skip + at : skip + at + 16, :].astype(F32)
            total = v if total is None else total + v
        out[to + at : to + at + 16, :] = total.astype(out.dtype)


def sums_body(n, plan, *refs):
    for parts, out in zip(plan, refs[n:]):
        to = 0
        for rows, terms in parts:
            add_rows(refs, rows, terms, out, to)
            to += rows


def sums(arrays, *plan):
    return pl.pallas_call(
        lambda *refs: sums_body(len(arrays), plan, *refs),
        out_shape=tuple(
            jax.ShapeDtypeStruct((sum(rows for rows, _ in parts), EMBED), BF16) for parts in plan
        ),
        in_specs=[VMEM] * len(arrays),
        out_specs=(VMEM,) * len(plan),
        compiler_params=PARAMS,
    )(*arrays)


def last_body(*refs):
    digits, image_out, text_out, loss_out = refs[7:]
    add_rows(refs, ROWS, [(i, 0) for i in range(4)], image_out, 0)
    add_rows(refs, ROWS, [(4, 0), (5, 0), (6, 0)], text_out, 0)
    total = -digits[:TAIL, :128].astype(F32)
    for r in refs[:7]:
        total += r[ROWS : ROWS + TAIL, :128].astype(F32)
    loss_out[...] = value_of(total)[:, 0:1] * (LN2 / (2.0 * ROWS * 256))


def last_call(shards, texts, digits):
    grad = jax.ShapeDtypeStruct((ROWS, EMBED), BF16)
    return pl.pallas_call(
        last_body,
        out_shape=(grad, grad, jax.ShapeDtypeStruct((1, 1), F32)),
        in_specs=[VMEM] * 8,
        out_specs=(VMEM,) * 3,
        compiler_params=PARAMS,
    )(*shards, *texts, digits)


def local(image_emb, text_emb, logit_scale):
    place = jnp.stack([lax.axis_index(n) for n in AXES]).astype(jnp.int32)

    chip, image = pack([text_emb, core_swap(text_emb), image_emb], ((0, 64), (1, 64)), ((2, 64),))
    next_1, next_4 = z_shift(chip, -1), z_shift(text_emb, 4)
    near = [plane_shift(image, k, True) for k in (1, 2, 3)]
    own, text_0, side = pack(
        [image] + near + [chip, next_1, next_4],
        ((0, 64), (1, 64), (2, 64), (3, 64)),
        ((4, 128), (5, 128)),
        ((5, 128), (6, 64)),
    )
    text_1 = z_shift(text_0, -2)
    near = [own] + [plane_shift(own, k, False) for k in (1, 2, 3)]
    logits, row_part, col_part, message, matched, images, texts = logits_call(
        place, logit_scale, near, [text_0, text_1, core_swap(text_1), core_swap(side), next_4]
    )

    spread = spread_call(place, row_part, col_part, matched, core_swap(message))
    mine, message = join_call(place, exchange(spread, plane_or_ring()))
    weights, text_2, text_3, digits = weights_call(
        place, logit_scale, logits, mine, core_swap(message), images
    )

    other_1, other_3 = core_swap(text_2), core_swap(text_3)
    text_1, far = text_call(logit_scale, weights, images)
    pairs = sums(
        [text_1, other_1, far, other_3, digits],
        ((256, ((0, 0), (1, 0))), (64, ((2, 0), (3, 128))), (TAIL, ((4, 0),))),
    )[0]
    image_parts = image_call(logit_scale, pairs, digits, weights, texts)
    pairs = z_shift(pairs, 2)
    back = [plane_shift(v, -k, False) for v, k in zip(image_parts, (2, 1, 3))]
    text_0, image_0 = rest_call(logit_scale, weights, images, texts)

    rows_tail = (TAIL, ((2, 320), (3, 0)))
    next_1, mine, next_4 = sums(
        [text_0, other_3, pairs, digits],
        ((128, ((0, 128), (1, 0), (2, 128))), rows_tail),
        ((128, ((0, 0), (2, 0))), rows_tail),
        ((80, ((2, 256),)),),
    )
    next_1, next_4 = z_shift(next_1, 1), z_shift(next_4, 2)
    rows_tail = (TAIL, ((0, 128), (1, 128)))
    mine, other = sums(
        [mine, next_1],
        ((64, ((0, 0), (1, 0))), rows_tail),
        ((64, ((0, 64), (1, 64))), rows_tail),
    )

    cols_tail = (TAIL, ((1, 256), (2, 256), (3, 256), (4, 16)))
    pieces = sums(
        [image_0] + back + [digits],
        *[((64, [(i, 64 * k) for i in range(4)]), cols_tail) for k in range(4)],
    )
    shards = [pieces[0]] + [plane_shift(pieces[k], -k, True) for k in (2, 1, 3)]
    image_grad, text_grad, mean_loss = last_call(shards, [mine, core_swap(other), next_4], digits)
    return mean_loss.reshape(1), image_grad, text_grad


def solution(mesh):
    fine = Mesh(mesh.devices.reshape(4, 2, 2, 4, 4), AXES)
    return jax.shard_map(
        local,
        mesh=fine,
        in_specs=(P(AXES, None), P(("zh", "y", "x", "zl", "core"), None), P()),
        out_specs=(P(), P(AXES, None), P(("zh", "y", "x", "zl", "core"), None)),
        check_vma=False,
    )
```

```python
import math

import jax
import jax.numpy as jnp
from jax import lax
from jax.experimental import pallas as pl
from jax.experimental.pallas import tpu as pltpu
from jax.sharding import Mesh, PartitionSpec as P

AXES = ("zl", "core", "zh", "y", "x")
NX, NY, NZ = 4, 4, 8
ROWS, EMBED = 64, 1280
CHUNK = 4 * ROWS
TAIL, DIGITS = 16, 13
BLOCK = 16 * ROWS
BF16, F32 = jnp.bfloat16, jnp.float32
LOG2E, LN2 = math.log2(math.e), math.log(2.0)
VMEM = pl.BlockSpec(memory_space=pltpu.VMEM)
SMEM = pl.BlockSpec(memory_space=pltpu.SMEM)
PARAMS = pltpu.CompilerParams(vmem_limit_bytes=12 * 1024 * 1024)


def plane_shift(v, k, primary):
    pairs = []
    for c in range(2):
        for h in range(2):
            for y in range(NY):
                for x in range(NX):
                    if (c == 0) == primary:
                        to = (y, (x + k) % NX)
                    else:
                        to = ((y + k) % NY, x)
                    base = (c * 2 + h) * NY
                    pairs.append(((base + y) * NX + x, (base + to[0]) * NX + to[1]))
    return lax.ppermute(v, ("core", "zh", "y", "x"), pairs)


def z_shift(v, k):
    pairs = []
    for c in range(2):
        for z in range(NZ):
            to = (z + (k if c == 0 else -k)) % NZ
            pairs.append((((z % 4) * 2 + c) * 2 + z // 4, ((to % 4) * 2 + c) * 2 + to // 4))
    return lax.ppermute(v, ("zl", "core", "zh"), pairs)


def core_swap(v):
    return lax.ppermute(v, "core", [(0, 1), (1, 0)])


def device(c, y, x, z):
    return ((((z % 4) * 2 + c) * 2 + z // 4) * NY + y) * NX + x


def plane_or_ring():
    out = [[device(0, y, x, z) for y in range(NY) for x in range(NX)] for z in range(NZ)]
    return out + [
        [device(1, y + d, x, z) for z in range(NZ) for d in (0, 2)] for y in range(2) for x in range(NX)
    ]


def exchange(v, groups):
    return lax.all_to_all(v, AXES, 0, 0, axis_index_groups=groups)


def row_place(where, a, b):
    zl, c, zh, y, x = where
    p, s = jnp.where(c == 0, b, a), jnp.where(c == 0, a, b)
    n = ((y - s) & 3) * 4 + ((x - p) & 3)
    return n, ((zl * 2 + c) * 2 + zh) * 16 + n


def col_place(where, j, i):
    zl, c, zh, y, x = where
    core = c if (i % 2 == 0) == (j < 2) else 1 - c
    sign = 1 - 2 * c
    off = ((0, 0, 1, 1), (2, 2, 3, 3), (-2, -2, -3, -3), (-1, -1, 4, 4))[j][i]
    off = 4 if off == 4 else sign * off
    z = (zh * 4 + zl + off) & 7
    return z * 2 + core, ((z >> 2) * 16 + y * 4 + x) * 8 + (z & 3) * 2 + core


def row_ids(where, a):
    span = lax.broadcasted_iota(jnp.int32, (ROWS, 128), 0)
    return [row_place(where, a, b)[1] * ROWS + span for b in range(4)]


def col_ids(where):
    lane = lax.broadcasted_iota(jnp.int32, (8, 128), 1)
    out = []
    for t in range(8):
        lo = col_place(where, t // 2, (t % 2) * 2)[1] * ROWS
        hi = col_place(where, t // 2, (t % 2) * 2 + 1)[1] * ROWS - ROWS
        out.append(lane + jnp.where(lane < ROWS, lo, hi))
    return out


PLANE_ORDER = (0, 1, 3, 2)
PART = jax.ShapeDtypeStruct((CHUNK, EMBED), BF16)
ALL = jax.ShapeDtypeStruct((BLOCK, EMBED), BF16)


def pack_body(plan, n, *refs):
    for parts, out in zip(plan, refs[n:]):
        row = 0
        for i, rows in parts:
            out[row : row + rows, :] = refs[i][...]
            row += rows


def pack(arrays, *plan):
    shapes = [jax.ShapeDtypeStruct((sum(p[1] for p in parts), EMBED), BF16) for parts in plan]
    return pl.pallas_call(
        lambda *refs: pack_body(plan, len(arrays), *refs),
        out_shape=tuple(shapes),
        in_specs=[VMEM] * len(arrays),
        out_specs=(VMEM,) * len(plan),
        compiler_params=PARAMS,
    )(*arrays)


def fold(v):
    return v.reshape(v.shape[0] // 8, 8, 128)


def column_part(logits, t, top):
    top = jnp.max(top, axis=0, keepdims=True)

    def step(i, total):
        tile = logits[pl.ds(pl.multiple_of(i * 128, 128), 128), t * 128 : (t + 1) * 128]
        return total + jnp.sum(fold(jnp.exp2(tile - top)), axis=0)

    total = lax.fori_loop(0, 8, step, jnp.zeros((8, 128), F32), unroll=True)
    return top + LOG2E * jnp.log(jnp.sum(total, axis=0, keepdims=True))


def logits_body(place, scale, *refs):
    images, texts = [refs[i] for i in PLANE_ORDER], refs[4:7]
    logits, row_out, col_out, message, match_out, all_images, all_texts = refs[9:16]
    row_wide = refs[16]
    all_texts[3 * CHUNK : BLOCK - ROWS, :] = refs[7][...]
    all_texts[BLOCK - ROWS :, :] = refs[8][...]
    where = [place[i] for i in range(5)]
    multiplier = scale[0] * LOG2E
    for j in range(4):
        if j < 3:
            all_texts[j * CHUNK : (j + 1) * CHUNK, :] = texts[j][...]
        all_images[j * CHUNK : (j + 1) * CHUNK, :] = images[j][...]
        for a in range(4):
            text = texts[j][...] if j < 3 else all_texts[3 * CHUNK :, :]
            logits[a * CHUNK : (a + 1) * CHUNK, j * CHUNK : (j + 1) * CHUNK] = multiplier * lax.dot_general(
                images[a][...], text, (((1,), (1,)), ((), ())), preferred_element_type=F32
            )
    cols = col_ids(where)
    step = 32
    matched = jnp.zeros((8, 128), F32)
    col_top = [jnp.full((8, 128), -jnp.inf, F32) for _ in range(8)]
    for a in range(4):
        ids = row_ids(where, a)
        for b in range(4):
            for half in range(ROWS // step):
                at = a * CHUNK + b * ROWS + half * step
                tiles = [logits[at : at + step, t * 128 : (t + 1) * 128] for t in range(8)]
                top = tiles[0]
                for t in range(1, 8):
                    top = jnp.maximum(top, tiles[t])
                top = jnp.max(top, axis=1, keepdims=True)
                mine = ids[b][half * step : (half + 1) * step]
                total = jnp.zeros((step, 128), F32)
                for t in range(8):
                    total += jnp.exp2(tiles[t] - top)
                    col_top[t] = jnp.maximum(col_top[t], jnp.max(fold(tiles[t]), axis=0))
                    hit = jnp.where(mine == cols[t][0:1], tiles[t], 0.0)
                    matched += jnp.sum(fold(hit), axis=0)
                part = top + LOG2E * jnp.log(jnp.sum(total, axis=1, keepdims=True))
                row_wide[at : at + step, :] = jnp.broadcast_to(part, (step, 128))
    matched = jnp.broadcast_to(jnp.sum(matched, keepdims=True), (8, 128))
    match_out[...] = matched
    message[16:24, :] = matched
    for t in range(8):
        part = column_part(logits, t, col_top[t])
        j, i = t // 2, (t % 2) * 2
        col_out[pl.ds(col_place(where, j, i)[0], 1), :] = part
        col_out[pl.ds(col_place(where, j, i + 1)[0], 1), :] = pltpu.roll(part, 64, 1)
        line = jnp.transpose(row_wide[t * 128 : (t + 1) * 128, :])[0:1]
        row_out[pl.ds(row_place(where, j, i)[0], 1), :] = line
        row_out[pl.ds(row_place(where, j, i + 1)[0], 1), :] = pltpu.roll(line, 64, 1)
    message[:16, :] = jnp.where(where[1] == 0, col_out[...], row_out[...])


def logits_call(place, scale, images, texts):
    return pl.pallas_call(
        logits_body,
        out_shape=(
            jax.ShapeDtypeStruct((BLOCK, BLOCK), F32),
            jax.ShapeDtypeStruct((16, 128), F32),
            jax.ShapeDtypeStruct((16, 128), F32),
            jax.ShapeDtypeStruct((24, 128), F32),
            jax.ShapeDtypeStruct((8, 128), F32),
            ALL,
            ALL,
        ),
        in_specs=[SMEM, SMEM] + [VMEM] * 9,
        out_specs=(VMEM,) * 7,
        scratch_shapes=[pltpu.VMEM((BLOCK, 128), F32)],
        compiler_params=PARAMS,
    )(place, scale, *images, *texts)


def pair_up(rows):
    low = lax.broadcasted_iota(jnp.int32, (1, 128), 1) < ROWS
    pairs = [
        jnp.where(low, rows[i : i + 1], pltpu.roll(rows[i + 1 : i + 2], 64, 1))
        for i in range(0, rows.shape[0], 2)
    ]
    return jnp.concatenate(pairs)


def spread_body(place, row, col, matched, got, out):
    first = place[1] == 0
    mine, other = row[...], got[:16, :]
    top = jnp.maximum(col[...], other)
    both = top + LOG2E * jnp.log(jnp.exp2(col[...] - top) + jnp.exp2(other - top))
    low = pair_up(jnp.where(first, mine, both))
    high = pair_up(other)
    hits = matched[...] + got[16:24, :]
    for i in range(16):
        out[i, :8, :] = low
        out[i, 8:16, :] = high
        out[i, 16:24, :] = hits


def spread_call(place, *parts):
    return pl.pallas_call(
        spread_body,
        out_shape=jax.ShapeDtypeStruct((16, 24, 128), F32),
        in_specs=[SMEM] + [VMEM] * 4,
        out_specs=VMEM,
        compiler_params=PARAMS,
    )(place, *parts)


def join_body(place, got, mine, message):
    first = place[1] == 0
    counts = [jnp.logical_or(first, (place[3] >> 1) == i % 2) for i in range(16)]
    parts = [jnp.where(counts[i], got[i, :16, :], -jnp.inf) for i in range(16)]
    top = parts[0]
    for p in parts[1:]:
        top = jnp.maximum(top, p)
    total = jnp.exp2(parts[0] - top)
    for p in parts[1:]:
        total += jnp.exp2(p - top)
    state = top + LOG2E * jnp.log(total)
    low, high = state[:8], state[8:]
    hits = got[0, 16:24, :]
    for i in range(1, 16):
        hits += got[i, 16:24, :]
    both = low + jnp.where(first, high, 0.0)
    share = jnp.sum(both, keepdims=True) - jnp.where(first, 2.0 * hits, 0.0)
    for out, pairs in ((mine, low), (message, jnp.where(first, high, low))):
        for i in range(8):
            out[2 * i : 2 * i + 1, :] = pairs[i : i + 1]
            out[2 * i + 1 : 2 * i + 2, :] = pltpu.roll(pairs[i : i + 1], 64, 1)
        out[16:24, :] = share


def join_call(place, got):
    return pl.pallas_call(
        join_body,
        out_shape=(jax.ShapeDtypeStruct((24, 128), F32),) * 2,
        in_specs=[SMEM, VMEM],
        out_specs=(VMEM,) * 2,
        compiler_params=PARAMS,
    )(place, got)


def digits_of(v):
    place = lax.broadcasted_iota(jnp.int32, (16, 128), 0)
    out = jnp.zeros((16, 128), F32)
    for i in range(DIGITS):
        unit = 16.0 ** (7 - i)
        d = jnp.floor(v * (1.0 / unit) + 0.5)
        v = v - d * unit
        out = jnp.where(place == i, d, out)
    return out


def value_of(digits):
    place = lax.broadcasted_iota(jnp.int32, (16, 128), 0)
    units = jnp.zeros((16, 128), F32)
    for i in range(DIGITS):
        units = jnp.where(place == i, 16.0 ** (7 - i), units)
    return jnp.sum(digits * units, axis=0, keepdims=True)


def weights_body(place, scale, logits, mine, other, images, *refs):
    weights, outs = refs[0], refs[1:4]
    row_wide, row_lse, col_lse = refs[4:]
    first = place[1] == 0
    shares = jnp.where(first, mine[16:17, :], other[16:17, :]), jnp.where(first, other[16:17, :], mine[16:17, :])
    for i, share in enumerate(shares):
        tail = digits_of(share).astype(BF16)
        for e in range(EMBED // 128):
            outs[2][i * TAIL : (i + 1) * TAIL, e * 128 : (e + 1) * 128] = tail
    row_lse[...] = jnp.where(first, mine[:16, :], other[:16, :]) + 1.0
    col_lse[...] = jnp.where(first, other[:16, :], mine[:16, :]) + 1.0
    where = [place[i] for i in range(5)]
    multiplier = scale[0]
    lane = lax.broadcasted_iota(jnp.int32, (1, 128), 1)
    cols = col_ids(where)
    col_line = []
    for t in range(8):
        j, i = t // 2, (t % 2) * 2
        lo = col_lse[pl.ds(col_place(where, j, i)[0], 1), :]
        hi = col_lse[pl.ds(col_place(where, j, i + 1)[0], 1), :]
        col_line.append(jnp.where(lane < ROWS, lo, pltpu.roll(hi, 64, 1)))
        lo = row_lse[pl.ds(row_place(where, j, i)[0], 1), :]
        hi = row_lse[pl.ds(row_place(where, j, i + 1)[0], 1), :]
        line = jnp.where(lane < ROWS, lo, pltpu.roll(hi, 64, 1))
        row_wide[t * 128 : (t + 1) * 128, :] = jnp.transpose(jnp.broadcast_to(line, (128, 128)))
    for a in range(4):
        ids = row_ids(where, a)
        for b in range(4):
            at = a * CHUNK + b * ROWS
            wide = row_wide[at : at + ROWS, :]
            for t in range(8):
                tile = logits[at : at + ROWS, t * 128 : (t + 1) * 128]
                both = jnp.exp2(tile - wide) + jnp.exp2(tile - col_line[t])
                both = both - jnp.where(ids[b] == cols[t][0:1], 1.0, 0.0)
                weights[at : at + ROWS, t * 128 : (t + 1) * 128] = both.astype(BF16)
    text_terms(multiplier, weights, images, ((2 * CHUNK, outs[0]), (3 * CHUNK, outs[1])))


def text_terms(multiplier, weights, images, outs):
    for skip, out in outs:
        for e in range(5):
            term = lax.dot_general(
                weights[:, skip : skip + out.shape[0]],
                images[:, e * 256 : (e + 1) * 256],
                (((0,), (0,)), ((), ())),
                preferred_element_type=F32,
            )
            out[:, e * 256 : (e + 1) * 256] = (multiplier * term).astype(BF16)


def image_terms(multiplier, weights, texts, outs):
    for a, out in outs.items():
        for e in range(5):
            term = jnp.dot(
                weights[a * CHUNK : (a + 1) * CHUNK, :],
                texts[:, e * 256 : (e + 1) * 256],
                preferred_element_type=F32,
            )
            out[:CHUNK, e * 256 : (e + 1) * 256] = (multiplier * term).astype(BF16)


def weights_call(place, scale, logits, mine, other, images):
    return pl.pallas_call(
        weights_body,
        out_shape=(
            jax.ShapeDtypeStruct((BLOCK, BLOCK), BF16),
            PART,
            jax.ShapeDtypeStruct((3 * ROWS, EMBED), BF16),
            jax.ShapeDtypeStruct((2 * TAIL, EMBED), BF16),
        ),
        in_specs=[SMEM, SMEM] + [VMEM] * 4,
        out_specs=(VMEM,) * 4,
        scratch_shapes=[
            pltpu.VMEM((BLOCK, 128), F32),
            pltpu.VMEM((16, 128), F32),
            pltpu.VMEM((16, 128), F32),
        ],
        compiler_params=PARAMS,
    )(place, scale, logits, mine, other, images)


def text_body(scale, weights, images, near, far):
    text_terms(scale[0], weights, images, ((CHUNK, near), (BLOCK - ROWS, far)))


def text_call(scale, weights, images):
    return pl.pallas_call(
        text_body,
        out_shape=(PART, jax.ShapeDtypeStruct((ROWS, EMBED), BF16)),
        in_specs=[SMEM] + [VMEM] * 2,
        out_specs=(VMEM,) * 2,
        compiler_params=PARAMS,
    )(scale, weights, images)


def image_body(scale, after, digits, weights, texts, *outs):
    image_terms(scale[0], weights, texts, dict(zip((2, 1, 3), outs)))
    for out in outs:
        out[CHUNK:, :] = digits[TAIL:, :]


def image_call(scale, after, digits, weights, texts):
    return pl.pallas_call(
        image_body,
        out_shape=(jax.ShapeDtypeStruct((CHUNK + TAIL, EMBED), BF16),) * 3,
        in_specs=[SMEM] + [VMEM] * 4,
        out_specs=(VMEM,) * 3,
        compiler_params=PARAMS,
    )(scale, after, digits, weights, texts)


def rest_body(scale, weights, images, texts, text_out, image_out):
    text_terms(scale[0], weights, images, ((0, text_out),))
    image_terms(scale[0], weights, texts, {0: image_out})


def rest_call(scale, weights, images, texts):
    return pl.pallas_call(
        rest_body,
        out_shape=(PART, PART),
        in_specs=[SMEM] + [VMEM] * 3,
        out_specs=(VMEM,) * 2,
        compiler_params=PARAMS,
    )(scale, weights, images, texts)


def add_rows(refs, rows, terms, out, to):
    for at in range(0, rows, 16):
        total = None
        for i, skip in terms:
            v = refs[i][skip + at : skip + at + 16, :].astype(F32)
            total = v if total is None else total + v
        out[to + at : to + at + 16, :] = total.astype(out.dtype)


def sums_body(n, plan, *refs):
    for parts, out in zip(plan, refs[n:]):
        to = 0
        for rows, terms in parts:
            add_rows(refs, rows, terms, out, to)
            to += rows


def sums(arrays, *plan):
    return pl.pallas_call(
        lambda *refs: sums_body(len(arrays), plan, *refs),
        out_shape=tuple(
            jax.ShapeDtypeStruct((sum(rows for rows, _ in parts), EMBED), BF16) for parts in plan
        ),
        in_specs=[VMEM] * len(arrays),
        out_specs=(VMEM,) * len(plan),
        compiler_params=PARAMS,
    )(*arrays)


def last_body(*refs):
    digits, image_out, text_out, loss_out = refs[6:]
    add_rows(refs, ROWS, [(i, 0) for i in range(4)], image_out, 0)
    add_rows(refs, ROWS, [(4, 0), (5, 0)], text_out, 0)
    total = -digits[:TAIL, :128].astype(F32)
    for r in refs[:6]:
        total += r[ROWS : ROWS + TAIL, :128].astype(F32)
    loss_out[...] = value_of(total)[:, 0:1] * (LN2 / (2.0 * ROWS * 256))


def last_call(shards, texts, digits):
    grad = jax.ShapeDtypeStruct((ROWS, EMBED), BF16)
    return pl.pallas_call(
        last_body,
        out_shape=(grad, grad, jax.ShapeDtypeStruct((1, 1), F32)),
        in_specs=[VMEM] * 7,
        out_specs=(VMEM,) * 3,
        compiler_params=PARAMS,
    )(*shards, *texts, digits)


def local(image_emb, text_emb, logit_scale):
    place = jnp.stack([lax.axis_index(n) for n in AXES]).astype(jnp.int32)

    chip, image = pack([text_emb, core_swap(text_emb), image_emb], ((0, 64), (1, 64)), ((2, 64),))
    next_1, next_4 = z_shift(chip, -1), z_shift(text_emb, 4)
    near = [plane_shift(image, k, True) for k in (1, 2, 3)]
    own, text_0, side = pack(
        [image] + near + [chip, next_1, next_4],
        ((0, 64), (1, 64), (2, 64), (3, 64)),
        ((4, 128), (5, 128)),
        ((5, 128), (6, 64)),
    )
    text_1 = z_shift(text_0, -2)
    near = [own] + [plane_shift(own, k, False) for k in PLANE_ORDER[1:]]
    logits, row_part, col_part, message, matched, images, texts = logits_call(
        place, logit_scale, near, [text_0, text_1, core_swap(text_1), core_swap(side), next_4]
    )

    spread = spread_call(place, row_part, col_part, matched, core_swap(message))
    mine, message = join_call(place, exchange(spread, plane_or_ring()))
    weights, text_2, text_3, digits = weights_call(
        place, logit_scale, logits, mine, core_swap(message), images
    )

    other_1, other_3 = core_swap(text_2), core_swap(text_3)
    text_1, far = text_call(logit_scale, weights, images)
    pairs = sums(
        [text_1, other_1, far, other_3, digits],
        ((256, ((0, 0), (1, 0))), (64, ((2, 0), (3, 128))), (TAIL, ((4, 0),))),
    )[0]
    image_parts = image_call(logit_scale, pairs, digits, weights, texts)
    pairs = z_shift(pairs, 2)
    back = [plane_shift(v, -k, False) for v, k in zip(image_parts, (2, 1, 3))]
    text_0, image_0 = rest_call(logit_scale, weights, images, texts)

    rows_tail = (TAIL, ((2, 320), (3, 0)))
    next_1, mine, next_4 = sums(
        [text_0, other_3, pairs, digits],
        ((128, ((0, 128), (1, 0), (2, 128))), rows_tail),
        ((128, ((0, 0), (2, 0))), rows_tail),
        ((80, ((2, 256),)),),
    )
    next_1, next_4 = z_shift(next_1, 1), z_shift(next_4, 2)
    (other,) = sums([mine, next_1], ((64, ((0, 64), (1, 64))), (TAIL, ((0, 128), (1, 128)))))
    (mine,) = sums(
        [mine, next_1, next_4], ((64, ((0, 0), (1, 0), (2, 0))), (TAIL, ((0, 128), (1, 128), (2, 64))))
    )

    cols_tail = (TAIL, ((1, 256), (2, 256), (3, 256), (4, 16)))
    pieces = sums(
        [image_0] + back + [digits],
        *[((64, [(i, 64 * k) for i in range(4)]), cols_tail) for k in range(4)],
    )
    shards = [pieces[0]] + [plane_shift(pieces[k], -k, True) for k in (2, 1, 3)]
    image_grad, text_grad, mean_loss = last_call(shards, [mine, core_swap(other)], digits)
    return mean_loss.reshape(1), image_grad, text_grad


def solution(mesh):
    fine = Mesh(mesh.devices.reshape(4, 2, 2, 4, 4), AXES)
    return jax.shard_map(
        local,
        mesh=fine,
        in_specs=(P(AXES, None), P(("zh", "y", "x", "zl", "core"), None), P()),
        out_specs=(P(), P(AXES, None), P(("zh", "y", "x", "zl", "core"), None)),
        check_vma=False,
    )
```

```python
import math

import jax
import jax.numpy as jnp
from jax import lax
from jax.experimental import pallas as pl
from jax.experimental.pallas import tpu as pltpu
from jax.sharding import Mesh, PartitionSpec as P

AXES = ("zl", "core", "zh", "y", "x")
NX, NY, NZ = 4, 4, 8
ROWS, EMBED = 64, 1280
CHUNK = 4 * ROWS
TAIL, DIGITS = 16, 13
BLOCK = 16 * ROWS
BF16, F32 = jnp.bfloat16, jnp.float32
LOG2E, LN2 = math.log2(math.e), math.log(2.0)
VMEM = pl.BlockSpec(memory_space=pltpu.VMEM)
SMEM = pl.BlockSpec(memory_space=pltpu.SMEM)
PARAMS = pltpu.CompilerParams(vmem_limit_bytes=12 * 1024 * 1024)


def plane_shift(v, k, primary):
    pairs = []
    for c in range(2):
        for h in range(2):
            for y in range(NY):
                for x in range(NX):
                    if (c == 0) == primary:
                        to = (y, (x + k) % NX)
                    else:
                        to = ((y + k) % NY, x)
                    base = (c * 2 + h) * NY
                    pairs.append(((base + y) * NX + x, (base + to[0]) * NX + to[1]))
    return lax.ppermute(v, ("core", "zh", "y", "x"), pairs)


def z_shift(v, k):
    pairs = []
    for c in range(2):
        for z in range(NZ):
            to = (z + (k if c == 0 else -k)) % NZ
            pairs.append((((z % 4) * 2 + c) * 2 + z // 4, ((to % 4) * 2 + c) * 2 + to // 4))
    return lax.ppermute(v, ("zl", "core", "zh"), pairs)


def core_swap(v):
    return lax.ppermute(v, "core", [(0, 1), (1, 0)])


def device(c, y, x, z):
    return ((((z % 4) * 2 + c) * 2 + z // 4) * NY + y) * NX + x


def plane_or_ring():
    out = [[device(0, y, x, z) for y in range(NY) for x in range(NX)] for z in range(NZ)]
    return out + [
        [device(1, y + d, x, z) for z in range(NZ) for d in (0, 2)] for y in range(2) for x in range(NX)
    ]


def exchange(v, groups):
    return lax.all_to_all(v, AXES, 0, 0, axis_index_groups=groups)


def row_place(where, a, b):
    zl, c, zh, y, x = where
    p, s = jnp.where(c == 0, b, a), jnp.where(c == 0, a, b)
    n = ((y - s) & 3) * 4 + ((x - p) & 3)
    return n, ((zl * 2 + c) * 2 + zh) * 16 + n


def col_place(where, j, i):
    zl, c, zh, y, x = where
    core = c if (i % 2 == 0) == (j < 2) else 1 - c
    sign = 1 - 2 * c
    off = ((0, 0, 1, 1), (2, 2, 3, 3), (-2, -2, -3, -3), (-1, -1, 4, 4))[j][i]
    off = 4 if off == 4 else sign * off
    z = (zh * 4 + zl + off) & 7
    return z * 2 + core, ((z >> 2) * 16 + y * 4 + x) * 8 + (z & 3) * 2 + core


def row_ids(where, a):
    span = lax.broadcasted_iota(jnp.int32, (ROWS, 128), 0)
    return [row_place(where, a, b)[1] * ROWS + span for b in range(4)]


def col_ids(where):
    lane = lax.broadcasted_iota(jnp.int32, (8, 128), 1)
    out = []
    for t in range(8):
        lo = col_place(where, t // 2, (t % 2) * 2)[1] * ROWS
        hi = col_place(where, t // 2, (t % 2) * 2 + 1)[1] * ROWS - ROWS
        out.append(lane + jnp.where(lane < ROWS, lo, hi))
    return out


PLANE_ORDER = (0, 1, 3, 2)
PART = jax.ShapeDtypeStruct((CHUNK, EMBED), BF16)
ALL = jax.ShapeDtypeStruct((BLOCK, EMBED), BF16)
HALF = jax.ShapeDtypeStruct((BLOCK // 2, EMBED), BF16)
HALF_LOGITS = jax.ShapeDtypeStruct((BLOCK, BLOCK // 2), F32)


def pack_body(plan, n, *refs):
    for parts, out in zip(plan, refs[n:]):
        row = 0
        for i, rows in parts:
            out[row : row + rows, :] = refs[i][...]
            row += rows


def pack(arrays, *plan):
    shapes = [jax.ShapeDtypeStruct((sum(p[1] for p in parts), EMBED), BF16) for parts in plan]
    return pl.pallas_call(
        lambda *refs: pack_body(plan, len(arrays), *refs),
        out_shape=tuple(shapes),
        in_specs=[VMEM] * len(arrays),
        out_specs=(VMEM,) * len(plan),
        compiler_params=PARAMS,
    )(*arrays)


def fold(v):
    return v.reshape(v.shape[0] // 8, 8, 128)


def column_part(logits, t, top):
    top = jnp.max(top, axis=0, keepdims=True)

    def step(i, total):
        tile = logits[pl.ds(pl.multiple_of(i * 128, 128), 128), t * 128 : (t + 1) * 128]
        return total + jnp.sum(fold(jnp.exp2(tile - top)), axis=0)

    total = lax.fori_loop(0, 8, step, jnp.zeros((8, 128), F32), unroll=True)
    return top + LOG2E * jnp.log(jnp.sum(total, axis=0, keepdims=True))


def block_logits(multiplier, images, texts, logits):
    for j in range(2):
        for a in range(4):
            logits[a * CHUNK : (a + 1) * CHUNK, j * CHUNK : (j + 1) * CHUNK] = multiplier * lax.dot_general(
                images[a * CHUNK : (a + 1) * CHUNK, :],
                texts[j * CHUNK : (j + 1) * CHUNK, :],
                (((1,), (1,)), ((), ())),
                preferred_element_type=F32,
            )


def first_body(scale, *refs):
    images, texts = [refs[i] for i in PLANE_ORDER], refs[4:6]
    logits, col_out, all_images, all_texts = refs[6:]
    for a in range(4):
        all_images[a * CHUNK : (a + 1) * CHUNK, :] = images[a][...]
    for j in range(2):
        all_texts[j * CHUNK : (j + 1) * CHUNK, :] = texts[j][:CHUNK, :]
    block_logits(scale[0] * LOG2E, all_images, all_texts, logits)
    for t in range(4):
        top = jnp.max(fold(logits[:128, t * 128 : (t + 1) * 128]), axis=0)
        for i in range(1, 8):
            tile = logits[i * 128 : (i + 1) * 128, t * 128 : (t + 1) * 128]
            top = jnp.maximum(top, jnp.max(fold(tile), axis=0))
        col_out[t : t + 1, :] = column_part(logits, t, top)


def first_call(scale, images, texts):
    return pl.pallas_call(
        first_body,
        out_shape=(HALF_LOGITS, jax.ShapeDtypeStruct((8, 128), F32), ALL, HALF),
        in_specs=[SMEM] + [VMEM] * 6,
        out_specs=(VMEM,) * 4,
        compiler_params=PARAMS,
    )(scale, *images, *texts)


def second_body(place, scale, logits_0, col_parts, images, text_1, text_2, side, *refs):
    logits_1, row_out, col_out, message, match_out, all_texts, row_wide = refs
    all_texts[:CHUNK, :] = text_2[:CHUNK, :]
    all_texts[CHUNK : CHUNK + 2 * ROWS, :] = side[...]
    all_texts[CHUNK + 2 * ROWS : CHUNK + 3 * ROWS, :] = text_2[CHUNK:, :]
    all_texts[CHUNK + 3 * ROWS :, :] = text_1[CHUNK:, :]
    where = [place[i] for i in range(5)]
    block_logits(scale[0] * LOG2E, images, all_texts, logits_1)
    halves = (logits_0, logits_1)
    cols = col_ids(where)
    step = 32
    matched = jnp.zeros((8, 128), F32)
    col_top = [jnp.full((8, 128), -jnp.inf, F32) for _ in range(4)]
    for a in range(4):
        ids = row_ids(where, a)
        for b in range(4):
            for half in range(ROWS // step):
                at = a * CHUNK + b * ROWS + half * step
                tiles = [
                    halves[t // 4][at : at + step, (t % 4) * 128 : (t % 4 + 1) * 128] for t in range(8)
                ]
                top = tiles[0]
                for t in range(1, 8):
                    top = jnp.maximum(top, tiles[t])
                top = jnp.max(top, axis=1, keepdims=True)
                mine = ids[b][half * step : (half + 1) * step]
                total = jnp.zeros((step, 128), F32)
                for t in range(8):
                    total += jnp.exp2(tiles[t] - top)
                    if t > 3:
                        col_top[t - 4] = jnp.maximum(col_top[t - 4], jnp.max(fold(tiles[t]), axis=0))
                    hit = jnp.where(mine == cols[t][0:1], tiles[t], 0.0)
                    matched += jnp.sum(fold(hit), axis=0)
                part = top + LOG2E * jnp.log(jnp.sum(total, axis=1, keepdims=True))
                row_wide[at : at + step, :] = jnp.broadcast_to(part, (step, 128))
    matched = jnp.broadcast_to(jnp.sum(matched, keepdims=True), (8, 128))
    match_out[...] = matched
    message[16:24, :] = matched
    for t in range(8):
        part = col_parts[t : t + 1, :] if t < 4 else column_part(logits_1, t - 4, col_top[t - 4])
        j, i = t // 2, (t % 2) * 2
        col_out[pl.ds(col_place(where, j, i)[0], 1), :] = part
        col_out[pl.ds(col_place(where, j, i + 1)[0], 1), :] = pltpu.roll(part, 64, 1)
        line = jnp.transpose(row_wide[t * 128 : (t + 1) * 128, :])[0:1]
        row_out[pl.ds(row_place(where, j, i)[0], 1), :] = line
        row_out[pl.ds(row_place(where, j, i + 1)[0], 1), :] = pltpu.roll(line, 64, 1)
    message[:16, :] = jnp.where(where[1] == 0, col_out[...], row_out[...])


def second_call(place, scale, *arrays):
    return pl.pallas_call(
        second_body,
        out_shape=(
            HALF_LOGITS,
            jax.ShapeDtypeStruct((16, 128), F32),
            jax.ShapeDtypeStruct((16, 128), F32),
            jax.ShapeDtypeStruct((24, 128), F32),
            jax.ShapeDtypeStruct((8, 128), F32),
            HALF,
        ),
        in_specs=[SMEM, SMEM] + [VMEM] * 6,
        out_specs=(VMEM,) * 6,
        scratch_shapes=[pltpu.VMEM((BLOCK, 128), F32)],
        compiler_params=PARAMS,
    )(place, scale, *arrays)


def pair_up(rows):
    low = lax.broadcasted_iota(jnp.int32, (1, 128), 1) < ROWS
    pairs = [
        jnp.where(low, rows[i : i + 1], pltpu.roll(rows[i + 1 : i + 2], 64, 1))
        for i in range(0, rows.shape[0], 2)
    ]
    return jnp.concatenate(pairs)


def spread_body(place, row, col, matched, got, out):
    first = place[1] == 0
    mine, other = row[...], got[:16, :]
    top = jnp.maximum(col[...], other)
    both = top + LOG2E * jnp.log(jnp.exp2(col[...] - top) + jnp.exp2(other - top))
    low = pair_up(jnp.where(first, mine, both))
    high = pair_up(other)
    hits = matched[...] + got[16:24, :]
    for i in range(16):
        out[i, :8, :] = low
        out[i, 8:16, :] = high
        out[i, 16:24, :] = hits


def spread_call(place, *parts):
    return pl.pallas_call(
        spread_body,
        out_shape=jax.ShapeDtypeStruct((16, 24, 128), F32),
        in_specs=[SMEM] + [VMEM] * 4,
        out_specs=VMEM,
        compiler_params=PARAMS,
    )(place, *parts)


def join_body(place, got, mine, message):
    first = place[1] == 0
    counts = [jnp.logical_or(first, (place[3] >> 1) == i % 2) for i in range(16)]
    parts = [jnp.where(counts[i], got[i, :16, :], -jnp.inf) for i in range(16)]
    top = parts[0]
    for p in parts[1:]:
        top = jnp.maximum(top, p)
    total = jnp.exp2(parts[0] - top)
    for p in parts[1:]:
        total += jnp.exp2(p - top)
    state = top + LOG2E * jnp.log(total)
    low, high = state[:8], state[8:]
    hits = got[0, 16:24, :]
    for i in range(1, 16):
        hits += got[i, 16:24, :]
    both = low + jnp.where(first, high, 0.0)
    share = jnp.sum(both, keepdims=True) - jnp.where(first, 2.0 * hits, 0.0)
    for out, pairs in ((mine, low), (message, jnp.where(first, high, low))):
        for i in range(8):
            out[2 * i : 2 * i + 1, :] = pairs[i : i + 1]
            out[2 * i + 1 : 2 * i + 2, :] = pltpu.roll(pairs[i : i + 1], 64, 1)
        out[16:24, :] = share


def join_call(place, got):
    return pl.pallas_call(
        join_body,
        out_shape=(jax.ShapeDtypeStruct((24, 128), F32),) * 2,
        in_specs=[SMEM, VMEM],
        out_specs=(VMEM,) * 2,
        compiler_params=PARAMS,
    )(place, got)


def digits_of(v):
    place = lax.broadcasted_iota(jnp.int32, (16, 128), 0)
    out = jnp.zeros((16, 128), F32)
    for i in range(DIGITS):
        unit = 16.0 ** (7 - i)
        d = jnp.floor(v * (1.0 / unit) + 0.5)
        v = v - d * unit
        out = jnp.where(place == i, d, out)
    return out


def value_of(digits):
    place = lax.broadcasted_iota(jnp.int32, (16, 128), 0)
    units = jnp.zeros((16, 128), F32)
    for i in range(DIGITS):
        units = jnp.where(place == i, 16.0 ** (7 - i), units)
    return jnp.sum(digits * units, axis=0, keepdims=True)


def weights_body(place, scale, logits_0, logits_1, mine, other, images, *refs):
    weights, outs = refs[0], refs[1:4]
    row_wide, row_lse, col_lse = refs[4:]
    first = place[1] == 0
    shares = jnp.where(first, mine[16:17, :], other[16:17, :]), jnp.where(first, other[16:17, :], mine[16:17, :])
    for i, share in enumerate(shares):
        tail = digits_of(share).astype(BF16)
        for e in range(EMBED // 128):
            outs[2][i * TAIL : (i + 1) * TAIL, e * 128 : (e + 1) * 128] = tail
    row_lse[...] = jnp.where(first, mine[:16, :], other[:16, :]) + 1.0
    col_lse[...] = jnp.where(first, other[:16, :], mine[:16, :]) + 1.0
    where = [place[i] for i in range(5)]
    multiplier = scale[0]
    lane = lax.broadcasted_iota(jnp.int32, (1, 128), 1)
    cols = col_ids(where)
    col_line = []
    for t in range(8):
        j, i = t // 2, (t % 2) * 2
        lo = col_lse[pl.ds(col_place(where, j, i)[0], 1), :]
        hi = col_lse[pl.ds(col_place(where, j, i + 1)[0], 1), :]
        col_line.append(jnp.where(lane < ROWS, lo, pltpu.roll(hi, 64, 1)))
        lo = row_lse[pl.ds(row_place(where, j, i)[0], 1), :]
        hi = row_lse[pl.ds(row_place(where, j, i + 1)[0], 1), :]
        line = jnp.where(lane < ROWS, lo, pltpu.roll(hi, 64, 1))
        row_wide[t * 128 : (t + 1) * 128, :] = jnp.transpose(jnp.broadcast_to(line, (128, 128)))
    for a in range(4):
        ids = row_ids(where, a)
        for b in range(4):
            at = a * CHUNK + b * ROWS
            wide = row_wide[at : at + ROWS, :]
            for t in range(8):
                tile = (logits_0, logits_1)[t // 4][at : at + ROWS, (t % 4) * 128 : (t % 4 + 1) * 128]
                both = jnp.exp2(tile - wide) + jnp.exp2(tile - col_line[t])
                both = both - jnp.where(ids[b] == cols[t][0:1], 1.0, 0.0)
                weights[at : at + ROWS, t * 128 : (t + 1) * 128] = both.astype(BF16)
    text_terms(multiplier, weights, images, ((2 * CHUNK, outs[0]), (3 * CHUNK, outs[1])))


def text_terms(multiplier, weights, images, outs):
    for skip, out in outs:
        for e in range(5):
            term = lax.dot_general(
                weights[:, skip : skip + out.shape[0]],
                images[:, e * 256 : (e + 1) * 256],
                (((0,), (0,)), ((), ())),
                preferred_element_type=F32,
            )
            out[:, e * 256 : (e + 1) * 256] = (multiplier * term).astype(BF16)


def image_terms(multiplier, weights, texts, outs):
    for a, out in outs.items():
        for e in range(5):
            term = sum(
                jnp.dot(
                    weights[a * CHUNK : (a + 1) * CHUNK, h * BLOCK // 2 : (h + 1) * BLOCK // 2],
                    texts[h][:, e * 256 : (e + 1) * 256],
                    preferred_element_type=F32,
                )
                for h in range(2)
            )
            out[:CHUNK, e * 256 : (e + 1) * 256] = (multiplier * term).astype(BF16)


def weights_call(place, scale, logits, mine, other, images):
    return pl.pallas_call(
        weights_body,
        out_shape=(
            jax.ShapeDtypeStruct((BLOCK, BLOCK), BF16),
            PART,
            jax.ShapeDtypeStruct((3 * ROWS, EMBED), BF16),
            jax.ShapeDtypeStruct((2 * TAIL, EMBED), BF16),
        ),
        in_specs=[SMEM, SMEM] + [VMEM] * 5,
        out_specs=(VMEM,) * 4,
        scratch_shapes=[
            pltpu.VMEM((BLOCK, 128), F32),
            pltpu.VMEM((16, 128), F32),
            pltpu.VMEM((16, 128), F32),
        ],
        compiler_params=PARAMS,
    )(place, scale, *logits, mine, other, images)


def text_body(scale, weights, images, near, far):
    text_terms(scale[0], weights, images, ((CHUNK, near), (BLOCK - ROWS, far)))


def text_call(scale, weights, images):
    return pl.pallas_call(
        text_body,
        out_shape=(PART, jax.ShapeDtypeStruct((ROWS, EMBED), BF16)),
        in_specs=[SMEM] + [VMEM] * 2,
        out_specs=(VMEM,) * 2,
        compiler_params=PARAMS,
    )(scale, weights, images)


def image_body(scale, after, digits, weights, text_0, text_1, *outs):
    image_terms(scale[0], weights, (text_0, text_1), dict(zip((2, 1, 3), outs)))
    for out in outs:
        out[CHUNK:, :] = digits[TAIL:, :]


def image_call(scale, after, digits, weights, texts):
    return pl.pallas_call(
        image_body,
        out_shape=(jax.ShapeDtypeStruct((CHUNK + TAIL, EMBED), BF16),) * 3,
        in_specs=[SMEM] + [VMEM] * 5,
        out_specs=(VMEM,) * 3,
        compiler_params=PARAMS,
    )(scale, after, digits, weights, *texts)


def rest_body(scale, weights, images, text_0, text_1, text_out, image_out):
    text_terms(scale[0], weights, images, ((0, text_out),))
    image_terms(scale[0], weights, (text_0, text_1), {0: image_out})


def rest_call(scale, weights, images, texts):
    return pl.pallas_call(
        rest_body,
        out_shape=(PART, PART),
        in_specs=[SMEM] + [VMEM] * 4,
        out_specs=(VMEM,) * 2,
        compiler_params=PARAMS,
    )(scale, weights, images, *texts)


def add_rows(refs, rows, terms, out, to):
    for at in range(0, rows, 16):
        total = None
        for i, skip in terms:
            v = refs[i][skip + at : skip + at + 16, :].astype(F32)
            total = v if total is None else total + v
        out[to + at : to + at + 16, :] = total.astype(out.dtype)


def sums_body(n, plan, *refs):
    for parts, out in zip(plan, refs[n:]):
        to = 0
        for rows, terms in parts:
            add_rows(refs, rows, terms, out, to)
            to += rows


def sums(arrays, *plan):
    return pl.pallas_call(
        lambda *refs: sums_body(len(arrays), plan, *refs),
        out_shape=tuple(
            jax.ShapeDtypeStruct((sum(rows for rows, _ in parts), EMBED), BF16) for parts in plan
        ),
        in_specs=[VMEM] * len(arrays),
        out_specs=(VMEM,) * len(plan),
        compiler_params=PARAMS,
    )(*arrays)


def last_body(*refs):
    digits, image_out, text_out, loss_out = refs[6:]
    add_rows(refs, ROWS, [(i, 0) for i in range(4)], image_out, 0)
    add_rows(refs, ROWS, [(4, 0), (5, 0)], text_out, 0)
    total = -digits[:TAIL, :128].astype(F32)
    for r in refs[:6]:
        total += r[ROWS : ROWS + TAIL, :128].astype(F32)
    loss_out[...] = value_of(total)[:, 0:1] * (LN2 / (2.0 * ROWS * 256))


def last_call(shards, texts, digits):
    grad = jax.ShapeDtypeStruct((ROWS, EMBED), BF16)
    return pl.pallas_call(
        last_body,
        out_shape=(grad, grad, jax.ShapeDtypeStruct((1, 1), F32)),
        in_specs=[VMEM] * 7,
        out_specs=(VMEM,) * 3,
        compiler_params=PARAMS,
    )(*shards, *texts, digits)


def local(image_emb, text_emb, logit_scale):
    place = jnp.stack([lax.axis_index(n) for n in AXES]).astype(jnp.int32)

    chip, image = pack([text_emb, core_swap(text_emb), image_emb], ((0, 64), (1, 64)), ((2, 64),))
    next_1, next_2 = z_shift(chip, -1), z_shift(text_emb, -2)
    near = [plane_shift(image, k, True) for k in (1, 2, 3)]
    own, text_0 = pack(
        [image] + near + [chip, next_1, next_2],
        ((0, 64), (1, 64), (2, 64), (3, 64)),
        ((4, 128), (5, 128), (6, 64)),
    )
    text_1 = z_shift(text_0, -2)
    near = [own] + [plane_shift(own, k, False) for k in PLANE_ORDER[1:]]
    (text_1,) = pack([text_1] + near[1:], ((0, CHUNK + ROWS),))
    logits_0, col_parts, images, texts_0 = first_call(logit_scale, near, [text_0, text_1])
    logits_1, row_part, col_part, message, matched, texts_1 = second_call(
        place, logit_scale, logits_0, col_parts, images, text_1, core_swap(text_1), core_swap(next_1)
    )
    logits, texts = (logits_0, logits_1), (texts_0, texts_1)

    spread = spread_call(place, row_part, col_part, matched, core_swap(message))
    mine, message = join_call(place, exchange(spread, plane_or_ring()))
    weights, text_2, text_3, digits = weights_call(
        place, logit_scale, logits, mine, core_swap(message), images
    )

    other_1, other_3 = core_swap(text_2), core_swap(text_3)
    text_1, far = text_call(logit_scale, weights, images)
    pairs = sums(
        [text_1, other_1, far, other_3, digits],
        ((256, ((0, 0), (1, 0))), (64, ((2, 0), (3, 128))), (TAIL, ((4, 0),))),
    )[0]
    image_parts = image_call(logit_scale, pairs, digits, weights, texts)
    pairs = z_shift(pairs, 2)
    back = [plane_shift(v, -k, False) for v, k in zip(image_parts, (2, 1, 3))]
    text_0, image_0 = rest_call(logit_scale, weights, images, texts)

    rows_tail = (TAIL, ((2, 320), (3, 0)))
    next_1, mine, next_4 = sums(
        [text_0, other_3, pairs, digits],
        ((128, ((0, 128), (1, 0), (2, 128))), rows_tail),
        ((128, ((0, 0), (2, 0))), rows_tail),
        ((80, ((2, 256),)),),
    )
    next_1, next_4 = z_shift(next_1, 1), z_shift(next_4, 2)
    mine, other = sums(
        [mine, next_1, next_4],
        ((64, ((0, 0), (1, 0), (2, 0))), (TAIL, ((0, 128), (1, 128), (2, 64)))),
        ((64, ((0, 64), (1, 64))), (TAIL, ((0, 128), (1, 128)))),
    )

    cols_tail = (TAIL, ((1, 256), (2, 256), (3, 256), (4, 16)))
    pieces = sums(
        [image_0] + back + [digits],
        *[((64, [(i, 64 * k) for i in range(4)]), cols_tail) for k in range(4)],
    )
    shards = [pieces[0]] + [plane_shift(pieces[k], -k, True) for k in (2, 1, 3)]
    image_grad, text_grad, mean_loss = last_call(shards, [mine, core_swap(other)], digits)
    return mean_loss.reshape(1), image_grad, text_grad


def solution(mesh):
    fine = Mesh(mesh.devices.reshape(4, 2, 2, 4, 4), AXES)
    return jax.shard_map(
        local,
        mesh=fine,
        in_specs=(P(AXES, None), P(("zh", "y", "x", "zl", "core"), None), P()),
        out_specs=(P(), P(AXES, None), P(("zh", "y", "x", "zl", "core"), None)),
        check_vma=False,
    )
```

```python
import math

import jax
import jax.numpy as jnp
from jax import lax
from jax.experimental import pallas as pl
from jax.experimental.pallas import tpu as pltpu
from jax.sharding import Mesh, PartitionSpec as P

AXES = ("zl", "core", "zh", "y", "x")
NX, NY, NZ = 4, 4, 8
ROWS, EMBED = 64, 1280
CHUNK = 4 * ROWS
TAIL, DIGITS = 16, 13
BLOCK = 16 * ROWS
BF16, F32 = jnp.bfloat16, jnp.float32
LOG2E, LN2 = math.log2(math.e), math.log(2.0)
VMEM = pl.BlockSpec(memory_space=pltpu.VMEM)
SMEM = pl.BlockSpec(memory_space=pltpu.SMEM)
PARAMS = pltpu.CompilerParams(vmem_limit_bytes=12 * 1024 * 1024)


def plane_shift(v, k, primary):
    pairs = []
    for c in range(2):
        for h in range(2):
            for y in range(NY):
                for x in range(NX):
                    if (c == 0) == primary:
                        to = (y, (x + k) % NX)
                    else:
                        to = ((y + k) % NY, x)
                    base = (c * 2 + h) * NY
                    pairs.append(((base + y) * NX + x, (base + to[0]) * NX + to[1]))
    return lax.ppermute(v, ("core", "zh", "y", "x"), pairs)


def z_shift(v, k):
    pairs = []
    for c in range(2):
        for z in range(NZ):
            to = (z + (k if c == 0 else -k)) % NZ
            pairs.append((((z % 4) * 2 + c) * 2 + z // 4, ((to % 4) * 2 + c) * 2 + to // 4))
    return lax.ppermute(v, ("zl", "core", "zh"), pairs)


def core_swap(v):
    return lax.ppermute(v, "core", [(0, 1), (1, 0)])


def device(c, y, x, z):
    return ((((z % 4) * 2 + c) * 2 + z // 4) * NY + y) * NX + x


def plane_or_ring():
    out = [[device(0, y, x, z) for y in range(NY) for x in range(NX)] for z in range(NZ)]
    return out + [
        [device(1, y + d, x, z) for z in range(NZ) for d in (0, 2)] for y in range(2) for x in range(NX)
    ]


def exchange(v, groups):
    return lax.all_to_all(v, AXES, 0, 0, axis_index_groups=groups)


def row_place(where, a, b):
    zl, c, zh, y, x = where
    p, s = jnp.where(c == 0, b, a), jnp.where(c == 0, a, b)
    n = ((y - s) & 3) * 4 + ((x - p) & 3)
    return n, ((zl * 2 + c) * 2 + zh) * 16 + n


def col_place(where, j, i):
    zl, c, zh, y, x = where
    core = c if (i % 2 == 0) == (j < 2) else 1 - c
    sign = 1 - 2 * c
    off = ((0, 0, 1, 1), (2, 2, 3, 3), (-2, -2, -3, -3), (-1, -1, 4, 4))[j][i]
    off = 4 if off == 4 else sign * off
    z = (zh * 4 + zl + off) & 7
    return z * 2 + core, ((z >> 2) * 16 + y * 4 + x) * 8 + (z & 3) * 2 + core


def row_ids(where, a):
    span = lax.broadcasted_iota(jnp.int32, (ROWS, 128), 0)
    return [row_place(where, a, b)[1] * ROWS + span for b in range(4)]


def col_ids(where):
    lane = lax.broadcasted_iota(jnp.int32, (8, 128), 1)
    out = []
    for t in range(8):
        lo = col_place(where, t // 2, (t % 2) * 2)[1] * ROWS
        hi = col_place(where, t // 2, (t % 2) * 2 + 1)[1] * ROWS - ROWS
        out.append(lane + jnp.where(lane < ROWS, lo, hi))
    return out


PLANE_ORDER = (0, 1, 3, 2)
PART = jax.ShapeDtypeStruct((CHUNK, EMBED), BF16)
ALL = jax.ShapeDtypeStruct((BLOCK, EMBED), BF16)


def pack_body(plan, n, *refs):
    for parts, out in zip(plan, refs[n:]):
        row = 0
        for i, rows in parts:
            out[row : row + rows, :] = refs[i][...]
            row += rows


def pack(arrays, *plan):
    shapes = [jax.ShapeDtypeStruct((sum(p[1] for p in parts), EMBED), BF16) for parts in plan]
    return pl.pallas_call(
        lambda *refs: pack_body(plan, len(arrays), *refs),
        out_shape=tuple(shapes),
        in_specs=[VMEM] * len(arrays),
        out_specs=(VMEM,) * len(plan),
        compiler_params=PARAMS,
    )(*arrays)


def fold(v):
    return v.reshape(v.shape[0] // 8, 8, 128)


def column_part(logits, t, top):
    top = jnp.max(top, axis=0, keepdims=True)

    def step(i, total):
        tile = logits[pl.ds(pl.multiple_of(i * 128, 128), 128), t * 128 : (t + 1) * 128]
        return total + jnp.sum(fold(jnp.exp2(tile - top)), axis=0)

    total = lax.fori_loop(0, 8, step, jnp.zeros((8, 128), F32), unroll=True)
    return top + LOG2E * jnp.log(jnp.sum(total, axis=0, keepdims=True))


def logits_body(place, scale, *refs):
    images, texts = [refs[i] for i in PLANE_ORDER], refs[4:7]
    logits, row_out, col_out, message, match_out, all_images, all_texts = refs[9:16]
    row_wide = refs[16]
    all_texts[3 * CHUNK : BLOCK - ROWS, :] = refs[7][...]
    all_texts[BLOCK - ROWS :, :] = refs[8][...]
    where = [place[i] for i in range(5)]
    multiplier = scale[0] * LOG2E
    for j in range(4):
        if j < 3:
            all_texts[j * CHUNK : (j + 1) * CHUNK, :] = texts[j][...]
        all_images[j * CHUNK : (j + 1) * CHUNK, :] = images[j][...]
        for a in range(4):
            text = texts[j][...] if j < 3 else all_texts[3 * CHUNK :, :]
            logits[a * CHUNK : (a + 1) * CHUNK, j * CHUNK : (j + 1) * CHUNK] = multiplier * lax.dot_general(
                images[a][...], text, (((1,), (1,)), ((), ())), preferred_element_type=F32
            )
    cols = col_ids(where)
    step = 32
    matched = jnp.zeros((8, 128), F32)
    col_top = [jnp.full((8, 128), -jnp.inf, F32) for _ in range(8)]
    for a in range(4):
        ids = row_ids(where, a)
        for b in range(4):
            for half in range(ROWS // step):
                at = a * CHUNK + b * ROWS + half * step
                tiles = [logits[at : at + step, t * 128 : (t + 1) * 128] for t in range(8)]
                top = tiles[0]
                for t in range(1, 8):
                    top = jnp.maximum(top, tiles[t])
                top = jnp.max(top, axis=1, keepdims=True)
                mine = ids[b][half * step : (half + 1) * step]
                total = jnp.zeros((step, 128), F32)
                for t in range(8):
                    total += jnp.exp2(tiles[t] - top)
                    col_top[t] = jnp.maximum(col_top[t], jnp.max(fold(tiles[t]), axis=0))
                    hit = jnp.where(mine == cols[t][0:1], tiles[t], 0.0)
                    matched += jnp.sum(fold(hit), axis=0)
                part = top + LOG2E * jnp.log(jnp.sum(total, axis=1, keepdims=True))
                row_wide[at : at + step, :] = jnp.broadcast_to(part, (step, 128))
    matched = jnp.broadcast_to(jnp.sum(matched, keepdims=True), (8, 128))
    match_out[...] = matched
    message[16:24, :] = matched
    for t in range(8):
        part = column_part(logits, t, col_top[t])
        j, i = t // 2, (t % 2) * 2
        col_out[pl.ds(col_place(where, j, i)[0], 1), :] = part
        col_out[pl.ds(col_place(where, j, i + 1)[0], 1), :] = pltpu.roll(part, 64, 1)
        line = jnp.transpose(row_wide[t * 128 : (t + 1) * 128, :])[0:1]
        row_out[pl.ds(row_place(where, j, i)[0], 1), :] = line
        row_out[pl.ds(row_place(where, j, i + 1)[0], 1), :] = pltpu.roll(line, 64, 1)
    message[:16, :] = jnp.where(where[1] == 0, col_out[...], row_out[...])


def logits_call(place, scale, images, texts):
    return pl.pallas_call(
        logits_body,
        out_shape=(
            jax.ShapeDtypeStruct((BLOCK, BLOCK), F32),
            jax.ShapeDtypeStruct((16, 128), F32),
            jax.ShapeDtypeStruct((16, 128), F32),
            jax.ShapeDtypeStruct((24, 128), F32),
            jax.ShapeDtypeStruct((8, 128), F32),
            ALL,
            ALL,
        ),
        in_specs=[SMEM, SMEM] + [VMEM] * 9,
        out_specs=(VMEM,) * 7,
        scratch_shapes=[pltpu.VMEM((BLOCK, 128), F32)],
        compiler_params=PARAMS,
    )(place, scale, *images, *texts)


def pair_up(rows):
    low = lax.broadcasted_iota(jnp.int32, (1, 128), 1) < ROWS
    pairs = [
        jnp.where(low, rows[i : i + 1], pltpu.roll(rows[i + 1 : i + 2], 64, 1))
        for i in range(0, rows.shape[0], 2)
    ]
    return jnp.concatenate(pairs)


def spread_body(place, row, col, matched, got, out):
    first = place[1] == 0
    mine, other = row[...], got[:16, :]
    top = jnp.maximum(col[...], other)
    both = top + LOG2E * jnp.log(jnp.exp2(col[...] - top) + jnp.exp2(other - top))
    low = pair_up(jnp.where(first, mine, both))
    high = pair_up(other)
    hits = matched[...] + got[16:24, :]
    for i in range(16):
        out[i, :8, :] = low
        out[i, 8:16, :] = high
        out[i, 16:24, :] = hits


def spread_call(place, *parts):
    return pl.pallas_call(
        spread_body,
        out_shape=jax.ShapeDtypeStruct((16, 24, 128), F32),
        in_specs=[SMEM] + [VMEM] * 4,
        out_specs=VMEM,
        compiler_params=PARAMS,
    )(place, *parts)


def join_body(place, got, mine, message):
    first = place[1] == 0
    counts = [jnp.logical_or(first, (place[3] >> 1) == i % 2) for i in range(16)]
    parts = [jnp.where(counts[i], got[i, :16, :], -jnp.inf) for i in range(16)]
    top = parts[0]
    for p in parts[1:]:
        top = jnp.maximum(top, p)
    total = jnp.exp2(parts[0] - top)
    for p in parts[1:]:
        total += jnp.exp2(p - top)
    state = top + LOG2E * jnp.log(total)
    low, high = state[:8], state[8:]
    hits = got[0, 16:24, :]
    for i in range(1, 16):
        hits += got[i, 16:24, :]
    both = low + jnp.where(first, high, 0.0)
    share = jnp.sum(both, keepdims=True) - jnp.where(first, 2.0 * hits, 0.0)
    for out, pairs in ((mine, low), (message, jnp.where(first, high, low))):
        for i in range(8):
            out[2 * i : 2 * i + 1, :] = pairs[i : i + 1]
            out[2 * i + 1 : 2 * i + 2, :] = pltpu.roll(pairs[i : i + 1], 64, 1)
        out[16:24, :] = share


def join_call(place, got):
    return pl.pallas_call(
        join_body,
        out_shape=(jax.ShapeDtypeStruct((24, 128), F32),) * 2,
        in_specs=[SMEM, VMEM],
        out_specs=(VMEM,) * 2,
        compiler_params=PARAMS,
    )(place, got)


def digits_of(v):
    place = lax.broadcasted_iota(jnp.int32, (16, 128), 0)
    out = jnp.zeros((16, 128), F32)
    for i in range(DIGITS):
        unit = 16.0 ** (7 - i)
        d = jnp.floor(v * (1.0 / unit) + 0.5)
        v = v - d * unit
        out = jnp.where(place == i, d, out)
    return out


def value_of(digits):
    place = lax.broadcasted_iota(jnp.int32, (16, 128), 0)
    units = jnp.zeros((16, 128), F32)
    for i in range(DIGITS):
        units = jnp.where(place == i, 16.0 ** (7 - i), units)
    return jnp.sum(digits * units, axis=0, keepdims=True)


def weights_body(place, scale, logits, mine, other, images, *refs):
    weights, outs = refs[0], refs[1:4]
    row_wide, row_lse, col_lse = refs[4:]
    first = place[1] == 0
    shares = jnp.where(first, mine[16:17, :], other[16:17, :]), jnp.where(first, other[16:17, :], mine[16:17, :])
    for i, share in enumerate((*shares, jnp.where(first, shares[0], 0.0))):
        tail = digits_of(share).astype(BF16)
        for e in range(EMBED // 128):
            outs[2][i * TAIL : (i + 1) * TAIL, e * 128 : (e + 1) * 128] = tail
    row_lse[...] = jnp.where(first, mine[:16, :], other[:16, :]) + 1.0
    col_lse[...] = jnp.where(first, other[:16, :], mine[:16, :]) + 1.0
    where = [place[i] for i in range(5)]
    multiplier = scale[0]
    lane = lax.broadcasted_iota(jnp.int32, (1, 128), 1)
    cols = col_ids(where)
    col_line = []
    for t in range(8):
        j, i = t // 2, (t % 2) * 2
        lo = col_lse[pl.ds(col_place(where, j, i)[0], 1), :]
        hi = col_lse[pl.ds(col_place(where, j, i + 1)[0], 1), :]
        col_line.append(jnp.where(lane < ROWS, lo, pltpu.roll(hi, 64, 1)))
        lo = row_lse[pl.ds(row_place(where, j, i)[0], 1), :]
        hi = row_lse[pl.ds(row_place(where, j, i + 1)[0], 1), :]
        line = jnp.where(lane < ROWS, lo, pltpu.roll(hi, 64, 1))
        row_wide[t * 128 : (t + 1) * 128, :] = jnp.transpose(jnp.broadcast_to(line, (128, 128)))
    for a in range(4):
        ids = row_ids(where, a)
        for b in range(4):
            at = a * CHUNK + b * ROWS
            wide = row_wide[at : at + ROWS, :]
            for t in range(8):
                tile = logits[at : at + ROWS, t * 128 : (t + 1) * 128]
                both = jnp.exp2(tile - wide) + jnp.exp2(tile - col_line[t])
                both = both - jnp.where(ids[b] == cols[t][0:1], 1.0, 0.0)
                weights[at : at + ROWS, t * 128 : (t + 1) * 128] = both.astype(BF16)
    text_terms(multiplier, weights, images, ((2 * CHUNK, outs[0]), (3 * CHUNK, outs[1])))


def text_terms(multiplier, weights, images, outs):
    for skip, out in outs:
        for e in range(5):
            term = lax.dot_general(
                weights[:, skip : skip + out.shape[0]],
                images[:, e * 256 : (e + 1) * 256],
                (((0,), (0,)), ((), ())),
                preferred_element_type=F32,
            )
            out[:, e * 256 : (e + 1) * 256] = (multiplier * term).astype(BF16)


def image_terms(multiplier, weights, texts, outs):
    for a, out in outs.items():
        for e in range(5):
            term = jnp.dot(
                weights[a * CHUNK : (a + 1) * CHUNK, :],
                texts[:, e * 256 : (e + 1) * 256],
                preferred_element_type=F32,
            )
            out[:CHUNK, e * 256 : (e + 1) * 256] = (multiplier * term).astype(BF16)


def weights_call(place, scale, logits, mine, other, images):
    return pl.pallas_call(
        weights_body,
        out_shape=(
            jax.ShapeDtypeStruct((BLOCK, BLOCK), BF16),
            PART,
            jax.ShapeDtypeStruct((3 * ROWS, EMBED), BF16),
            jax.ShapeDtypeStruct((3 * TAIL, EMBED), BF16),
        ),
        in_specs=[SMEM, SMEM] + [VMEM] * 4,
        out_specs=(VMEM,) * 4,
        scratch_shapes=[
            pltpu.VMEM((BLOCK, 128), F32),
            pltpu.VMEM((16, 128), F32),
            pltpu.VMEM((16, 128), F32),
        ],
        compiler_params=PARAMS,
    )(place, scale, logits, mine, other, images)


def text_body(scale, weights, images, near, far):
    text_terms(scale[0], weights, images, ((CHUNK, near), (BLOCK - ROWS, far)))


def text_call(scale, weights, images):
    return pl.pallas_call(
        text_body,
        out_shape=(PART, jax.ShapeDtypeStruct((ROWS, EMBED), BF16)),
        in_specs=[SMEM] + [VMEM] * 2,
        out_specs=(VMEM,) * 2,
        compiler_params=PARAMS,
    )(scale, weights, images)


def image_body(scale, after, digits, weights, texts, *outs):
    image_terms(scale[0], weights, texts, dict(zip((2, 1, 3), outs)))
    for out in outs:
        out[CHUNK:, :] = digits[TAIL : 2 * TAIL, :]


def image_call(scale, after, digits, weights, texts):
    return pl.pallas_call(
        image_body,
        out_shape=(jax.ShapeDtypeStruct((CHUNK + TAIL, EMBED), BF16),) * 3,
        in_specs=[SMEM] + [VMEM] * 4,
        out_specs=(VMEM,) * 3,
        compiler_params=PARAMS,
    )(scale, after, digits, weights, texts)


def rest_body(scale, weights, images, texts, text_out, image_out):
    text_terms(scale[0], weights, images, ((0, text_out),))
    image_terms(scale[0], weights, texts, {0: image_out})


def rest_call(scale, weights, images, texts):
    return pl.pallas_call(
        rest_body,
        out_shape=(PART, PART),
        in_specs=[SMEM] + [VMEM] * 3,
        out_specs=(VMEM,) * 2,
        compiler_params=PARAMS,
    )(scale, weights, images, texts)


def add_rows(refs, rows, terms, out, to):
    for at in range(0, rows, 16):
        total = None
        for i, skip in terms:
            v = refs[i][skip + at : skip + at + 16, :].astype(F32)
            total = v if total is None else total + v
        out[to + at : to + at + 16, :] = total.astype(out.dtype)


def sums_body(n, plan, *refs):
    for parts, out in zip(plan, refs[n:]):
        to = 0
        for rows, terms in parts:
            add_rows(refs, rows, terms, out, to)
            to += rows


def sums(arrays, *plan):
    return pl.pallas_call(
        lambda *refs: sums_body(len(arrays), plan, *refs),
        out_shape=tuple(
            jax.ShapeDtypeStruct((sum(rows for rows, _ in parts), EMBED), BF16) for parts in plan
        ),
        in_specs=[VMEM] * len(arrays),
        out_specs=(VMEM,) * len(plan),
        compiler_params=PARAMS,
    )(*arrays)


def last_body(*refs):
    digits, image_out, text_out, loss_out = refs[6:]
    add_rows(refs, ROWS, [(i, 0) for i in range(4)], image_out, 0)
    add_rows(refs, ROWS, [(4, 0), (5, 0)], text_out, 0)
    total = -digits[:TAIL, :128].astype(F32)
    for r in refs[:6]:
        total += r[ROWS : ROWS + TAIL, :128].astype(F32)
    loss_out[...] = value_of(total)[:, 0:1] * (LN2 / (2.0 * ROWS * 256))


def last_call(shards, texts, digits):
    grad = jax.ShapeDtypeStruct((ROWS, EMBED), BF16)
    return pl.pallas_call(
        last_body,
        out_shape=(grad, grad, jax.ShapeDtypeStruct((1, 1), F32)),
        in_specs=[VMEM] * 7,
        out_specs=(VMEM,) * 3,
        compiler_params=PARAMS,
    )(*shards, *texts, digits)


def local(image_emb, text_emb, logit_scale):
    place = jnp.stack([lax.axis_index(n) for n in AXES]).astype(jnp.int32)

    chip, image = pack([text_emb, core_swap(text_emb), image_emb], ((0, 64), (1, 64)), ((2, 64),))
    next_1, next_4 = z_shift(chip, -1), z_shift(text_emb, 4)
    near = [plane_shift(image, k, True) for k in (1, 2, 3)]
    own, text_0, side = pack(
        [image] + near + [chip, next_1, next_4],
        ((0, 64), (1, 64), (2, 64), (3, 64)),
        ((4, 128), (5, 128)),
        ((5, 128), (6, 64)),
    )
    text_1 = z_shift(text_0, -2)
    near = [own] + [plane_shift(own, k, False) for k in PLANE_ORDER[1:]]
    logits, row_part, col_part, message, matched, images, texts = logits_call(
        place, logit_scale, near, [text_0, text_1, core_swap(text_1), core_swap(side), next_4]
    )

    spread = spread_call(place, row_part, col_part, matched, core_swap(message))
    mine, message = join_call(place, exchange(spread, plane_or_ring()))
    weights, text_2, text_3, digits = weights_call(
        place, logit_scale, logits, mine, core_swap(message), images
    )

    other_1, other_3 = core_swap(text_2), core_swap(text_3)
    text_1, far = text_call(logit_scale, weights, images)
    pairs, far = sums(
        [text_1, other_1, far, other_3, digits],
        ((256, ((0, 0), (1, 0))), (TAIL, ((4, 0),))),
        ((64, ((2, 0), (3, 128))), (TAIL, ((4, 2 * TAIL),))),
    )
    image_parts = image_call(logit_scale, pairs, digits, weights, texts)
    pairs, far = z_shift(pairs, 2), z_shift(far, 3)
    back = [plane_shift(v, -k, False) for v, k in zip(image_parts, (2, 1, 3))]
    text_0, image_0 = rest_call(logit_scale, weights, images, texts)

    next_1, mine = sums(
        [text_0, other_3, pairs, far, digits],
        (
            (64, ((0, 128), (1, 0), (2, 128), (3, 0))),
            (64, ((0, 192), (1, 64), (2, 192))),
            (TAIL, ((2, 256), (3, 64), (4, 0))),
        ),
        ((128, ((0, 0), (2, 0))), (TAIL, ((2, 256), (4, 0)))),
    )
    next_1 = z_shift(next_1, 1)
    rows_tail = (TAIL, ((0, 128), (1, 128)))
    mine, other = sums(
        [mine, next_1],
        ((64, ((0, 0), (1, 0))), rows_tail),
        ((64, ((0, 64), (1, 64))), rows_tail),
    )

    cols_tail = (TAIL, ((1, 256), (2, 256), (3, 256), (4, 16)))
    pieces = sums(
        [image_0] + back + [digits],
        *[((64, [(i, 64 * k) for i in range(4)]), cols_tail) for k in range(4)],
    )
    shards = [pieces[0]] + [plane_shift(pieces[k], -k, True) for k in (2, 1, 3)]
    image_grad, text_grad, mean_loss = last_call(shards, [mine, core_swap(other)], digits)
    return mean_loss.reshape(1), image_grad, text_grad


def solution(mesh):
    fine = Mesh(mesh.devices.reshape(4, 2, 2, 4, 4), AXES)
    return jax.shard_map(
        local,
        mesh=fine,
        in_specs=(P(AXES, None), P(("zh", "y", "x", "zl", "core"), None), P()),
        out_specs=(P(), P(AXES, None), P(("zh", "y", "x", "zl", "core"), None)),
        check_vma=False,
    )
```

```python
import math

import jax
import jax.numpy as jnp
from jax import lax
from jax.experimental import pallas as pl
from jax.experimental.pallas import tpu as pltpu
from jax.sharding import Mesh, PartitionSpec as P

AXES = ("zl", "core", "zh", "y", "x")
NX, NY, NZ = 4, 4, 8
ROWS, EMBED = 64, 1280
CHUNK = 4 * ROWS
TAIL, DIGITS = 16, 13
BLOCK = 16 * ROWS
BF16, F32 = jnp.bfloat16, jnp.float32
LOG2E, LN2 = math.log2(math.e), math.log(2.0)
VMEM = pl.BlockSpec(memory_space=pltpu.VMEM)
SMEM = pl.BlockSpec(memory_space=pltpu.SMEM)
PARAMS = pltpu.CompilerParams(vmem_limit_bytes=12 * 1024 * 1024)


def plane_shift(v, k, primary):
    pairs = []
    for c in range(2):
        for h in range(2):
            for y in range(NY):
                for x in range(NX):
                    if (c == 0) == primary:
                        to = (y, (x + k) % NX)
                    else:
                        to = ((y + k) % NY, x)
                    base = (c * 2 + h) * NY
                    pairs.append(((base + y) * NX + x, (base + to[0]) * NX + to[1]))
    return lax.ppermute(v, ("core", "zh", "y", "x"), pairs)


def z_shift(v, k):
    pairs = []
    for c in range(2):
        for z in range(NZ):
            to = (z + (k if c == 0 else -k)) % NZ
            pairs.append((((z % 4) * 2 + c) * 2 + z // 4, ((to % 4) * 2 + c) * 2 + to // 4))
    return lax.ppermute(v, ("zl", "core", "zh"), pairs)


def core_swap(v):
    return lax.ppermute(v, "core", [(0, 1), (1, 0)])


def device(c, y, x, z):
    return ((((z % 4) * 2 + c) * 2 + z // 4) * NY + y) * NX + x


def plane_or_ring():
    out = [[device(0, y, x, z) for y in range(NY) for x in range(NX)] for z in range(NZ)]
    return out + [
        [device(1, y + d, x, z) for z in range(NZ) for d in (0, 1)] for y in (0, 2) for x in range(NX)
    ]


def exchange(v, groups):
    return lax.all_to_all(v, AXES, 0, 0, axis_index_groups=groups)


def row_place(where, a, b):
    zl, c, zh, y, x = where
    p, s = jnp.where(c == 0, b, a), jnp.where(c == 0, a, b)
    n = ((y - s) & 3) * 4 + ((x - p) & 3)
    return n, ((zl * 2 + c) * 2 + zh) * 16 + n


def col_place(where, j, i):
    zl, c, zh, y, x = where
    core = c if (i % 2 == 0) == (j < 2) else 1 - c
    sign = 1 - 2 * c
    off = ((0, 0, 1, 1), (2, 2, 3, 3), (-2, -2, -3, -3), (-1, -1, 4, 4))[j][i]
    off = 4 if off == 4 else sign * off
    z = (zh * 4 + zl + off) & 7
    return z * 2 + core, ((z >> 2) * 16 + y * 4 + x) * 8 + (z & 3) * 2 + core


def row_ids(where, a):
    span = lax.broadcasted_iota(jnp.int32, (ROWS, 128), 0)
    return [row_place(where, a, b)[1] * ROWS + span for b in range(4)]


def col_ids(where):
    lane = lax.broadcasted_iota(jnp.int32, (8, 128), 1)
    out = []
    for t in range(8):
        lo = col_place(where, t // 2, (t % 2) * 2)[1] * ROWS
        hi = col_place(where, t // 2, (t % 2) * 2 + 1)[1] * ROWS - ROWS
        out.append(lane + jnp.where(lane < ROWS, lo, hi))
    return out


PLANE_ORDER = (0, 1, 3, 2)
PART = jax.ShapeDtypeStruct((CHUNK, EMBED), BF16)
ALL = jax.ShapeDtypeStruct((BLOCK, EMBED), BF16)


def pack_body(plan, n, *refs):
    for parts, out in zip(plan, refs[n:]):
        row = 0
        for i, rows in parts:
            out[row : row + rows, :] = refs[i][...]
            row += rows


def pack(arrays, *plan):
    shapes = [jax.ShapeDtypeStruct((sum(p[1] for p in parts), EMBED), BF16) for parts in plan]
    return pl.pallas_call(
        lambda *refs: pack_body(plan, len(arrays), *refs),
        out_shape=tuple(shapes),
        in_specs=[VMEM] * len(arrays),
        out_specs=(VMEM,) * len(plan),
        compiler_params=PARAMS,
    )(*arrays)


def fold(v):
    return v.reshape(v.shape[0] // 8, 8, 128)


def column_part(logits, t, top):
    top = jnp.max(top, axis=0, keepdims=True)

    def step(i, total):
        tile = logits[pl.ds(pl.multiple_of(i * 128, 128), 128), t * 128 : (t + 1) * 128]
        return total + jnp.sum(fold(jnp.exp2(tile - top)), axis=0)

    total = lax.fori_loop(0, 8, step, jnp.zeros((8, 128), F32), unroll=True)
    return top + LOG2E * jnp.log(jnp.sum(total, axis=0, keepdims=True))


def logits_body(place, scale, *refs):
    images, texts = [refs[i] for i in PLANE_ORDER], refs[4:7]
    logits, row_out, col_out, message, match_out, all_images, all_texts = refs[9:16]
    row_wide = refs[16]
    all_texts[3 * CHUNK : BLOCK - ROWS, :] = refs[7][...]
    all_texts[BLOCK - ROWS :, :] = refs[8][...]
    where = [place[i] for i in range(5)]
    multiplier = scale[0] * LOG2E
    for j in range(3):
        all_texts[j * CHUNK : (j + 1) * CHUNK, :] = texts[j][...]

    def chunk_logits(a):
        all_images[a * CHUNK : (a + 1) * CHUNK, :] = images[a][...]
        for j in range(4):
            text = texts[j][...] if j < 3 else all_texts[3 * CHUNK :, :]
            logits[a * CHUNK : (a + 1) * CHUNK, j * CHUNK : (j + 1) * CHUNK] = multiplier * lax.dot_general(
                images[a][...], text, (((1,), (1,)), ((), ())), preferred_element_type=F32
            )

    chunk_logits(0)
    cols = col_ids(where)
    step = 32
    matched = jnp.zeros((8, 128), F32)
    col_top = [jnp.full((8, 128), -jnp.inf, F32) for _ in range(8)]
    for a in range(4):
        if a < 3:
            chunk_logits(a + 1)
        ids = row_ids(where, a)
        for b in range(4):
            for half in range(ROWS // step):
                at = a * CHUNK + b * ROWS + half * step
                tiles = [logits[at : at + step, t * 128 : (t + 1) * 128] for t in range(8)]
                top = tiles[0]
                for t in range(1, 8):
                    top = jnp.maximum(top, tiles[t])
                top = jnp.max(top, axis=1, keepdims=True)
                mine = ids[b][half * step : (half + 1) * step]
                total = jnp.zeros((step, 128), F32)
                for t in range(8):
                    total += jnp.exp2(tiles[t] - top)
                    col_top[t] = jnp.maximum(col_top[t], jnp.max(fold(tiles[t]), axis=0))
                    hit = jnp.where(mine == cols[t][0:1], tiles[t], 0.0)
                    matched += jnp.sum(fold(hit), axis=0)
                part = top + LOG2E * jnp.log(jnp.sum(total, axis=1, keepdims=True))
                row_wide[at : at + step, :] = jnp.broadcast_to(part, (step, 128))
    matched = jnp.broadcast_to(jnp.sum(matched, keepdims=True), (8, 128))
    match_out[...] = matched
    message[16:24, :] = matched
    for t in range(8):
        part = column_part(logits, t, col_top[t])
        j, i = t // 2, (t % 2) * 2
        col_out[pl.ds(col_place(where, j, i)[0], 1), :] = part
        col_out[pl.ds(col_place(where, j, i + 1)[0], 1), :] = pltpu.roll(part, 64, 1)
        line = jnp.transpose(row_wide[t * 128 : (t + 1) * 128, :])[0:1]
        row_out[pl.ds(row_place(where, j, i)[0], 1), :] = line
        row_out[pl.ds(row_place(where, j, i + 1)[0], 1), :] = pltpu.roll(line, 64, 1)
    message[:16, :] = jnp.where(where[1] == 0, col_out[...], row_out[...])


def logits_call(place, scale, images, texts):
    return pl.pallas_call(
        logits_body,
        out_shape=(
            jax.ShapeDtypeStruct((BLOCK, BLOCK), F32),
            jax.ShapeDtypeStruct((16, 128), F32),
            jax.ShapeDtypeStruct((16, 128), F32),
            jax.ShapeDtypeStruct((24, 128), F32),
            jax.ShapeDtypeStruct((8, 128), F32),
            ALL,
            ALL,
        ),
        in_specs=[SMEM, SMEM] + [VMEM] * 9,
        out_specs=(VMEM,) * 7,
        scratch_shapes=[pltpu.VMEM((BLOCK, 128), F32)],
        compiler_params=PARAMS,
    )(place, scale, *images, *texts)


def pair_up(rows):
    low = lax.broadcasted_iota(jnp.int32, (1, 128), 1) < ROWS
    pairs = [
        jnp.where(low, rows[i : i + 1], pltpu.roll(rows[i + 1 : i + 2], 64, 1))
        for i in range(0, rows.shape[0], 2)
    ]
    return jnp.concatenate(pairs)


def spread_body(place, row, col, matched, got, out):
    first = place[1] == 0
    mine, other = row[...], got[:16, :]
    top = jnp.maximum(col[...], other)
    both = top + LOG2E * jnp.log(jnp.exp2(col[...] - top) + jnp.exp2(other - top))
    low = pair_up(jnp.where(first, mine, both))
    high = pair_up(other)
    hits = matched[...] + got[16:24, :]
    for i in range(16):
        out[i, :8, :] = low
        out[i, 8:16, :] = high
        out[i, 16:24, :] = hits


def spread_call(place, *parts):
    return pl.pallas_call(
        spread_body,
        out_shape=jax.ShapeDtypeStruct((16, 24, 128), F32),
        in_specs=[SMEM] + [VMEM] * 4,
        out_specs=VMEM,
        compiler_params=PARAMS,
    )(place, *parts)


def join_body(place, got, mine, message):
    first = place[1] == 0
    counts = [jnp.logical_or(first, (place[3] & 1) == i % 2) for i in range(16)]
    parts = [jnp.where(counts[i], got[i, :16, :], -jnp.inf) for i in range(16)]
    top = parts[0]
    for p in parts[1:]:
        top = jnp.maximum(top, p)
    total = jnp.exp2(parts[0] - top)
    for p in parts[1:]:
        total += jnp.exp2(p - top)
    state = top + LOG2E * jnp.log(total)
    low, high = state[:8], state[8:]
    hits = got[0, 16:24, :]
    for i in range(1, 16):
        hits += got[i, 16:24, :]
    both = low + jnp.where(first, high, 0.0)
    share = jnp.sum(both, keepdims=True) - jnp.where(first, 2.0 * hits, 0.0)
    for out, pairs in ((mine, low), (message, jnp.where(first, high, low))):
        for i in range(8):
            out[2 * i : 2 * i + 1, :] = pairs[i : i + 1]
            out[2 * i + 1 : 2 * i + 2, :] = pltpu.roll(pairs[i : i + 1], 64, 1)
        out[16:24, :] = share


def join_call(place, got):
    return pl.pallas_call(
        join_body,
        out_shape=(jax.ShapeDtypeStruct((24, 128), F32),) * 2,
        in_specs=[SMEM, VMEM],
        out_specs=(VMEM,) * 2,
        compiler_params=PARAMS,
    )(place, got)


def digits_of(v):
    place = lax.broadcasted_iota(jnp.int32, (16, 128), 0)
    out = jnp.zeros((16, 128), F32)
    for i in range(DIGITS):
        unit = 16.0 ** (7 - i)
        d = jnp.floor(v * (1.0 / unit) + 0.5)
        v = v - d * unit
        out = jnp.where(place == i, d, out)
    return out


def value_of(digits):
    place = lax.broadcasted_iota(jnp.int32, (16, 128), 0)
    units = jnp.zeros((16, 128), F32)
    for i in range(DIGITS):
        units = jnp.where(place == i, 16.0 ** (7 - i), units)
    return jnp.sum(digits * units, axis=0, keepdims=True)


def weights_body(place, scale, logits, mine, other, images, *refs):
    weights, outs = refs[0], refs[1:5]
    row_wide, row_lse, col_lse = refs[5:]
    first = place[1] == 0
    shares = jnp.where(first, mine[16:17, :], other[16:17, :]), jnp.where(first, other[16:17, :], mine[16:17, :])
    for i, share in enumerate(shares):
        tail = digits_of(share).astype(BF16)
        for e in range(EMBED // 128):
            outs[3][i * TAIL : (i + 1) * TAIL, e * 128 : (e + 1) * 128] = tail
    row_lse[...] = jnp.where(first, mine[:16, :], other[:16, :]) + 1.0
    col_lse[...] = jnp.where(first, other[:16, :], mine[:16, :]) + 1.0
    where = [place[i] for i in range(5)]
    multiplier = scale[0]
    lane = lax.broadcasted_iota(jnp.int32, (1, 128), 1)
    cols = col_ids(where)
    col_line = []
    for t in range(8):
        j, i = t // 2, (t % 2) * 2
        lo = col_lse[pl.ds(col_place(where, j, i)[0], 1), :]
        hi = col_lse[pl.ds(col_place(where, j, i + 1)[0], 1), :]
        col_line.append(jnp.where(lane < ROWS, lo, pltpu.roll(hi, 64, 1)))
        lo = row_lse[pl.ds(row_place(where, j, i)[0], 1), :]
        hi = row_lse[pl.ds(row_place(where, j, i + 1)[0], 1), :]
        line = jnp.where(lane < ROWS, lo, pltpu.roll(hi, 64, 1))
        row_wide[t * 128 : (t + 1) * 128, :] = jnp.transpose(jnp.broadcast_to(line, (128, 128)))
    for a in range(4):
        ids = row_ids(where, a)
        for b in range(4):
            at = a * CHUNK + b * ROWS
            wide = row_wide[at : at + ROWS, :]
            for t in range(8):
                tile = logits[at : at + ROWS, t * 128 : (t + 1) * 128]
                both = jnp.exp2(tile - wide) + jnp.exp2(tile - col_line[t])
                both = both - jnp.where(ids[b] == cols[t][0:1], 1.0, 0.0)
                weights[at : at + ROWS, t * 128 : (t + 1) * 128] = both.astype(BF16)
    text_terms(multiplier, weights, images, 2 * CHUNK, outs[:3])


def text_terms(multiplier, weights, images, at, outs):
    rows = sum(out.shape[0] for out in outs)
    for e in range(5):
        term = multiplier * lax.dot_general(
            weights[:, at : at + rows],
            images[:, e * 256 : (e + 1) * 256],
            (((0,), (0,)), ((), ())),
            preferred_element_type=F32,
        )
        skip = 0
        for out in outs:
            out[:, e * 256 : (e + 1) * 256] = term[skip : skip + out.shape[0]].astype(BF16)
            skip += out.shape[0]


def image_terms(multiplier, weights, texts, at, outs):
    for e in range(5):
        term = multiplier * jnp.dot(
            weights[at * CHUNK : (at + len(outs)) * CHUNK, :],
            texts[:, e * 256 : (e + 1) * 256],
            preferred_element_type=F32,
        )
        for i, out in enumerate(outs):
            out[:CHUNK, e * 256 : (e + 1) * 256] = term[i * CHUNK : (i + 1) * CHUNK].astype(BF16)


def weights_call(place, scale, logits, mine, other, images):
    return pl.pallas_call(
        weights_body,
        out_shape=(
            jax.ShapeDtypeStruct((BLOCK, BLOCK), BF16),
            PART,
            jax.ShapeDtypeStruct((3 * ROWS, EMBED), BF16),
            jax.ShapeDtypeStruct((ROWS, EMBED), BF16),
            jax.ShapeDtypeStruct((2 * TAIL, EMBED), BF16),
        ),
        in_specs=[SMEM, SMEM] + [VMEM] * 4,
        out_specs=(VMEM,) * 5,
        scratch_shapes=[
            pltpu.VMEM((BLOCK, 128), F32),
            pltpu.VMEM((16, 128), F32),
            pltpu.VMEM((16, 128), F32),
        ],
        compiler_params=PARAMS,
    )(place, scale, logits, mine, other, images)


def text_body(scale, weights, images, out):
    text_terms(scale[0], weights, images, CHUNK, [out])


def text_call(scale, weights, images):
    return pl.pallas_call(
        text_body,
        out_shape=PART,
        in_specs=[SMEM] + [VMEM] * 2,
        out_specs=VMEM,
        compiler_params=PARAMS,
    )(scale, weights, images)


def image_body(scale, after, digits, weights, texts, *outs):
    image_terms(scale[0], weights, texts, 1, outs)
    for out in outs:
        out[CHUNK:, :] = digits[TAIL:, :]


def image_call(scale, after, digits, weights, texts):
    return pl.pallas_call(
        image_body,
        out_shape=(jax.ShapeDtypeStruct((CHUNK + TAIL, EMBED), BF16),) * 3,
        in_specs=[SMEM] + [VMEM] * 4,
        out_specs=(VMEM,) * 3,
        compiler_params=PARAMS,
    )(scale, after, digits, weights, texts)


def rest_body(scale, weights, images, texts, text_out, image_out):
    text_terms(scale[0], weights, images, 0, [text_out])
    image_terms(scale[0], weights, texts, 0, [image_out])


def rest_call(scale, weights, images, texts):
    return pl.pallas_call(
        rest_body,
        out_shape=(PART, PART),
        in_specs=[SMEM] + [VMEM] * 3,
        out_specs=(VMEM,) * 2,
        compiler_params=PARAMS,
    )(scale, weights, images, texts)


def add_rows(refs, rows, terms, out, to):
    for at in range(0, rows, 16):
        total = None
        for i, skip in terms:
            v = refs[i][skip + at : skip + at + 16, :].astype(F32)
            total = v if total is None else total + v
        out[to + at : to + at + 16, :] = total.astype(out.dtype)


def sums_body(n, plan, *refs):
    for parts, out in zip(plan, refs[n:]):
        to = 0
        for rows, terms in parts:
            add_rows(refs, rows, terms, out, to)
            to += rows


def sums(arrays, *plan):
    return pl.pallas_call(
        lambda *refs: sums_body(len(arrays), plan, *refs),
        out_shape=tuple(
            jax.ShapeDtypeStruct((sum(rows for rows, _ in parts), EMBED), BF16) for parts in plan
        ),
        in_specs=[VMEM] * len(arrays),
        out_specs=(VMEM,) * len(plan),
        compiler_params=PARAMS,
    )(*arrays)


def last_body(*refs):
    digits, image_out, text_out, loss_out = refs[6:]
    add_rows(refs, ROWS, [(i, 0) for i in range(4)], image_out, 0)
    add_rows(refs, ROWS, [(4, 0), (5, 0)], text_out, 0)
    total = -digits[:TAIL, :128].astype(F32)
    for r in refs[:6]:
        total += r[ROWS : ROWS + TAIL, :128].astype(F32)
    loss_out[...] = value_of(total)[:, 0:1] * (LN2 / (2.0 * ROWS * 256))


def last_call(shards, texts, digits):
    grad = jax.ShapeDtypeStruct((ROWS, EMBED), BF16)
    return pl.pallas_call(
        last_body,
        out_shape=(grad, grad, jax.ShapeDtypeStruct((1, 1), F32)),
        in_specs=[VMEM] * 7,
        out_specs=(VMEM,) * 3,
        compiler_params=PARAMS,
    )(*shards, *texts, digits)


def local(image_emb, text_emb, logit_scale):
    place = jnp.stack([lax.axis_index(n) for n in AXES]).astype(jnp.int32)

    chip, image = pack([text_emb, core_swap(text_emb), image_emb], ((0, 64), (1, 64)), ((2, 64),))
    next_1, next_4 = z_shift(chip, -1), z_shift(text_emb, 4)
    near = [plane_shift(image, k, True) for k in (1, 2, 3)]
    own, text_0, side = pack(
        [image] + near + [chip, next_1, next_4],
        ((0, 64), (1, 64), (2, 64), (3, 64)),
        ((4, 128), (5, 128)),
        ((5, 128), (6, 64)),
    )
    text_1 = z_shift(text_0, -2)
    near = [own] + [plane_shift(own, k, False) for k in PLANE_ORDER[1:]]
    logits, row_part, col_part, message, matched, images, texts = logits_call(
        place, logit_scale, near, [text_0, text_1, core_swap(text_1), core_swap(side), next_4]
    )

    spread = spread_call(place, row_part, col_part, matched, core_swap(message))
    mine, message = join_call(place, exchange(spread, plane_or_ring()))
    weights, text_2, text_3, far, digits = weights_call(
        place, logit_scale, logits, mine, core_swap(message), images
    )

    other_1, other_3 = core_swap(text_2), core_swap(text_3)
    text_1 = text_call(logit_scale, weights, images)
    pairs = sums(
        [text_1, other_1, far, other_3, digits],
        ((256, ((0, 0), (1, 0))), (64, ((2, 0), (3, 128))), (TAIL, ((4, 0),))),
    )[0]
    image_parts = image_call(logit_scale, pairs, digits, weights, texts)
    pairs = z_shift(pairs, 2)
    back = [plane_shift(v, -k, False) for v, k in ((image_parts[k - 1], k) for k in (2, 1, 3))]
    text_0, image_0 = rest_call(logit_scale, weights, images, texts)

    rows_tail = (TAIL, ((2, 320), (3, 0)))
    next_1, mine, next_4 = sums(
        [text_0, other_3, pairs, digits],
        ((128, ((0, 128), (1, 0), (2, 128))), rows_tail),
        ((128, ((0, 0), (2, 0))), rows_tail),
        ((80, ((2, 256),)),),
    )
    next_1, next_4 = z_shift(next_1, 1), z_shift(next_4, 2)
    (other,) = sums([mine, next_1], ((64, ((0, 64), (1, 64))), (TAIL, ((0, 128), (1, 128)))))
    (mine,) = sums(
        [mine, next_1, next_4], ((64, ((0, 0), (1, 0), (2, 0))), (TAIL, ((0, 128), (1, 128), (2, 64))))
    )

    cols_tail = (TAIL, ((1, 256), (2, 256), (3, 256), (4, 16)))
    pieces = sums(
        [image_0] + back + [digits],
        *[((64, [(i, 64 * k) for i in range(4)]), cols_tail) for k in range(4)],
    )
    shards = [pieces[0]] + [plane_shift(pieces[k], -k, True) for k in (2, 1, 3)]
    image_grad, text_grad, mean_loss = last_call(shards, [mine, core_swap(other)], digits)
    return mean_loss.reshape(1), image_grad, text_grad


def solution(mesh):
    fine = Mesh(mesh.devices.reshape(4, 2, 2, 4, 4), AXES)
    return jax.shard_map(
        local,
        mesh=fine,
        in_specs=(P(AXES, None), P(("zh", "y", "x", "zl", "core"), None), P()),
        out_specs=(P(), P(AXES, None), P(("zh", "y", "x", "zl", "core"), None)),
        check_vma=False,
    )
```

```python
import math

import jax
import jax.numpy as jnp
from jax import lax
from jax.experimental import pallas as pl
from jax.experimental.pallas import tpu as pltpu
from jax.sharding import Mesh, PartitionSpec as P

AXES = ("zl", "core", "zh", "y", "x")
NX, NY, NZ = 4, 4, 8
ROWS, EMBED = 64, 1280
CHUNK = 4 * ROWS
TAIL, DIGITS = 16, 13
BLOCK = 16 * ROWS
BF16, F32 = jnp.bfloat16, jnp.float32
LOG2E, LN2 = math.log2(math.e), math.log(2.0)
VMEM = pl.BlockSpec(memory_space=pltpu.VMEM)
SMEM = pl.BlockSpec(memory_space=pltpu.SMEM)
PARAMS = pltpu.CompilerParams(vmem_limit_bytes=12 * 1024 * 1024)


def plane_shift(v, k, primary):
    pairs = []
    for c in range(2):
        for h in range(2):
            for y in range(NY):
                for x in range(NX):
                    if (c == 0) == primary:
                        to = (y, (x + k) % NX)
                    else:
                        to = ((y + k) % NY, x)
                    base = (c * 2 + h) * NY
                    pairs.append(((base + y) * NX + x, (base + to[0]) * NX + to[1]))
    return lax.ppermute(v, ("core", "zh", "y", "x"), pairs)


def z_shift(v, k):
    pairs = []
    for c in range(2):
        for z in range(NZ):
            to = (z + (k if c == 0 else -k)) % NZ
            pairs.append((((z % 4) * 2 + c) * 2 + z // 4, ((to % 4) * 2 + c) * 2 + to // 4))
    return lax.ppermute(v, ("zl", "core", "zh"), pairs)


def core_swap(v):
    return lax.ppermute(v, "core", [(0, 1), (1, 0)])


def device(c, y, x, z):
    return ((((z % 4) * 2 + c) * 2 + z // 4) * NY + y) * NX + x


def plane_or_ring():
    out = [[device(0, y, x, z) for y in range(NY) for x in range(NX)] for z in range(NZ)]
    return out + [
        [device(1, y + d, x, z) for z in range(NZ) for d in (0, 1)] for y in (0, 2) for x in range(NX)
    ]


def exchange(v, groups):
    return lax.all_to_all(v, AXES, 0, 0, axis_index_groups=groups)


def row_place(where, a, b):
    zl, c, zh, y, x = where
    p, s = jnp.where(c == 0, b, a), jnp.where(c == 0, a, b)
    n = ((y - s) & 3) * 4 + ((x - p) & 3)
    return n, ((zl * 2 + c) * 2 + zh) * 16 + n


def col_place(where, j, i):
    zl, c, zh, y, x = where
    core = c if (i % 2 == 0) == (j < 2) else 1 - c
    sign = 1 - 2 * c
    off = ((0, 0, 1, 1), (2, 2, 3, 3), (-2, -2, -3, -3), (-1, -1, 4, 4))[j][i]
    off = 4 if off == 4 else sign * off
    z = (zh * 4 + zl + off) & 7
    return z * 2 + core, ((z >> 2) * 16 + y * 4 + x) * 8 + (z & 3) * 2 + core


def row_ids(where, a):
    span = lax.broadcasted_iota(jnp.int32, (ROWS, 128), 0)
    return [row_place(where, a, b)[1] * ROWS + span for b in range(4)]


def col_ids(where):
    lane = lax.broadcasted_iota(jnp.int32, (8, 128), 1)
    out = []
    for t in range(8):
        lo = col_place(where, t // 2, (t % 2) * 2)[1] * ROWS
        hi = col_place(where, t // 2, (t % 2) * 2 + 1)[1] * ROWS - ROWS
        out.append(lane + jnp.where(lane < ROWS, lo, hi))
    return out


PLANE_ORDER = (0, 1, 3, 2)
PART = jax.ShapeDtypeStruct((CHUNK, EMBED), BF16)
ALL = jax.ShapeDtypeStruct((BLOCK, EMBED), BF16)


def pack_body(plan, n, *refs):
    for parts, out in zip(plan, refs[n:]):
        row = 0
        for i, rows in parts:
            out[row : row + rows, :] = refs[i][...]
            row += rows


def pack(arrays, *plan):
    shapes = [jax.ShapeDtypeStruct((sum(p[1] for p in parts), EMBED), BF16) for parts in plan]
    return pl.pallas_call(
        lambda *refs: pack_body(plan, len(arrays), *refs),
        out_shape=tuple(shapes),
        in_specs=[VMEM] * len(arrays),
        out_specs=(VMEM,) * len(plan),
        compiler_params=PARAMS,
    )(*arrays)


def fold(v):
    return v.reshape(v.shape[0] // 8, 8, 128)


def column_part(logits, t, top):
    top = jnp.max(top, axis=0, keepdims=True)

    def step(i, total):
        tile = logits[pl.ds(pl.multiple_of(i * 128, 128), 128), t * 128 : (t + 1) * 128]
        return total + jnp.sum(fold(jnp.exp2(tile - top)), axis=0)

    total = lax.fori_loop(0, 8, step, jnp.zeros((8, 128), F32), unroll=True)
    return top + LOG2E * jnp.log(jnp.sum(total, axis=0, keepdims=True))


def logits_body(place, scale, *refs):
    images, texts = [refs[i] for i in PLANE_ORDER], refs[4:7]
    logits, row_out, col_out, message, match_out, all_images, all_texts = refs[9:16]
    row_wide = refs[16]
    all_texts[3 * CHUNK : BLOCK - ROWS, :] = refs[7][...]
    all_texts[BLOCK - ROWS :, :] = refs[8][...]
    where = [place[i] for i in range(5)]
    multiplier = scale[0] * LOG2E
    for j in range(3):
        all_texts[j * CHUNK : (j + 1) * CHUNK, :] = texts[j][...]

    def chunk_logits(a):
        all_images[a * CHUNK : (a + 1) * CHUNK, :] = images[a][...]
        for j in range(4):
            text = texts[j][...] if j < 3 else all_texts[3 * CHUNK :, :]
            logits[a * CHUNK : (a + 1) * CHUNK, j * CHUNK : (j + 1) * CHUNK] = multiplier * lax.dot_general(
                images[a][...], text, (((1,), (1,)), ((), ())), preferred_element_type=F32
            )

    chunk_logits(0)
    cols = col_ids(where)
    step = 32
    matched = jnp.zeros((8, 128), F32)
    col_top = [jnp.full((8, 128), -jnp.inf, F32) for _ in range(8)]
    for a in range(4):
        if a < 3:
            chunk_logits(a + 1)
        ids = row_ids(where, a)
        for b in range(4):
            for half in range(ROWS // step):
                at = a * CHUNK + b * ROWS + half * step
                tiles = [logits[at : at + step, t * 128 : (t + 1) * 128] for t in range(8)]
                top = tiles[0]
                for t in range(1, 8):
                    top = jnp.maximum(top, tiles[t])
                top = jnp.max(top, axis=1, keepdims=True)
                mine = ids[b][half * step : (half + 1) * step]
                total = jnp.zeros((step, 128), F32)
                for t in range(8):
                    total += jnp.exp2(tiles[t] - top)
                    col_top[t] = jnp.maximum(col_top[t], jnp.max(fold(tiles[t]), axis=0))
                    hit = jnp.where(mine == cols[t][0:1], tiles[t], 0.0)
                    matched += jnp.sum(fold(hit), axis=0)
                part = top + LOG2E * jnp.log(jnp.sum(total, axis=1, keepdims=True))
                row_wide[at : at + step, :] = jnp.broadcast_to(part, (step, 128))
    matched = jnp.broadcast_to(jnp.sum(matched, keepdims=True), (8, 128))
    match_out[...] = matched
    message[16:24, :] = matched
    for t in range(8):
        part = column_part(logits, t, col_top[t])
        j, i = t // 2, (t % 2) * 2
        col_out[pl.ds(col_place(where, j, i)[0], 1), :] = part
        col_out[pl.ds(col_place(where, j, i + 1)[0], 1), :] = pltpu.roll(part, 64, 1)
        line = jnp.transpose(row_wide[t * 128 : (t + 1) * 128, :])[0:1]
        row_out[pl.ds(row_place(where, j, i)[0], 1), :] = line
        row_out[pl.ds(row_place(where, j, i + 1)[0], 1), :] = pltpu.roll(line, 64, 1)
    message[:16, :] = jnp.where(where[1] == 0, col_out[...], row_out[...])


def logits_call(place, scale, images, texts):
    return pl.pallas_call(
        logits_body,
        out_shape=(
            jax.ShapeDtypeStruct((BLOCK, BLOCK), F32),
            jax.ShapeDtypeStruct((16, 128), F32),
            jax.ShapeDtypeStruct((16, 128), F32),
            jax.ShapeDtypeStruct((24, 128), F32),
            jax.ShapeDtypeStruct((8, 128), F32),
            ALL,
            ALL,
        ),
        in_specs=[SMEM, SMEM] + [VMEM] * 9,
        out_specs=(VMEM,) * 7,
        scratch_shapes=[pltpu.VMEM((BLOCK, 128), F32)],
        compiler_params=PARAMS,
    )(place, scale, *images, *texts)


def pair_up(rows):
    low = lax.broadcasted_iota(jnp.int32, (1, 128), 1) < ROWS
    pairs = [
        jnp.where(low, rows[i : i + 1], pltpu.roll(rows[i + 1 : i + 2], 64, 1))
        for i in range(0, rows.shape[0], 2)
    ]
    return jnp.concatenate(pairs)


def spread_body(place, row, col, matched, got, out):
    first = place[1] == 0
    mine, other = row[...], got[:16, :]
    top = jnp.maximum(col[...], other)
    both = top + LOG2E * jnp.log(jnp.exp2(col[...] - top) + jnp.exp2(other - top))
    low = pair_up(jnp.where(first, mine, both))
    high = pair_up(other)
    hits = matched[...] + got[16:24, :]
    for i in range(16):
        out[i, :8, :] = low
        out[i, 8:16, :] = high
        out[i, 16:24, :] = hits


def spread_call(place, *parts):
    return pl.pallas_call(
        spread_body,
        out_shape=jax.ShapeDtypeStruct((16, 24, 128), F32),
        in_specs=[SMEM] + [VMEM] * 4,
        out_specs=VMEM,
        compiler_params=PARAMS,
    )(place, *parts)


def join_body(place, got, mine, message):
    first = place[1] == 0
    counts = [jnp.logical_or(first, (place[3] & 1) == i % 2) for i in range(16)]
    parts = [jnp.where(counts[i], got[i, :16, :], -jnp.inf) for i in range(16)]
    top = parts[0]
    for p in parts[1:]:
        top = jnp.maximum(top, p)
    total = jnp.exp2(parts[0] - top)
    for p in parts[1:]:
        total += jnp.exp2(p - top)
    state = top + LOG2E * jnp.log(total)
    low, high = state[:8], state[8:]
    hits = got[0, 16:24, :]
    for i in range(1, 16):
        hits += got[i, 16:24, :]
    both = low + jnp.where(first, high, 0.0)
    share = jnp.sum(both, keepdims=True) - jnp.where(first, 2.0 * hits, 0.0)
    for out, pairs in ((mine, low), (message, jnp.where(first, high, low))):
        for i in range(8):
            out[2 * i : 2 * i + 1, :] = pairs[i : i + 1]
            out[2 * i + 1 : 2 * i + 2, :] = pltpu.roll(pairs[i : i + 1], 64, 1)
        out[16:24, :] = share


def join_call(place, got):
    return pl.pallas_call(
        join_body,
        out_shape=(jax.ShapeDtypeStruct((24, 128), F32),) * 2,
        in_specs=[SMEM, VMEM],
        out_specs=(VMEM,) * 2,
        compiler_params=PARAMS,
    )(place, got)


def digits_of(v):
    place = lax.broadcasted_iota(jnp.int32, (16, 128), 0)
    out = jnp.zeros((16, 128), F32)
    for i in range(DIGITS):
        unit = 16.0 ** (7 - i)
        d = jnp.floor(v * (1.0 / unit) + 0.5)
        v = v - d * unit
        out = jnp.where(place == i, d, out)
    return out


def value_of(digits):
    place = lax.broadcasted_iota(jnp.int32, (16, 128), 0)
    units = jnp.zeros((16, 128), F32)
    for i in range(DIGITS):
        units = jnp.where(place == i, 16.0 ** (7 - i), units)
    return jnp.sum(digits * units, axis=0, keepdims=True)


def weights_body(place, scale, logits, mine, other, images, *refs):
    weights, outs = refs[0], refs[1:5]
    row_wide, row_lse, col_lse = refs[5:]
    first = place[1] == 0
    shares = jnp.where(first, mine[16:17, :], other[16:17, :]), jnp.where(first, other[16:17, :], mine[16:17, :])
    for i, share in enumerate(shares):
        tail = digits_of(share).astype(BF16)
        for e in range(EMBED // 128):
            outs[3][i * TAIL : (i + 1) * TAIL, e * 128 : (e + 1) * 128] = tail
    row_lse[...] = jnp.where(first, mine[:16, :], other[:16, :]) + 1.0
    col_lse[...] = jnp.where(first, other[:16, :], mine[:16, :]) + 1.0
    where = [place[i] for i in range(5)]
    multiplier = scale[0]
    lane = lax.broadcasted_iota(jnp.int32, (1, 128), 1)
    cols = col_ids(where)
    col_line = []
    for t in range(8):
        j, i = t // 2, (t % 2) * 2
        lo = col_lse[pl.ds(col_place(where, j, i)[0], 1), :]
        hi = col_lse[pl.ds(col_place(where, j, i + 1)[0], 1), :]
        col_line.append(jnp.where(lane < ROWS, lo, pltpu.roll(hi, 64, 1)))
        lo = row_lse[pl.ds(row_place(where, j, i)[0], 1), :]
        hi = row_lse[pl.ds(row_place(where, j, i + 1)[0], 1), :]
        line = jnp.where(lane < ROWS, lo, pltpu.roll(hi, 64, 1))
        row_wide[t * 128 : (t + 1) * 128, :] = jnp.transpose(jnp.broadcast_to(line, (128, 128)))
    for a in range(4):
        ids = row_ids(where, a)
        for b in range(4):
            at = a * CHUNK + b * ROWS
            wide = row_wide[at : at + ROWS, :]
            for t in range(8):
                tile = logits[at : at + ROWS, t * 128 : (t + 1) * 128]
                both = jnp.exp2(tile - wide) + jnp.exp2(tile - col_line[t])
                both = both - jnp.where(ids[b] == cols[t][0:1], 1.0, 0.0)
                weights[at : at + ROWS, t * 128 : (t + 1) * 128] = both.astype(BF16)
    text_terms(multiplier, weights, images, 2 * CHUNK, outs[:3])


def text_terms(multiplier, weights, images, at, outs):
    rows = sum(out.shape[0] for out in outs)
    for e in range(5):
        term = multiplier * lax.dot_general(
            weights[:, at : at + rows],
            images[:, e * 256 : (e + 1) * 256],
            (((0,), (0,)), ((), ())),
            preferred_element_type=F32,
        )
        skip = 0
        for out in outs:
            out[:, e * 256 : (e + 1) * 256] = term[skip : skip + out.shape[0]].astype(BF16)
            skip += out.shape[0]


def image_terms(multiplier, weights, texts, at, outs):
    for e in range(5):
        term = multiplier * jnp.dot(
            weights[at * CHUNK : (at + len(outs)) * CHUNK, :],
            texts[:, e * 256 : (e + 1) * 256],
            preferred_element_type=F32,
        )
        for i, out in enumerate(outs):
            out[:CHUNK, e * 256 : (e + 1) * 256] = term[i * CHUNK : (i + 1) * CHUNK].astype(BF16)


def weights_call(place, scale, logits, mine, other, images):
    return pl.pallas_call(
        weights_body,
        out_shape=(
            jax.ShapeDtypeStruct((BLOCK, BLOCK), BF16),
            PART,
            jax.ShapeDtypeStruct((3 * ROWS, EMBED), BF16),
            jax.ShapeDtypeStruct((ROWS, EMBED), BF16),
            jax.ShapeDtypeStruct((2 * TAIL, EMBED), BF16),
        ),
        in_specs=[SMEM, SMEM] + [VMEM] * 4,
        out_specs=(VMEM,) * 5,
        scratch_shapes=[
            pltpu.VMEM((BLOCK, 128), F32),
            pltpu.VMEM((16, 128), F32),
            pltpu.VMEM((16, 128), F32),
        ],
        compiler_params=PARAMS,
    )(place, scale, logits, mine, other, images)


def text_body(scale, weights, images, out):
    text_terms(scale[0], weights, images, CHUNK, [out])


def text_call(scale, weights, images):
    return pl.pallas_call(
        text_body,
        out_shape=PART,
        in_specs=[SMEM] + [VMEM] * 2,
        out_specs=VMEM,
        compiler_params=PARAMS,
    )(scale, weights, images)


def image_body(scale, digits, weights, texts, *outs):
    image_terms(scale[0], weights, texts, 1, outs)
    for out in outs:
        out[CHUNK:, :] = digits[TAIL:, :]


def image_call(scale, digits, weights, texts):
    return pl.pallas_call(
        image_body,
        out_shape=(jax.ShapeDtypeStruct((CHUNK + TAIL, EMBED), BF16),) * 3,
        in_specs=[SMEM] + [VMEM] * 3,
        out_specs=(VMEM,) * 3,
        compiler_params=PARAMS,
    )(scale, digits, weights, texts)


def rest_body(scale, weights, images, texts, text_out, image_out):
    text_terms(scale[0], weights, images, 0, [text_out])
    image_terms(scale[0], weights, texts, 0, [image_out])


def rest_call(scale, weights, images, texts):
    return pl.pallas_call(
        rest_body,
        out_shape=(PART, PART),
        in_specs=[SMEM] + [VMEM] * 3,
        out_specs=(VMEM,) * 2,
        compiler_params=PARAMS,
    )(scale, weights, images, texts)


def add_rows(refs, rows, terms, out, to):
    for at in range(0, rows, 16):
        total = None
        for i, skip in terms:
            v = refs[i][skip + at : skip + at + 16, :].astype(F32)
            total = v if total is None else total + v
        out[to + at : to + at + 16, :] = total.astype(out.dtype)


def sums_body(n, plan, *refs):
    for parts, out in zip(plan, refs[n:]):
        to = 0
        for rows, terms in parts:
            add_rows(refs, rows, terms, out, to)
            to += rows


def sums(arrays, *plan):
    return pl.pallas_call(
        lambda *refs: sums_body(len(arrays), plan, *refs),
        out_shape=tuple(
            jax.ShapeDtypeStruct((sum(rows for rows, _ in parts), EMBED), BF16) for parts in plan
        ),
        in_specs=[VMEM] * len(arrays),
        out_specs=(VMEM,) * len(plan),
        compiler_params=PARAMS,
    )(*arrays)


def last_body(*refs):
    digits, image_out, text_out, loss_out = refs[6:]
    add_rows(refs, ROWS, [(i, 0) for i in range(4)], image_out, 0)
    add_rows(refs, ROWS, [(4, 0), (5, 0)], text_out, 0)
    total = -digits[:TAIL, :128].astype(F32)
    for r in refs[:6]:
        total += r[ROWS : ROWS + TAIL, :128].astype(F32)
    loss_out[...] = value_of(total)[:, 0:1] * (LN2 / (2.0 * ROWS * 256))


def last_call(shards, texts, digits):
    grad = jax.ShapeDtypeStruct((ROWS, EMBED), BF16)
    return pl.pallas_call(
        last_body,
        out_shape=(grad, grad, jax.ShapeDtypeStruct((1, 1), F32)),
        in_specs=[VMEM] * 7,
        out_specs=(VMEM,) * 3,
        compiler_params=PARAMS,
    )(*shards, *texts, digits)


def local(image_emb, text_emb, logit_scale):
    place = jnp.stack([lax.axis_index(n) for n in AXES]).astype(jnp.int32)

    chip, image = pack([text_emb, core_swap(text_emb), image_emb], ((0, 64), (1, 64)), ((2, 64),))
    next_1, next_4 = z_shift(chip, -1), z_shift(text_emb, 4)
    near = [plane_shift(image, k, True) for k in (1, 2, 3)]
    own, text_0, side = pack(
        [image] + near + [chip, next_1, next_4],
        ((0, 64), (1, 64), (2, 64), (3, 64)),
        ((4, 128), (5, 128)),
        ((5, 128), (6, 64)),
    )
    text_1 = z_shift(text_0, -2)
    near = [own] + [plane_shift(own, k, False) for k in PLANE_ORDER[1:]]
    logits, row_part, col_part, message, matched, images, texts = logits_call(
        place, logit_scale, near, [text_0, text_1, core_swap(text_1), core_swap(side), next_4]
    )

    spread = spread_call(place, row_part, col_part, matched, core_swap(message))
    mine, message = join_call(place, exchange(spread, plane_or_ring()))
    weights, text_2, text_3, far, digits = weights_call(
        place, logit_scale, logits, mine, core_swap(message), images
    )

    other_1, other_3 = core_swap(text_2), core_swap(text_3)
    text_1 = text_call(logit_scale, weights, images)
    image_parts = image_call(logit_scale, digits, weights, texts)
    pairs = sums(
        [text_1, other_1, far, other_3, digits, image_parts[0]],
        ((256, ((0, 0), (1, 0))), (64, ((2, 0), (3, 128))), (TAIL, ((4, 0),))),
    )[0]
    pairs = z_shift(pairs, 2)
    back = [plane_shift(v, -k, False) for v, k in ((image_parts[k - 1], k) for k in (2, 1, 3))]
    text_0, image_0 = rest_call(logit_scale, weights, images, texts)

    rows_tail = (TAIL, ((2, 320), (3, 0)))
    next_1, mine, next_4 = sums(
        [text_0, other_3, pairs, digits],
        ((128, ((0, 128), (1, 0), (2, 128))), rows_tail),
        ((128, ((0, 0), (2, 0))), rows_tail),
        ((80, ((2, 256),)),),
    )
    next_1, next_4 = z_shift(next_1, 1), z_shift(next_4, 2)
    (other,) = sums([mine, next_1], ((64, ((0, 64), (1, 64))), (TAIL, ((0, 128), (1, 128)))))
    (mine,) = sums(
        [mine, next_1, next_4], ((64, ((0, 0), (1, 0), (2, 0))), (TAIL, ((0, 128), (1, 128), (2, 64))))
    )

    cols_tail = (TAIL, ((1, 256), (2, 256), (3, 256), (4, 16)))
    pieces = sums(
        [image_0] + back + [digits],
        *[((64, [(i, 64 * k) for i in range(4)]), cols_tail) for k in range(4)],
    )
    shards = [pieces[0]] + [plane_shift(pieces[k], -k, True) for k in (2, 1, 3)]
    image_grad, text_grad, mean_loss = last_call(shards, [mine, core_swap(other)], digits)
    return mean_loss.reshape(1), image_grad, text_grad


def solution(mesh):
    fine = Mesh(mesh.devices.reshape(4, 2, 2, 4, 4), AXES)
    return jax.shard_map(
        local,
        mesh=fine,
        in_specs=(P(AXES, None), P(("zh", "y", "x", "zl", "core"), None), P()),
        out_specs=(P(), P(AXES, None), P(("zh", "y", "x", "zl", "core"), None)),
        check_vma=False,
    )
```

```python
import math

import jax
import jax.numpy as jnp
from jax import lax
from jax.experimental import pallas as pl
from jax.experimental.pallas import tpu as pltpu
from jax.sharding import Mesh, PartitionSpec as P

AXES = ("zl", "core", "zh", "y", "x")
NX, NY, NZ = 4, 4, 8
ROWS, EMBED = 64, 1280
CHUNK = 4 * ROWS
TAIL, DIGITS = 16, 13
BLOCK = 16 * ROWS
BF16, F32 = jnp.bfloat16, jnp.float32
LOG2E, LN2 = math.log2(math.e), math.log(2.0)
VMEM = pl.BlockSpec(memory_space=pltpu.VMEM)
SMEM = pl.BlockSpec(memory_space=pltpu.SMEM)
PARAMS = pltpu.CompilerParams(vmem_limit_bytes=12 * 1024 * 1024)


def plane_shift(v, k, primary):
    pairs = []
    for c in range(2):
        for h in range(2):
            for y in range(NY):
                for x in range(NX):
                    if (c == 0) == primary:
                        to = (y, (x + k) % NX)
                    else:
                        to = ((y + k) % NY, x)
                    base = (c * 2 + h) * NY
                    pairs.append(((base + y) * NX + x, (base + to[0]) * NX + to[1]))
    return lax.ppermute(v, ("core", "zh", "y", "x"), pairs)


def z_shift(v, k):
    pairs = []
    for c in range(2):
        for z in range(NZ):
            to = (z + (k if c == 0 else -k)) % NZ
            pairs.append((((z % 4) * 2 + c) * 2 + z // 4, ((to % 4) * 2 + c) * 2 + to // 4))
    return lax.ppermute(v, ("zl", "core", "zh"), pairs)


def core_swap(v):
    return lax.ppermute(v, "core", [(0, 1), (1, 0)])


def device(c, y, x, z):
    return ((((z % 4) * 2 + c) * 2 + z // 4) * NY + y) * NX + x


def plane_or_ring():
    out = [[device(0, y, x, z) for y in range(NY) for x in range(NX)] for z in range(NZ)]
    return out + [
        [device(1, y + d, x, z) for z in range(NZ) for d in (0, 1)] for y in (0, 2) for x in range(NX)
    ]


def exchange(v, groups):
    return lax.all_to_all(v, AXES, 0, 0, axis_index_groups=groups)


def row_place(where, a, b):
    zl, c, zh, y, x = where
    p, s = jnp.where(c == 0, b, a), jnp.where(c == 0, a, b)
    n = ((y - s) & 3) * 4 + ((x - p) & 3)
    return n, ((zl * 2 + c) * 2 + zh) * 16 + n


def col_place(where, j, i):
    zl, c, zh, y, x = where
    core = c if (i % 2 == 0) == (j < 2) else 1 - c
    sign = 1 - 2 * c
    off = ((0, 0, 1, 1), (2, 2, 3, 3), (-2, -2, -3, -3), (-1, -1, 4, 4))[j][i]
    off = 4 if off == 4 else sign * off
    z = (zh * 4 + zl + off) & 7
    return z * 2 + core, ((z >> 2) * 16 + y * 4 + x) * 8 + (z & 3) * 2 + core


def row_ids(where, a):
    span = lax.broadcasted_iota(jnp.int32, (ROWS, 128), 0)
    return [row_place(where, a, b)[1] * ROWS + span for b in range(4)]


def col_ids(where):
    lane = lax.broadcasted_iota(jnp.int32, (8, 128), 1)
    out = []
    for t in range(8):
        lo = col_place(where, t // 2, (t % 2) * 2)[1] * ROWS
        hi = col_place(where, t // 2, (t % 2) * 2 + 1)[1] * ROWS - ROWS
        out.append(lane + jnp.where(lane < ROWS, lo, hi))
    return out


PLANE_ORDER = (0, 1, 3, 2)
PART = jax.ShapeDtypeStruct((CHUNK, EMBED), BF16)
ALL = jax.ShapeDtypeStruct((BLOCK, EMBED), BF16)
HALF_WEIGHTS = jax.ShapeDtypeStruct((BLOCK, BLOCK // 2), BF16)


def pack_body(plan, n, *refs):
    for parts, out in zip(plan, refs[n:]):
        row = 0
        for i, rows in parts:
            out[row : row + rows, :] = refs[i][...]
            row += rows


def pack(arrays, *plan):
    shapes = [jax.ShapeDtypeStruct((sum(p[1] for p in parts), EMBED), BF16) for parts in plan]
    return pl.pallas_call(
        lambda *refs: pack_body(plan, len(arrays), *refs),
        out_shape=tuple(shapes),
        in_specs=[VMEM] * len(arrays),
        out_specs=(VMEM,) * len(plan),
        compiler_params=PARAMS,
    )(*arrays)


def fold(v):
    return v.reshape(v.shape[0] // 8, 8, 128)


def column_part(logits, t, top):
    top = jnp.max(top, axis=0, keepdims=True)

    def step(i, total):
        tile = logits[pl.ds(pl.multiple_of(i * 128, 128), 128), t * 128 : (t + 1) * 128]
        return total + jnp.sum(fold(jnp.exp2(tile - top)), axis=0)

    total = lax.fori_loop(0, 8, step, jnp.zeros((8, 128), F32), unroll=True)
    return top + LOG2E * jnp.log(jnp.sum(total, axis=0, keepdims=True))


def logits_body(place, scale, *refs):
    images, texts = [refs[i] for i in PLANE_ORDER], refs[4:7]
    logits, row_out, col_out, message, match_out, all_images, all_texts = refs[9:16]
    row_wide = refs[16]
    all_texts[3 * CHUNK : BLOCK - ROWS, :] = refs[7][...]
    all_texts[BLOCK - ROWS :, :] = refs[8][...]
    where = [place[i] for i in range(5)]
    multiplier = scale[0] * LOG2E
    for j in range(3):
        all_texts[j * CHUNK : (j + 1) * CHUNK, :] = texts[j][...]

    def chunk_logits(a):
        all_images[a * CHUNK : (a + 1) * CHUNK, :] = images[a][...]
        for j in range(4):
            text = texts[j][...] if j < 3 else all_texts[3 * CHUNK :, :]
            logits[a * CHUNK : (a + 1) * CHUNK, j * CHUNK : (j + 1) * CHUNK] = multiplier * lax.dot_general(
                images[a][...], text, (((1,), (1,)), ((), ())), preferred_element_type=F32
            )

    chunk_logits(0)
    cols = col_ids(where)
    step = 32
    matched = jnp.zeros((8, 128), F32)
    col_top = [jnp.full((8, 128), -jnp.inf, F32) for _ in range(8)]
    for a in range(4):
        if a < 3:
            chunk_logits(a + 1)
        ids = row_ids(where, a)
        for b in range(4):
            for half in range(ROWS // step):
                at = a * CHUNK + b * ROWS + half * step
                tiles = [logits[at : at + step, t * 128 : (t + 1) * 128] for t in range(8)]
                top = tiles[0]
                for t in range(1, 8):
                    top = jnp.maximum(top, tiles[t])
                top = jnp.max(top, axis=1, keepdims=True)
                mine = ids[b][half * step : (half + 1) * step]
                total = jnp.zeros((step, 128), F32)
                for t in range(8):
                    total += jnp.exp2(tiles[t] - top)
                    col_top[t] = jnp.maximum(col_top[t], jnp.max(fold(tiles[t]), axis=0))
                    hit = jnp.where(mine == cols[t][0:1], tiles[t], 0.0)
                    matched += jnp.sum(fold(hit), axis=0)
                part = top + LOG2E * jnp.log(jnp.sum(total, axis=1, keepdims=True))
                row_wide[at : at + step, :] = jnp.broadcast_to(part, (step, 128))
    matched = jnp.broadcast_to(jnp.sum(matched, keepdims=True), (8, 128))
    match_out[...] = matched
    message[16:24, :] = matched
    for t in range(8):
        part = column_part(logits, t, col_top[t])
        j, i = t // 2, (t % 2) * 2
        col_out[pl.ds(col_place(where, j, i)[0], 1), :] = part
        col_out[pl.ds(col_place(where, j, i + 1)[0], 1), :] = pltpu.roll(part, 64, 1)
        line = jnp.transpose(row_wide[t * 128 : (t + 1) * 128, :])[0:1]
        row_out[pl.ds(row_place(where, j, i)[0], 1), :] = line
        row_out[pl.ds(row_place(where, j, i + 1)[0], 1), :] = pltpu.roll(line, 64, 1)
    message[:16, :] = jnp.where(where[1] == 0, col_out[...], row_out[...])


def logits_call(place, scale, images, texts):
    return pl.pallas_call(
        logits_body,
        out_shape=(
            jax.ShapeDtypeStruct((BLOCK, BLOCK), F32),
            jax.ShapeDtypeStruct((16, 128), F32),
            jax.ShapeDtypeStruct((16, 128), F32),
            jax.ShapeDtypeStruct((24, 128), F32),
            jax.ShapeDtypeStruct((8, 128), F32),
            ALL,
            ALL,
        ),
        in_specs=[SMEM, SMEM] + [VMEM] * 9,
        out_specs=(VMEM,) * 7,
        scratch_shapes=[pltpu.VMEM((BLOCK, 128), F32)],
        compiler_params=PARAMS,
    )(place, scale, *images, *texts)


def pair_up(rows):
    low = lax.broadcasted_iota(jnp.int32, (1, 128), 1) < ROWS
    pairs = [
        jnp.where(low, rows[i : i + 1], pltpu.roll(rows[i + 1 : i + 2], 64, 1))
        for i in range(0, rows.shape[0], 2)
    ]
    return jnp.concatenate(pairs)


def spread_body(place, row, col, matched, got, out):
    first = place[1] == 0
    mine, other = row[...], got[:16, :]
    top = jnp.maximum(col[...], other)
    both = top + LOG2E * jnp.log(jnp.exp2(col[...] - top) + jnp.exp2(other - top))
    low = pair_up(jnp.where(first, mine, both))
    high = pair_up(other)
    hits = matched[...] + got[16:24, :]
    for i in range(16):
        out[i, :8, :] = low
        out[i, 8:16, :] = high
        out[i, 16:24, :] = hits


def spread_call(place, *parts):
    return pl.pallas_call(
        spread_body,
        out_shape=jax.ShapeDtypeStruct((16, 24, 128), F32),
        in_specs=[SMEM] + [VMEM] * 4,
        out_specs=VMEM,
        compiler_params=PARAMS,
    )(place, *parts)


def join_body(place, got, mine, message):
    first = place[1] == 0
    counts = [jnp.logical_or(first, (place[3] & 1) == i % 2) for i in range(16)]
    parts = [jnp.where(counts[i], got[i, :16, :], -jnp.inf) for i in range(16)]
    top = parts[0]
    for p in parts[1:]:
        top = jnp.maximum(top, p)
    total = jnp.exp2(parts[0] - top)
    for p in parts[1:]:
        total += jnp.exp2(p - top)
    state = top + LOG2E * jnp.log(total)
    low, high = state[:8], state[8:]
    hits = got[0, 16:24, :]
    for i in range(1, 16):
        hits += got[i, 16:24, :]
    both = low + jnp.where(first, high, 0.0)
    share = jnp.sum(both, keepdims=True) - jnp.where(first, 2.0 * hits, 0.0)
    for out, pairs in ((mine, low), (message, jnp.where(first, high, low))):
        for i in range(8):
            out[2 * i : 2 * i + 1, :] = pairs[i : i + 1]
            out[2 * i + 1 : 2 * i + 2, :] = pltpu.roll(pairs[i : i + 1], 64, 1)
        out[16:24, :] = share


def join_call(place, got):
    return pl.pallas_call(
        join_body,
        out_shape=(jax.ShapeDtypeStruct((24, 128), F32),) * 2,
        in_specs=[SMEM, VMEM],
        out_specs=(VMEM,) * 2,
        compiler_params=PARAMS,
    )(place, got)


def digits_of(v):
    place = lax.broadcasted_iota(jnp.int32, (16, 128), 0)
    out = jnp.zeros((16, 128), F32)
    for i in range(DIGITS):
        unit = 16.0 ** (7 - i)
        d = jnp.floor(v * (1.0 / unit) + 0.5)
        v = v - d * unit
        out = jnp.where(place == i, d, out)
    return out


def value_of(digits):
    place = lax.broadcasted_iota(jnp.int32, (16, 128), 0)
    units = jnp.zeros((16, 128), F32)
    for i in range(DIGITS):
        units = jnp.where(place == i, 16.0 ** (7 - i), units)
    return jnp.sum(digits * units, axis=0, keepdims=True)


def half_weights(where, logits, at, row_wide, col_lines, weights):
    cols = col_ids(where)
    for a in range(4):
        ids = row_ids(where, a)
        for b in range(4):
            rows = slice(a * CHUNK + b * ROWS, a * CHUNK + (b + 1) * ROWS)
            wide = row_wide[rows, :]
            for t in range(4):
                tile = logits[rows, (at + t) * 128 : (at + t + 1) * 128]
                both = jnp.exp2(tile - wide) + jnp.exp2(tile - col_lines[at + t : at + t + 1, :])
                both = both - jnp.where(ids[b] == cols[at + t][0:1], 1.0, 0.0)
                weights[rows, t * 128 : (t + 1) * 128] = both.astype(BF16)


def high_body(place, scale, logits, mine, other, images, *refs):
    weights, outs, digits, row_wide, col_lines = refs[0], refs[1:4], refs[4], refs[5], refs[6]
    row_lse, col_lse = refs[7:]
    where = [place[i] for i in range(5)]
    first = place[1] == 0
    shares = jnp.where(first, mine[16:17, :], other[16:17, :]), jnp.where(first, other[16:17, :], mine[16:17, :])
    for i, share in enumerate(shares):
        tail = digits_of(share).astype(BF16)
        for e in range(EMBED // 128):
            digits[i * TAIL : (i + 1) * TAIL, e * 128 : (e + 1) * 128] = tail
    row_lse[...] = jnp.where(first, mine[:16, :], other[:16, :]) + 1.0
    col_lse[...] = jnp.where(first, other[:16, :], mine[:16, :]) + 1.0
    lane = lax.broadcasted_iota(jnp.int32, (1, 128), 1)
    for t in range(8):
        j, i = t // 2, (t % 2) * 2
        lo = col_lse[pl.ds(col_place(where, j, i)[0], 1), :]
        hi = col_lse[pl.ds(col_place(where, j, i + 1)[0], 1), :]
        col_lines[t : t + 1, :] = jnp.where(lane < ROWS, lo, pltpu.roll(hi, 64, 1))
        lo = row_lse[pl.ds(row_place(where, j, i)[0], 1), :]
        hi = row_lse[pl.ds(row_place(where, j, i + 1)[0], 1), :]
        line = jnp.where(lane < ROWS, lo, pltpu.roll(hi, 64, 1))
        row_wide[t * 128 : (t + 1) * 128, :] = jnp.transpose(jnp.broadcast_to(line, (128, 128)))
    half_weights(where, logits, 4, row_wide, col_lines, weights)
    text_terms(scale[0], weights, images, 0, outs)


def high_call(place, scale, logits, mine, other, images):
    return pl.pallas_call(
        high_body,
        out_shape=(
            HALF_WEIGHTS,
            PART,
            jax.ShapeDtypeStruct((3 * ROWS, EMBED), BF16),
            jax.ShapeDtypeStruct((ROWS, EMBED), BF16),
            jax.ShapeDtypeStruct((2 * TAIL, EMBED), BF16),
            jax.ShapeDtypeStruct((BLOCK, 128), F32),
            jax.ShapeDtypeStruct((8, 128), F32),
        ),
        in_specs=[SMEM, SMEM] + [VMEM] * 4,
        out_specs=(VMEM,) * 7,
        scratch_shapes=[pltpu.VMEM((16, 128), F32), pltpu.VMEM((16, 128), F32)],
        compiler_params=PARAMS,
    )(place, scale, logits, mine, other, images)


def low_body(place, scale, logits, row_wide, col_lines, images, weights, out):
    half_weights([place[i] for i in range(5)], logits, 0, row_wide, col_lines, weights)
    text_terms(scale[0], weights, images, CHUNK, [out])


def low_call(place, scale, logits, row_wide, col_lines, images):
    return pl.pallas_call(
        low_body,
        out_shape=(HALF_WEIGHTS, PART),
        in_specs=[SMEM, SMEM] + [VMEM] * 4,
        out_specs=(VMEM,) * 2,
        compiler_params=PARAMS,
    )(place, scale, logits, row_wide, col_lines, images)


def text_terms(multiplier, weights, images, at, outs):
    rows = sum(out.shape[0] for out in outs)
    for e in range(5):
        term = multiplier * lax.dot_general(
            weights[:, at : at + rows],
            images[:, e * 256 : (e + 1) * 256],
            (((0,), (0,)), ((), ())),
            preferred_element_type=F32,
        )
        skip = 0
        for out in outs:
            out[:, e * 256 : (e + 1) * 256] = term[skip : skip + out.shape[0]].astype(BF16)
            skip += out.shape[0]


def image_terms(multiplier, weights, texts, at, outs):
    for e in range(5):
        term = multiplier * sum(
            jnp.dot(
                half[at * CHUNK : (at + len(outs)) * CHUNK, :],
                texts[h * BLOCK // 2 : (h + 1) * BLOCK // 2, e * 256 : (e + 1) * 256],
                preferred_element_type=F32,
            )
            for h, half in enumerate(weights)
        )
        for i, out in enumerate(outs):
            out[:CHUNK, e * 256 : (e + 1) * 256] = term[i * CHUNK : (i + 1) * CHUNK].astype(BF16)


def image_body(scale, after, digits, low, high, texts, *outs):
    image_terms(scale[0], (low, high), texts, 1, outs)
    for out in outs:
        out[CHUNK:, :] = digits[TAIL:, :]


def image_call(scale, after, digits, weights, texts):
    return pl.pallas_call(
        image_body,
        out_shape=(jax.ShapeDtypeStruct((CHUNK + TAIL, EMBED), BF16),) * 3,
        in_specs=[SMEM] + [VMEM] * 5,
        out_specs=(VMEM,) * 3,
        compiler_params=PARAMS,
    )(scale, after, digits, *weights, texts)


def rest_body(scale, low, high, images, texts, text_out, image_out):
    text_terms(scale[0], low, images, 0, [text_out])
    image_terms(scale[0], (low, high), texts, 0, [image_out])


def rest_call(scale, weights, images, texts):
    return pl.pallas_call(
        rest_body,
        out_shape=(PART, PART),
        in_specs=[SMEM] + [VMEM] * 4,
        out_specs=(VMEM,) * 2,
        compiler_params=PARAMS,
    )(scale, *weights, images, texts)


def add_rows(refs, rows, terms, out, to):
    for at in range(0, rows, 16):
        total = None
        for i, skip in terms:
            v = refs[i][skip + at : skip + at + 16, :].astype(F32)
            total = v if total is None else total + v
        out[to + at : to + at + 16, :] = total.astype(out.dtype)


def sums_body(n, plan, *refs):
    for parts, out in zip(plan, refs[n:]):
        to = 0
        for rows, terms in parts:
            add_rows(refs, rows, terms, out, to)
            to += rows


def sums(arrays, *plan):
    return pl.pallas_call(
        lambda *refs: sums_body(len(arrays), plan, *refs),
        out_shape=tuple(
            jax.ShapeDtypeStruct((sum(rows for rows, _ in parts), EMBED), BF16) for parts in plan
        ),
        in_specs=[VMEM] * len(arrays),
        out_specs=(VMEM,) * len(plan),
        compiler_params=PARAMS,
    )(*arrays)


def last_body(*refs):
    digits, image_out, text_out, loss_out = refs[6:]
    add_rows(refs, ROWS, [(i, 0) for i in range(4)], image_out, 0)
    add_rows(refs, ROWS, [(4, 0), (5, 0)], text_out, 0)
    total = -digits[:TAIL, :128].astype(F32)
    for r in refs[:6]:
        total += r[ROWS : ROWS + TAIL, :128].astype(F32)
    loss_out[...] = value_of(total)[:, 0:1] * (LN2 / (2.0 * ROWS * 256))


def last_call(shards, texts, digits):
    grad = jax.ShapeDtypeStruct((ROWS, EMBED), BF16)
    return pl.pallas_call(
        last_body,
        out_shape=(grad, grad, jax.ShapeDtypeStruct((1, 1), F32)),
        in_specs=[VMEM] * 7,
        out_specs=(VMEM,) * 3,
        compiler_params=PARAMS,
    )(*shards, *texts, digits)


def local(image_emb, text_emb, logit_scale):
    place = jnp.stack([lax.axis_index(n) for n in AXES]).astype(jnp.int32)

    chip, image = pack([text_emb, core_swap(text_emb), image_emb], ((0, 64), (1, 64)), ((2, 64),))
    next_1, next_4 = z_shift(chip, -1), z_shift(text_emb, 4)
    near = [plane_shift(image, k, True) for k in (1, 2, 3)]
    own, text_0, side = pack(
        [image] + near + [chip, next_1, next_4],
        ((0, 64), (1, 64), (2, 64), (3, 64)),
        ((4, 128), (5, 128)),
        ((5, 128), (6, 64)),
    )
    text_1 = z_shift(text_0, -2)
    near = [own] + [plane_shift(own, k, False) for k in PLANE_ORDER[1:]]
    logits, row_part, col_part, message, matched, images, texts = logits_call(
        place, logit_scale, near, [text_0, text_1, core_swap(text_1), core_swap(side), next_4]
    )

    spread = spread_call(place, row_part, col_part, matched, core_swap(message))
    mine, message = join_call(place, exchange(spread, plane_or_ring()))
    high, text_2, text_3, far, digits, row_wide, col_lines = high_call(
        place, logit_scale, logits, mine, core_swap(message), images
    )

    other_1, other_3 = core_swap(text_2), core_swap(text_3)
    low, text_1 = low_call(place, logit_scale, logits, row_wide, col_lines, images)
    weights = low, high
    pairs = sums(
        [text_1, other_1, far, other_3, digits],
        ((256, ((0, 0), (1, 0))), (64, ((2, 0), (3, 128))), (TAIL, ((4, 0),))),
    )[0]
    image_parts = image_call(logit_scale, pairs, digits, weights, texts)
    pairs = z_shift(pairs, 2)
    back = [plane_shift(v, -k, False) for v, k in ((image_parts[k - 1], k) for k in (2, 1, 3))]
    text_0, image_0 = rest_call(logit_scale, weights, images, texts)

    rows_tail = (TAIL, ((2, 320), (3, 0)))
    next_1, mine, next_4 = sums(
        [text_0, other_3, pairs, digits],
        ((128, ((0, 128), (1, 0), (2, 128))), rows_tail),
        ((128, ((0, 0), (2, 0))), rows_tail),
        ((80, ((2, 256),)),),
    )
    next_1, next_4 = z_shift(next_1, 1), z_shift(next_4, 2)
    (other,) = sums([mine, next_1], ((64, ((0, 64), (1, 64))), (TAIL, ((0, 128), (1, 128)))))
    (mine,) = sums(
        [mine, next_1, next_4], ((64, ((0, 0), (1, 0), (2, 0))), (TAIL, ((0, 128), (1, 128), (2, 64))))
    )

    cols_tail = (TAIL, ((1, 256), (2, 256), (3, 256), (4, 16)))
    pieces = sums(
        [image_0] + back + [digits],
        *[((64, [(i, 64 * k) for i in range(4)]), cols_tail) for k in range(4)],
    )
    shards = [pieces[0]] + [plane_shift(pieces[k], -k, True) for k in (2, 1, 3)]
    image_grad, text_grad, mean_loss = last_call(shards, [mine, core_swap(other)], digits)
    return mean_loss.reshape(1), image_grad, text_grad


def solution(mesh):
    fine = Mesh(mesh.devices.reshape(4, 2, 2, 4, 4), AXES)
    return jax.shard_map(
        local,
        mesh=fine,
        in_specs=(P(AXES, None), P(("zh", "y", "x", "zl", "core"), None), P()),
        out_specs=(P(), P(AXES, None), P(("zh", "y", "x", "zl", "core"), None)),
        check_vma=False,
    )
```

```python
import math

import jax
import jax.numpy as jnp
from jax import lax
from jax.experimental import pallas as pl
from jax.experimental.pallas import tpu as pltpu
from jax.sharding import Mesh, PartitionSpec as P

AXES = ("zl", "core", "zh", "y", "x")
NX, NY, NZ = 4, 4, 8
ROWS, EMBED = 64, 1280
CHUNK = 4 * ROWS
TAIL, DIGITS = 16, 13
BLOCK = 16 * ROWS
BF16, F32 = jnp.bfloat16, jnp.float32
LOG2E, LN2 = math.log2(math.e), math.log(2.0)
VMEM = pl.BlockSpec(memory_space=pltpu.VMEM)
SMEM = pl.BlockSpec(memory_space=pltpu.SMEM)
PARAMS = pltpu.CompilerParams(vmem_limit_bytes=12 * 1024 * 1024)


def plane_shift(v, k, primary):
    pairs = []
    for c in range(2):
        for h in range(2):
            for y in range(NY):
                for x in range(NX):
                    if (c == 0) == primary:
                        to = (y, (x + k) % NX)
                    else:
                        to = ((y + k) % NY, x)
                    base = (c * 2 + h) * NY
                    pairs.append(((base + y) * NX + x, (base + to[0]) * NX + to[1]))
    return lax.ppermute(v, ("core", "zh", "y", "x"), pairs)


def z_shift(v, k):
    pairs = []
    for c in range(2):
        for z in range(NZ):
            to = (z + (k if c == 0 else -k)) % NZ
            pairs.append((((z % 4) * 2 + c) * 2 + z // 4, ((to % 4) * 2 + c) * 2 + to // 4))
    return lax.ppermute(v, ("zl", "core", "zh"), pairs)


def core_swap(v):
    return lax.ppermute(v, "core", [(0, 1), (1, 0)])


def device(c, y, x, z):
    return ((((z % 4) * 2 + c) * 2 + z // 4) * NY + y) * NX + x


def plane_or_ring():
    out = [[device(0, y, x, z) for y in range(NY) for x in range(NX)] for z in range(NZ)]
    return out + [
        [device(1, y + d, x, z) for z in range(NZ) for d in (0, 1)] for y in (0, 2) for x in range(NX)
    ]


def exchange(v, groups):
    return lax.all_to_all(v, AXES, 0, 0, axis_index_groups=groups)


def row_place(where, a, b):
    zl, c, zh, y, x = where
    p, s = jnp.where(c == 0, b, a), jnp.where(c == 0, a, b)
    n = ((y - s) & 3) * 4 + ((x - p) & 3)
    return n, ((zl * 2 + c) * 2 + zh) * 16 + n


def col_place(where, j, i):
    zl, c, zh, y, x = where
    core = c if (i % 2 == 0) == (j < 2) else 1 - c
    sign = 1 - 2 * c
    off = ((0, 0, 1, 1), (2, 2, 3, 3), (-2, -2, -3, -3), (-1, -1, 4, 4))[j][i]
    off = 4 if off == 4 else sign * off
    z = (zh * 4 + zl + off) & 7
    return z * 2 + core, ((z >> 2) * 16 + y * 4 + x) * 8 + (z & 3) * 2 + core


def row_ids(where, a):
    span = lax.broadcasted_iota(jnp.int32, (ROWS, 128), 0)
    return [row_place(where, a, b)[1] * ROWS + span for b in range(4)]


def col_ids(where):
    lane = lax.broadcasted_iota(jnp.int32, (8, 128), 1)
    out = []
    for t in range(8):
        lo = col_place(where, t // 2, (t % 2) * 2)[1] * ROWS
        hi = col_place(where, t // 2, (t % 2) * 2 + 1)[1] * ROWS - ROWS
        out.append(lane + jnp.where(lane < ROWS, lo, hi))
    return out


PLANE_ORDER = (0, 1, 3, 2)
PART = jax.ShapeDtypeStruct((CHUNK, EMBED), BF16)
ALL = jax.ShapeDtypeStruct((BLOCK, EMBED), BF16)
HALF_WEIGHTS = jax.ShapeDtypeStruct((BLOCK, BLOCK // 2), BF16)


def pack_body(plan, n, *refs):
    for parts, out in zip(plan, refs[n:]):
        row = 0
        for i, rows in parts:
            out[row : row + rows, :] = refs[i][...]
            row += rows


def pack(arrays, *plan):
    shapes = [jax.ShapeDtypeStruct((sum(p[1] for p in parts), EMBED), BF16) for parts in plan]
    return pl.pallas_call(
        lambda *refs: pack_body(plan, len(arrays), *refs),
        out_shape=tuple(shapes),
        in_specs=[VMEM] * len(arrays),
        out_specs=(VMEM,) * len(plan),
        compiler_params=PARAMS,
    )(*arrays)


def fold(v):
    return v.reshape(v.shape[0] // 8, 8, 128)


def two_sums(v):
    coarse = 8.0 * jnp.floor(v * 0.125 + 0.5)
    parts = [jnp.sum(p, keepdims=True) for p in (coarse, v - coarse)]
    return jnp.where(lax.broadcasted_iota(jnp.int32, (8, 128), 0) < 4, *parts)


def column_part(logits, t, top):
    top = jnp.max(top, axis=0, keepdims=True)

    def step(i, total):
        tile = logits[pl.ds(pl.multiple_of(i * 128, 128), 128), t * 128 : (t + 1) * 128]
        return total + jnp.sum(fold(jnp.exp2(tile - top)), axis=0)

    total = lax.fori_loop(0, 8, step, jnp.zeros((8, 128), F32), unroll=True)
    return top + LOG2E * jnp.log(jnp.sum(total, axis=0, keepdims=True))


def logits_body(place, scale, *refs):
    images, texts = [refs[i] for i in PLANE_ORDER], refs[4:7]
    logits, row_out, col_out, message, match_out, all_images, all_texts = refs[9:16]
    row_wide = refs[16]
    all_texts[3 * CHUNK : BLOCK - ROWS, :] = refs[7][...]
    all_texts[BLOCK - ROWS :, :] = refs[8][...]
    where = [place[i] for i in range(5)]
    multiplier = scale[0] * LOG2E
    for j in range(3):
        all_texts[j * CHUNK : (j + 1) * CHUNK, :] = texts[j][...]

    def chunk_logits(a):
        all_images[a * CHUNK : (a + 1) * CHUNK, :] = images[a][...]
        for j in range(4):
            text = texts[j][...] if j < 3 else all_texts[3 * CHUNK :, :]
            logits[a * CHUNK : (a + 1) * CHUNK, j * CHUNK : (j + 1) * CHUNK] = multiplier * lax.dot_general(
                images[a][...], text, (((1,), (1,)), ((), ())), preferred_element_type=F32
            )

    chunk_logits(0)
    cols = col_ids(where)
    step = 32
    matched = jnp.zeros((8, 128), F32)
    col_top = [jnp.full((8, 128), -jnp.inf, F32) for _ in range(8)]
    for a in range(4):
        if a < 3:
            chunk_logits(a + 1)
        ids = row_ids(where, a)
        for b in range(4):
            for half in range(ROWS // step):
                at = a * CHUNK + b * ROWS + half * step
                tiles = [logits[at : at + step, t * 128 : (t + 1) * 128] for t in range(8)]
                top = tiles[0]
                for t in range(1, 8):
                    top = jnp.maximum(top, tiles[t])
                top = jnp.max(top, axis=1, keepdims=True)
                mine = ids[b][half * step : (half + 1) * step]
                total = jnp.zeros((step, 128), F32)
                for t in range(8):
                    total += jnp.exp2(tiles[t] - top)
                    col_top[t] = jnp.maximum(col_top[t], jnp.max(fold(tiles[t]), axis=0))
                    hit = jnp.where(mine == cols[t][0:1], tiles[t], 0.0)
                    matched += jnp.sum(fold(hit), axis=0)
                part = top + LOG2E * jnp.log(jnp.sum(total, axis=1, keepdims=True))
                row_wide[at : at + step, :] = jnp.broadcast_to(part, (step, 128))
    matched = two_sums(matched)
    match_out[...] = matched
    message[16:24, :] = matched
    for t in range(8):
        part = column_part(logits, t, col_top[t])
        j, i = t // 2, (t % 2) * 2
        col_out[pl.ds(col_place(where, j, i)[0], 1), :] = part
        col_out[pl.ds(col_place(where, j, i + 1)[0], 1), :] = pltpu.roll(part, 64, 1)
        line = jnp.transpose(row_wide[t * 128 : (t + 1) * 128, :])[0:1]
        row_out[pl.ds(row_place(where, j, i)[0], 1), :] = line
        row_out[pl.ds(row_place(where, j, i + 1)[0], 1), :] = pltpu.roll(line, 64, 1)
    message[:16, :] = jnp.where(where[1] == 0, col_out[...], row_out[...])


def logits_call(place, scale, images, texts):
    return pl.pallas_call(
        logits_body,
        out_shape=(
            jax.ShapeDtypeStruct((BLOCK, BLOCK), F32),
            jax.ShapeDtypeStruct((16, 128), F32),
            jax.ShapeDtypeStruct((16, 128), F32),
            jax.ShapeDtypeStruct((24, 128), F32),
            jax.ShapeDtypeStruct((8, 128), F32),
            ALL,
            ALL,
        ),
        in_specs=[SMEM, SMEM] + [VMEM] * 9,
        out_specs=(VMEM,) * 7,
        scratch_shapes=[pltpu.VMEM((BLOCK, 128), F32)],
        compiler_params=PARAMS,
    )(place, scale, *images, *texts)


def pair_up(rows):
    low = lax.broadcasted_iota(jnp.int32, (1, 128), 1) < ROWS
    pairs = [
        jnp.where(low, rows[i : i + 1], pltpu.roll(rows[i + 1 : i + 2], 64, 1))
        for i in range(0, rows.shape[0], 2)
    ]
    return jnp.concatenate(pairs)


def spread_body(place, row, col, matched, got, out):
    first = place[1] == 0
    mine, other = row[...], got[:16, :]
    top = jnp.maximum(col[...], other)
    both = top + LOG2E * jnp.log(jnp.exp2(col[...] - top) + jnp.exp2(other - top))
    low = pair_up(jnp.where(first, mine, both))
    high = pair_up(other)
    hits = matched[...] + got[16:24, :]
    for i in range(16):
        out[i, :8, :] = low
        out[i, 8:16, :] = high
        out[i, 16:24, :] = hits


def spread_call(place, *parts):
    return pl.pallas_call(
        spread_body,
        out_shape=jax.ShapeDtypeStruct((16, 24, 128), F32),
        in_specs=[SMEM] + [VMEM] * 4,
        out_specs=VMEM,
        compiler_params=PARAMS,
    )(place, *parts)


def join_body(place, got, mine, message):
    first = place[1] == 0
    counts = [jnp.logical_or(first, (place[3] & 1) == i % 2) for i in range(16)]
    parts = [jnp.where(counts[i], got[i, :16, :], -jnp.inf) for i in range(16)]
    top = parts[0]
    for p in parts[1:]:
        top = jnp.maximum(top, p)
    total = jnp.exp2(parts[0] - top)
    for p in parts[1:]:
        total += jnp.exp2(p - top)
    state = top + LOG2E * jnp.log(total)
    low, high = state[:8], state[8:]
    hits = got[0, 16:24, :]
    for i in range(1, 16):
        hits += got[i, 16:24, :]
    share = two_sums(low) + jnp.where(first, two_sums(high) - 2.0 * hits, 0.0)
    for out, pairs in ((mine, low), (message, jnp.where(first, high, low))):
        for i in range(8):
            out[2 * i : 2 * i + 1, :] = pairs[i : i + 1]
            out[2 * i + 1 : 2 * i + 2, :] = pltpu.roll(pairs[i : i + 1], 64, 1)
        out[16:24, :] = share


def join_call(place, got):
    return pl.pallas_call(
        join_body,
        out_shape=(jax.ShapeDtypeStruct((24, 128), F32),) * 2,
        in_specs=[SMEM, VMEM],
        out_specs=(VMEM,) * 2,
        compiler_params=PARAMS,
    )(place, got)


def digits_of(v):
    place = lax.broadcasted_iota(jnp.int32, (16, 128), 0)
    out = jnp.zeros((16, 128), F32)
    for i in range(DIGITS):
        unit = 16.0 ** (7 - i)
        d = jnp.floor(v * (1.0 / unit) + 0.5)
        v = v - d * unit
        out = jnp.where(place == i, d, out)
    return out


def value_of(digits):
    total = digits[0:1] * 16.0**7
    for i in range(1, DIGITS):
        total = total + digits[i : i + 1] * 16.0 ** (7 - i)
    return total


def half_weights(where, logits, at, row_wide, col_lines, weights):
    cols = col_ids(where)
    for a in range(4):
        ids = row_ids(where, a)
        for b in range(4):
            rows = slice(a * CHUNK + b * ROWS, a * CHUNK + (b + 1) * ROWS)
            wide = row_wide[rows, :]
            for t in range(4):
                tile = logits[rows, (at + t) * 128 : (at + t + 1) * 128]
                both = jnp.exp2(tile - wide) + jnp.exp2(tile - col_lines[at + t : at + t + 1, :])
                both = both - jnp.where(ids[b] == cols[at + t][0:1], 1.0, 0.0)
                weights[rows, t * 128 : (t + 1) * 128] = both.astype(BF16)


def high_body(place, scale, logits, mine, other, images, *refs):
    weights, outs, digits, row_wide, col_lines = refs[0], refs[1:4], refs[4], refs[5], refs[6]
    row_lse, col_lse = refs[7:]
    where = [place[i] for i in range(5)]
    first = place[1] == 0
    for i, own in enumerate((first, jnp.logical_not(first))):
        tail = sum(
            digits_of(jnp.where(own, mine[r : r + 1, :], other[r : r + 1, :])) for r in (16, 20)
        ).astype(BF16)
        for e in range(EMBED // 128):
            digits[i * TAIL : (i + 1) * TAIL, e * 128 : (e + 1) * 128] = tail
    row_lse[...] = jnp.where(first, mine[:16, :], other[:16, :]) + 1.0
    col_lse[...] = jnp.where(first, other[:16, :], mine[:16, :]) + 1.0
    lane = lax.broadcasted_iota(jnp.int32, (1, 128), 1)
    for t in range(8):
        j, i = t // 2, (t % 2) * 2
        lo = col_lse[pl.ds(col_place(where, j, i)[0], 1), :]
        hi = col_lse[pl.ds(col_place(where, j, i + 1)[0], 1), :]
        col_lines[t : t + 1, :] = jnp.where(lane < ROWS, lo, pltpu.roll(hi, 64, 1))
        lo = row_lse[pl.ds(row_place(where, j, i)[0], 1), :]
        hi = row_lse[pl.ds(row_place(where, j, i + 1)[0], 1), :]
        line = jnp.where(lane < ROWS, lo, pltpu.roll(hi, 64, 1))
        row_wide[t * 128 : (t + 1) * 128, :] = jnp.transpose(jnp.broadcast_to(line, (128, 128)))
    half_weights(where, logits, 4, row_wide, col_lines, weights)
    text_terms(scale[0], weights, images, 0, outs)


def high_call(place, scale, logits, mine, other, images):
    return pl.pallas_call(
        high_body,
        out_shape=(
            HALF_WEIGHTS,
            PART,
            jax.ShapeDtypeStruct((3 * ROWS, EMBED), BF16),
            jax.ShapeDtypeStruct((ROWS, EMBED), BF16),
            jax.ShapeDtypeStruct((2 * TAIL, EMBED), BF16),
            jax.ShapeDtypeStruct((BLOCK, 128), F32),
            jax.ShapeDtypeStruct((8, 128), F32),
        ),
        in_specs=[SMEM, SMEM] + [VMEM] * 4,
        out_specs=(VMEM,) * 7,
        scratch_shapes=[pltpu.VMEM((16, 128), F32), pltpu.VMEM((16, 128), F32)],
        compiler_params=PARAMS,
    )(place, scale, logits, mine, other, images)


def low_body(place, scale, logits, row_wide, col_lines, images, weights, out):
    half_weights([place[i] for i in range(5)], logits, 0, row_wide, col_lines, weights)
    text_terms(scale[0], weights, images, CHUNK, [out])


def low_call(place, scale, logits, row_wide, col_lines, images):
    return pl.pallas_call(
        low_body,
        out_shape=(HALF_WEIGHTS, PART),
        in_specs=[SMEM, SMEM] + [VMEM] * 4,
        out_specs=(VMEM,) * 2,
        compiler_params=PARAMS,
    )(place, scale, logits, row_wide, col_lines, images)


def text_terms(multiplier, weights, images, at, outs):
    rows = sum(out.shape[0] for out in outs)
    for e in range(5):
        term = multiplier * lax.dot_general(
            weights[:, at : at + rows],
            images[:, e * 256 : (e + 1) * 256],
            (((0,), (0,)), ((), ())),
            preferred_element_type=F32,
        )
        skip = 0
        for out in outs:
            out[:, e * 256 : (e + 1) * 256] = term[skip : skip + out.shape[0]].astype(BF16)
            skip += out.shape[0]


def image_terms(multiplier, weights, texts, at, outs):
    for e in range(5):
        term = multiplier * sum(
            jnp.dot(
                half[at * CHUNK : (at + len(outs)) * CHUNK, :],
                texts[h * BLOCK // 2 : (h + 1) * BLOCK // 2, e * 256 : (e + 1) * 256],
                preferred_element_type=F32,
            )
            for h, half in enumerate(weights)
        )
        for i, out in enumerate(outs):
            out[:CHUNK, e * 256 : (e + 1) * 256] = term[i * CHUNK : (i + 1) * CHUNK].astype(BF16)


def image_body(scale, after, digits, low, high, texts, *outs):
    image_terms(scale[0], (low, high), texts, 1, outs)
    for out in outs:
        out[CHUNK:, :] = digits[TAIL:, :]


def image_call(scale, after, digits, weights, texts):
    return pl.pallas_call(
        image_body,
        out_shape=(jax.ShapeDtypeStruct((CHUNK + TAIL, EMBED), BF16),) * 3,
        in_specs=[SMEM] + [VMEM] * 5,
        out_specs=(VMEM,) * 3,
        compiler_params=PARAMS,
    )(scale, after, digits, *weights, texts)


def rest_body(scale, low, high, images, texts, text_out, image_out):
    text_terms(scale[0], low, images, 0, [text_out])
    image_terms(scale[0], (low, high), texts, 0, [image_out])


def rest_call(scale, weights, images, texts):
    return pl.pallas_call(
        rest_body,
        out_shape=(PART, PART),
        in_specs=[SMEM] + [VMEM] * 4,
        out_specs=(VMEM,) * 2,
        compiler_params=PARAMS,
    )(scale, *weights, images, texts)


def add_rows(refs, rows, terms, out, to):
    for at in range(0, rows, 16):
        total = None
        for i, skip in terms:
            v = refs[i][skip + at : skip + at + 16, :].astype(F32)
            total = v if total is None else total + v
        out[to + at : to + at + 16, :] = total.astype(out.dtype)


def sums_body(n, plan, *refs):
    for parts, out in zip(plan, refs[n:]):
        to = 0
        for rows, terms in parts:
            add_rows(refs, rows, terms, out, to)
            to += rows


def sums(arrays, *plan):
    return pl.pallas_call(
        lambda *refs: sums_body(len(arrays), plan, *refs),
        out_shape=tuple(
            jax.ShapeDtypeStruct((sum(rows for rows, _ in parts), EMBED), BF16) for parts in plan
        ),
        in_specs=[VMEM] * len(arrays),
        out_specs=(VMEM,) * len(plan),
        compiler_params=PARAMS,
    )(*arrays)


def last_body(*refs):
    digits, image_out, text_out, loss_out = refs[6:]
    add_rows(refs, ROWS, [(i, 0) for i in range(4)], image_out, 0)
    add_rows(refs, ROWS, [(4, 0), (5, 0)], text_out, 0)
    total = -digits[:TAIL, :128].astype(F32)
    for r in refs[:6]:
        total += r[ROWS : ROWS + TAIL, :128].astype(F32)
    loss_out[...] = value_of(total)[:, 0:1] * (LN2 / (2.0 * ROWS * 256))


def last_call(shards, texts, digits):
    grad = jax.ShapeDtypeStruct((ROWS, EMBED), BF16)
    return pl.pallas_call(
        last_body,
        out_shape=(grad, grad, jax.ShapeDtypeStruct((1, 1), F32)),
        in_specs=[VMEM] * 7,
        out_specs=(VMEM,) * 3,
        compiler_params=PARAMS,
    )(*shards, *texts, digits)


def local(image_emb, text_emb, logit_scale):
    place = jnp.stack([lax.axis_index(n) for n in AXES]).astype(jnp.int32)

    chip, image = pack([text_emb, core_swap(text_emb), image_emb], ((0, 64), (1, 64)), ((2, 64),))
    next_1, next_4 = z_shift(chip, -1), z_shift(text_emb, 4)
    near = [plane_shift(image, k, True) for k in (1, 2, 3)]
    own, text_0, side = pack(
        [image] + near + [chip, next_1, next_4],
        ((0, 64), (1, 64), (2, 64), (3, 64)),
        ((4, 128), (5, 128)),
        ((5, 128), (6, 64)),
    )
    text_1 = z_shift(text_0, -2)
    near = [own] + [plane_shift(own, k, False) for k in PLANE_ORDER[1:]]
    logits, row_part, col_part, message, matched, images, texts = logits_call(
        place, logit_scale, near, [text_0, text_1, core_swap(text_1), core_swap(side), next_4]
    )

    spread = spread_call(place, row_part, col_part, matched, core_swap(message))
    mine, message = join_call(place, exchange(spread, plane_or_ring()))
    high, text_2, text_3, far, digits, row_wide, col_lines = high_call(
        place, logit_scale, logits, mine, core_swap(message), images
    )

    other_1, other_3 = core_swap(text_2), core_swap(text_3)
    low, text_1 = low_call(place, logit_scale, logits, row_wide, col_lines, images)
    weights = low, high
    pairs = sums(
        [text_1, other_1, far, other_3, digits],
        ((256, ((0, 0), (1, 0))), (64, ((2, 0), (3, 128))), (TAIL, ((4, 0),))),
    )[0]
    image_parts = image_call(logit_scale, pairs, digits, weights, texts)
    pairs = z_shift(pairs, 2)
    back = [plane_shift(v, -k, False) for v, k in ((image_parts[k - 1], k) for k in (2, 1, 3))]
    text_0, image_0 = rest_call(logit_scale, weights, images, texts)

    rows_tail = (TAIL, ((2, 320), (3, 0)))
    next_1, mine, next_4 = sums(
        [text_0, other_3, pairs, digits],
        ((128, ((0, 128), (1, 0), (2, 128))), rows_tail),
        ((128, ((0, 0), (2, 0))), rows_tail),
        ((80, ((2, 256),)),),
    )
    next_1, next_4 = z_shift(next_1, 1), z_shift(next_4, 2)
    (other,) = sums([mine, next_1], ((64, ((0, 64), (1, 64))), (TAIL, ((0, 128), (1, 128)))))
    (mine,) = sums(
        [mine, next_1, next_4], ((64, ((0, 0), (1, 0), (2, 0))), (TAIL, ((0, 128), (1, 128), (2, 64))))
    )

    cols_tail = (TAIL, ((1, 256), (2, 256), (3, 256), (4, 16)))
    pieces = sums(
        [image_0] + back + [digits],
        *[((64, [(i, 64 * k) for i in range(4)]), cols_tail) for k in range(4)],
    )
    shards = [pieces[0]] + [plane_shift(pieces[k], -k, True) for k in (2, 1, 3)]
    image_grad, text_grad, mean_loss = last_call(shards, [mine, core_swap(other)], digits)
    return mean_loss.reshape(1), image_grad, text_grad


def solution(mesh):
    fine = Mesh(mesh.devices.reshape(4, 2, 2, 4, 4), AXES)
    return jax.shard_map(
        local,
        mesh=fine,
        in_specs=(P(AXES, None), P(("zh", "y", "x", "zl", "core"), None), P()),
        out_specs=(P(), P(AXES, None), P(("zh", "y", "x", "zl", "core"), None)),
        check_vma=False,
    )
```

```python
import math

import jax
import jax.numpy as jnp
from jax import lax
from jax.experimental import pallas as pl
from jax.experimental.pallas import tpu as pltpu
from jax.sharding import Mesh, PartitionSpec as P

AXES = ("zl", "core", "zh", "y", "x")
NX, NY, NZ = 4, 4, 8
ROWS, EMBED = 64, 1280
CHUNK = 4 * ROWS
TAIL, DIGITS = 16, 13
BLOCK = 16 * ROWS
BF16, F32 = jnp.bfloat16, jnp.float32
LOG2E, LN2 = math.log2(math.e), math.log(2.0)
VMEM = pl.BlockSpec(memory_space=pltpu.VMEM)
SMEM = pl.BlockSpec(memory_space=pltpu.SMEM)
PARAMS = pltpu.CompilerParams(vmem_limit_bytes=12 * 1024 * 1024)


def plane_shift(v, k, primary):
    pairs = []
    for c in range(2):
        for h in range(2):
            for y in range(NY):
                for x in range(NX):
                    if (c == 0) == primary:
                        to = (y, (x + k) % NX)
                    else:
                        to = ((y + k) % NY, x)
                    base = (c * 2 + h) * NY
                    pairs.append(((base + y) * NX + x, (base + to[0]) * NX + to[1]))
    return lax.ppermute(v, ("core", "zh", "y", "x"), pairs)


def z_shift(v, k):
    pairs = []
    for c in range(2):
        for z in range(NZ):
            to = (z + (k if c == 0 else -k)) % NZ
            pairs.append((((z % 4) * 2 + c) * 2 + z // 4, ((to % 4) * 2 + c) * 2 + to // 4))
    return lax.ppermute(v, ("zl", "core", "zh"), pairs)


def core_swap(v):
    return lax.ppermute(v, "core", [(0, 1), (1, 0)])


def device(c, y, x, z):
    return ((((z % 4) * 2 + c) * 2 + z // 4) * NY + y) * NX + x


def plane_or_ring():
    out = [[device(0, y, x, z) for y in range(NY) for x in range(NX)] for z in range(NZ)]
    return out + [
        [device(1, y + d, x, z) for z in range(NZ) for d in (0, 1)] for y in (0, 2) for x in range(NX)
    ]


def exchange(v, groups):
    return lax.all_to_all(v, AXES, 0, 0, axis_index_groups=groups)


def row_place(where, a, b):
    zl, c, zh, y, x = where
    p, s = jnp.where(c == 0, b, a), jnp.where(c == 0, a, b)
    n = ((y - s) & 3) * 4 + ((x - p) & 3)
    return n, ((zl * 2 + c) * 2 + zh) * 16 + n


def col_place(where, j, i):
    zl, c, zh, y, x = where
    core = c if (i % 2 == 0) == (j < 2) else 1 - c
    sign = 1 - 2 * c
    off = ((0, 0, 1, 1), (2, 2, 3, 3), (-2, -2, -3, -3), (-1, -1, 4, 4))[j][i]
    off = 4 if off == 4 else sign * off
    z = (zh * 4 + zl + off) & 7
    return z * 2 + core, ((z >> 2) * 16 + y * 4 + x) * 8 + (z & 3) * 2 + core


def row_ids(where, a):
    span = lax.broadcasted_iota(jnp.int32, (ROWS, 128), 0)
    return [row_place(where, a, b)[1] * ROWS + span for b in range(4)]


def col_ids(where):
    lane = lax.broadcasted_iota(jnp.int32, (8, 128), 1)
    out = []
    for t in range(8):
        lo = col_place(where, t // 2, (t % 2) * 2)[1] * ROWS
        hi = col_place(where, t // 2, (t % 2) * 2 + 1)[1] * ROWS - ROWS
        out.append(lane + jnp.where(lane < ROWS, lo, hi))
    return out


PLANE_ORDER = (0, 1, 3, 2)
PART = jax.ShapeDtypeStruct((CHUNK, EMBED), BF16)
ALL = jax.ShapeDtypeStruct((BLOCK, EMBED), BF16)
HALF_WEIGHTS = jax.ShapeDtypeStruct((BLOCK, BLOCK // 2), BF16)


def pack_body(plan, n, *refs):
    for parts, out in zip(plan, refs[n:]):
        row = 0
        for i, rows in parts:
            out[row : row + rows, :] = refs[i][...]
            row += rows


def pack(arrays, *plan):
    shapes = [jax.ShapeDtypeStruct((sum(p[1] for p in parts), EMBED), BF16) for parts in plan]
    return pl.pallas_call(
        lambda *refs: pack_body(plan, len(arrays), *refs),
        out_shape=tuple(shapes),
        in_specs=[VMEM] * len(arrays),
        out_specs=(VMEM,) * len(plan),
        compiler_params=PARAMS,
    )(*arrays)


def fold(v):
    return v.reshape(v.shape[0] // 8, 8, 128)


def two_sums(v):
    coarse = 8.0 * jnp.floor(v * 0.125 + 0.5)
    parts = [jnp.sum(p, keepdims=True) for p in (coarse, v - coarse)]
    return jnp.where(lax.broadcasted_iota(jnp.int32, (8, 128), 0) < 4, *parts)


def column_part(logits, t, top):
    top = jnp.max(top, axis=0, keepdims=True)

    def step(i, total):
        tile = logits[pl.ds(pl.multiple_of(i * 128, 128), 128), t * 128 : (t + 1) * 128]
        return total + jnp.sum(fold(jnp.exp2(tile - top)), axis=0)

    total = lax.fori_loop(0, 8, step, jnp.zeros((8, 128), F32), unroll=True)
    return top + LOG2E * jnp.log(jnp.sum(total, axis=0, keepdims=True))


def logits_body(place, scale, *refs):
    images, texts = [refs[i] for i in PLANE_ORDER], refs[4:7]
    logits, row_out, col_out, message, match_out, all_images, all_texts = refs[9:16]
    row_wide = refs[16]
    all_texts[3 * CHUNK : BLOCK - ROWS, :] = refs[7][...]
    all_texts[BLOCK - ROWS :, :] = refs[8][...]
    where = [place[i] for i in range(5)]
    multiplier = scale[0] * LOG2E
    for j in range(3):
        all_texts[j * CHUNK : (j + 1) * CHUNK, :] = texts[j][...]

    def chunk_logits(a):
        all_images[a * CHUNK : (a + 1) * CHUNK, :] = images[a][...]
        for j in range(4):
            text = texts[j][...] if j < 3 else all_texts[3 * CHUNK :, :]
            logits[a * CHUNK : (a + 1) * CHUNK, j * CHUNK : (j + 1) * CHUNK] = multiplier * lax.dot_general(
                images[a][...], text, (((1,), (1,)), ((), ())), preferred_element_type=F32
            )

    chunk_logits(0)
    cols = col_ids(where)
    step = 32
    matched = jnp.zeros((8, 128), F32)
    col_top = [jnp.full((8, 128), -jnp.inf, F32) for _ in range(8)]
    for a in range(4):
        if a < 3:
            chunk_logits(a + 1)
        ids = row_ids(where, a)
        for b in range(4):
            for half in range(ROWS // step):
                at = a * CHUNK + b * ROWS + half * step
                tiles = [logits[at : at + step, t * 128 : (t + 1) * 128] for t in range(8)]
                top = tiles[0]
                for t in range(1, 8):
                    top = jnp.maximum(top, tiles[t])
                top = jnp.max(top, axis=1, keepdims=True)
                mine = ids[b][half * step : (half + 1) * step]
                total = jnp.zeros((step, 128), F32)
                for t in range(8):
                    total += jnp.exp2(tiles[t] - top)
                    col_top[t] = jnp.maximum(col_top[t], jnp.max(fold(tiles[t]), axis=0))
                    hit = jnp.where(mine == cols[t][0:1], tiles[t], 0.0)
                    matched += jnp.sum(fold(hit), axis=0)
                part = top + LOG2E * jnp.log(jnp.sum(total, axis=1, keepdims=True))
                row_wide[at : at + step, :] = jnp.broadcast_to(part, (step, 128))
    matched = two_sums(matched)
    match_out[...] = matched
    message[16:24, :] = matched
    for t in range(8):
        part = column_part(logits, t, col_top[t])
        j, i = t // 2, (t % 2) * 2
        col_out[pl.ds(col_place(where, j, i)[0], 1), :] = part
        col_out[pl.ds(col_place(where, j, i + 1)[0], 1), :] = pltpu.roll(part, 64, 1)
        line = jnp.transpose(row_wide[t * 128 : (t + 1) * 128, :])[0:1]
        row_out[pl.ds(row_place(where, j, i)[0], 1), :] = line
        row_out[pl.ds(row_place(where, j, i + 1)[0], 1), :] = pltpu.roll(line, 64, 1)
    message[:16, :] = jnp.where(where[1] == 0, col_out[...], row_out[...])


def logits_call(place, scale, images, texts):
    return pl.pallas_call(
        logits_body,
        out_shape=(
            jax.ShapeDtypeStruct((BLOCK, BLOCK), F32),
            jax.ShapeDtypeStruct((16, 128), F32),
            jax.ShapeDtypeStruct((16, 128), F32),
            jax.ShapeDtypeStruct((24, 128), F32),
            jax.ShapeDtypeStruct((8, 128), F32),
            ALL,
            ALL,
        ),
        in_specs=[SMEM, SMEM] + [VMEM] * 9,
        out_specs=(VMEM,) * 7,
        scratch_shapes=[pltpu.VMEM((BLOCK, 128), F32)],
        compiler_params=PARAMS,
    )(place, scale, *images, *texts)


def pair_up(rows):
    low = lax.broadcasted_iota(jnp.int32, (1, 128), 1) < ROWS
    pairs = [
        jnp.where(low, rows[i : i + 1], pltpu.roll(rows[i + 1 : i + 2], 64, 1))
        for i in range(0, rows.shape[0], 2)
    ]
    return jnp.concatenate(pairs)


def spread_body(place, row, col, matched, got, out):
    first = place[1] == 0
    mine, other = row[...], got[:16, :]
    top = jnp.maximum(col[...], other)
    both = top + LOG2E * jnp.log(jnp.exp2(col[...] - top) + jnp.exp2(other - top))
    low = pair_up(jnp.where(first, mine, both))
    high = pair_up(other)
    hits = matched[...] + got[16:24, :]
    for i in range(16):
        out[i, :8, :] = low
        out[i, 8:16, :] = high
        out[i, 16:24, :] = hits


def spread_call(place, *parts):
    return pl.pallas_call(
        spread_body,
        out_shape=jax.ShapeDtypeStruct((16, 24, 128), F32),
        in_specs=[SMEM] + [VMEM] * 4,
        out_specs=VMEM,
        compiler_params=PARAMS,
    )(place, *parts)


def join_body(place, got, mine, message):
    first = place[1] == 0
    counts = [jnp.logical_or(first, (place[3] & 1) == i % 2) for i in range(16)]
    parts = [jnp.where(counts[i], got[i, :16, :], -jnp.inf) for i in range(16)]
    top = parts[0]
    for p in parts[1:]:
        top = jnp.maximum(top, p)
    total = jnp.exp2(parts[0] - top)
    for p in parts[1:]:
        total += jnp.exp2(p - top)
    state = top + LOG2E * jnp.log(total)
    low, high = state[:8], state[8:]
    hits = got[0, 16:24, :]
    for i in range(1, 16):
        hits += got[i, 16:24, :]
    share = two_sums(low) + jnp.where(first, two_sums(high) - 2.0 * hits, 0.0)
    for out, pairs in ((mine, low), (message, jnp.where(first, high, low))):
        for i in range(8):
            out[2 * i : 2 * i + 1, :] = pairs[i : i + 1]
            out[2 * i + 1 : 2 * i + 2, :] = pltpu.roll(pairs[i : i + 1], 64, 1)
        out[16:24, :] = share


def join_call(place, got):
    return pl.pallas_call(
        join_body,
        out_shape=(jax.ShapeDtypeStruct((24, 128), F32),) * 2,
        in_specs=[SMEM, VMEM],
        out_specs=(VMEM,) * 2,
        compiler_params=PARAMS,
    )(place, got)


def digits_of(v):
    place = lax.broadcasted_iota(jnp.int32, (16, 128), 0)
    out = jnp.zeros((16, 128), F32)
    for i in range(DIGITS):
        unit = 16.0 ** (7 - i)
        d = jnp.floor(v * (1.0 / unit) + 0.5)
        v = v - d * unit
        out = jnp.where(place == i, d, out)
    return out


def value_of(digits):
    total = digits[0:1] * 16.0**7
    for i in range(1, DIGITS):
        total = total + digits[i : i + 1] * 16.0 ** (7 - i)
    return total


def half_weights(where, logits, at, row_wide, col_lines, weights):
    cols = col_ids(where)
    for a in range(4):
        ids = row_ids(where, a)
        for b in range(4):
            rows = slice(a * CHUNK + b * ROWS, a * CHUNK + (b + 1) * ROWS)
            wide = row_wide[rows, :]
            for t in range(4):
                tile = logits[rows, (at + t) * 128 : (at + t + 1) * 128]
                both = jnp.exp2(tile - wide) + jnp.exp2(tile - col_lines[at + t : at + t + 1, :])
                both = both - jnp.where(ids[b] == cols[at + t][0:1], 1.0, 0.0)
                weights[rows, t * 128 : (t + 1) * 128] = both.astype(BF16)


def high_body(place, scale, logits, mine, other, images, *refs):
    weights, outs, digits, row_wide, col_lines = refs[0], refs[1:4], refs[4], refs[5], refs[6]
    row_lse, col_lse = refs[7:]
    where = [place[i] for i in range(5)]
    first = place[1] == 0
    for i, own in enumerate((first, jnp.logical_not(first))):
        tail = sum(
            digits_of(jnp.where(own, mine[r : r + 1, :], other[r : r + 1, :])) for r in (16, 20)
        ).astype(BF16)
        for e in range(EMBED // 128):
            digits[i * TAIL : (i + 1) * TAIL, e * 128 : (e + 1) * 128] = tail
    row_lse[...] = jnp.where(first, mine[:16, :], other[:16, :]) + 1.0
    col_lse[...] = jnp.where(first, other[:16, :], mine[:16, :]) + 1.0
    lane = lax.broadcasted_iota(jnp.int32, (1, 128), 1)
    for t in range(8):
        j, i = t // 2, (t % 2) * 2
        lo = col_lse[pl.ds(col_place(where, j, i)[0], 1), :]
        hi = col_lse[pl.ds(col_place(where, j, i + 1)[0], 1), :]
        col_lines[t : t + 1, :] = jnp.where(lane < ROWS, lo, pltpu.roll(hi, 64, 1))
        lo = row_lse[pl.ds(row_place(where, j, i)[0], 1), :]
        hi = row_lse[pl.ds(row_place(where, j, i + 1)[0], 1), :]
        line = jnp.where(lane < ROWS, lo, pltpu.roll(hi, 64, 1))
        row_wide[t * 128 : (t + 1) * 128, :] = jnp.transpose(jnp.broadcast_to(line, (128, 128)))
    half_weights(where, logits, 4, row_wide, col_lines, weights)
    text_terms(scale[0], weights, images, 0, outs)


def high_call(place, scale, logits, mine, other, images):
    return pl.pallas_call(
        high_body,
        out_shape=(
            HALF_WEIGHTS,
            PART,
            jax.ShapeDtypeStruct((3 * ROWS, EMBED), BF16),
            jax.ShapeDtypeStruct((ROWS, EMBED), BF16),
            jax.ShapeDtypeStruct((2 * TAIL, EMBED), BF16),
            jax.ShapeDtypeStruct((BLOCK, 128), F32),
            jax.ShapeDtypeStruct((8, 128), F32),
        ),
        in_specs=[SMEM, SMEM] + [VMEM] * 4,
        out_specs=(VMEM,) * 7,
        scratch_shapes=[pltpu.VMEM((16, 128), F32), pltpu.VMEM((16, 128), F32)],
        compiler_params=PARAMS,
    )(place, scale, logits, mine, other, images)


def low_body(place, scale, logits, row_wide, col_lines, images, weights, out):
    half_weights([place[i] for i in range(5)], logits, 0, row_wide, col_lines, weights)
    text_terms(scale[0], weights, images, CHUNK, [out])


def low_call(place, scale, logits, row_wide, col_lines, images):
    return pl.pallas_call(
        low_body,
        out_shape=(HALF_WEIGHTS, PART),
        in_specs=[SMEM, SMEM] + [VMEM] * 4,
        out_specs=(VMEM,) * 2,
        compiler_params=PARAMS,
    )(place, scale, logits, row_wide, col_lines, images)


def text_terms(multiplier, weights, images, at, outs):
    rows = sum(out.shape[0] for out in outs)
    for e in range(5):
        term = multiplier * lax.dot_general(
            weights[:, at : at + rows],
            images[:, e * 256 : (e + 1) * 256],
            (((0,), (0,)), ((), ())),
            preferred_element_type=F32,
        )
        skip = 0
        for out in outs:
            out[:, e * 256 : (e + 1) * 256] = term[skip : skip + out.shape[0]].astype(BF16)
            skip += out.shape[0]


def image_terms(multiplier, weights, texts, at, outs):
    for e in range(5):
        term = multiplier * sum(
            jnp.dot(
                half[at * CHUNK : (at + len(outs)) * CHUNK, :],
                texts[h * BLOCK // 2 : (h + 1) * BLOCK // 2, e * 256 : (e + 1) * 256],
                preferred_element_type=F32,
            )
            for h, half in enumerate(weights)
        )
        for i, out in enumerate(outs):
            out[:CHUNK, e * 256 : (e + 1) * 256] = term[i * CHUNK : (i + 1) * CHUNK].astype(BF16)


def image_body(scale, after, digits, low, high, texts, *outs):
    image_terms(scale[0], (low, high), texts, 1, outs)
    for out in outs:
        out[CHUNK:, :] = digits[TAIL:, :]


def image_call(scale, after, digits, weights, texts):
    return pl.pallas_call(
        image_body,
        out_shape=(jax.ShapeDtypeStruct((CHUNK + TAIL, EMBED), BF16),) * 3,
        in_specs=[SMEM] + [VMEM] * 5,
        out_specs=(VMEM,) * 3,
        compiler_params=PARAMS,
    )(scale, after, digits, *weights, texts)


def rest_body(scale, low, high, images, texts, text_out, image_out):
    text_terms(scale[0], low, images, 0, [text_out])
    image_terms(scale[0], (low, high), texts, 0, [image_out])


def rest_call(scale, weights, images, texts):
    return pl.pallas_call(
        rest_body,
        out_shape=(PART, PART),
        in_specs=[SMEM] + [VMEM] * 4,
        out_specs=(VMEM,) * 2,
        compiler_params=PARAMS,
    )(scale, *weights, images, texts)


def add_rows(refs, rows, terms, out, to):
    for at in range(0, rows, 16):
        total = None
        for i, skip in terms:
            v = refs[i][skip + at : skip + at + 16, :].astype(F32)
            total = v if total is None else total + v
        out[to + at : to + at + 16, :] = total.astype(out.dtype)


def sums_body(n, plan, *refs):
    for parts, out in zip(plan, refs[n:]):
        to = 0
        for rows, terms in parts:
            add_rows(refs, rows, terms, out, to)
            to += rows


def sums(arrays, *plan):
    return pl.pallas_call(
        lambda *refs: sums_body(len(arrays), plan, *refs),
        out_shape=tuple(
            jax.ShapeDtypeStruct((sum(rows for rows, _ in parts), EMBED), BF16) for parts in plan
        ),
        in_specs=[VMEM] * len(arrays),
        out_specs=(VMEM,) * len(plan),
        compiler_params=PARAMS,
    )(*arrays)


def last_body(*refs):
    digits, image_out, text_out, loss_out = refs[6:]
    add_rows(refs, ROWS, [(i, 0) for i in range(4)], image_out, 0)
    add_rows(refs, ROWS, [(4, 0), (5, 0)], text_out, 0)
    total = -digits[:TAIL, :128].astype(F32)
    for r in refs[:6]:
        total += r[ROWS : ROWS + TAIL, :128].astype(F32)
    loss_out[...] = value_of(total)[:, 0:1] * (LN2 / (2.0 * ROWS * 256))


def last_call(shards, texts, digits):
    grad = jax.ShapeDtypeStruct((ROWS, EMBED), BF16)
    return pl.pallas_call(
        last_body,
        out_shape=(grad, grad, jax.ShapeDtypeStruct((1, 1), F32)),
        in_specs=[VMEM] * 7,
        out_specs=(VMEM,) * 3,
        compiler_params=PARAMS,
    )(*shards, *texts, digits)


def local(image_emb, text_emb, logit_scale):
    place = jnp.stack([lax.axis_index(n) for n in AXES]).astype(jnp.int32)

    (text,) = pack([text_emb], ((0, 64),))
    (image,) = pack([image_emb], ((0, 64),))
    (chip,) = pack([text, core_swap(text_emb)], ((0, 64), (1, 64)))
    next_1, next_4 = z_shift(chip, -1), z_shift(text_emb, 4)
    near = [plane_shift(image_emb, k, True) for k in (1, 2, 3)]
    own, text_0 = pack(
        [image] + near + [chip, next_1, next_4],
        ((0, 64), (1, 64), (2, 64), (3, 64)),
        ((4, 128), (5, 128)),
    )
    (side,) = pack([next_1, next_4], ((0, 128), (1, 64)))
    text_1 = z_shift(text_0, -2)
    near = [own] + [plane_shift(own, k, False) for k in PLANE_ORDER[1:]]
    logits, row_part, col_part, message, matched, images, texts = logits_call(
        place, logit_scale, near, [text_0, text_1, core_swap(text_1), core_swap(side), next_4]
    )

    spread = spread_call(place, row_part, col_part, matched, core_swap(message))
    mine, message = join_call(place, exchange(spread, plane_or_ring()))
    high, text_2, text_3, far, digits, row_wide, col_lines = high_call(
        place, logit_scale, logits, mine, core_swap(message), images
    )

    other_1, other_3 = core_swap(text_2), core_swap(text_3)
    low, text_1 = low_call(place, logit_scale, logits, row_wide, col_lines, images)
    weights = low, high
    pairs = sums(
        [text_1, other_1, far, other_3, digits],
        ((256, ((0, 0), (1, 0))), (64, ((2, 0), (3, 128))), (TAIL, ((4, 0),))),
    )[0]
    image_parts = image_call(logit_scale, pairs, digits, weights, texts)
    pairs = z_shift(pairs, 2)
    back = [plane_shift(v, -k, False) for v, k in ((image_parts[k - 1], k) for k in (2, 1, 3))]
    text_0, image_0 = rest_call(logit_scale, weights, images, texts)

    rows_tail = (TAIL, ((2, 320), (3, 0)))
    next_1, mine, next_4 = sums(
        [text_0, other_3, pairs, digits],
        ((128, ((0, 128), (1, 0), (2, 128))), rows_tail),
        ((128, ((0, 0), (2, 0))), rows_tail),
        ((80, ((2, 256),)),),
    )
    next_1, next_4 = z_shift(next_1, 1), z_shift(next_4, 2)
    (other,) = sums([mine, next_1], ((64, ((0, 64), (1, 64))), (TAIL, ((0, 128), (1, 128)))))
    (mine,) = sums(
        [mine, next_1, next_4], ((64, ((0, 0), (1, 0), (2, 0))), (TAIL, ((0, 128), (1, 128), (2, 64))))
    )

    cols_tail = (TAIL, ((1, 256), (2, 256), (3, 256), (4, 16)))
    pieces = sums(
        [image_0] + back + [digits],
        *[((64, [(i, 64 * k) for i in range(4)]), cols_tail) for k in range(4)],
    )
    shards = [pieces[0]] + [plane_shift(pieces[k], -k, True) for k in (2, 1, 3)]
    image_grad, text_grad, mean_loss = last_call(shards, [mine, core_swap(other)], digits)
    return mean_loss.reshape(1), image_grad, text_grad


def solution(mesh):
    fine = Mesh(mesh.devices.reshape(4, 2, 2, 4, 4), AXES)
    return jax.shard_map(
        local,
        mesh=fine,
        in_specs=(P(AXES, None), P(("zh", "y", "x", "zl", "core"), None), P()),
        out_specs=(P(), P(AXES, None), P(("zh", "y", "x", "zl", "core"), None)),
        check_vma=False,
    )
```

```python
import math

import jax
import jax.numpy as jnp
from jax import lax
from jax.experimental import pallas as pl
from jax.experimental.pallas import tpu as pltpu
from jax.sharding import Mesh, PartitionSpec as P

AXES = ("zl", "core", "zh", "y", "x")
NX, NY, NZ = 4, 4, 8
ROWS, EMBED = 64, 1280
CHUNK = 4 * ROWS
TAIL, DIGITS = 16, 13
BLOCK = 16 * ROWS
BF16, F32 = jnp.bfloat16, jnp.float32
LOG2E, LN2 = math.log2(math.e), math.log(2.0)
VMEM = pl.BlockSpec(memory_space=pltpu.VMEM)
SMEM = pl.BlockSpec(memory_space=pltpu.SMEM)
PARAMS = pltpu.CompilerParams(vmem_limit_bytes=12 * 1024 * 1024)


def plane_shift(v, k, primary):
    pairs = []
    for c in range(2):
        for h in range(2):
            for y in range(NY):
                for x in range(NX):
                    if (c == 0) == primary:
                        to = (y, (x + k) % NX)
                    else:
                        to = ((y + k) % NY, x)
                    base = (c * 2 + h) * NY
                    pairs.append(((base + y) * NX + x, (base + to[0]) * NX + to[1]))
    return lax.ppermute(v, ("core", "zh", "y", "x"), pairs)


def z_shift(v, k):
    pairs = []
    for c in range(2):
        for z in range(NZ):
            to = (z + (k if c == 0 else -k)) % NZ
            pairs.append((((z % 4) * 2 + c) * 2 + z // 4, ((to % 4) * 2 + c) * 2 + to // 4))
    return lax.ppermute(v, ("zl", "core", "zh"), pairs)


def core_swap(v):
    return lax.ppermute(v, "core", [(0, 1), (1, 0)])


def device(c, y, x, z):
    return ((((z % 4) * 2 + c) * 2 + z // 4) * NY + y) * NX + x


def plane_or_ring():
    out = [[device(0, y, x, z) for y in range(NY) for x in range(NX)] for z in range(NZ)]
    return out + [
        [device(1, y + d, x, z) for z in range(NZ) for d in (0, 1)] for y in (0, 2) for x in range(NX)
    ]


def exchange(v, groups):
    return lax.all_to_all(v, AXES, 0, 0, axis_index_groups=groups)


def row_place(where, a, b):
    zl, c, zh, y, x = where
    p, s = jnp.where(c == 0, b, a), jnp.where(c == 0, a, b)
    n = ((y - s) & 3) * 4 + ((x - p) & 3)
    return n, ((zl * 2 + c) * 2 + zh) * 16 + n


def col_place(where, j, i):
    zl, c, zh, y, x = where
    core = c if (i % 2 == 0) == (j < 2) else 1 - c
    sign = 1 - 2 * c
    off = ((0, 0, 1, 1), (2, 2, 3, 3), (-2, -2, -3, -3), (-1, -1, 4, 4))[j][i]
    off = 4 if off == 4 else sign * off
    z = (zh * 4 + zl + off) & 7
    return z * 2 + core, ((z >> 2) * 16 + y * 4 + x) * 8 + (z & 3) * 2 + core


def row_ids(where, a):
    span = lax.broadcasted_iota(jnp.int32, (ROWS, 128), 0)
    return [row_place(where, a, b)[1] * ROWS + span for b in range(4)]


def col_ids(where):
    lane = lax.broadcasted_iota(jnp.int32, (8, 128), 1)
    out = []
    for t in range(8):
        lo = col_place(where, t // 2, (t % 2) * 2)[1] * ROWS
        hi = col_place(where, t // 2, (t % 2) * 2 + 1)[1] * ROWS - ROWS
        out.append(lane + jnp.where(lane < ROWS, lo, hi))
    return out


PLANE_ORDER = (0, 1, 3, 2)
PART = jax.ShapeDtypeStruct((CHUNK, EMBED), BF16)
ALL = jax.ShapeDtypeStruct((BLOCK, EMBED), BF16)
HALF_WEIGHTS = jax.ShapeDtypeStruct((BLOCK, BLOCK // 2), BF16)


def pack_body(plan, n, *refs):
    for parts, out in zip(plan, refs[n:]):
        row = 0
        for i, rows in parts:
            out[row : row + rows, :] = refs[i][...]
            row += rows


def pack(arrays, *plan):
    shapes = [jax.ShapeDtypeStruct((sum(p[1] for p in parts), EMBED), BF16) for parts in plan]
    return pl.pallas_call(
        lambda *refs: pack_body(plan, len(arrays), *refs),
        out_shape=tuple(shapes),
        in_specs=[VMEM] * len(arrays),
        out_specs=(VMEM,) * len(plan),
        compiler_params=PARAMS,
    )(*arrays)


def fold(v):
    return v.reshape(v.shape[0] // 8, 8, 128)


def two_sums(v):
    coarse = 8.0 * jnp.floor(v * 0.125 + 0.5)
    parts = [jnp.sum(p, keepdims=True) for p in (coarse, v - coarse)]
    return jnp.where(lax.broadcasted_iota(jnp.int32, (8, 128), 0) < 4, *parts)


def column_part(logits, t, top):
    top = jnp.max(top, axis=0, keepdims=True)

    def step(i, total):
        tile = logits[pl.ds(pl.multiple_of(i * 128, 128), 128), t * 128 : (t + 1) * 128]
        return total + jnp.sum(fold(jnp.exp2(tile - top)), axis=0)

    total = lax.fori_loop(0, 8, step, jnp.zeros((8, 128), F32), unroll=True)
    return top + LOG2E * jnp.log(jnp.sum(total, axis=0, keepdims=True))


def logits_body(place, scale, *refs):
    images, texts = [refs[i] for i in PLANE_ORDER], refs[4:7]
    logits, row_out, col_out, message, match_out, all_images, all_texts = refs[9:16]
    row_wide = refs[16]
    all_texts[3 * CHUNK : BLOCK - ROWS, :] = refs[7][...]
    all_texts[BLOCK - ROWS :, :] = refs[8][2 * ROWS :, :]
    where = [place[i] for i in range(5)]
    multiplier = scale[0] * LOG2E
    for j in range(3):
        all_texts[j * CHUNK : (j + 1) * CHUNK, :] = texts[j][...]

    def chunk_logits(a):
        all_images[a * CHUNK : (a + 1) * CHUNK, :] = images[a][...]
        for j in range(4):
            text = texts[j][...] if j < 3 else all_texts[3 * CHUNK :, :]
            logits[a * CHUNK : (a + 1) * CHUNK, j * CHUNK : (j + 1) * CHUNK] = multiplier * lax.dot_general(
                images[a][...], text, (((1,), (1,)), ((), ())), preferred_element_type=F32
            )

    chunk_logits(0)
    cols = col_ids(where)
    step = 32
    matched = jnp.zeros((8, 128), F32)
    col_top = [jnp.full((8, 128), -jnp.inf, F32) for _ in range(8)]
    for a in range(4):
        if a < 3:
            chunk_logits(a + 1)
        ids = row_ids(where, a)
        for b in range(4):
            for half in range(ROWS // step):
                at = a * CHUNK + b * ROWS + half * step
                tiles = [logits[at : at + step, t * 128 : (t + 1) * 128] for t in range(8)]
                top = tiles[0]
                for t in range(1, 8):
                    top = jnp.maximum(top, tiles[t])
                top = jnp.max(top, axis=1, keepdims=True)
                mine = ids[b][half * step : (half + 1) * step]
                total = jnp.zeros((step, 128), F32)
                for t in range(8):
                    total += jnp.exp2(tiles[t] - top)
                    col_top[t] = jnp.maximum(col_top[t], jnp.max(fold(tiles[t]), axis=0))
                    hit = jnp.where(mine == cols[t][0:1], tiles[t], 0.0)
                    matched += jnp.sum(fold(hit), axis=0)
                part = top + LOG2E * jnp.log(jnp.sum(total, axis=1, keepdims=True))
                row_wide[at : at + step, :] = jnp.broadcast_to(part, (step, 128))
    matched = two_sums(matched)
    match_out[...] = matched
    message[16:24, :] = matched
    for t in range(8):
        part = column_part(logits, t, col_top[t])
        j, i = t // 2, (t % 2) * 2
        col_out[pl.ds(col_place(where, j, i)[0], 1), :] = part
        col_out[pl.ds(col_place(where, j, i + 1)[0], 1), :] = pltpu.roll(part, 64, 1)
        line = jnp.transpose(row_wide[t * 128 : (t + 1) * 128, :])[0:1]
        row_out[pl.ds(row_place(where, j, i)[0], 1), :] = line
        row_out[pl.ds(row_place(where, j, i + 1)[0], 1), :] = pltpu.roll(line, 64, 1)
    message[:16, :] = jnp.where(where[1] == 0, col_out[...], row_out[...])


def logits_call(place, scale, images, texts):
    return pl.pallas_call(
        logits_body,
        out_shape=(
            jax.ShapeDtypeStruct((BLOCK, BLOCK), F32),
            jax.ShapeDtypeStruct((16, 128), F32),
            jax.ShapeDtypeStruct((16, 128), F32),
            jax.ShapeDtypeStruct((24, 128), F32),
            jax.ShapeDtypeStruct((8, 128), F32),
            ALL,
            ALL,
        ),
        in_specs=[SMEM, SMEM] + [VMEM] * 9,
        out_specs=(VMEM,) * 7,
        scratch_shapes=[pltpu.VMEM((BLOCK, 128), F32)],
        compiler_params=PARAMS,
    )(place, scale, *images, *texts)


def pair_up(rows):
    low = lax.broadcasted_iota(jnp.int32, (1, 128), 1) < ROWS
    pairs = [
        jnp.where(low, rows[i : i + 1], pltpu.roll(rows[i + 1 : i + 2], 64, 1))
        for i in range(0, rows.shape[0], 2)
    ]
    return jnp.concatenate(pairs)


def spread_body(place, row, col, matched, got, out):
    first = place[1] == 0
    mine, other = row[...], got[:16, :]
    top = jnp.maximum(col[...], other)
    both = top + LOG2E * jnp.log(jnp.exp2(col[...] - top) + jnp.exp2(other - top))
    low = pair_up(jnp.where(first, mine, both))
    high = pair_up(other)
    hits = matched[...] + got[16:24, :]
    for i in range(16):
        out[i, :8, :] = low
        out[i, 8:16, :] = high
        out[i, 16:24, :] = hits


def spread_call(place, *parts):
    return pl.pallas_call(
        spread_body,
        out_shape=jax.ShapeDtypeStruct((16, 24, 128), F32),
        in_specs=[SMEM] + [VMEM] * 4,
        out_specs=VMEM,
        compiler_params=PARAMS,
    )(place, *parts)


def join_body(place, got, mine, message):
    first = place[1] == 0
    counts = [jnp.logical_or(first, (place[3] & 1) == i % 2) for i in range(16)]
    parts = [jnp.where(counts[i], got[i, :16, :], -jnp.inf) for i in range(16)]
    top = parts[0]
    for p in parts[1:]:
        top = jnp.maximum(top, p)
    total = jnp.exp2(parts[0] - top)
    for p in parts[1:]:
        total += jnp.exp2(p - top)
    state = top + LOG2E * jnp.log(total)
    low, high = state[:8], state[8:]
    hits = got[0, 16:24, :]
    for i in range(1, 16):
        hits += got[i, 16:24, :]
    share = two_sums(low) + jnp.where(first, two_sums(high) - 2.0 * hits, 0.0)
    for out, pairs in ((mine, low), (message, jnp.where(first, high, low))):
        for i in range(8):
            out[2 * i : 2 * i + 1, :] = pairs[i : i + 1]
            out[2 * i + 1 : 2 * i + 2, :] = pltpu.roll(pairs[i : i + 1], 64, 1)
        out[16:24, :] = share


def join_call(place, got):
    return pl.pallas_call(
        join_body,
        out_shape=(jax.ShapeDtypeStruct((24, 128), F32),) * 2,
        in_specs=[SMEM, VMEM],
        out_specs=(VMEM,) * 2,
        compiler_params=PARAMS,
    )(place, got)


def digits_of(v):
    place = lax.broadcasted_iota(jnp.int32, (16, 128), 0)
    out = jnp.zeros((16, 128), F32)
    for i in range(DIGITS):
        unit = 16.0 ** (7 - i)
        d = jnp.floor(v * (1.0 / unit) + 0.5)
        v = v - d * unit
        out = jnp.where(place == i, d, out)
    return out


def value_of(digits):
    total = digits[0:1] * 16.0**7
    for i in range(1, DIGITS):
        total = total + digits[i : i + 1] * 16.0 ** (7 - i)
    return total


def half_weights(where, logits, at, row_wide, col_lines, weights):
    cols = col_ids(where)
    for a in range(4):
        ids = row_ids(where, a)
        for b in range(4):
            rows = slice(a * CHUNK + b * ROWS, a * CHUNK + (b + 1) * ROWS)
            wide = row_wide[rows, :]
            for t in range(4):
                tile = logits[rows, (at + t) * 128 : (at + t + 1) * 128]
                both = jnp.exp2(tile - wide) + jnp.exp2(tile - col_lines[at + t : at + t + 1, :])
                both = both - jnp.where(ids[b] == cols[at + t][0:1], 1.0, 0.0)
                weights[rows, t * 128 : (t + 1) * 128] = both.astype(BF16)


def high_body(place, scale, logits, mine, other, images, *refs):
    weights, outs, digits, row_wide, col_lines = refs[0], refs[1:4], refs[4], refs[5], refs[6]
    row_lse, col_lse = refs[7:]
    where = [place[i] for i in range(5)]
    first = place[1] == 0
    for i, own in enumerate((first, jnp.logical_not(first))):
        tail = sum(
            digits_of(jnp.where(own, mine[r : r + 1, :], other[r : r + 1, :])) for r in (16, 20)
        ).astype(BF16)
        for e in range(EMBED // 128):
            digits[i * TAIL : (i + 1) * TAIL, e * 128 : (e + 1) * 128] = tail
    row_lse[...] = jnp.where(first, mine[:16, :], other[:16, :]) + 1.0
    col_lse[...] = jnp.where(first, other[:16, :], mine[:16, :]) + 1.0
    lane = lax.broadcasted_iota(jnp.int32, (1, 128), 1)
    for t in range(8):
        j, i = t // 2, (t % 2) * 2
        lo = col_lse[pl.ds(col_place(where, j, i)[0], 1), :]
        hi = col_lse[pl.ds(col_place(where, j, i + 1)[0], 1), :]
        col_lines[t : t + 1, :] = jnp.where(lane < ROWS, lo, pltpu.roll(hi, 64, 1))
        lo = row_lse[pl.ds(row_place(where, j, i)[0], 1), :]
        hi = row_lse[pl.ds(row_place(where, j, i + 1)[0], 1), :]
        line = jnp.where(lane < ROWS, lo, pltpu.roll(hi, 64, 1))
        row_wide[t * 128 : (t + 1) * 128, :] = jnp.transpose(jnp.broadcast_to(line, (128, 128)))
    half_weights(where, logits, 4, row_wide, col_lines, weights)
    text_terms(scale[0], weights, images, 0, outs)


def high_call(place, scale, logits, mine, other, images):
    return pl.pallas_call(
        high_body,
        out_shape=(
            HALF_WEIGHTS,
            PART,
            jax.ShapeDtypeStruct((3 * ROWS, EMBED), BF16),
            jax.ShapeDtypeStruct((ROWS, EMBED), BF16),
            jax.ShapeDtypeStruct((2 * TAIL, EMBED), BF16),
            jax.ShapeDtypeStruct((BLOCK, 128), F32),
            jax.ShapeDtypeStruct((8, 128), F32),
        ),
        in_specs=[SMEM, SMEM] + [VMEM] * 4,
        out_specs=(VMEM,) * 7,
        scratch_shapes=[pltpu.VMEM((16, 128), F32), pltpu.VMEM((16, 128), F32)],
        compiler_params=PARAMS,
    )(place, scale, logits, mine, other, images)


def low_body(place, scale, logits, row_wide, col_lines, images, weights, out):
    half_weights([place[i] for i in range(5)], logits, 0, row_wide, col_lines, weights)
    text_terms(scale[0], weights, images, CHUNK, [out])


def low_call(place, scale, logits, row_wide, col_lines, images):
    return pl.pallas_call(
        low_body,
        out_shape=(HALF_WEIGHTS, PART),
        in_specs=[SMEM, SMEM] + [VMEM] * 4,
        out_specs=(VMEM,) * 2,
        compiler_params=PARAMS,
    )(place, scale, logits, row_wide, col_lines, images)


def text_terms(multiplier, weights, images, at, outs):
    rows = sum(out.shape[0] for out in outs)
    for e in range(5):
        term = multiplier * lax.dot_general(
            weights[:, at : at + rows],
            images[:, e * 256 : (e + 1) * 256],
            (((0,), (0,)), ((), ())),
            preferred_element_type=F32,
        )
        skip = 0
        for out in outs:
            out[:, e * 256 : (e + 1) * 256] = term[skip : skip + out.shape[0]].astype(BF16)
            skip += out.shape[0]


def image_terms(multiplier, weights, texts, at, outs):
    for e in range(5):
        term = multiplier * sum(
            jnp.dot(
                half[at * CHUNK : (at + len(outs)) * CHUNK, :],
                texts[h * BLOCK // 2 : (h + 1) * BLOCK // 2, e * 256 : (e + 1) * 256],
                preferred_element_type=F32,
            )
            for h, half in enumerate(weights)
        )
        for i, out in enumerate(outs):
            out[:CHUNK, e * 256 : (e + 1) * 256] = term[i * CHUNK : (i + 1) * CHUNK].astype(BF16)


def image_body(scale, after, digits, low, high, texts, *outs):
    image_terms(scale[0], (low, high), texts, 1, outs)
    for out in outs:
        out[CHUNK:, :] = digits[TAIL:, :]


def image_call(scale, after, digits, weights, texts):
    return pl.pallas_call(
        image_body,
        out_shape=(jax.ShapeDtypeStruct((CHUNK + TAIL, EMBED), BF16),) * 3,
        in_specs=[SMEM] + [VMEM] * 5,
        out_specs=(VMEM,) * 3,
        compiler_params=PARAMS,
    )(scale, after, digits, *weights, texts)


def rest_body(scale, low, high, images, texts, text_out, image_out):
    text_terms(scale[0], low, images, 0, [text_out])
    image_terms(scale[0], (low, high), texts, 0, [image_out])


def rest_call(scale, weights, images, texts):
    return pl.pallas_call(
        rest_body,
        out_shape=(PART, PART),
        in_specs=[SMEM] + [VMEM] * 4,
        out_specs=(VMEM,) * 2,
        compiler_params=PARAMS,
    )(scale, *weights, images, texts)


def add_rows(refs, rows, terms, out, to):
    for at in range(0, rows, 16):
        total = None
        for i, skip in terms:
            v = refs[i][skip + at : skip + at + 16, :].astype(F32)
            total = v if total is None else total + v
        out[to + at : to + at + 16, :] = total.astype(out.dtype)


def sums_body(n, plan, *refs):
    for parts, out in zip(plan, refs[n:]):
        to = 0
        for rows, terms in parts:
            add_rows(refs, rows, terms, out, to)
            to += rows


def sums(arrays, *plan):
    return pl.pallas_call(
        lambda *refs: sums_body(len(arrays), plan, *refs),
        out_shape=tuple(
            jax.ShapeDtypeStruct((sum(rows for rows, _ in parts), EMBED), BF16) for parts in plan
        ),
        in_specs=[VMEM] * len(arrays),
        out_specs=(VMEM,) * len(plan),
        compiler_params=PARAMS,
    )(*arrays)


def last_body(*refs):
    digits, image_out, text_out, loss_out = refs[6:]
    add_rows(refs, ROWS, [(i, 0) for i in range(4)], image_out, 0)
    add_rows(refs, ROWS, [(4, 0), (5, 0)], text_out, 0)
    total = -digits[:TAIL, :128].astype(F32)
    for r in refs[:6]:
        total += r[ROWS : ROWS + TAIL, :128].astype(F32)
    loss_out[...] = value_of(total)[:, 0:1] * (LN2 / (2.0 * ROWS * 256))


def last_call(shards, texts, digits):
    grad = jax.ShapeDtypeStruct((ROWS, EMBED), BF16)
    return pl.pallas_call(
        last_body,
        out_shape=(grad, grad, jax.ShapeDtypeStruct((1, 1), F32)),
        in_specs=[VMEM] * 7,
        out_specs=(VMEM,) * 3,
        compiler_params=PARAMS,
    )(*shards, *texts, digits)


def local(image_emb, text_emb, logit_scale):
    place = jnp.stack([lax.axis_index(n) for n in AXES]).astype(jnp.int32)

    (text,) = pack([text_emb], ((0, 64),))
    (image,) = pack([image_emb], ((0, 64),))
    (chip,) = pack([text, core_swap(text_emb)], ((0, 64), (1, 64)))
    next_1, next_4 = z_shift(chip, -1), z_shift(text_emb, 4)
    near = [plane_shift(image_emb, k, True) for k in (1, 2, 3)]
    own, text_0 = pack(
        [image] + near + [chip, next_1, next_4],
        ((0, 64), (1, 64), (2, 64), (3, 64)),
        ((4, 128), (5, 128)),
    )
    (side,) = pack([next_1, next_4], ((0, 128), (1, 64)))
    text_1 = z_shift(text_0, -2)
    near = [own] + [plane_shift(own, k, False) for k in PLANE_ORDER[1:]]
    logits, row_part, col_part, message, matched, images, texts = logits_call(
        place, logit_scale, near, [text_0, text_1, core_swap(text_1), core_swap(side), side]
    )

    spread = spread_call(place, row_part, col_part, matched, core_swap(message))
    mine, message = join_call(place, exchange(spread, plane_or_ring()))
    high, text_2, text_3, far, digits, row_wide, col_lines = high_call(
        place, logit_scale, logits, mine, core_swap(message), images
    )

    other_1, other_3 = core_swap(text_2), core_swap(text_3)
    low, text_1 = low_call(place, logit_scale, logits, row_wide, col_lines, images)
    weights = low, high
    pairs = sums(
        [text_1, other_1, far, other_3, digits],
        ((256, ((0, 0), (1, 0))), (64, ((2, 0), (3, 128))), (TAIL, ((4, 0),))),
    )[0]
    image_parts = image_call(logit_scale, pairs, digits, weights, texts)
    pairs = z_shift(pairs, 2)
    back = [plane_shift(v, -k, False) for v, k in ((image_parts[k - 1], k) for k in (2, 1, 3))]
    text_0, image_0 = rest_call(logit_scale, weights, images, texts)

    rows_tail = (TAIL, ((2, 320), (3, 0)))
    next_1, mine, next_4 = sums(
        [text_0, other_3, pairs, digits],
        ((128, ((0, 128), (1, 0), (2, 128))), rows_tail),
        ((128, ((0, 0), (2, 0))), rows_tail),
        ((80, ((2, 256),)),),
    )
    next_1, next_4 = z_shift(next_1, 1), z_shift(next_4, 2)
    (other,) = sums([mine, next_1], ((64, ((0, 64), (1, 64))), (TAIL, ((0, 128), (1, 128)))))
    (mine,) = sums(
        [mine, next_1, next_4], ((64, ((0, 0), (1, 0), (2, 0))), (TAIL, ((0, 128), (1, 128), (2, 64))))
    )

    cols_tail = (TAIL, ((1, 256), (2, 256), (3, 256), (4, 16)))
    pieces = sums(
        [image_0] + back + [digits],
        *[((64, [(i, 64 * k) for i in range(4)]), cols_tail) for k in range(4)],
    )
    shards = [pieces[0]] + [plane_shift(pieces[k], -k, True) for k in (2, 1, 3)]
    image_grad, text_grad, mean_loss = last_call(shards, [mine, core_swap(other)], digits)
    return mean_loss.reshape(1), image_grad, text_grad


def solution(mesh):
    fine = Mesh(mesh.devices.reshape(4, 2, 2, 4, 4), AXES)
    return jax.shard_map(
        local,
        mesh=fine,
        in_specs=(P(AXES, None), P(("zh", "y", "x", "zl", "core"), None), P()),
        out_specs=(P(), P(AXES, None), P(("zh", "y", "x", "zl", "core"), None)),
        check_vma=False,
    )
```

```python
import math

import jax
import jax.numpy as jnp
from jax import lax
from jax.experimental import pallas as pl
from jax.experimental.pallas import tpu as pltpu
from jax.sharding import Mesh, PartitionSpec as P

AXES = ("zl", "core", "zh", "y", "x")
NX, NY, NZ = 4, 4, 8
ROWS, EMBED = 64, 1280
CHUNK = 4 * ROWS
TAIL, DIGITS = 16, 13
BLOCK = 16 * ROWS
BF16, F32 = jnp.bfloat16, jnp.float32
LOG2E, LN2 = math.log2(math.e), math.log(2.0)
VMEM = pl.BlockSpec(memory_space=pltpu.VMEM)
SMEM = pl.BlockSpec(memory_space=pltpu.SMEM)
PARAMS = pltpu.CompilerParams(vmem_limit_bytes=12 * 1024 * 1024)


def plane_shift(v, k, primary):
    pairs = []
    for c in range(2):
        for h in range(2):
            for y in range(NY):
                for x in range(NX):
                    if (c == 0) == primary:
                        to = (y, (x + k) % NX)
                    else:
                        to = ((y + k) % NY, x)
                    base = (c * 2 + h) * NY
                    pairs.append(((base + y) * NX + x, (base + to[0]) * NX + to[1]))
    return lax.ppermute(v, ("core", "zh", "y", "x"), pairs)


def z_shift(v, k):
    pairs = []
    for c in range(2):
        for z in range(NZ):
            to = (z + (k if c == 0 else -k)) % NZ
            pairs.append((((z % 4) * 2 + c) * 2 + z // 4, ((to % 4) * 2 + c) * 2 + to // 4))
    return lax.ppermute(v, ("zl", "core", "zh"), pairs)


def core_swap(v):
    return lax.ppermute(v, "core", [(0, 1), (1, 0)])


def device(c, y, x, z):
    return ((((z % 4) * 2 + c) * 2 + z // 4) * NY + y) * NX + x


def plane_or_ring():
    out = [[device(0, y, x, z) for y in range(NY) for x in range(NX)] for z in range(NZ)]
    return out + [
        [device(1, y + d, x, z) for z in range(NZ) for d in (0, 1)] for y in (0, 2) for x in range(NX)
    ]


def exchange(v, groups):
    return lax.all_to_all(v, AXES, 0, 0, axis_index_groups=groups)


def row_place(where, a, b):
    zl, c, zh, y, x = where
    p, s = jnp.where(c == 0, b, a), jnp.where(c == 0, a, b)
    n = ((y - s) & 3) * 4 + ((x - p) & 3)
    return n, ((zl * 2 + c) * 2 + zh) * 16 + n


def col_place(where, j, i):
    zl, c, zh, y, x = where
    core = c if (i % 2 == 0) == (j < 2) else 1 - c
    sign = 1 - 2 * c
    off = ((0, 0, 1, 1), (2, 2, 3, 3), (-2, -2, -3, -3), (-1, -1, 4, 4))[j][i]
    off = 4 if off == 4 else sign * off
    z = (zh * 4 + zl + off) & 7
    return z * 2 + core, ((z >> 2) * 16 + y * 4 + x) * 8 + (z & 3) * 2 + core


def row_ids(where, a):
    span = lax.broadcasted_iota(jnp.int32, (ROWS, 128), 0)
    return [row_place(where, a, b)[1] * ROWS + span for b in range(4)]


def has_match(where, a, b):
    block = row_place(where, a, b)[1]
    return jnp.logical_and(((block >> 5) & 3) == where[3], ((block >> 3) & 3) == where[4])


def col_ids(where):
    lane = lax.broadcasted_iota(jnp.int32, (8, 128), 1)
    out = []
    for t in range(8):
        lo = col_place(where, t // 2, (t % 2) * 2)[1] * ROWS
        hi = col_place(where, t // 2, (t % 2) * 2 + 1)[1] * ROWS - ROWS
        out.append(lane + jnp.where(lane < ROWS, lo, hi))
    return out


PLANE_ORDER = (0, 1, 3, 2)
PART = jax.ShapeDtypeStruct((CHUNK, EMBED), BF16)
ALL = jax.ShapeDtypeStruct((BLOCK, EMBED), BF16)
HALF_WEIGHTS = jax.ShapeDtypeStruct((BLOCK, BLOCK // 2), BF16)


def pack_body(plan, n, *refs):
    for parts, out in zip(plan, refs[n:]):
        row = 0
        for i, rows in parts:
            out[row : row + rows, :] = refs[i][...]
            row += rows


def pack(arrays, *plan):
    shapes = [jax.ShapeDtypeStruct((sum(p[1] for p in parts), EMBED), BF16) for parts in plan]
    return pl.pallas_call(
        lambda *refs: pack_body(plan, len(arrays), *refs),
        out_shape=tuple(shapes),
        in_specs=[VMEM] * len(arrays),
        out_specs=(VMEM,) * len(plan),
        compiler_params=PARAMS,
    )(*arrays)


def fold(v):
    return v.reshape(v.shape[0] // 8, 8, 128)


def two_sums(v):
    coarse = 8.0 * jnp.floor(v * 0.125 + 0.5)
    parts = [jnp.sum(p, keepdims=True) for p in (coarse, v - coarse)]
    return jnp.where(lax.broadcasted_iota(jnp.int32, (8, 128), 0) < 4, *parts)


def column_part(logits, t, top):
    top = jnp.max(top, axis=0, keepdims=True)

    def step(i, total):
        tile = logits[pl.ds(pl.multiple_of(i * 128, 128), 128), t * 128 : (t + 1) * 128]
        return total + jnp.sum(fold(jnp.exp2(tile - top)), axis=0)

    total = lax.fori_loop(0, 8, step, jnp.zeros((8, 128), F32), unroll=True)
    return top + LOG2E * jnp.log(jnp.sum(total, axis=0, keepdims=True))


def logits_body(place, scale, *refs):
    images, texts = [refs[i] for i in PLANE_ORDER], refs[4:7]
    logits, row_out, col_out, message, match_out, all_images, all_texts = refs[9:16]
    row_wide = refs[16]
    all_texts[3 * CHUNK : BLOCK - ROWS, :] = refs[7][...]
    all_texts[BLOCK - ROWS :, :] = refs[8][...]
    where = [place[i] for i in range(5)]
    multiplier = scale[0] * LOG2E
    for j in range(3):
        all_texts[j * CHUNK : (j + 1) * CHUNK, :] = texts[j][...]

    def chunk_logits(a):
        all_images[a * CHUNK : (a + 1) * CHUNK, :] = images[a][...]
        for j in range(4):
            text = texts[j][...] if j < 3 else all_texts[3 * CHUNK :, :]
            logits[a * CHUNK : (a + 1) * CHUNK, j * CHUNK : (j + 1) * CHUNK] = multiplier * lax.dot_general(
                images[a][...], text, (((1,), (1,)), ((), ())), preferred_element_type=F32
            )

    chunk_logits(0)
    cols = col_ids(where)
    step = 32
    col_top = [jnp.full((8, 128), -jnp.inf, F32) for _ in range(8)]
    for a in range(4):
        if a < 3:
            chunk_logits(a + 1)
        for b in range(4):
            for half in range(ROWS // step):
                at = a * CHUNK + b * ROWS + half * step
                tiles = [logits[at : at + step, t * 128 : (t + 1) * 128] for t in range(8)]
                top = tiles[0]
                for t in range(1, 8):
                    top = jnp.maximum(top, tiles[t])
                top = jnp.max(top, axis=1, keepdims=True)
                total = jnp.zeros((step, 128), F32)
                for t in range(8):
                    total += jnp.exp2(tiles[t] - top)
                    col_top[t] = jnp.maximum(col_top[t], jnp.max(fold(tiles[t]), axis=0))
                part = top + LOG2E * jnp.log(jnp.sum(total, axis=1, keepdims=True))
                row_wide[at : at + step, :] = jnp.broadcast_to(part, (step, 128))
    match_out[...] = jnp.zeros((8, 128), F32)
    for a in range(4):
        for b in range(4):

            @pl.when(has_match(where, a, b))
            def _(a=a, b=b):
                at = a * CHUNK + b * ROWS
                mine = row_ids(where, a)[b]
                for t in range(8):
                    hit = jnp.where(mine == cols[t][0:1], logits[at : at + ROWS, t * 128 : (t + 1) * 128], 0.0)
                    match_out[...] += jnp.sum(fold(hit), axis=0)

    matched = two_sums(match_out[...])
    match_out[...] = matched
    message[16:24, :] = matched
    for t in range(8):
        part = column_part(logits, t, col_top[t])
        j, i = t // 2, (t % 2) * 2
        col_out[pl.ds(col_place(where, j, i)[0], 1), :] = part
        col_out[pl.ds(col_place(where, j, i + 1)[0], 1), :] = pltpu.roll(part, 64, 1)
        line = jnp.transpose(row_wide[t * 128 : (t + 1) * 128, :])[0:1]
        row_out[pl.ds(row_place(where, j, i)[0], 1), :] = line
        row_out[pl.ds(row_place(where, j, i + 1)[0], 1), :] = pltpu.roll(line, 64, 1)
    message[:16, :] = jnp.where(where[1] == 0, col_out[...], row_out[...])


def logits_call(place, scale, images, texts):
    return pl.pallas_call(
        logits_body,
        out_shape=(
            jax.ShapeDtypeStruct((BLOCK, BLOCK), F32),
            jax.ShapeDtypeStruct((16, 128), F32),
            jax.ShapeDtypeStruct((16, 128), F32),
            jax.ShapeDtypeStruct((24, 128), F32),
            jax.ShapeDtypeStruct((8, 128), F32),
            ALL,
            ALL,
        ),
        in_specs=[SMEM, SMEM] + [VMEM] * 9,
        out_specs=(VMEM,) * 7,
        scratch_shapes=[pltpu.VMEM((BLOCK, 128), F32)],
        compiler_params=PARAMS,
    )(place, scale, *images, *texts)


def pair_up(rows):
    low = lax.broadcasted_iota(jnp.int32, (1, 128), 1) < ROWS
    pairs = [
        jnp.where(low, rows[i : i + 1], pltpu.roll(rows[i + 1 : i + 2], 64, 1))
        for i in range(0, rows.shape[0], 2)
    ]
    return jnp.concatenate(pairs)


def spread_body(place, row, col, matched, got, out):
    first = place[1] == 0
    mine, other = row[...], got[:16, :]
    top = jnp.maximum(col[...], other)
    both = top + LOG2E * jnp.log(jnp.exp2(col[...] - top) + jnp.exp2(other - top))
    low = pair_up(jnp.where(first, mine, both))
    high = pair_up(other)
    hits = matched[...] + got[16:24, :]
    for i in range(16):
        out[i, :8, :] = low
        out[i, 8:16, :] = high
        out[i, 16:24, :] = hits


def spread_call(place, *parts):
    return pl.pallas_call(
        spread_body,
        out_shape=jax.ShapeDtypeStruct((16, 24, 128), F32),
        in_specs=[SMEM] + [VMEM] * 4,
        out_specs=VMEM,
        compiler_params=PARAMS,
    )(place, *parts)


def join_body(place, got, mine, message):
    first = place[1] == 0
    counts = [jnp.logical_or(first, (place[3] & 1) == i % 2) for i in range(16)]
    parts = [jnp.where(counts[i], got[i, :16, :], -jnp.inf) for i in range(16)]
    top = parts[0]
    for p in parts[1:]:
        top = jnp.maximum(top, p)
    total = jnp.exp2(parts[0] - top)
    for p in parts[1:]:
        total += jnp.exp2(p - top)
    state = top + LOG2E * jnp.log(total)
    low, high = state[:8], state[8:]
    hits = got[0, 16:24, :]
    for i in range(1, 16):
        hits += got[i, 16:24, :]
    share = two_sums(low) + jnp.where(first, two_sums(high) - 2.0 * hits, 0.0)
    for out, pairs in ((mine, low), (message, jnp.where(first, high, low))):
        for i in range(8):
            out[2 * i : 2 * i + 1, :] = pairs[i : i + 1]
            out[2 * i + 1 : 2 * i + 2, :] = pltpu.roll(pairs[i : i + 1], 64, 1)
        out[16:24, :] = share


def join_call(place, got):
    return pl.pallas_call(
        join_body,
        out_shape=(jax.ShapeDtypeStruct((24, 128), F32),) * 2,
        in_specs=[SMEM, VMEM],
        out_specs=(VMEM,) * 2,
        compiler_params=PARAMS,
    )(place, got)


def digits_of(v):
    place = lax.broadcasted_iota(jnp.int32, (16, 128), 0)
    out = jnp.zeros((16, 128), F32)
    for i in range(DIGITS):
        unit = 16.0 ** (7 - i)
        d = jnp.floor(v * (1.0 / unit) + 0.5)
        v = v - d * unit
        out = jnp.where(place == i, d, out)
    return out


def value_of(digits):
    total = digits[0:1] * 16.0**7
    for i in range(1, DIGITS):
        total = total + digits[i : i + 1] * 16.0 ** (7 - i)
    return total


def half_weights(where, logits, at, row_wide, col_lines, weights):
    cols = col_ids(where)

    def block(a, b, labels):
        rows = slice(a * CHUNK + b * ROWS, a * CHUNK + (b + 1) * ROWS)
        wide = row_wide[rows, :]
        for t in range(4):
            tile = logits[rows, (at + t) * 128 : (at + t + 1) * 128]
            both = jnp.exp2(tile - wide) + jnp.exp2(tile - col_lines[at + t : at + t + 1, :])
            if labels is not None:
                both = both - jnp.where(labels == cols[at + t][0:1], 1.0, 0.0)
            weights[rows, t * 128 : (t + 1) * 128] = both.astype(BF16)

    places = [(a, b) for a in range(4) for b in range(4)]
    for a, b in places:
        block(a, b, None)
    for a, b in places:

        @pl.when(has_match(where, a, b))
        def _(a=a, b=b):
            block(a, b, row_ids(where, a)[b])


def high_body(place, scale, logits, mine, other, images, *refs):
    weights, outs, digits, row_wide, col_lines = refs[0], refs[1:4], refs[4], refs[5], refs[6]
    row_lse, col_lse = refs[7:]
    where = [place[i] for i in range(5)]
    first = place[1] == 0
    for i, own in enumerate((first, jnp.logical_not(first))):
        tail = sum(
            digits_of(jnp.where(own, mine[r : r + 1, :], other[r : r + 1, :])) for r in (16, 20)
        ).astype(BF16)
        for e in range(EMBED // 128):
            digits[i * TAIL : (i + 1) * TAIL, e * 128 : (e + 1) * 128] = tail
    row_lse[...] = jnp.where(first, mine[:16, :], other[:16, :]) + 1.0
    col_lse[...] = jnp.where(first, other[:16, :], mine[:16, :]) + 1.0
    lane = lax.broadcasted_iota(jnp.int32, (1, 128), 1)
    for t in range(8):
        j, i = t // 2, (t % 2) * 2
        lo = col_lse[pl.ds(col_place(where, j, i)[0], 1), :]
        hi = col_lse[pl.ds(col_place(where, j, i + 1)[0], 1), :]
        col_lines[t : t + 1, :] = jnp.where(lane < ROWS, lo, pltpu.roll(hi, 64, 1))
        lo = row_lse[pl.ds(row_place(where, j, i)[0], 1), :]
        hi = row_lse[pl.ds(row_place(where, j, i + 1)[0], 1), :]
        line = jnp.where(lane < ROWS, lo, pltpu.roll(hi, 64, 1))
        row_wide[t * 128 : (t + 1) * 128, :] = jnp.transpose(jnp.broadcast_to(line, (128, 128)))
    half_weights(where, logits, 4, row_wide, col_lines, weights)
    text_terms(scale[0], weights, images, 0, outs)


def high_call(place, scale, logits, mine, other, images):
    return pl.pallas_call(
        high_body,
        out_shape=(
            HALF_WEIGHTS,
            PART,
            jax.ShapeDtypeStruct((3 * ROWS, EMBED), BF16),
            jax.ShapeDtypeStruct((ROWS, EMBED), BF16),
            jax.ShapeDtypeStruct((2 * TAIL, EMBED), BF16),
            jax.ShapeDtypeStruct((BLOCK, 128), F32),
            jax.ShapeDtypeStruct((8, 128), F32),
        ),
        in_specs=[SMEM, SMEM] + [VMEM] * 4,
        out_specs=(VMEM,) * 7,
        scratch_shapes=[pltpu.VMEM((16, 128), F32), pltpu.VMEM((16, 128), F32)],
        compiler_params=PARAMS,
    )(place, scale, logits, mine, other, images)


def low_body(place, scale, logits, row_wide, col_lines, images, weights, out):
    half_weights([place[i] for i in range(5)], logits, 0, row_wide, col_lines, weights)
    text_terms(scale[0], weights, images, CHUNK, [out])


def low_call(place, scale, logits, row_wide, col_lines, images):
    return pl.pallas_call(
        low_body,
        out_shape=(HALF_WEIGHTS, PART),
        in_specs=[SMEM, SMEM] + [VMEM] * 4,
        out_specs=(VMEM,) * 2,
        compiler_params=PARAMS,
    )(place, scale, logits, row_wide, col_lines, images)


def text_terms(multiplier, weights, images, at, outs):
    rows = sum(out.shape[0] for out in outs)
    for e in range(5):
        term = multiplier * lax.dot_general(
            weights[:, at : at + rows],
            images[:, e * 256 : (e + 1) * 256],
            (((0,), (0,)), ((), ())),
            preferred_element_type=F32,
        )
        skip = 0
        for out in outs:
            out[:, e * 256 : (e + 1) * 256] = term[skip : skip + out.shape[0]].astype(BF16)
            skip += out.shape[0]


def image_terms(multiplier, weights, texts, at, outs):
    for e in range(5):
        term = multiplier * sum(
            jnp.dot(
                half[at * CHUNK : (at + len(outs)) * CHUNK, :],
                texts[h * BLOCK // 2 : (h + 1) * BLOCK // 2, e * 256 : (e + 1) * 256],
                preferred_element_type=F32,
            )
            for h, half in enumerate(weights)
        )
        for i, out in enumerate(outs):
            out[:CHUNK, e * 256 : (e + 1) * 256] = term[i * CHUNK : (i + 1) * CHUNK].astype(BF16)


def image_body(scale, after, digits, low, high, texts, *outs):
    image_terms(scale[0], (low, high), texts, 1, outs)
    for out in outs:
        out[CHUNK:, :] = digits[TAIL:, :]


def image_call(scale, after, digits, weights, texts):
    return pl.pallas_call(
        image_body,
        out_shape=(jax.ShapeDtypeStruct((CHUNK + TAIL, EMBED), BF16),) * 3,
        in_specs=[SMEM] + [VMEM] * 5,
        out_specs=(VMEM,) * 3,
        compiler_params=PARAMS,
    )(scale, after, digits, *weights, texts)


def rest_body(scale, low, high, images, texts, text_out, image_out):
    text_terms(scale[0], low, images, 0, [text_out])
    image_terms(scale[0], (low, high), texts, 0, [image_out])


def rest_call(scale, weights, images, texts):
    return pl.pallas_call(
        rest_body,
        out_shape=(PART, PART),
        in_specs=[SMEM] + [VMEM] * 4,
        out_specs=(VMEM,) * 2,
        compiler_params=PARAMS,
    )(scale, *weights, images, texts)


def add_rows(refs, rows, terms, out, to):
    for at in range(0, rows, 16):
        total = None
        for i, skip in terms:
            v = refs[i][skip + at : skip + at + 16, :].astype(F32)
            total = v if total is None else total + v
        out[to + at : to + at + 16, :] = total.astype(out.dtype)


def sums_body(n, plan, *refs):
    for parts, out in zip(plan, refs[n:]):
        to = 0
        for rows, terms in parts:
            add_rows(refs, rows, terms, out, to)
            to += rows


def sums(arrays, *plan):
    return pl.pallas_call(
        lambda *refs: sums_body(len(arrays), plan, *refs),
        out_shape=tuple(
            jax.ShapeDtypeStruct((sum(rows for rows, _ in parts), EMBED), BF16) for parts in plan
        ),
        in_specs=[VMEM] * len(arrays),
        out_specs=(VMEM,) * len(plan),
        compiler_params=PARAMS,
    )(*arrays)


def last_body(*refs):
    digits, image_out, text_out, loss_out = refs[6:]
    add_rows(refs, ROWS, [(i, 0) for i in range(4)], image_out, 0)
    add_rows(refs, ROWS, [(4, 0), (5, 0)], text_out, 0)
    total = -digits[:TAIL, :128].astype(F32)
    for r in refs[:6]:
        total += r[ROWS : ROWS + TAIL, :128].astype(F32)
    loss_out[...] = value_of(total)[:, 0:1] * (LN2 / (2.0 * ROWS * 256))


def last_call(shards, texts, digits):
    grad = jax.ShapeDtypeStruct((ROWS, EMBED), BF16)
    return pl.pallas_call(
        last_body,
        out_shape=(grad, grad, jax.ShapeDtypeStruct((1, 1), F32)),
        in_specs=[VMEM] * 7,
        out_specs=(VMEM,) * 3,
        compiler_params=PARAMS,
    )(*shards, *texts, digits)


def local(image_emb, text_emb, logit_scale):
    place = jnp.stack([lax.axis_index(n) for n in AXES]).astype(jnp.int32)

    (text,) = pack([text_emb], ((0, 64),))
    (image,) = pack([image_emb], ((0, 64),))
    (chip,) = pack([text, core_swap(text_emb)], ((0, 64), (1, 64)))
    next_1, next_4 = z_shift(chip, -1), z_shift(text_emb, 4)
    near = [plane_shift(image_emb, k, True) for k in (1, 2, 3)]
    own, text_0 = pack(
        [image] + near + [chip, next_1, next_4],
        ((0, 64), (1, 64), (2, 64), (3, 64)),
        ((4, 128), (5, 128)),
    )
    (side,) = pack([next_1, next_4], ((0, 128), (1, 64)))
    text_1 = z_shift(text_0, -2)
    near = [own] + [plane_shift(own, k, False) for k in PLANE_ORDER[1:]]
    logits, row_part, col_part, message, matched, images, texts = logits_call(
        place, logit_scale, near, [text_0, text_1, core_swap(text_1), core_swap(side), next_4]
    )

    spread = spread_call(place, row_part, col_part, matched, core_swap(message))
    mine, message = join_call(place, exchange(spread, plane_or_ring()))
    high, text_2, text_3, far, digits, row_wide, col_lines = high_call(
        place, logit_scale, logits, mine, core_swap(message), images
    )

    other_1, other_3 = core_swap(text_2), core_swap(text_3)
    low, text_1 = low_call(place, logit_scale, logits, row_wide, col_lines, images)
    weights = low, high
    pairs = sums(
        [text_1, other_1, far, other_3, digits],
        ((256, ((0, 0), (1, 0))), (64, ((2, 0), (3, 128))), (TAIL, ((4, 0),))),
    )[0]
    image_parts = image_call(logit_scale, pairs, digits, weights, texts)
    pairs = z_shift(pairs, 2)
    back = [plane_shift(v, -k, False) for v, k in ((image_parts[k - 1], k) for k in (2, 1, 3))]
    text_0, image_0 = rest_call(logit_scale, weights, images, texts)

    rows_tail = (TAIL, ((2, 320), (3, 0)))
    next_1, mine, next_4 = sums(
        [text_0, other_3, pairs, digits],
        ((128, ((0, 128), (1, 0), (2, 128))), rows_tail),
        ((128, ((0, 0), (2, 0))), rows_tail),
        ((80, ((2, 256),)),),
    )
    next_1, next_4 = z_shift(next_1, 1), z_shift(next_4, 2)
    (other,) = sums([mine, next_1], ((64, ((0, 64), (1, 64))), (TAIL, ((0, 128), (1, 128)))))
    (mine,) = sums(
        [mine, next_1, next_4], ((64, ((0, 0), (1, 0), (2, 0))), (TAIL, ((0, 128), (1, 128), (2, 64))))
    )

    cols_tail = (TAIL, ((1, 256), (2, 256), (3, 256), (4, 16)))
    pieces = sums(
        [image_0] + back + [digits],
        *[((64, [(i, 64 * k) for i in range(4)]), cols_tail) for k in range(4)],
    )
    shards = [pieces[0]] + [plane_shift(pieces[k], -k, True) for k in (2, 1, 3)]
    image_grad, text_grad, mean_loss = last_call(shards, [mine, core_swap(other)], digits)
    return mean_loss.reshape(1), image_grad, text_grad


def solution(mesh):
    fine = Mesh(mesh.devices.reshape(4, 2, 2, 4, 4), AXES)
    return jax.shard_map(
        local,
        mesh=fine,
        in_specs=(P(AXES, None), P(("zh", "y", "x", "zl", "core"), None), P()),
        out_specs=(P(), P(AXES, None), P(("zh", "y", "x", "zl", "core"), None)),
        check_vma=False,
    )
```

```python
import math

import jax
import jax.numpy as jnp
from jax import lax
from jax.experimental import pallas as pl
from jax.experimental.pallas import tpu as pltpu
from jax.sharding import Mesh, PartitionSpec as P

AXES = ("zl", "core", "zh", "y", "x")
NX, NY, NZ = 4, 4, 8
ROWS, EMBED = 64, 1280
CHUNK = 4 * ROWS
TAIL, DIGITS = 16, 13
BLOCK = 16 * ROWS
BF16, F32 = jnp.bfloat16, jnp.float32
LOG2E, LN2 = math.log2(math.e), math.log(2.0)
VMEM = pl.BlockSpec(memory_space=pltpu.VMEM)
SMEM = pl.BlockSpec(memory_space=pltpu.SMEM)
PARAMS = pltpu.CompilerParams(vmem_limit_bytes=12 * 1024 * 1024)


def plane_shift(v, k, primary):
    pairs = []
    for c in range(2):
        for h in range(2):
            for y in range(NY):
                for x in range(NX):
                    if (c == 0) == primary:
                        to = (y, (x + k) % NX)
                    else:
                        to = ((y + k) % NY, x)
                    base = (c * 2 + h) * NY
                    pairs.append(((base + y) * NX + x, (base + to[0]) * NX + to[1]))
    return lax.ppermute(v, ("core", "zh", "y", "x"), pairs)


def z_shift(v, k):
    pairs = []
    for c in range(2):
        for z in range(NZ):
            to = (z + (k if c == 0 else -k)) % NZ
            pairs.append((((z % 4) * 2 + c) * 2 + z // 4, ((to % 4) * 2 + c) * 2 + to // 4))
    return lax.ppermute(v, ("zl", "core", "zh"), pairs)


def core_swap(v):
    return lax.ppermute(v, "core", [(0, 1), (1, 0)])


def device(c, y, x, z):
    return ((((z % 4) * 2 + c) * 2 + z // 4) * NY + y) * NX + x


def plane_or_ring():
    out = [[device(0, y, x, z) for y in range(NY) for x in range(NX)] for z in range(NZ)]
    return out + [
        [device(1, y + d, x, z) for z in range(NZ) for d in (0, 1)] for y in (0, 2) for x in range(NX)
    ]


def exchange(v, groups):
    return lax.all_to_all(v, AXES, 0, 0, axis_index_groups=groups)


def row_place(where, a, b):
    zl, c, zh, y, x = where
    p, s = jnp.where(c == 0, b, a), jnp.where(c == 0, a, b)
    n = ((y - s) & 3) * 4 + ((x - p) & 3)
    return n, ((zl * 2 + c) * 2 + zh) * 16 + n


def col_place(where, j, i):
    zl, c, zh, y, x = where
    core = c if (i % 2 == 0) == (j < 2) else 1 - c
    sign = 1 - 2 * c
    off = ((0, 0, 1, 1), (2, 2, 3, 3), (-2, -2, -3, -3), (-1, -1, 4, 4))[j][i]
    off = 4 if off == 4 else sign * off
    z = (zh * 4 + zl + off) & 7
    return z * 2 + core, ((z >> 2) * 16 + y * 4 + x) * 8 + (z & 3) * 2 + core


def row_ids(where, a):
    span = lax.broadcasted_iota(jnp.int32, (ROWS, 128), 0)
    return [row_place(where, a, b)[1] * ROWS + span for b in range(4)]


def col_ids(where):
    lane = lax.broadcasted_iota(jnp.int32, (8, 128), 1)
    out = []
    for t in range(8):
        lo = col_place(where, t // 2, (t % 2) * 2)[1] * ROWS
        hi = col_place(where, t // 2, (t % 2) * 2 + 1)[1] * ROWS - ROWS
        out.append(lane + jnp.where(lane < ROWS, lo, hi))
    return out


PLANE_ORDER = (0, 1, 3, 2)
PART = jax.ShapeDtypeStruct((CHUNK, EMBED), BF16)
ALL = jax.ShapeDtypeStruct((BLOCK, EMBED), BF16)
HALF_WEIGHTS = jax.ShapeDtypeStruct((BLOCK, BLOCK // 2), BF16)


def pack_body(plan, n, *refs):
    for parts, out in zip(plan, refs[n:]):
        row = 0
        for i, rows in parts:
            out[row : row + rows, :] = refs[i][...]
            row += rows


def pack(arrays, *plan):
    shapes = [jax.ShapeDtypeStruct((sum(p[1] for p in parts), EMBED), BF16) for parts in plan]
    return pl.pallas_call(
        lambda *refs: pack_body(plan, len(arrays), *refs),
        out_shape=tuple(shapes),
        in_specs=[VMEM] * len(arrays),
        out_specs=(VMEM,) * len(plan),
        compiler_params=PARAMS,
    )(*arrays)


def fold(v):
    return v.reshape(v.shape[0] // 8, 8, 128)


def two_sums(v):
    coarse = 8.0 * jnp.floor(v * 0.125 + 0.5)
    parts = [jnp.sum(p, keepdims=True) for p in (coarse, v - coarse)]
    return jnp.where(lax.broadcasted_iota(jnp.int32, (8, 128), 0) < 4, *parts)


def column_part(logits, t, top):
    top = jnp.max(top, axis=0, keepdims=True)

    def step(i, total):
        tile = logits[pl.ds(pl.multiple_of(i * 128, 128), 128), t * 128 : (t + 1) * 128]
        return total + jnp.sum(fold(jnp.exp2(tile - top)), axis=0)

    total = lax.fori_loop(0, 8, step, jnp.zeros((8, 128), F32), unroll=True)
    return top + LOG2E * jnp.log(jnp.sum(total, axis=0, keepdims=True))


def logits_body(place, scale, *refs):
    images, texts = [refs[i] for i in PLANE_ORDER], refs[4:7]
    logits, row_out, col_out, message, match_out, all_images, all_texts = refs[9:16]
    row_wide = refs[16]
    all_texts[3 * CHUNK : BLOCK - ROWS, :] = refs[7][...]
    all_texts[BLOCK - ROWS :, :] = refs[8][...]
    where = [place[i] for i in range(5)]
    multiplier = scale[0] * LOG2E
    for j in range(3):
        all_texts[j * CHUNK : (j + 1) * CHUNK, :] = texts[j][...]

    def chunk_logits(a):
        all_images[a * CHUNK : (a + 1) * CHUNK, :] = images[a][...]
        for j in range(4):
            text = texts[j][...] if j < 3 else all_texts[3 * CHUNK :, :]
            logits[a * CHUNK : (a + 1) * CHUNK, j * CHUNK : (j + 1) * CHUNK] = multiplier * lax.dot_general(
                images[a][...], text, (((1,), (1,)), ((), ())), preferred_element_type=F32
            )

    chunk_logits(0)
    cols = col_ids(where)
    step = 32
    matched = jnp.zeros((8, 128), F32)
    col_top = [jnp.full((8, 128), -jnp.inf, F32) for _ in range(8)]
    for a in range(4):
        if a < 3:
            chunk_logits(a + 1)
        ids = row_ids(where, a)
        for b in range(4):
            for half in range(ROWS // step):
                at = a * CHUNK + b * ROWS + half * step
                tiles = [logits[at : at + step, t * 128 : (t + 1) * 128] for t in range(8)]
                top = tiles[0]
                for t in range(1, 8):
                    top = jnp.maximum(top, tiles[t])
                top = jnp.max(top, axis=1, keepdims=True)
                mine = ids[b][half * step : (half + 1) * step]
                total = jnp.zeros((step, 128), F32)
                for t in range(8):
                    total += jnp.exp2(tiles[t] - top)
                    col_top[t] = jnp.maximum(col_top[t], jnp.max(fold(tiles[t]), axis=0))
                    hit = jnp.where(mine == cols[t][0:1], tiles[t], 0.0)
                    matched += jnp.sum(fold(hit), axis=0)
                part = top + LOG2E * jnp.log(jnp.sum(total, axis=1, keepdims=True))
                row_wide[at : at + step, :] = jnp.broadcast_to(part, (step, 128))
    matched = two_sums(matched)
    match_out[...] = matched
    message[16:24, :] = matched
    for t in range(8):
        part = column_part(logits, t, col_top[t])
        j, i = t // 2, (t % 2) * 2
        col_out[pl.ds(col_place(where, j, i)[0], 1), :] = part
        col_out[pl.ds(col_place(where, j, i + 1)[0], 1), :] = pltpu.roll(part, 64, 1)
        line = jnp.transpose(row_wide[t * 128 : (t + 1) * 128, :])[0:1]
        row_out[pl.ds(row_place(where, j, i)[0], 1), :] = line
        row_out[pl.ds(row_place(where, j, i + 1)[0], 1), :] = pltpu.roll(line, 64, 1)
    message[:16, :] = jnp.where(where[1] == 0, col_out[...], row_out[...])


def logits_call(place, scale, images, texts):
    return pl.pallas_call(
        logits_body,
        out_shape=(
            jax.ShapeDtypeStruct((BLOCK, BLOCK), F32),
            jax.ShapeDtypeStruct((16, 128), F32),
            jax.ShapeDtypeStruct((16, 128), F32),
            jax.ShapeDtypeStruct((24, 128), F32),
            jax.ShapeDtypeStruct((8, 128), F32),
            ALL,
            ALL,
        ),
        in_specs=[SMEM, SMEM] + [VMEM] * 9,
        out_specs=(VMEM,) * 7,
        scratch_shapes=[pltpu.VMEM((BLOCK, 128), F32)],
        compiler_params=PARAMS,
    )(place, scale, *images, *texts)


def pair_up(rows):
    low = lax.broadcasted_iota(jnp.int32, (1, 128), 1) < ROWS
    pairs = [
        jnp.where(low, rows[i : i + 1], pltpu.roll(rows[i + 1 : i + 2], 64, 1))
        for i in range(0, rows.shape[0], 2)
    ]
    return jnp.concatenate(pairs)


def spread_body(place, row, col, matched, got, out):
    first = place[1] == 0
    mine, other = row[...], got[:16, :]
    top = jnp.maximum(col[...], other)
    both = top + LOG2E * jnp.log(jnp.exp2(col[...] - top) + jnp.exp2(other - top))
    low = pair_up(jnp.where(first, mine, both))
    high = pair_up(other)
    hits = matched[...] + got[16:24, :]
    for i in range(16):
        out[i, :8, :] = low
        out[i, 8:16, :] = high
        out[i, 16:24, :] = hits


def spread_call(place, *parts):
    return pl.pallas_call(
        spread_body,
        out_shape=jax.ShapeDtypeStruct((16, 24, 128), F32),
        in_specs=[SMEM] + [VMEM] * 4,
        out_specs=VMEM,
        compiler_params=PARAMS,
    )(place, *parts)


def join_body(place, got, mine, message):
    first = place[1] == 0
    counts = [jnp.logical_or(first, (place[3] & 1) == i % 2) for i in range(16)]
    parts = [jnp.where(counts[i], got[i, :16, :], -jnp.inf) for i in range(16)]
    top = parts[0]
    for p in parts[1:]:
        top = jnp.maximum(top, p)
    total = jnp.exp2(parts[0] - top)
    for p in parts[1:]:
        total += jnp.exp2(p - top)
    state = top + LOG2E * jnp.log(total)
    low, high = state[:8], state[8:]
    hits = got[0, 16:24, :]
    for i in range(1, 16):
        hits += got[i, 16:24, :]
    share = two_sums(low) + jnp.where(first, two_sums(high) - 2.0 * hits, 0.0)
    for out, pairs in ((mine, low), (message, jnp.where(first, high, low))):
        for i in range(8):
            out[2 * i : 2 * i + 1, :] = pairs[i : i + 1]
            out[2 * i + 1 : 2 * i + 2, :] = pltpu.roll(pairs[i : i + 1], 64, 1)
        out[16:24, :] = share


def join_call(place, got):
    return pl.pallas_call(
        join_body,
        out_shape=(jax.ShapeDtypeStruct((24, 128), F32),) * 2,
        in_specs=[SMEM, VMEM],
        out_specs=(VMEM,) * 2,
        compiler_params=PARAMS,
    )(place, got)


def digits_of(v):
    place = lax.broadcasted_iota(jnp.int32, (16, 128), 0)
    out = jnp.zeros((16, 128), F32)
    for i in range(DIGITS):
        unit = 16.0 ** (7 - i)
        d = jnp.floor(v * (1.0 / unit) + 0.5)
        v = v - d * unit
        out = jnp.where(place == i, d, out)
    return out


def value_of(digits):
    total = digits[0:1] * 16.0**7
    for i in range(1, DIGITS):
        total = total + digits[i : i + 1] * 16.0 ** (7 - i)
    return total


def half_weights(where, logits, at, row_wide, col_lines, weights):
    cols = col_ids(where)
    for a in range(4):
        ids = row_ids(where, a)
        for b in range(4):
            rows = slice(a * CHUNK + b * ROWS, a * CHUNK + (b + 1) * ROWS)
            wide = row_wide[rows, :]
            for t in range(4):
                tile = logits[rows, (at + t) * 128 : (at + t + 1) * 128]
                both = jnp.exp2(tile - wide) + jnp.exp2(tile - col_lines[at + t : at + t + 1, :])
                both = both - jnp.where(ids[b] == cols[at + t][0:1], 1.0, 0.0)
                weights[rows, t * 128 : (t + 1) * 128] = both.astype(BF16)


def high_body(place, scale, logits, mine, other, images, *refs):
    weights, outs, digits, row_wide, col_lines = refs[0], refs[1:4], refs[4], refs[5], refs[6]
    row_lse, col_lse = refs[7:]
    where = [place[i] for i in range(5)]
    first = place[1] == 0
    for i, own in enumerate((first, jnp.logical_not(first))):
        tail = sum(
            digits_of(jnp.where(own, mine[r : r + 1, :], other[r : r + 1, :])) for r in (16, 20)
        ).astype(BF16)
        for e in range(EMBED // 128):
            digits[i * TAIL : (i + 1) * TAIL, e * 128 : (e + 1) * 128] = tail
    row_lse[...] = jnp.where(first, mine[:16, :], other[:16, :]) + 1.0
    col_lse[...] = jnp.where(first, other[:16, :], mine[:16, :]) + 1.0
    lane = lax.broadcasted_iota(jnp.int32, (1, 128), 1)
    for t in range(8):
        j, i = t // 2, (t % 2) * 2
        lo = col_lse[pl.ds(col_place(where, j, i)[0], 1), :]
        hi = col_lse[pl.ds(col_place(where, j, i + 1)[0], 1), :]
        col_lines[t : t + 1, :] = jnp.where(lane < ROWS, lo, pltpu.roll(hi, 64, 1))
        lo = row_lse[pl.ds(row_place(where, j, i)[0], 1), :]
        hi = row_lse[pl.ds(row_place(where, j, i + 1)[0], 1), :]
        line = jnp.where(lane < ROWS, lo, pltpu.roll(hi, 64, 1))
        row_wide[t * 128 : (t + 1) * 128, :] = jnp.transpose(jnp.broadcast_to(line, (128, 128)))
    half_weights(where, logits, 4, row_wide, col_lines, weights)
    text_terms(scale[0], weights, images, 0, outs)


def high_call(place, scale, logits, mine, other, images):
    return pl.pallas_call(
        high_body,
        out_shape=(
            HALF_WEIGHTS,
            PART,
            jax.ShapeDtypeStruct((3 * ROWS, EMBED), BF16),
            jax.ShapeDtypeStruct((ROWS, EMBED), BF16),
            jax.ShapeDtypeStruct((2 * TAIL, EMBED), BF16),
            jax.ShapeDtypeStruct((BLOCK, 128), F32),
            jax.ShapeDtypeStruct((8, 128), F32),
        ),
        in_specs=[SMEM, SMEM] + [VMEM] * 4,
        out_specs=(VMEM,) * 7,
        scratch_shapes=[pltpu.VMEM((16, 128), F32), pltpu.VMEM((16, 128), F32)],
        compiler_params=PARAMS,
    )(place, scale, logits, mine, other, images)


def low_body(place, scale, logits, row_wide, col_lines, images, weights, out):
    half_weights([place[i] for i in range(5)], logits, 0, row_wide, col_lines, weights)
    text_terms(scale[0], weights, images, CHUNK, [out])


def low_call(place, scale, logits, row_wide, col_lines, images):
    return pl.pallas_call(
        low_body,
        out_shape=(HALF_WEIGHTS, PART),
        in_specs=[SMEM, SMEM] + [VMEM] * 4,
        out_specs=(VMEM,) * 2,
        compiler_params=PARAMS,
    )(place, scale, logits, row_wide, col_lines, images)


def text_terms(multiplier, weights, images, at, outs):
    rows = sum(out.shape[0] for out in outs)
    for e in range(5):
        term = multiplier * lax.dot_general(
            weights[:, at : at + rows],
            images[:, e * 256 : (e + 1) * 256],
            (((0,), (0,)), ((), ())),
            preferred_element_type=F32,
        )
        skip = 0
        for out in outs:
            out[:, e * 256 : (e + 1) * 256] = term[skip : skip + out.shape[0]].astype(BF16)
            skip += out.shape[0]


def image_terms(multiplier, weights, texts, at, outs):
    for e in range(5):
        term = multiplier * sum(
            jnp.dot(
                half[at * CHUNK : (at + len(outs)) * CHUNK, :],
                texts[h * BLOCK // 2 : (h + 1) * BLOCK // 2, e * 256 : (e + 1) * 256],
                preferred_element_type=F32,
            )
            for h, half in enumerate(weights)
        )
        for i, out in enumerate(outs):
            out[:CHUNK, e * 256 : (e + 1) * 256] = term[i * CHUNK : (i + 1) * CHUNK].astype(BF16)


def image_body(scale, after, digits, low, high, texts, *outs):
    image_terms(scale[0], (low, high), texts, 1, outs)
    for out in outs:
        out[CHUNK:, :] = digits[TAIL:, :]


def image_call(scale, after, digits, weights, texts):
    return pl.pallas_call(
        image_body,
        out_shape=(jax.ShapeDtypeStruct((CHUNK + TAIL, EMBED), BF16),) * 3,
        in_specs=[SMEM] + [VMEM] * 5,
        out_specs=(VMEM,) * 3,
        compiler_params=PARAMS,
    )(scale, after, digits, *weights, texts)


def rest_body(scale, low, high, images, texts, text_out, image_out):
    text_terms(scale[0], low, images, 0, [text_out])
    image_terms(scale[0], (low, high), texts, 0, [image_out])


def rest_call(scale, weights, images, texts):
    return pl.pallas_call(
        rest_body,
        out_shape=(PART, PART),
        in_specs=[SMEM] + [VMEM] * 4,
        out_specs=(VMEM,) * 2,
        compiler_params=PARAMS,
    )(scale, *weights, images, texts)


def add_rows(refs, rows, terms, out, to):
    for at in range(0, rows, 16):
        total = None
        for i, skip in terms:
            v = refs[i][skip + at : skip + at + 16, :].astype(F32)
            total = v if total is None else total + v
        out[to + at : to + at + 16, :] = total.astype(out.dtype)


def sums_body(n, plan, *refs):
    for parts, out in zip(plan, refs[n:]):
        to = 0
        for rows, terms in parts:
            add_rows(refs, rows, terms, out, to)
            to += rows


def sums(arrays, *plan):
    return pl.pallas_call(
        lambda *refs: sums_body(len(arrays), plan, *refs),
        out_shape=tuple(
            jax.ShapeDtypeStruct((sum(rows for rows, _ in parts), EMBED), BF16) for parts in plan
        ),
        in_specs=[VMEM] * len(arrays),
        out_specs=(VMEM,) * len(plan),
        compiler_params=PARAMS,
    )(*arrays)


def last_body(*refs):
    digits, image_out, text_out, loss_out = refs[6:]
    add_rows(refs, ROWS, [(i, 0) for i in range(4)], image_out, 0)
    add_rows(refs, ROWS, [(4, 0), (5, 0)], text_out, 0)
    total = -digits[:TAIL, :128].astype(F32)
    for r in refs[:6]:
        total += r[ROWS : ROWS + TAIL, :128].astype(F32)
    loss_out[...] = value_of(total)[:, 0:1] * (LN2 / (2.0 * ROWS * 256))


def last_call(shards, texts, digits):
    grad = jax.ShapeDtypeStruct((ROWS, EMBED), BF16)
    return pl.pallas_call(
        last_body,
        out_shape=(grad, grad, jax.ShapeDtypeStruct((1, 1), F32)),
        in_specs=[VMEM] * 7,
        out_specs=(VMEM,) * 3,
        compiler_params=PARAMS,
    )(*shards, *texts, digits)


def local(image_emb, text_emb, logit_scale):
    place = jnp.stack([lax.axis_index(n) for n in AXES]).astype(jnp.int32)

    (text,) = pack([text_emb], ((0, 64),))
    (image,) = pack([image_emb], ((0, 64),))
    (chip,) = pack([text, core_swap(text_emb)], ((0, 64), (1, 64)))
    next_1, next_4 = z_shift(chip, -1), z_shift(text_emb, 4)
    near = [plane_shift(image_emb, k, True) for k in (1, 2, 3)]
    own, text_0 = pack(
        [image] + near + [chip, next_1, next_4],
        ((0, 64), (1, 64), (2, 64), (3, 64)),
        ((4, 128), (5, 128)),
    )
    (side,) = pack([next_1, next_4], ((0, 128), (1, 64)))
    text_1 = z_shift(text_0, -2)
    near = [own] + [plane_shift(own, k, False) for k in PLANE_ORDER[1:]]
    logits, row_part, col_part, message, matched, images, texts = logits_call(
        place, logit_scale, near, [text_0, text_1, core_swap(text_1), core_swap(side), next_4]
    )

    spread = spread_call(place, row_part, col_part, matched, core_swap(message))
    mine, message = join_call(place, exchange(spread, plane_or_ring()))
    high, text_2, text_3, far, digits, row_wide, col_lines = high_call(
        place, logit_scale, logits, mine, core_swap(message), images
    )

    other_1, other_3 = core_swap(text_2), core_swap(text_3)
    low, text_1 = low_call(place, logit_scale, logits, row_wide, col_lines, images)
    weights = low, high
    pairs = sums(
        [text_1, other_1, far, other_3, digits],
        ((256, ((0, 0), (1, 0))), (64, ((2, 0), (3, 128))), (TAIL, ((4, 0),))),
    )[0]
    image_parts = image_call(logit_scale, pairs, digits, weights, texts)
    pairs = z_shift(pairs, 2)
    back = [plane_shift(v, -k, False) for v, k in ((image_parts[k - 1], k) for k in (2, 1, 3))]
    text_0, image_0 = rest_call(logit_scale, weights, images, texts)

    rows_tail = (TAIL, ((2, 320), (3, 0)))
    next_1, mine, next_4 = sums(
        [text_0, other_3, pairs, digits],
        ((128, ((0, 128), (1, 0), (2, 128))), rows_tail),
        ((128, ((0, 0), (2, 0))), rows_tail),
        ((80, ((2, 256),)),),
    )
    next_1, next_4 = z_shift(next_1, 1), z_shift(next_4, 2)
    mine, other = sums(
        [mine, next_1, next_4],
        ((64, ((0, 0), (1, 0), (2, 0))), (TAIL, ((0, 128), (1, 128), (2, 64)))),
        ((64, ((0, 64), (1, 64))), (TAIL, ((0, 128), (1, 128)))),
    )

    cols_tail = (TAIL, ((1, 256), (2, 256), (3, 256), (4, 16)))
    pieces = sums(
        [image_0] + back + [digits],
        *[((64, [(i, 64 * k) for i in range(4)]), cols_tail) for k in range(4)],
    )
    shards = [pieces[0]] + [plane_shift(pieces[k], -k, True) for k in (2, 1, 3)]
    image_grad, text_grad, mean_loss = last_call(shards, [mine, core_swap(other)], digits)
    return mean_loss.reshape(1), image_grad, text_grad


def solution(mesh):
    fine = Mesh(mesh.devices.reshape(4, 2, 2, 4, 4), AXES)
    return jax.shard_map(
        local,
        mesh=fine,
        in_specs=(P(AXES, None), P(("zh", "y", "x", "zl", "core"), None), P()),
        out_specs=(P(), P(AXES, None), P(("zh", "y", "x", "zl", "core"), None)),
        check_vma=False,
    )
```
